32 devices in a mesh: dp: 4 (over z), fsdp: 8 (over y, x, core).
Axes of the slice: x: 2, y: 2, z: 4, core: 2. Of those that a mesh axis runs over, the one named last changes fastest.
Arguments:
- tokens: bfloat16 [8192, 2048], P(('dp', 'fsdp')), may hold values from -6 to 6
- block_counts: int32 [4, 8], P('dp', 'fsdp'), may hold values from 1 to 256, as said below
- decay_rate: float32 [16], replicated, may hold values from 3e-05 to 0.033
- query_weight: bfloat16 [2048, 2048], P(('dp', 'fsdp')), may hold values from -0.125 to 0.125
- key_weight: bfloat16 [2048, 2048], P(('dp', 'fsdp')), may hold values from -0.125 to 0.125
- value_weight: bfloat16 [2048, 2048], P(('dp', 'fsdp')), may hold values from -0.125 to 0.125
- gate_weight: bfloat16 [2048, 2048], P(('dp', 'fsdp')), may hold values from -0.125 to 0.125
- out_weight: bfloat16 [2048, 2048], P(('dp', 'fsdp')), may hold values from -0.125 to 0.125
- first_weight: bfloat16 [2048, 5632], P(('dp', 'fsdp')), may hold values from -0.125 to 0.125
- second_weight: bfloat16 [2048, 5632], P(('dp', 'fsdp')), may hold values from -0.125 to 0.125
- down_weight: bfloat16 [5632, 2048], P(('dp', 'fsdp')), may hold values from -0.078125 to 0.078125
- cotangent: bfloat16 [8192, 2048], P(('dp', 'fsdp')), may hold values from -6 to 6
Outputs:
- block_out: bfloat16 [8192, 2048], P(('dp', 'fsdp'))
- tokens_grad: float32 [8192, 2048], P(('dp', 'fsdp'))
- query_grad: float32 [2048, 2048], P(('dp', 'fsdp'))
- key_grad: float32 [2048, 2048], P(('dp', 'fsdp'))
- value_grad: float32 [2048, 2048], P(('dp', 'fsdp'))
- gate_grad: float32 [2048, 2048], P(('dp', 'fsdp'))
- out_grad: float32 [2048, 2048], P(('dp', 'fsdp'))
- first_grad: float32 [2048, 5632], P(('dp', 'fsdp'))
- second_grad: float32 [2048, 5632], P(('dp', 'fsdp'))
- down_grad: float32 [5632, 2048], P(('dp', 'fsdp'))
The draws below stay inside these ranges and needn't reach their ends.
Inputs may be any that keep to these rules, and one draw needn't show every extreme that they name: `block_counts`: in each row, blocks are full of live slots except the last block of each sequence, which holds 1 to 255 live slots; the last block of a row ends a sequence; every sequence covers 4 blocks or more, and some row holds a single sequence.
All inputs are finite; a program needn't handle non-finite values.
Results may differ from the reference program's by a relative error of at most 0.015.
Values may be sent and summed in bfloat16 or wider, within the bound.
A program may use at most 352 MiB of HBM per device.

```python
import math
from functools import partial
import jax
import jax.numpy as jnp
from jax import lax

D = 2048
HEADS = 16
HEAD_DIM = 128
FF = 5632
TOK_DEV = 256
MIN_BLOCKS = 4
SEQS = 4
SEQ_BLOCKS = 8
TOKENS = 8192


def draw_block_counts(key, part):
    key = jax.random.fold_in(key, 7)
    key_cut, key_tail, key_whole = jax.random.split(key, 3)
    cut_flags = jax.random.randint(key_cut, (SEQ_BLOCKS, SEQS), 0, 3) == 0
    whole_row = jax.random.randint(key_whole, (), 0, SEQS)
    row_index = lax.iota(jnp.int32, SEQS)
    densest_row = (whole_row + 1) % SEQS

    def layout_step(carry, item):
        run_blocks = carry
        block_place, cut_here = item
        allowed = (block_place > 0) & (run_blocks >= MIN_BLOCKS) & (SEQ_BLOCKS - block_place >= MIN_BLOCKS)
        begins = allowed & (cut_here | (row_index == densest_row)) & (row_index != whole_row)
        run_blocks = jnp.where(begins, 1, run_blocks + 1)
        return (run_blocks, begins)
    initial = jnp.zeros((SEQS,), jnp.int32)
    finished, begin_flags = lax.scan(layout_step, initial, (lax.iota(jnp.int32, SEQ_BLOCKS), cut_flags))
    begins = begin_flags.T
    is_last = jnp.concatenate([begins[:, 1:], jnp.ones((SEQS, 1), bool)], axis=1)
    tail_count = jax.random.randint(key_tail, (SEQS, SEQ_BLOCKS), 1, TOK_DEV)
    block_index = lax.iota(jnp.int32, SEQ_BLOCKS)
    single_slot = (row_index[:, None] == whole_row) & (block_index[None, :] == SEQ_BLOCKS - 1)
    tail_count = jnp.where(single_slot, 1, tail_count)
    counts = jnp.where(is_last, tail_count, TOK_DEV)
    return counts.astype(jnp.int32)


def shard_levels(stream_key, dims, cuts, low, high):
    def one(dim, blocks):
        draws = jax.random.uniform(jax.random.fold_in(jax.random.fold_in(stream_key, 6), dim), (blocks,), jnp.float32, low / len(cuts), high / len(cuts))
        return jnp.repeat(jnp.exp(draws), dims[dim] // blocks).reshape((-1,) + (1,) * (len(dims) - dim - 1))

    loudness = one(*cuts[0])
    for cut in cuts[1:]:
        loudness = loudness * one(*cut)
    return loudness


def noise(rng, dims, spread, limit, pieces=(), dtype=jnp.bfloat16):
    array = spread * jax.random.normal(rng, dims, jnp.float32)
    if pieces:
        array = array * shard_levels(rng, dims, pieces, -0.22, 0.18)
    return jnp.clip(array, -limit, limit).astype(dtype)


def setup_inputs(seed: int = 0) -> dict:
    arg_keys = jax.random.split(jax.random.key(seed), 13)
    tokens = noise(arg_keys[0], (TOKENS, D), 1.0, 6.0, ((0, 32),))
    block_counts = draw_block_counts(jax.random.fold_in(arg_keys[12], 71), 0)
    decay_rate = jnp.clip(jnp.exp(jax.random.uniform(arg_keys[2], (HEADS,), jnp.float32, math.log(2.9999999242136255e-05), math.log(0.033))), 2.9999999242136255e-05, 0.033)
    query_weight = noise(arg_keys[3], (D, D), D ** -0.5, 0.125, ((0, 32),))
    key_weight = noise(arg_keys[4], (D, D), D ** -0.5, 0.125, ((0, 32),))
    value_weight = noise(arg_keys[5], (D, D), D ** -0.5, 0.125, ((0, 32),))
    gate_weight = noise(arg_keys[6], (D, D), D ** -0.5, 0.125, ((0, 32),))
    out_weight = noise(arg_keys[7], (D, D), D ** -0.5, 0.125, ((0, 32),))
    first_weight = noise(arg_keys[8], (D, FF), D ** -0.5, 0.125, ((0, 32),))
    second_weight = noise(arg_keys[9], (D, FF), D ** -0.5, 0.125, ((0, 32),))
    down_weight = noise(arg_keys[10], (FF, D), FF ** -0.5, 0.078125, ((0, 32),))
    cotangent = noise(arg_keys[11], (TOKENS, D), 1.0, 6.0, ((0, 32),))
    return {"tokens": tokens, "block_counts": block_counts, "decay_rate": decay_rate, "query_weight": query_weight, "key_weight": key_weight, "value_weight": value_weight, "gate_weight": gate_weight, "out_weight": out_weight, "first_weight": first_weight, "second_weight": second_weight, "down_weight": down_weight, "cotangent": cotangent}


EPS = 1e-06
HIGH = lax.Precision.HIGHEST

@jax.custom_vjp
def low(v):
    return lax.optimization_barrier(v.astype(jnp.bfloat16)).astype(jnp.float32)

@jax.custom_vjp
def low_back(v):
    return v

def low_keep(v):
    return (low(v), None)

def low_pass(kept, grad):
    return (grad,)

def back_keep(v):
    return (v, None)

def back_low(kept, grad):
    return (low(grad),)
low.defvjp(low_keep, low_pass)
low_back.defvjp(back_keep, back_low)

def simple_norm(value):
    return value * lax.rsqrt(lax.optimization_barrier(jnp.mean(value * value, axis=-1, keepdims=True)) + EPS)

def matmul(left, right):
    return jnp.dot(left, right, precision=HIGH)

def decay_tables(count, rates, rows):
    pos = lax.iota(jnp.int32, rows)
    live = pos < count
    keep = (pos[:, None] >= pos[None, :]) & live[:, None] & live[None, :]
    spacing = jnp.where(keep, (pos[:, None] - pos[None, :]).astype(jnp.float32), 0.0)
    mask = jnp.where(keep[None], jnp.exp(-rates[:, None, None] * spacing[None]), 0.0)
    ahead = jnp.where(live[:, None], jnp.exp(-rates[None, :] * (count - pos)[:, None].astype(jnp.float32)), 0.0)
    behind = jnp.where(live[:, None], jnp.exp(-rates[None, :] * pos[:, None].astype(jnp.float32)), 0.0)
    fade = jnp.exp(-rates * count.astype(jnp.float32))
    return (mask, ahead, behind, fade)

def sequence_mix(rates, packed):
    query, keys, value, counts = packed
    rows = query.shape[1]

    def block_terms(block_q, block_k, block_v, count):
        mask, ahead, behind, fade = decay_tables(count, rates, rows)
        raw = low_back(jnp.einsum('ihe,jhe->hij', block_q, block_k, precision=HIGH))
        probs = low(raw * mask)
        intra = jnp.einsum('hij,jhe->ihe', probs, block_v, precision=HIGH)
        local = jnp.einsum('jhe,jhf->hef', block_k, block_v * ahead[:, :, None], precision=HIGH)
        return (intra, local, behind, fade)
    intra, local, behind, fade = jax.vmap(block_terms)(query, keys, value, counts)
    starts = jnp.concatenate([jnp.ones((1,), bool), counts[:-1] < rows])

    def carry_step(state, item):
        local_b, fade_b, start_b = item
        state_in = jnp.where(start_b, jnp.zeros_like(state), state)
        return (fade_b[:, None, None] * state_in + local_b, state_in)
    start = jnp.zeros(local.shape[1:], jnp.float32)
    last, entering = lax.scan(carry_step, start, (local, fade, starts))
    inter = behind[..., None] * jnp.einsum('bihe,bhef->bihf', query, entering, precision=HIGH)
    return intra + inter

def reference(tokens, block_counts, decay_rate, query_weight, key_weight, value_weight, gate_weight, out_weight, first_weight, second_weight, down_weight, cotangent):
    shape = (SEQS, SEQ_BLOCKS, TOK_DEV, HEADS, HEAD_DIM)

    def forward(inputs, w_query, w_key, w_value, w_gate, w_out, w_first, w_second, w_down):
        hidden = low(simple_norm(inputs))
        q_pre = low_back(matmul(hidden, w_query))
        k_pre = low_back(matmul(hidden, w_key))
        value = low(low_back(matmul(hidden, w_value)))
        gate = low_back(matmul(hidden, w_gate))
        query = low(jax.nn.silu(q_pre))
        keys = low(jax.nn.silu(k_pre))
        heads_out = lax.map(jax.checkpoint(partial(sequence_mix, decay_rate)), (query.reshape(shape), keys.reshape(shape), value.reshape(shape), block_counts))
        attn = low_back(heads_out.reshape(TOKENS, D))
        mixed = low(simple_norm(attn) * gate)
        middle = inputs + low_back(matmul(mixed, w_out))
        mid = low(simple_norm(middle))
        first = low_back(matmul(mid, w_first))
        second = low_back(matmul(mid, w_second))
        product = low(first * second)
        return middle + low_back(matmul(product, w_down))
    result, pull = jax.vjp(forward, tokens.astype(jnp.float32), query_weight.astype(jnp.float32), key_weight.astype(jnp.float32), value_weight.astype(jnp.float32), gate_weight.astype(jnp.float32), out_weight.astype(jnp.float32), first_weight.astype(jnp.float32), second_weight.astype(jnp.float32), down_weight.astype(jnp.float32))
    grads = pull(cotangent.astype(jnp.float32))
    return (result.astype(jnp.bfloat16), grads[0], grads[1], grads[2], grads[3], grads[4], grads[5], grads[6], grads[7], grads[8])
```

```python
import jax
import jax.numpy as jnp
from jax import lax
from jax.sharding import PartitionSpec as P

HEADS = 16
HEAD_DIM = 128


EPS = 1e-06
HIGH = lax.Precision.HIGHEST


def carried_in(part, axis, combine, identity):
    place = lax.axis_index(axis)
    gathered = jax.tree.map(lambda a: lax.all_gather(a, axis), part)
    state = jax.tree.map(lambda a, e: jnp.zeros_like(a) + jnp.asarray(e, a.dtype), part, identity)

    def carried_one(lap, state):
        return combine(
            state, jax.tree.map(lambda a: lax.dynamic_index_in_dim(a, lap, 0, False), gathered)
        )

    return lax.fori_loop(0, place, carried_one, state)


def prefix_2(value, axis, join, neutral):
    count = lax.axis_size(axis)
    place = lax.axis_index(axis)
    ahead = count - 1 - place
    gathered = jax.tree.map(
        lambda a, kind: lax.all_gather(a.astype(kind), axis), value, (jnp.bfloat16, jnp.bfloat16)
    )
    state = jax.tree.map(lambda a, e: jnp.zeros_like(a) + jnp.asarray(e, a.dtype), value, neutral)

    def prefix_one(lap, state):
        source = count - 1 - lap
        return join(
            state,
            jax.tree.map(
                lambda a, own: lax.dynamic_index_in_dim(a, source, 0, False).astype(own.dtype),
                gathered,
                value,
            ),
        )

    return lax.fori_loop(0, ahead, prefix_one, state)


def normed(value):
    scale = lax.rsqrt(jnp.mean(value * value, axis=-1, keepdims=True) + EPS)
    return (value * scale, scale)


def norm_back(value, scale, grad):
    inner = jnp.mean(grad * value, axis=-1, keepdims=True)
    return scale * (grad - value * scale * scale * inner)


def silu_slope(value):
    sig = jax.nn.sigmoid(value)
    return sig * (1.0 + value * (1.0 - sig))


def chain_step(earlier, later):
    e_fade, e_state = earlier
    l_fade, l_state = later
    return (l_fade * e_fade, l_fade[:, None, None] * e_state + l_state)


def matmul(left, right):
    return jnp.dot(left, right, preferred_element_type=jnp.float32)


def matmul_tn(left, right):
    return lax.dot_general(
        left, right, (((0,), (0,)), ((), ())), preferred_element_type=jnp.float32
    )


def matmul_nt(left, right):
    return lax.dot_general(
        left, right, (((1,), (1,)), ((), ())), preferred_element_type=jnp.float32
    )


def decay_tables(count, rates, rows):
    pos = lax.iota(jnp.int32, rows)
    live = pos < count
    keep = (pos[:, None] >= pos[None, :]) & live[:, None] & live[None, :]
    spacing = jnp.where(keep, (pos[:, None] - pos[None, :]).astype(jnp.float32), 0.0)
    mask = jnp.where(keep[None], jnp.exp(-rates[:, None, None] * spacing[None]), 0.0)
    ahead = jnp.where(
        live[:, None], jnp.exp(-rates[None, :] * (count - pos)[:, None].astype(jnp.float32)), 0.0
    )
    behind = jnp.where(
        live[:, None], jnp.exp(-rates[None, :] * pos[:, None].astype(jnp.float32)), 0.0
    )
    fade = jnp.exp(-rates * count.astype(jnp.float32))
    return (mask, ahead, behind, fade)


def shards(
    tokens,
    block_counts,
    decay_rate,
    query_weight,
    key_weight,
    value_weight,
    gate_weight,
    out_weight,
    first_weight,
    second_weight,
    down_weight,
    cotangent,
):
    rows = tokens.shape[0]
    gathered = (
        lax.all_gather(query_weight, ("dp", "fsdp"), axis=0, tiled=True),
        lax.all_gather(key_weight, ("dp", "fsdp"), axis=0, tiled=True),
        lax.all_gather(value_weight, ("dp", "fsdp"), axis=0, tiled=True),
        lax.all_gather(gate_weight, ("dp", "fsdp"), axis=0, tiled=True),
        lax.all_gather(out_weight, ("dp", "fsdp"), axis=0, tiled=True),
        lax.all_gather(first_weight, ("dp", "fsdp"), axis=0, tiled=True),
        lax.all_gather(second_weight, ("dp", "fsdp"), axis=0, tiled=True),
        lax.all_gather(down_weight, ("dp", "fsdp"), axis=0, tiled=True),
    )
    w_query, w_key, w_value, w_gate, w_out, w_first, w_second, w_down = gathered
    count = block_counts[0, 0]
    closes = count < rows
    mask, ahead, behind, fade = decay_tables(count, decay_rate, rows)
    passing = jnp.where(closes, 0.0, fade)
    inputs = tokens.astype(jnp.float32)
    in_normed, in_scale = normed(inputs)
    hidden = in_normed.astype(jnp.bfloat16)
    q_pre = matmul(hidden, w_query)
    k_pre = matmul(hidden, w_key)
    value = matmul(hidden, w_value).astype(jnp.bfloat16)
    gate = matmul(hidden, w_gate)
    query = jax.nn.silu(q_pre).astype(jnp.bfloat16)
    keys = jax.nn.silu(k_pre).astype(jnp.bfloat16)
    query_heads = query.reshape(rows, HEADS, HEAD_DIM)
    key_heads = keys.reshape(rows, HEADS, HEAD_DIM)
    value_heads = value.reshape(rows, HEADS, HEAD_DIM)
    query_wide = query_heads.astype(jnp.float32)
    key_wide = key_heads.astype(jnp.float32)
    value_ahead = value_heads.astype(jnp.float32) * ahead[:, :, None]
    raw = jnp.einsum("ihe,jhe->hij", query_heads, key_heads, preferred_element_type=jnp.float32)
    probs = (raw * mask).astype(jnp.bfloat16)
    intra = jnp.einsum("hij,jhe->ihe", probs, value_heads, preferred_element_type=jnp.float32)
    local = jnp.einsum("jhe,jhf->hef", key_wide, value_ahead, precision=HIGH)
    local_sent = jnp.where(closes, 0.0, local)
    prefix = carried_in(
        (passing, local_sent), "fsdp", chain_step, (jnp.ones_like(fade), jnp.zeros_like(local))
    )
    entering = prefix[1]
    inter = behind[:, :, None] * jnp.einsum("ihe,hef->ihf", query_wide, entering, precision=HIGH)
    attn = (intra + inter).reshape(rows, HEADS * HEAD_DIM)
    attn_normed, attn_scale = normed(attn)
    mixed = (attn_normed * gate).astype(jnp.bfloat16)
    middle = inputs + matmul(mixed, w_out)
    mid_normed, mid_scale = normed(middle)
    mid = mid_normed.astype(jnp.bfloat16)
    first = matmul(mid, w_first)
    second = matmul(mid, w_second)
    product = (first * second).astype(jnp.bfloat16)
    block_out = (middle + matmul(product, w_down)).astype(jnp.bfloat16)
    w_first, w_second, w_down = (
        lax.all_gather(first_weight, ("dp", "fsdp"), axis=0, tiled=True),
        lax.all_gather(second_weight, ("dp", "fsdp"), axis=0, tiled=True),
        lax.all_gather(down_weight, ("dp", "fsdp"), axis=0, tiled=True),
    )
    grad_product = matmul_nt(cotangent, w_down)
    grad_first = (grad_product * second).astype(jnp.bfloat16)
    grad_second = (grad_product * first).astype(jnp.bfloat16)
    grad_mid = matmul_nt(grad_first, w_first) + matmul_nt(grad_second, w_second)
    grad_middle = cotangent.astype(jnp.float32) + norm_back(middle, mid_scale, grad_mid)

    def scattered(left, right, after):
        left, _ = lax.optimization_barrier((left, after))
        term = matmul_tn(left, right)
        return lax.psum_scatter(term, ("dp", "fsdp"), scatter_dimension=0, tiled=True)

    down_grad = scattered(product, cotangent, grad_middle)
    first_grad = scattered(mid, grad_first, down_grad)
    second_grad = scattered(mid, grad_second, first_grad)
    grad_middle, _ = lax.optimization_barrier((grad_middle, second_grad))
    w_query, w_key, w_value, w_gate, w_out = (
        lax.all_gather(query_weight, ("dp", "fsdp"), axis=0, tiled=True),
        lax.all_gather(key_weight, ("dp", "fsdp"), axis=0, tiled=True),
        lax.all_gather(value_weight, ("dp", "fsdp"), axis=0, tiled=True),
        lax.all_gather(gate_weight, ("dp", "fsdp"), axis=0, tiled=True),
        lax.all_gather(out_weight, ("dp", "fsdp"), axis=0, tiled=True),
    )
    grad_mid_low = grad_middle.astype(jnp.bfloat16)
    out_term = matmul_tn(mixed, grad_mid_low)
    grad_mixed = matmul_nt(grad_mid_low, w_out)
    grad_gate = (grad_mixed * attn_normed).astype(jnp.bfloat16)
    grad_attn = norm_back(attn, attn_scale, grad_mixed * gate).astype(jnp.bfloat16)
    grad_heads = grad_attn.reshape(rows, HEADS, HEAD_DIM)
    grad_heads_wide = grad_heads.astype(jnp.float32) * behind[:, :, None]
    grad_probs = jnp.einsum(
        "ihe,jhe->hij", grad_heads, value_heads, preferred_element_type=jnp.float32
    )
    grad_raw = (grad_probs * mask).astype(jnp.bfloat16)
    grad_entering = jnp.einsum("ihe,ihf->hef", query_wide, grad_heads_wide, precision=HIGH)
    suffix = prefix_2(
        (passing, grad_entering),
        "fsdp",
        chain_step,
        (jnp.ones_like(fade), jnp.zeros_like(grad_entering)),
    )
    grad_leaving = jnp.where(closes, 0.0, suffix[1])
    grad_query = jnp.einsum("hij,jhe->ihe", grad_raw, key_heads, preferred_element_type=jnp.float32)
    grad_query = grad_query + jnp.einsum("ihf,hef->ihe", grad_heads_wide, entering, precision=HIGH)
    grad_keys = jnp.einsum(
        "hij,ihe->jhe", grad_raw, query_heads, preferred_element_type=jnp.float32
    )
    grad_keys = grad_keys + jnp.einsum("hef,jhf->jhe", grad_leaving, value_ahead, precision=HIGH)
    grad_value = jnp.einsum("hij,ihe->jhe", probs, grad_heads, preferred_element_type=jnp.float32)
    grad_value = grad_value + ahead[:, :, None] * jnp.einsum(
        "hef,jhe->jhf", grad_leaving, key_wide, precision=HIGH
    )
    width = HEADS * HEAD_DIM
    grad_q_pre = (grad_query.reshape(rows, width) * silu_slope(q_pre)).astype(jnp.bfloat16)
    grad_k_pre = (grad_keys.reshape(rows, width) * silu_slope(k_pre)).astype(jnp.bfloat16)
    grad_v = grad_value.reshape(rows, width).astype(jnp.bfloat16)
    query_term = matmul_tn(hidden, grad_q_pre)
    key_term = matmul_tn(hidden, grad_k_pre)
    value_term = matmul_tn(hidden, grad_v)
    gate_term = matmul_tn(hidden, grad_gate)
    grad_hidden = matmul_nt(grad_q_pre, w_query) + matmul_nt(grad_k_pre, w_key)
    grad_hidden = grad_hidden + matmul_nt(grad_v, w_value) + matmul_nt(grad_gate, w_gate)
    tokens_grad = grad_middle + norm_back(inputs, in_scale, grad_hidden)
    query_grad, key_grad, value_grad, gate_grad, out_grad = (
        lax.psum_scatter(query_term, ("dp", "fsdp"), scatter_dimension=0, tiled=True),
        lax.psum_scatter(key_term, ("dp", "fsdp"), scatter_dimension=0, tiled=True),
        lax.psum_scatter(value_term, ("dp", "fsdp"), scatter_dimension=0, tiled=True),
        lax.psum_scatter(gate_term, ("dp", "fsdp"), scatter_dimension=0, tiled=True),
        lax.psum_scatter(out_term, ("dp", "fsdp"), scatter_dimension=0, tiled=True),
    )
    return (
        block_out,
        tokens_grad,
        query_grad,
        key_grad,
        value_grad,
        gate_grad,
        out_grad,
        first_grad,
        second_grad,
        down_grad,
    )


def fast_plan(
    tokens, block_counts, decay_rate, query_weight, key_weight, value_weight, gate_weight,
    out_weight, first_weight, second_weight, down_weight, cotangent,
):
    rows, width = tokens.shape
    nz = lax.axis_size("dp")
    nf = lax.axis_size("fsdp")
    chips = nf // 2
    plane = lax.axis_index("fsdp")
    chip, core = plane // 2, plane % 2
    bf = jnp.bfloat16
    groups = HEADS // chips
    half = groups // 2
    own_heads = chips * (half * core + jnp.arange(half)) + chip

    def columns(weight):
        r = weight.shape[0]
        w = weight.reshape(r, 2, half, chips, HEAD_DIM).transpose(3, 1, 0, 2, 4)
        w = w.reshape(nf, r, half * HEAD_DIM)
        w = lax.all_to_all(w, "fsdp", 0, 0, tiled=True).reshape(nf * r, half * HEAD_DIM)
        return lax.all_gather(w, "dp", axis=0, tiled=True)

    def columns_ff(weight):
        r, n = weight.shape
        w = weight.reshape(r, nz, nf, n // (nz * nf)).transpose(2, 0, 1, 3).reshape(nf, r, n // nf)
        w = lax.all_to_all(w, "fsdp", 0, 0, tiled=True).reshape(nf * r, n // nf)
        return lax.all_gather(w, "dp", axis=0, tiled=True)

    swap = [(i, i ^ 1) for i in range(nf)]

    def cross(x):
        keep = lax.dynamic_slice_in_dim(x, core * half, half, 0)
        send = lax.dynamic_slice_in_dim(x, (1 - core) * half, half, 0)
        got = lax.ppermute(send, "fsdp", swap)
        lo = jnp.where(core == 0, keep, got)
        hi = jnp.where(core == 0, got, keep)
        return jnp.stack([lo, hi], axis=1)

    def uncross(x):
        keep = lax.dynamic_index_in_dim(x, core, 1, False)
        send = lax.dynamic_index_in_dim(x, 1 - core, 1, False)
        got = lax.ppermute(send, "fsdp", swap)
        lo = jnp.where(core == 0, keep, got)
        hi = jnp.where(core == 0, got, keep)
        return jnp.concatenate([lo, hi], axis=0)

    wq, wk, wv, wg = (columns(w) for w in (query_weight, key_weight, value_weight, gate_weight))
    wo = cross(lax.all_gather(out_weight, "dp", axis=0)).reshape(half * HEAD_DIM, width)
    w1, w2 = columns_ff(first_weight), columns_ff(second_weight)
    wd = lax.all_gather(down_weight, "dp", axis=0, tiled=True)

    counts = lax.all_gather(block_counts[0, 0], "fsdp")
    rates = decay_rate[own_heads]
    pos = lax.iota(jnp.int32, rows)
    gap = (pos[:, None] - pos[None, :]).astype(jnp.float32)
    base = jnp.where(gap >= 0, jnp.exp(-rates[:, None, None] * jnp.maximum(gap, 0.0)), 0.0)
    live = pos[None, :] < counts[:, None]
    mask = base[None] * live[:, None, :, None]
    left = (counts[:, None] - pos[None, :]).astype(jnp.float32)
    ahead = jnp.where(live[..., None], jnp.exp(-rates * left[..., None]), 0.0)
    behind = jnp.where(live[..., None], jnp.exp(-rates * pos[None, :, None].astype(jnp.float32)), 0.0)
    fade = jnp.exp(-rates[None] * counts[:, None].astype(jnp.float32))
    closes = counts < rows

    inputs = tokens.astype(jnp.float32)
    in_normed, in_scale = normed(inputs)
    hidden = lax.all_gather(in_normed.astype(bf), "fsdp", axis=0, tiled=True)
    cot = lax.all_gather(cotangent, "fsdp", axis=0, tiled=True)
    shape = (nf, rows, half, HEAD_DIM)
    q_pre, k_pre = matmul(hidden, wq), matmul(hidden, wk)
    value = matmul(hidden, wv).astype(bf).reshape(shape)
    gate = matmul(hidden, wg)
    query = jax.nn.silu(q_pre).astype(bf).reshape(shape)
    keys = jax.nn.silu(k_pre).astype(bf).reshape(shape)
    q32, k32 = query.astype(jnp.float32), keys.astype(jnp.float32)
    value_ahead = value.astype(jnp.float32) * ahead[..., None]
    raw = jnp.einsum("bihe,bjhe->bhij", query, keys, preferred_element_type=jnp.float32)
    probs = (raw * mask).astype(bf)
    intra = jnp.einsum("bhij,bjhe->bihe", probs, value, preferred_element_type=jnp.float32)
    local = jnp.einsum("bjhe,bjhf->bhef", k32, value_ahead, precision=HIGH)
    state = jnp.zeros_like(local[0])
    entering = []
    for b in range(nf):
        entering.append(state)
        state = jnp.where(closes[b], 0.0, fade[b][:, None, None] * state + local[b])
    entering = jnp.stack(entering)
    inter = behind[..., None] * jnp.einsum("bihe,bhef->bihf", q32, entering, precision=HIGH)
    attn = (intra + inter).reshape(nf * rows, half * HEAD_DIM)
    squares = lax.psum(jnp.sum(attn * attn, axis=-1), "fsdp")
    scale = lax.rsqrt(squares / width + EPS)[:, None]
    attn_normed = attn * scale
    mixed = (attn_normed * gate).astype(bf)
    out_part = matmul(mixed, wo)
    out_own = lax.psum_scatter(out_part.astype(bf), "fsdp", scatter_dimension=0, tiled=True).astype(jnp.float32)
    middle = inputs + out_own
    mid_normed, mid_scale = normed(middle)
    mid = lax.all_gather(mid_normed.astype(bf), "fsdp", axis=0, tiled=True)
    first, second = matmul(mid, w1), matmul(mid, w2)
    product = (first * second).astype(bf)
    down_part = matmul(product, wd).astype(bf)
    block_out = (middle + lax.psum_scatter(down_part, "fsdp", scatter_dimension=0, tiled=True).astype(jnp.float32)).astype(bf)

    down_term = matmul_tn(product, cot)
    grad_product = matmul_nt(cot, wd)
    grad_first = (grad_product * second).astype(bf)
    grad_second = (grad_product * first).astype(bf)
    first_term = matmul_tn(mid, grad_first)
    second_term = matmul_tn(mid, grad_second)
    grad_mid = (matmul_nt(grad_first, w1) + matmul_nt(grad_second, w2)).astype(bf)
    grad_mid = lax.psum_scatter(grad_mid, "fsdp", scatter_dimension=0, tiled=True).astype(jnp.float32)
    grad_middle = cotangent.astype(jnp.float32) + norm_back(middle, mid_scale, grad_mid)
    low = grad_middle.astype(bf)
    inner = jnp.sum(low.astype(jnp.float32) * out_own, axis=-1)
    inner = lax.all_gather(inner, "fsdp", axis=0, tiled=True)[:, None] / (scale * width)
    low = lax.all_gather(low, "fsdp", axis=0, tiled=True)
    out_term = matmul_tn(mixed, low)
    grad_mixed = matmul_nt(low, wo)
    grad_gate = (grad_mixed * attn_normed).astype(bf)
    grad_attn = (scale * (grad_mixed * gate - attn * scale * scale * inner)).astype(bf)
    g = grad_attn.reshape(shape)
    g32 = g.astype(jnp.float32) * behind[..., None]
    grad_probs = jnp.einsum("bihe,bjhe->bhij", g, value, preferred_element_type=jnp.float32)
    grad_raw = (grad_probs * mask).astype(bf)
    grad_entering = jnp.einsum("bihe,bihf->bhef", q32, g32, precision=HIGH)
    state = jnp.zeros_like(grad_entering[0])
    leaving = [None] * nf
    for b in reversed(range(nf)):
        leaving[b] = jnp.where(closes[b], 0.0, state)
        state = grad_entering[b] + fade[b][:, None, None] * leaving[b]
    leaving = jnp.stack(leaving)
    grad_query = jnp.einsum("bhij,bjhe->bihe", grad_raw, keys, preferred_element_type=jnp.float32)
    grad_query += jnp.einsum("bihf,bhef->bihe", g32, entering, precision=HIGH)
    grad_keys = jnp.einsum("bhij,bihe->bjhe", grad_raw, query, preferred_element_type=jnp.float32)
    grad_keys += jnp.einsum("bhef,bjhf->bjhe", leaving, value_ahead, precision=HIGH)
    grad_value = jnp.einsum("bhij,bihe->bjhe", probs, g, preferred_element_type=jnp.float32)
    grad_value += ahead[..., None] * jnp.einsum("bhef,bjhe->bjhf", leaving, k32, precision=HIGH)
    flat = (nf * rows, half * HEAD_DIM)
    gq = (grad_query.reshape(flat) * silu_slope(q_pre)).astype(bf)
    gk = (grad_keys.reshape(flat) * silu_slope(k_pre)).astype(bf)
    gv = grad_value.reshape(flat).astype(bf)
    grad_hidden = matmul_nt(gq, wq) + matmul_nt(gk, wk) + matmul_nt(gv, wv) + matmul_nt(grad_gate, wg)
    grad_hidden = lax.psum_scatter(grad_hidden.astype(bf), "fsdp", scatter_dimension=0, tiled=True).astype(jnp.float32)
    tokens_grad = grad_middle + norm_back(inputs, in_scale, grad_hidden)

    def columns_back(term):
        t = lax.psum_scatter(term.astype(bf), "dp", scatter_dimension=0, tiled=True)
        t = t.reshape(nf, -1, half * HEAD_DIM)
        r = t.shape[1]
        t = lax.all_to_all(t, "fsdp", 0, 0, tiled=True)
        t = t.reshape(chips, 2, r, half, HEAD_DIM).transpose(2, 1, 3, 0, 4)
        return t.reshape(r, width).astype(jnp.float32)

    def columns_ff_back(term):
        t = lax.psum_scatter(term.astype(bf), "dp", scatter_dimension=0, tiled=True)
        n = t.shape[1]
        t = t.reshape(nf, -1, n)
        r = t.shape[1]
        t = lax.all_to_all(t, "fsdp", 0, 0, tiled=True)
        t = t.reshape(nf, r, nz, n // nz).transpose(1, 2, 0, 3)
        return t.reshape(r, n * nf).astype(jnp.float32)

    grads = [columns_back(matmul_tn(hidden, g)) for g in (gq, gk, gv, grad_gate)]
    out_term = uncross(out_term.astype(bf).reshape(half, 2, -1, width))
    out_grad = lax.psum_scatter(out_term, "dp", scatter_dimension=0, tiled=False).astype(jnp.float32)
    first_grad = columns_ff_back(first_term)
    second_grad = columns_ff_back(second_term)
    down_grad = lax.psum_scatter(down_term.astype(bf), "dp", scatter_dimension=0, tiled=True).astype(jnp.float32)
    return (block_out, tokens_grad, *grads, out_grad, first_grad, second_grad, down_grad)


def fits(mesh):
    return mesh.shape["dp"] == 4 and mesh.shape["fsdp"] == 8


def solution(mesh):
    return jax.shard_map(
        fast_plan if fits(mesh) else shards,
        mesh=mesh,
        in_specs=(
            P(("dp", "fsdp"), None),
            P("dp", "fsdp"),
            P(),
            P(("dp", "fsdp"), None),
            P(("dp", "fsdp"), None),
            P(("dp", "fsdp"), None),
            P(("dp", "fsdp"), None),
            P(("dp", "fsdp"), None),
            P(("dp", "fsdp"), None),
            P(("dp", "fsdp"), None),
            P(("dp", "fsdp"), None),
            P(("dp", "fsdp"), None),
        ),
        out_specs=(
            P(("dp", "fsdp"), None),
            P(("dp", "fsdp"), None),
            P(("dp", "fsdp"), None),
            P(("dp", "fsdp"), None),
            P(("dp", "fsdp"), None),
            P(("dp", "fsdp"), None),
            P(("dp", "fsdp"), None),
            P(("dp", "fsdp"), None),
            P(("dp", "fsdp"), None),
            P(("dp", "fsdp"), None),
        ),
        check_vma=False,
    )
```

```python
import functools

import jax
import jax.numpy as jnp
from jax import lax
from jax.experimental import pallas as pl
from jax.experimental.pallas import tpu as pltpu
from jax.sharding import PartitionSpec as P

HEADS = 16
HEAD_DIM = 128


EPS = 1e-06
HIGH = lax.Precision.HIGHEST


def carried_in(part, axis, combine, identity):
    place = lax.axis_index(axis)
    gathered = jax.tree.map(lambda a: lax.all_gather(a, axis), part)
    state = jax.tree.map(lambda a, e: jnp.zeros_like(a) + jnp.asarray(e, a.dtype), part, identity)

    def carried_one(lap, state):
        return combine(
            state, jax.tree.map(lambda a: lax.dynamic_index_in_dim(a, lap, 0, False), gathered)
        )

    return lax.fori_loop(0, place, carried_one, state)


def prefix_2(value, axis, join, neutral):
    count = lax.axis_size(axis)
    place = lax.axis_index(axis)
    ahead = count - 1 - place
    gathered = jax.tree.map(
        lambda a, kind: lax.all_gather(a.astype(kind), axis), value, (jnp.bfloat16, jnp.bfloat16)
    )
    state = jax.tree.map(lambda a, e: jnp.zeros_like(a) + jnp.asarray(e, a.dtype), value, neutral)

    def prefix_one(lap, state):
        source = count - 1 - lap
        return join(
            state,
            jax.tree.map(
                lambda a, own: lax.dynamic_index_in_dim(a, source, 0, False).astype(own.dtype),
                gathered,
                value,
            ),
        )

    return lax.fori_loop(0, ahead, prefix_one, state)


def normed(value):
    scale = lax.rsqrt(jnp.mean(value * value, axis=-1, keepdims=True) + EPS)
    return (value * scale, scale)


def norm_back(value, scale, grad):
    inner = jnp.mean(grad * value, axis=-1, keepdims=True)
    return scale * (grad - value * scale * scale * inner)


def silu_slope(value):
    sig = jax.nn.sigmoid(value)
    return sig * (1.0 + value * (1.0 - sig))


def chain_step(earlier, later):
    e_fade, e_state = earlier
    l_fade, l_state = later
    return (l_fade * e_fade, l_fade[:, None, None] * e_state + l_state)


def matmul(left, right):
    return jnp.dot(left, right, preferred_element_type=jnp.float32)


def matmul_tn(left, right):
    return lax.dot_general(
        left, right, (((0,), (0,)), ((), ())), preferred_element_type=jnp.float32
    )


def matmul_nt(left, right):
    return lax.dot_general(
        left, right, (((1,), (1,)), ((), ())), preferred_element_type=jnp.float32
    )


def decay_tables(count, rates, rows):
    pos = lax.iota(jnp.int32, rows)
    live = pos < count
    keep = (pos[:, None] >= pos[None, :]) & live[:, None] & live[None, :]
    spacing = jnp.where(keep, (pos[:, None] - pos[None, :]).astype(jnp.float32), 0.0)
    mask = jnp.where(keep[None], jnp.exp(-rates[:, None, None] * spacing[None]), 0.0)
    ahead = jnp.where(
        live[:, None], jnp.exp(-rates[None, :] * (count - pos)[:, None].astype(jnp.float32)), 0.0
    )
    behind = jnp.where(
        live[:, None], jnp.exp(-rates[None, :] * pos[:, None].astype(jnp.float32)), 0.0
    )
    fade = jnp.exp(-rates * count.astype(jnp.float32))
    return (mask, ahead, behind, fade)


def shards(
    tokens,
    block_counts,
    decay_rate,
    query_weight,
    key_weight,
    value_weight,
    gate_weight,
    out_weight,
    first_weight,
    second_weight,
    down_weight,
    cotangent,
):
    rows = tokens.shape[0]
    gathered = (
        lax.all_gather(query_weight, ("dp", "fsdp"), axis=0, tiled=True),
        lax.all_gather(key_weight, ("dp", "fsdp"), axis=0, tiled=True),
        lax.all_gather(value_weight, ("dp", "fsdp"), axis=0, tiled=True),
        lax.all_gather(gate_weight, ("dp", "fsdp"), axis=0, tiled=True),
        lax.all_gather(out_weight, ("dp", "fsdp"), axis=0, tiled=True),
        lax.all_gather(first_weight, ("dp", "fsdp"), axis=0, tiled=True),
        lax.all_gather(second_weight, ("dp", "fsdp"), axis=0, tiled=True),
        lax.all_gather(down_weight, ("dp", "fsdp"), axis=0, tiled=True),
    )
    w_query, w_key, w_value, w_gate, w_out, w_first, w_second, w_down = gathered
    count = block_counts[0, 0]
    closes = count < rows
    mask, ahead, behind, fade = decay_tables(count, decay_rate, rows)
    passing = jnp.where(closes, 0.0, fade)
    inputs = tokens.astype(jnp.float32)
    in_normed, in_scale = normed(inputs)
    hidden = in_normed.astype(jnp.bfloat16)
    q_pre = matmul(hidden, w_query)
    k_pre = matmul(hidden, w_key)
    value = matmul(hidden, w_value).astype(jnp.bfloat16)
    gate = matmul(hidden, w_gate)
    query = jax.nn.silu(q_pre).astype(jnp.bfloat16)
    keys = jax.nn.silu(k_pre).astype(jnp.bfloat16)
    query_heads = query.reshape(rows, HEADS, HEAD_DIM)
    key_heads = keys.reshape(rows, HEADS, HEAD_DIM)
    value_heads = value.reshape(rows, HEADS, HEAD_DIM)
    query_wide = query_heads.astype(jnp.float32)
    key_wide = key_heads.astype(jnp.float32)
    value_ahead = value_heads.astype(jnp.float32) * ahead[:, :, None]
    raw = jnp.einsum("ihe,jhe->hij", query_heads, key_heads, preferred_element_type=jnp.float32)
    probs = (raw * mask).astype(jnp.bfloat16)
    intra = jnp.einsum("hij,jhe->ihe", probs, value_heads, preferred_element_type=jnp.float32)
    local = jnp.einsum("jhe,jhf->hef", key_wide, value_ahead, precision=HIGH)
    local_sent = jnp.where(closes, 0.0, local)
    prefix = carried_in(
        (passing, local_sent), "fsdp", chain_step, (jnp.ones_like(fade), jnp.zeros_like(local))
    )
    entering = prefix[1]
    inter = behind[:, :, None] * jnp.einsum("ihe,hef->ihf", query_wide, entering, precision=HIGH)
    attn = (intra + inter).reshape(rows, HEADS * HEAD_DIM)
    attn_normed, attn_scale = normed(attn)
    mixed = (attn_normed * gate).astype(jnp.bfloat16)
    middle = inputs + matmul(mixed, w_out)
    mid_normed, mid_scale = normed(middle)
    mid = mid_normed.astype(jnp.bfloat16)
    first = matmul(mid, w_first)
    second = matmul(mid, w_second)
    product = (first * second).astype(jnp.bfloat16)
    block_out = (middle + matmul(product, w_down)).astype(jnp.bfloat16)
    w_first, w_second, w_down = (
        lax.all_gather(first_weight, ("dp", "fsdp"), axis=0, tiled=True),
        lax.all_gather(second_weight, ("dp", "fsdp"), axis=0, tiled=True),
        lax.all_gather(down_weight, ("dp", "fsdp"), axis=0, tiled=True),
    )
    grad_product = matmul_nt(cotangent, w_down)
    grad_first = (grad_product * second).astype(jnp.bfloat16)
    grad_second = (grad_product * first).astype(jnp.bfloat16)
    grad_mid = matmul_nt(grad_first, w_first) + matmul_nt(grad_second, w_second)
    grad_middle = cotangent.astype(jnp.float32) + norm_back(middle, mid_scale, grad_mid)

    def scattered(left, right, after):
        left, _ = lax.optimization_barrier((left, after))
        term = matmul_tn(left, right)
        return lax.psum_scatter(term, ("dp", "fsdp"), scatter_dimension=0, tiled=True)

    down_grad = scattered(product, cotangent, grad_middle)
    first_grad = scattered(mid, grad_first, down_grad)
    second_grad = scattered(mid, grad_second, first_grad)
    grad_middle, _ = lax.optimization_barrier((grad_middle, second_grad))
    w_query, w_key, w_value, w_gate, w_out = (
        lax.all_gather(query_weight, ("dp", "fsdp"), axis=0, tiled=True),
        lax.all_gather(key_weight, ("dp", "fsdp"), axis=0, tiled=True),
        lax.all_gather(value_weight, ("dp", "fsdp"), axis=0, tiled=True),
        lax.all_gather(gate_weight, ("dp", "fsdp"), axis=0, tiled=True),
        lax.all_gather(out_weight, ("dp", "fsdp"), axis=0, tiled=True),
    )
    grad_mid_low = grad_middle.astype(jnp.bfloat16)
    out_term = matmul_tn(mixed, grad_mid_low)
    grad_mixed = matmul_nt(grad_mid_low, w_out)
    grad_gate = (grad_mixed * attn_normed).astype(jnp.bfloat16)
    grad_attn = norm_back(attn, attn_scale, grad_mixed * gate).astype(jnp.bfloat16)
    grad_heads = grad_attn.reshape(rows, HEADS, HEAD_DIM)
    grad_heads_wide = grad_heads.astype(jnp.float32) * behind[:, :, None]
    grad_probs = jnp.einsum(
        "ihe,jhe->hij", grad_heads, value_heads, preferred_element_type=jnp.float32
    )
    grad_raw = (grad_probs * mask).astype(jnp.bfloat16)
    grad_entering = jnp.einsum("ihe,ihf->hef", query_wide, grad_heads_wide, precision=HIGH)
    suffix = prefix_2(
        (passing, grad_entering),
        "fsdp",
        chain_step,
        (jnp.ones_like(fade), jnp.zeros_like(grad_entering)),
    )
    grad_leaving = jnp.where(closes, 0.0, suffix[1])
    grad_query = jnp.einsum("hij,jhe->ihe", grad_raw, key_heads, preferred_element_type=jnp.float32)
    grad_query = grad_query + jnp.einsum("ihf,hef->ihe", grad_heads_wide, entering, precision=HIGH)
    grad_keys = jnp.einsum(
        "hij,ihe->jhe", grad_raw, query_heads, preferred_element_type=jnp.float32
    )
    grad_keys = grad_keys + jnp.einsum("hef,jhf->jhe", grad_leaving, value_ahead, precision=HIGH)
    grad_value = jnp.einsum("hij,ihe->jhe", probs, grad_heads, preferred_element_type=jnp.float32)
    grad_value = grad_value + ahead[:, :, None] * jnp.einsum(
        "hef,jhe->jhf", grad_leaving, key_wide, precision=HIGH
    )
    width = HEADS * HEAD_DIM
    grad_q_pre = (grad_query.reshape(rows, width) * silu_slope(q_pre)).astype(jnp.bfloat16)
    grad_k_pre = (grad_keys.reshape(rows, width) * silu_slope(k_pre)).astype(jnp.bfloat16)
    grad_v = grad_value.reshape(rows, width).astype(jnp.bfloat16)
    query_term = matmul_tn(hidden, grad_q_pre)
    key_term = matmul_tn(hidden, grad_k_pre)
    value_term = matmul_tn(hidden, grad_v)
    gate_term = matmul_tn(hidden, grad_gate)
    grad_hidden = matmul_nt(grad_q_pre, w_query) + matmul_nt(grad_k_pre, w_key)
    grad_hidden = grad_hidden + matmul_nt(grad_v, w_value) + matmul_nt(grad_gate, w_gate)
    tokens_grad = grad_middle + norm_back(inputs, in_scale, grad_hidden)
    query_grad, key_grad, value_grad, gate_grad, out_grad = (
        lax.psum_scatter(query_term, ("dp", "fsdp"), scatter_dimension=0, tiled=True),
        lax.psum_scatter(key_term, ("dp", "fsdp"), scatter_dimension=0, tiled=True),
        lax.psum_scatter(value_term, ("dp", "fsdp"), scatter_dimension=0, tiled=True),
        lax.psum_scatter(gate_term, ("dp", "fsdp"), scatter_dimension=0, tiled=True),
        lax.psum_scatter(out_term, ("dp", "fsdp"), scatter_dimension=0, tiled=True),
    )
    return (
        block_out,
        tokens_grad,
        query_grad,
        key_grad,
        value_grad,
        gate_grad,
        out_grad,
        first_grad,
        second_grad,
        down_grad,
    )


MESH = pl.DeviceIdType.MESH
VMEM_BYTES = 60 * 2**20


def place():
    plane = lax.axis_index("fsdp")
    return lax.axis_index("dp"), plane // 4, (plane // 2) % 2, plane % 2


def other(i, way):
    return i + way - 2 * i * way


def member(y, x, core):
    return (y * 2 + x) * 2 + core


def greet(devices):
    barrier = pltpu.get_barrier_semaphore()
    for device in devices:
        pl.semaphore_signal(barrier, inc=1, device_id=device, device_id_type=MESH)
    pl.semaphore_wait(barrier, len(devices))


def remote(src, dst, send, recv, device):
    return pltpu.make_async_remote_copy(
        src_ref=src, dst_ref=dst, send_sem=send, recv_sem=recv, device_id=device, device_id_type=MESH
    )


def gather_kernel(x_ref, o_ref, local, send, recv):
    z, y, x, core = place()
    me, mate = member(y, x, core), member(y, x, 1 - core)
    on_x, on_y, across = member(y, 1 - x, core), member(1 - y, x, core), member(1 - y, 1 - x, core)
    greet([(z, mate), (z, on_x), (z, on_y)])
    half = x_ref.shape[0] // 2
    low, high = pl.ds(0, half), pl.ds(half, half)

    def own(part, n, device):
        return remote(x_ref.at[part], o_ref.at[me, part], send.at[n], recv.at[n], (z, device))

    def pass_on(block, part, n, device):
        ref = o_ref.at[block, part]
        return remote(ref, ref, send.at[n], recv.at[n], (z, device))

    keep = pltpu.make_async_copy(x_ref, o_ref.at[me], local)
    first = [own(low, 0, on_y), own(high, 1, on_x), own(high, 2, on_y), own(low, 3, on_x)]
    mine = remote(x_ref, o_ref.at[me], send.at[4], recv.at[4], (z, mate))
    for copy in first:
        copy.start()
    mine.start()
    keep.start()
    first[0].wait_recv()
    relay_x = pass_on(on_y, low, 5, on_x)
    relay_x.start()
    first[1].wait_recv()
    relay_y = pass_on(on_x, high, 6, on_y)
    relay_y.start()
    first[2].wait_recv()
    y_mate = remote(o_ref.at[on_y], o_ref.at[on_y], send.at[7], recv.at[7], (z, mate))
    y_mate.start()
    first[3].wait_recv()
    x_mate = remote(o_ref.at[on_x], o_ref.at[on_x], send.at[8], recv.at[8], (z, mate))
    x_mate.start()
    relay_x.wait_recv()
    low_mate = pass_on(across, low, 9, mate)
    low_mate.start()
    relay_y.wait_recv()
    high_mate = pass_on(across, high, 10, mate)
    high_mate.start()
    keep.wait()
    mine.wait_recv()
    for copy in (y_mate, x_mate, low_mate, high_mate):
        copy.wait_recv()
    for copy in (*first, mine, relay_x, relay_y, y_mate, x_mate, low_mate, high_mate):
        copy.wait_send()


def plane_gather(value, number):
    rows, width = value.shape
    return pl.pallas_call(
        gather_kernel,
        out_shape=jax.ShapeDtypeStruct((8, rows, width), value.dtype),
        in_specs=[pl.BlockSpec(memory_space=pl.ANY)],
        out_specs=pl.BlockSpec(memory_space=pl.ANY),
        scratch_shapes=[
            pltpu.SemaphoreType.DMA,
            pltpu.SemaphoreType.DMA((11,)),
            pltpu.SemaphoreType.DMA((11,)),
        ],
        compiler_params=pltpu.CompilerParams(collective_id=number, has_side_effects=True),
        cost_estimate=pl.CostEstimate(flops=0, bytes_accessed=16 * rows * width * 10, transcendentals=0),
        name=f"plane_gather_{number}",
    )(value).reshape(8 * rows, width)


def swap_kernel(x_ref, o_ref, local, send, recv):
    z, y, x, core = place()
    me = member(y, x, core)
    peers = [(dy, dx, dc) for dy in (1, 0) for dx in (1, 0) for dc in (0, 1) if dy + dx + dc]
    devices = [member(other(y, dy), other(x, dx), other(core, dc)) for dy, dx, dc in peers]
    greet([(z, d) for d in devices])
    keep = pltpu.make_async_copy(x_ref.at[me], o_ref.at[me], local)
    copies = [
        remote(x_ref.at[d], o_ref.at[me], send.at[n], recv.at[n], (z, d)) for n, d in enumerate(devices)
    ]
    for copy in copies:
        copy.start()
    keep.start()
    keep.wait()
    for copy in copies:
        copy.wait()


def plane_swap(value, number):
    return pl.pallas_call(
        swap_kernel,
        out_shape=jax.ShapeDtypeStruct(value.shape, value.dtype),
        in_specs=[pl.BlockSpec(memory_space=pl.ANY)],
        out_specs=pl.BlockSpec(memory_space=pl.ANY),
        scratch_shapes=[
            pltpu.SemaphoreType.DMA,
            pltpu.SemaphoreType.DMA((7,)),
            pltpu.SemaphoreType.DMA((7,)),
        ],
        compiler_params=pltpu.CompilerParams(collective_id=number, has_side_effects=True),
        cost_estimate=pl.CostEstimate(flops=0, bytes_accessed=20 * value.size, transcendentals=0),
        name=f"plane_swap_{number}",
    )(value)


def scatter_kernel(pairs, flip, tile, *refs):
    lefts, rights = refs[:pairs], refs[pairs : 2 * pairs]
    o_ref, to_mate, from_mate, to_far, from_far, s_mate, r_mate, s_far, r_far = refs[2 * pairs :]
    z, y, x, core = place()
    rows, width = o_ref.shape
    mate = member(y, x, 1 - core)

    def target(i, c):
        return member(other(y, 1 - i % 2), other(x, 1 - i // 2), c)

    greet([(z, mate)] + [(z, target(i, core)) for i in range(3)])

    def each_tile(block, use):
        here = pl.ds(pl.multiple_of(block * rows, rows), rows)

        @pl.loop(0, width // tile)
        def _(t):
            cols = pl.ds(pl.multiple_of(t * tile, tile), tile)
            total = None
            for left, right in zip(lefts, rights):
                if flip:
                    term = matmul_nt(left[here, :], right[cols, :])
                else:
                    term = matmul(left[here, :], right[:, cols])
                total = term if total is None else total + term
            use(cols, total)

    def mate_copy(i):
        return remote(to_mate.at[i], from_mate.at[i], s_mate.at[i], r_mate.at[i], (z, mate))

    def far_copy(i):
        return remote(to_far.at[i], from_far.at[i], s_far.at[i], r_far.at[i], (z, target(i, core)))

    @pl.loop(0, 4)
    def _(i):
        def use(cols, total):
            to_mate[i, :, cols] = total.astype(jnp.bfloat16)

        each_tile(target(i, 1 - core), use)
        mate_copy(i).start()

    @pl.loop(0, 3)
    def _(i):
        mate_copy(i).wait_recv()

        def use(cols, total):
            total = total + from_mate[i, :, cols].astype(jnp.float32)
            to_far[i, :, cols] = total.astype(jnp.bfloat16)

        each_tile(target(i, core), use)
        far_copy(i).start()

    mate_copy(3).wait_recv()

    def use(cols, total):
        o_ref[:, cols] = total + from_mate[3, :, cols].astype(jnp.float32)

    each_tile(target(3, core), use)
    for i in (1, 2, 0):
        far_copy(i).wait_recv()
        o_ref[...] += from_far[i].astype(jnp.float32)
    for i in range(4):
        mate_copy(i).wait_send()
    for i in range(3):
        far_copy(i).wait_send()


def plane_scatter(lefts, rights, flip, number):
    rows = lefts[0].shape[0] // 8
    width = rights[0].shape[0 if flip else 1]
    depth = sum(left.shape[1] for left in lefts)
    vmem = pl.BlockSpec(memory_space=pltpu.VMEM)
    buffers = [pltpu.VMEM((n, rows, width), jnp.bfloat16) for n in (4, 4, 3, 3)]
    return pl.pallas_call(
        functools.partial(scatter_kernel, len(lefts), flip, 512),
        out_shape=jax.ShapeDtypeStruct((rows, width), jnp.float32),
        in_specs=[vmem] * (2 * len(lefts)),
        out_specs=vmem,
        scratch_shapes=buffers + [pltpu.SemaphoreType.DMA((n,)) for n in (4, 4, 3, 3)],
        compiler_params=pltpu.CompilerParams(
            collective_id=number, has_side_effects=True, vmem_limit_bytes=VMEM_BYTES
        ),
        cost_estimate=pl.CostEstimate(
            flops=16 * rows * width * depth, bytes_accessed=200 * rows * width, transcendentals=0
        ),
        name=f"plane_scatter_{number}",
    )(*lefts, *rights)


def fast_plan(
    tokens, block_counts, decay_rate, query_weight, key_weight, value_weight, gate_weight,
    out_weight, first_weight, second_weight, down_weight, cotangent,
):
    rows, width = tokens.shape
    nz = lax.axis_size("dp")
    nf = lax.axis_size("fsdp")
    chips = nf // 2
    plane = lax.axis_index("fsdp")
    chip, core = plane // 2, plane % 2
    bf = jnp.bfloat16
    groups = HEADS // chips
    half = groups // 2
    own_heads = chips * (half * core + jnp.arange(half)) + chip

    def columns(weight):
        r = weight.shape[0]
        w = weight.reshape(r, 2, half, chips, HEAD_DIM).transpose(3, 1, 0, 2, 4)
        return w.reshape(nf, r, half * HEAD_DIM)

    def columns_ff(weight):
        r, n = weight.shape
        return weight.reshape(r, nz, nf, n // (nz * nf)).transpose(2, 0, 1, 3).reshape(nf, r, n // nf)

    def along(weight):
        weight = weight.reshape(-1, weight.shape[-1])
        return lax.all_gather(weight, "dp", axis=0, tiled=True)

    swap = [(i, i ^ 1) for i in range(nf)]

    def cross(x):
        keep = lax.dynamic_slice_in_dim(x, core * half, half, 0)
        send = lax.dynamic_slice_in_dim(x, (1 - core) * half, half, 0)
        got = lax.ppermute(send, "fsdp", swap)
        lo = jnp.where(core == 0, keep, got)
        hi = jnp.where(core == 0, got, keep)
        return jnp.stack([lo, hi], axis=1)

    def uncross(x):
        keep = lax.dynamic_index_in_dim(x, core, 1, False)
        send = lax.dynamic_index_in_dim(x, 1 - core, 1, False)
        got = lax.ppermute(send, "fsdp", swap)
        lo = jnp.where(core == 0, keep, got)
        hi = jnp.where(core == 0, got, keep)
        return jnp.concatenate([lo, hi], axis=0)

    heads_weight = jnp.concatenate(
        [columns(w) for w in (query_weight, key_weight, value_weight, gate_weight)], axis=-1
    )
    w_heads = along(plane_swap(heads_weight, 0))
    own = half * HEAD_DIM
    wq, wk, wv, wg = (w_heads[:, i * own : (i + 1) * own] for i in range(4))
    wo = cross(lax.all_gather(out_weight, "dp", axis=0)).reshape(half * HEAD_DIM, width)
    w1 = along(plane_swap(columns_ff(first_weight), 1))
    w2 = along(plane_swap(columns_ff(second_weight), 2))
    wd = lax.all_gather(down_weight, "dp", axis=0, tiled=True)

    counts = lax.all_gather(block_counts[0, 0], "fsdp")
    rates = decay_rate[own_heads]
    pos = lax.iota(jnp.int32, rows)
    gap = (pos[:, None] - pos[None, :]).astype(jnp.float32)
    base = jnp.where(gap >= 0, jnp.exp(-rates[:, None, None] * jnp.maximum(gap, 0.0)), 0.0)
    live = pos[None, :] < counts[:, None]
    mask = base[None] * live[:, None, :, None]
    left = (counts[:, None] - pos[None, :]).astype(jnp.float32)
    ahead = jnp.where(live[..., None], jnp.exp(-rates * left[..., None]), 0.0)
    behind = jnp.where(live[..., None], jnp.exp(-rates * pos[None, :, None].astype(jnp.float32)), 0.0)
    fade = jnp.exp(-rates[None] * counts[:, None].astype(jnp.float32))
    closes = counts < rows

    inputs = tokens.astype(jnp.float32)
    in_normed, in_scale = normed(inputs)
    hidden = plane_gather(in_normed.astype(bf), 3)
    cot = plane_gather(cotangent, 4)
    shape = (nf, rows, half, HEAD_DIM)
    q_pre, k_pre = matmul(hidden, wq), matmul(hidden, wk)
    value = matmul(hidden, wv).astype(bf).reshape(shape)
    gate = matmul(hidden, wg)
    query = jax.nn.silu(q_pre).astype(bf).reshape(shape)
    keys = jax.nn.silu(k_pre).astype(bf).reshape(shape)
    q32, k32 = query.astype(jnp.float32), keys.astype(jnp.float32)
    value_ahead = value.astype(jnp.float32) * ahead[..., None]
    raw = jnp.einsum("bihe,bjhe->bhij", query, keys, preferred_element_type=jnp.float32)
    probs = (raw * mask).astype(bf)
    intra = jnp.einsum("bhij,bjhe->bihe", probs, value, preferred_element_type=jnp.float32)
    local = jnp.einsum("bjhe,bjhf->bhef", k32, value_ahead, precision=HIGH)
    state = jnp.zeros_like(local[0])
    entering = []
    for b in range(nf):
        entering.append(state)
        state = jnp.where(closes[b], 0.0, fade[b][:, None, None] * state + local[b])
    entering = jnp.stack(entering)
    inter = behind[..., None] * jnp.einsum("bihe,bhef->bihf", q32, entering, precision=HIGH)
    attn = (intra + inter).reshape(nf * rows, half * HEAD_DIM)
    squares = lax.psum(jnp.sum(attn * attn, axis=-1), "fsdp")
    scale = lax.rsqrt(squares / width + EPS)[:, None]
    attn_normed = attn * scale
    mixed = (attn_normed * gate).astype(bf)
    out_own = plane_scatter([mixed], [wo], False, 5)
    middle = inputs + out_own
    mid_normed, mid_scale = normed(middle)
    mid = plane_gather(mid_normed.astype(bf), 6)
    first, second = matmul(mid, w1), matmul(mid, w2)
    product = (first * second).astype(bf)
    block_out = (middle + plane_scatter([product], [wd], False, 7)).astype(bf)

    down_term = matmul_tn(product, cot)
    grad_product = matmul_nt(cot, wd)
    grad_first = (grad_product * second).astype(bf)
    grad_second = (grad_product * first).astype(bf)
    first_term = matmul_tn(mid, grad_first)
    second_term = matmul_tn(mid, grad_second)
    grad_mid = plane_scatter([grad_first, grad_second], [w1, w2], True, 8)
    grad_middle = cotangent.astype(jnp.float32) + norm_back(middle, mid_scale, grad_mid)
    low = grad_middle.astype(bf)
    inner = jnp.sum(low.astype(jnp.float32) * out_own, axis=-1)
    inner = lax.all_gather(inner, "fsdp", axis=0, tiled=True)[:, None] / (scale * width)
    low = plane_gather(low, 9)
    out_term = matmul_tn(mixed, low)
    grad_mixed = matmul_nt(low, wo)
    grad_gate = (grad_mixed * attn_normed).astype(bf)
    grad_attn = (scale * (grad_mixed * gate - attn * scale * scale * inner)).astype(bf)
    g = grad_attn.reshape(shape)
    g32 = g.astype(jnp.float32) * behind[..., None]
    grad_probs = jnp.einsum("bihe,bjhe->bhij", g, value, preferred_element_type=jnp.float32)
    grad_raw = (grad_probs * mask).astype(bf)
    grad_entering = jnp.einsum("bihe,bihf->bhef", q32, g32, precision=HIGH)
    state = jnp.zeros_like(grad_entering[0])
    leaving = [None] * nf
    for b in reversed(range(nf)):
        leaving[b] = jnp.where(closes[b], 0.0, state)
        state = grad_entering[b] + fade[b][:, None, None] * leaving[b]
    leaving = jnp.stack(leaving)
    grad_query = jnp.einsum("bhij,bjhe->bihe", grad_raw, keys, preferred_element_type=jnp.float32)
    grad_query += jnp.einsum("bihf,bhef->bihe", g32, entering, precision=HIGH)
    grad_keys = jnp.einsum("bhij,bihe->bjhe", grad_raw, query, preferred_element_type=jnp.float32)
    grad_keys += jnp.einsum("bhef,bjhf->bjhe", leaving, value_ahead, precision=HIGH)
    grad_value = jnp.einsum("bhij,bihe->bjhe", probs, g, preferred_element_type=jnp.float32)
    grad_value += ahead[..., None] * jnp.einsum("bhef,bjhe->bjhf", leaving, k32, precision=HIGH)
    flat = (nf * rows, half * HEAD_DIM)
    gq = (grad_query.reshape(flat) * silu_slope(q_pre)).astype(bf)
    gk = (grad_keys.reshape(flat) * silu_slope(k_pre)).astype(bf)
    gv = grad_value.reshape(flat).astype(bf)
    grad_heads = jnp.concatenate([gq, gk, gv, grad_gate], axis=-1)
    grad_hidden = plane_scatter([grad_heads], [w_heads], True, 10)
    tokens_grad = grad_middle + norm_back(inputs, in_scale, grad_hidden)

    def back_along(term, number):
        t = lax.psum_scatter(term.astype(bf), "dp", scatter_dimension=0, tiled=True)
        return plane_swap(t.reshape(nf, -1, t.shape[1]), number)

    def columns_back(t):
        r = t.shape[1]
        t = t.reshape(chips, 2, r, half, HEAD_DIM).transpose(2, 1, 3, 0, 4)
        return t.reshape(r, width).astype(jnp.float32)

    def columns_ff_back(t):
        r, n = t.shape[1:]
        t = t.reshape(nf, r, nz, n // nz).transpose(1, 2, 0, 3)
        return t.reshape(r, n * nf).astype(jnp.float32)

    heads_grad = back_along(matmul_tn(hidden, grad_heads), 11)
    grads = [columns_back(heads_grad[..., i * own : (i + 1) * own]) for i in range(4)]
    out_term = uncross(out_term.astype(bf).reshape(half, 2, -1, width))
    out_grad = lax.psum_scatter(out_term, "dp", scatter_dimension=0, tiled=False).astype(jnp.float32)
    first_grad = columns_ff_back(back_along(first_term, 12))
    second_grad = columns_ff_back(back_along(second_term, 13))
    down_grad = lax.psum_scatter(down_term.astype(bf), "dp", scatter_dimension=0, tiled=True).astype(jnp.float32)
    return (block_out, tokens_grad, *grads, out_grad, first_grad, second_grad, down_grad)


def fits(mesh):
    return mesh.shape["dp"] == 4 and mesh.shape["fsdp"] == 8


def solution(mesh):
    return jax.shard_map(
        fast_plan if fits(mesh) else shards,
        mesh=mesh,
        in_specs=(
            P(("dp", "fsdp"), None),
            P("dp", "fsdp"),
            P(),
            P(("dp", "fsdp"), None),
            P(("dp", "fsdp"), None),
            P(("dp", "fsdp"), None),
            P(("dp", "fsdp"), None),
            P(("dp", "fsdp"), None),
            P(("dp", "fsdp"), None),
            P(("dp", "fsdp"), None),
            P(("dp", "fsdp"), None),
            P(("dp", "fsdp"), None),
        ),
        out_specs=(
            P(("dp", "fsdp"), None),
            P(("dp", "fsdp"), None),
            P(("dp", "fsdp"), None),
            P(("dp", "fsdp"), None),
            P(("dp", "fsdp"), None),
            P(("dp", "fsdp"), None),
            P(("dp", "fsdp"), None),
            P(("dp", "fsdp"), None),
            P(("dp", "fsdp"), None),
            P(("dp", "fsdp"), None),
        ),
        check_vma=False,
    )
```

```python
import functools

import jax
import jax.numpy as jnp
from jax import lax
from jax.experimental import pallas as pl
from jax.experimental.pallas import tpu as pltpu
from jax.sharding import PartitionSpec as P

HEADS = 16
HEAD_DIM = 128


EPS = 1e-06
HIGH = lax.Precision.HIGHEST


def carried_in(part, axis, combine, identity):
    place = lax.axis_index(axis)
    gathered = jax.tree.map(lambda a: lax.all_gather(a, axis), part)
    state = jax.tree.map(lambda a, e: jnp.zeros_like(a) + jnp.asarray(e, a.dtype), part, identity)

    def carried_one(lap, state):
        return combine(
            state, jax.tree.map(lambda a: lax.dynamic_index_in_dim(a, lap, 0, False), gathered)
        )

    return lax.fori_loop(0, place, carried_one, state)


def prefix_2(value, axis, join, neutral):
    count = lax.axis_size(axis)
    place = lax.axis_index(axis)
    ahead = count - 1 - place
    gathered = jax.tree.map(
        lambda a, kind: lax.all_gather(a.astype(kind), axis), value, (jnp.bfloat16, jnp.bfloat16)
    )
    state = jax.tree.map(lambda a, e: jnp.zeros_like(a) + jnp.asarray(e, a.dtype), value, neutral)

    def prefix_one(lap, state):
        source = count - 1 - lap
        return join(
            state,
            jax.tree.map(
                lambda a, own: lax.dynamic_index_in_dim(a, source, 0, False).astype(own.dtype),
                gathered,
                value,
            ),
        )

    return lax.fori_loop(0, ahead, prefix_one, state)


def normed(value):
    scale = lax.rsqrt(jnp.mean(value * value, axis=-1, keepdims=True) + EPS)
    return (value * scale, scale)


def norm_back(value, scale, grad):
    inner = jnp.mean(grad * value, axis=-1, keepdims=True)
    return scale * (grad - value * scale * scale * inner)


def silu_slope(value):
    sig = jax.nn.sigmoid(value)
    return sig * (1.0 + value * (1.0 - sig))


def chain_step(earlier, later):
    e_fade, e_state = earlier
    l_fade, l_state = later
    return (l_fade * e_fade, l_fade[:, None, None] * e_state + l_state)


def matmul(left, right):
    return jnp.dot(left, right, preferred_element_type=jnp.float32)


def matmul_tn(left, right):
    return lax.dot_general(
        left, right, (((0,), (0,)), ((), ())), preferred_element_type=jnp.float32
    )


def matmul_nt(left, right):
    return lax.dot_general(
        left, right, (((1,), (1,)), ((), ())), preferred_element_type=jnp.float32
    )


def decay_tables(count, rates, rows):
    pos = lax.iota(jnp.int32, rows)
    live = pos < count
    keep = (pos[:, None] >= pos[None, :]) & live[:, None] & live[None, :]
    spacing = jnp.where(keep, (pos[:, None] - pos[None, :]).astype(jnp.float32), 0.0)
    mask = jnp.where(keep[None], jnp.exp(-rates[:, None, None] * spacing[None]), 0.0)
    ahead = jnp.where(
        live[:, None], jnp.exp(-rates[None, :] * (count - pos)[:, None].astype(jnp.float32)), 0.0
    )
    behind = jnp.where(
        live[:, None], jnp.exp(-rates[None, :] * pos[:, None].astype(jnp.float32)), 0.0
    )
    fade = jnp.exp(-rates * count.astype(jnp.float32))
    return (mask, ahead, behind, fade)


def shards(
    tokens,
    block_counts,
    decay_rate,
    query_weight,
    key_weight,
    value_weight,
    gate_weight,
    out_weight,
    first_weight,
    second_weight,
    down_weight,
    cotangent,
):
    rows = tokens.shape[0]
    gathered = (
        lax.all_gather(query_weight, ("dp", "fsdp"), axis=0, tiled=True),
        lax.all_gather(key_weight, ("dp", "fsdp"), axis=0, tiled=True),
        lax.all_gather(value_weight, ("dp", "fsdp"), axis=0, tiled=True),
        lax.all_gather(gate_weight, ("dp", "fsdp"), axis=0, tiled=True),
        lax.all_gather(out_weight, ("dp", "fsdp"), axis=0, tiled=True),
        lax.all_gather(first_weight, ("dp", "fsdp"), axis=0, tiled=True),
        lax.all_gather(second_weight, ("dp", "fsdp"), axis=0, tiled=True),
        lax.all_gather(down_weight, ("dp", "fsdp"), axis=0, tiled=True),
    )
    w_query, w_key, w_value, w_gate, w_out, w_first, w_second, w_down = gathered
    count = block_counts[0, 0]
    closes = count < rows
    mask, ahead, behind, fade = decay_tables(count, decay_rate, rows)
    passing = jnp.where(closes, 0.0, fade)
    inputs = tokens.astype(jnp.float32)
    in_normed, in_scale = normed(inputs)
    hidden = in_normed.astype(jnp.bfloat16)
    q_pre = matmul(hidden, w_query)
    k_pre = matmul(hidden, w_key)
    value = matmul(hidden, w_value).astype(jnp.bfloat16)
    gate = matmul(hidden, w_gate)
    query = jax.nn.silu(q_pre).astype(jnp.bfloat16)
    keys = jax.nn.silu(k_pre).astype(jnp.bfloat16)
    query_heads = query.reshape(rows, HEADS, HEAD_DIM)
    key_heads = keys.reshape(rows, HEADS, HEAD_DIM)
    value_heads = value.reshape(rows, HEADS, HEAD_DIM)
    query_wide = query_heads.astype(jnp.float32)
    key_wide = key_heads.astype(jnp.float32)
    value_ahead = value_heads.astype(jnp.float32) * ahead[:, :, None]
    raw = jnp.einsum("ihe,jhe->hij", query_heads, key_heads, preferred_element_type=jnp.float32)
    probs = (raw * mask).astype(jnp.bfloat16)
    intra = jnp.einsum("hij,jhe->ihe", probs, value_heads, preferred_element_type=jnp.float32)
    local = jnp.einsum("jhe,jhf->hef", key_wide, value_ahead, precision=HIGH)
    local_sent = jnp.where(closes, 0.0, local)
    prefix = carried_in(
        (passing, local_sent), "fsdp", chain_step, (jnp.ones_like(fade), jnp.zeros_like(local))
    )
    entering = prefix[1]
    inter = behind[:, :, None] * jnp.einsum("ihe,hef->ihf", query_wide, entering, precision=HIGH)
    attn = (intra + inter).reshape(rows, HEADS * HEAD_DIM)
    attn_normed, attn_scale = normed(attn)
    mixed = (attn_normed * gate).astype(jnp.bfloat16)
    middle = inputs + matmul(mixed, w_out)
    mid_normed, mid_scale = normed(middle)
    mid = mid_normed.astype(jnp.bfloat16)
    first = matmul(mid, w_first)
    second = matmul(mid, w_second)
    product = (first * second).astype(jnp.bfloat16)
    block_out = (middle + matmul(product, w_down)).astype(jnp.bfloat16)
    w_first, w_second, w_down = (
        lax.all_gather(first_weight, ("dp", "fsdp"), axis=0, tiled=True),
        lax.all_gather(second_weight, ("dp", "fsdp"), axis=0, tiled=True),
        lax.all_gather(down_weight, ("dp", "fsdp"), axis=0, tiled=True),
    )
    grad_product = matmul_nt(cotangent, w_down)
    grad_first = (grad_product * second).astype(jnp.bfloat16)
    grad_second = (grad_product * first).astype(jnp.bfloat16)
    grad_mid = matmul_nt(grad_first, w_first) + matmul_nt(grad_second, w_second)
    grad_middle = cotangent.astype(jnp.float32) + norm_back(middle, mid_scale, grad_mid)

    def scattered(left, right, after):
        left, _ = lax.optimization_barrier((left, after))
        term = matmul_tn(left, right)
        return lax.psum_scatter(term, ("dp", "fsdp"), scatter_dimension=0, tiled=True)

    down_grad = scattered(product, cotangent, grad_middle)
    first_grad = scattered(mid, grad_first, down_grad)
    second_grad = scattered(mid, grad_second, first_grad)
    grad_middle, _ = lax.optimization_barrier((grad_middle, second_grad))
    w_query, w_key, w_value, w_gate, w_out = (
        lax.all_gather(query_weight, ("dp", "fsdp"), axis=0, tiled=True),
        lax.all_gather(key_weight, ("dp", "fsdp"), axis=0, tiled=True),
        lax.all_gather(value_weight, ("dp", "fsdp"), axis=0, tiled=True),
        lax.all_gather(gate_weight, ("dp", "fsdp"), axis=0, tiled=True),
        lax.all_gather(out_weight, ("dp", "fsdp"), axis=0, tiled=True),
    )
    grad_mid_low = grad_middle.astype(jnp.bfloat16)
    out_term = matmul_tn(mixed, grad_mid_low)
    grad_mixed = matmul_nt(grad_mid_low, w_out)
    grad_gate = (grad_mixed * attn_normed).astype(jnp.bfloat16)
    grad_attn = norm_back(attn, attn_scale, grad_mixed * gate).astype(jnp.bfloat16)
    grad_heads = grad_attn.reshape(rows, HEADS, HEAD_DIM)
    grad_heads_wide = grad_heads.astype(jnp.float32) * behind[:, :, None]
    grad_probs = jnp.einsum(
        "ihe,jhe->hij", grad_heads, value_heads, preferred_element_type=jnp.float32
    )
    grad_raw = (grad_probs * mask).astype(jnp.bfloat16)
    grad_entering = jnp.einsum("ihe,ihf->hef", query_wide, grad_heads_wide, precision=HIGH)
    suffix = prefix_2(
        (passing, grad_entering),
        "fsdp",
        chain_step,
        (jnp.ones_like(fade), jnp.zeros_like(grad_entering)),
    )
    grad_leaving = jnp.where(closes, 0.0, suffix[1])
    grad_query = jnp.einsum("hij,jhe->ihe", grad_raw, key_heads, preferred_element_type=jnp.float32)
    grad_query = grad_query + jnp.einsum("ihf,hef->ihe", grad_heads_wide, entering, precision=HIGH)
    grad_keys = jnp.einsum(
        "hij,ihe->jhe", grad_raw, query_heads, preferred_element_type=jnp.float32
    )
    grad_keys = grad_keys + jnp.einsum("hef,jhf->jhe", grad_leaving, value_ahead, precision=HIGH)
    grad_value = jnp.einsum("hij,ihe->jhe", probs, grad_heads, preferred_element_type=jnp.float32)
    grad_value = grad_value + ahead[:, :, None] * jnp.einsum(
        "hef,jhe->jhf", grad_leaving, key_wide, precision=HIGH
    )
    width = HEADS * HEAD_DIM
    grad_q_pre = (grad_query.reshape(rows, width) * silu_slope(q_pre)).astype(jnp.bfloat16)
    grad_k_pre = (grad_keys.reshape(rows, width) * silu_slope(k_pre)).astype(jnp.bfloat16)
    grad_v = grad_value.reshape(rows, width).astype(jnp.bfloat16)
    query_term = matmul_tn(hidden, grad_q_pre)
    key_term = matmul_tn(hidden, grad_k_pre)
    value_term = matmul_tn(hidden, grad_v)
    gate_term = matmul_tn(hidden, grad_gate)
    grad_hidden = matmul_nt(grad_q_pre, w_query) + matmul_nt(grad_k_pre, w_key)
    grad_hidden = grad_hidden + matmul_nt(grad_v, w_value) + matmul_nt(grad_gate, w_gate)
    tokens_grad = grad_middle + norm_back(inputs, in_scale, grad_hidden)
    query_grad, key_grad, value_grad, gate_grad, out_grad = (
        lax.psum_scatter(query_term, ("dp", "fsdp"), scatter_dimension=0, tiled=True),
        lax.psum_scatter(key_term, ("dp", "fsdp"), scatter_dimension=0, tiled=True),
        lax.psum_scatter(value_term, ("dp", "fsdp"), scatter_dimension=0, tiled=True),
        lax.psum_scatter(gate_term, ("dp", "fsdp"), scatter_dimension=0, tiled=True),
        lax.psum_scatter(out_term, ("dp", "fsdp"), scatter_dimension=0, tiled=True),
    )
    return (
        block_out,
        tokens_grad,
        query_grad,
        key_grad,
        value_grad,
        gate_grad,
        out_grad,
        first_grad,
        second_grad,
        down_grad,
    )


MESH = pl.DeviceIdType.MESH
VMEM_BYTES = 60 * 2**20
ANY = pl.BlockSpec(memory_space=pl.ANY)
VMEM = pl.BlockSpec(memory_space=pltpu.VMEM)
SMEM = pl.BlockSpec(memory_space=pltpu.SMEM)


def place():
    plane = lax.axis_index("fsdp")
    return lax.axis_index("dp"), plane // 4, (plane // 2) % 2, plane % 2


def other(i, way):
    return i + way - 2 * i * way


def member(y, x, core):
    return (y * 2 + x) * 2 + core


def plane_peers(y, x, core):
    ways = [(dy, dx, dc) for dy in (1, 0) for dx in (1, 0) for dc in (0, 1) if dy + dx + dc]
    return [member(other(y, dy), other(x, dx), other(core, dc)) for dy, dx, dc in ways]


def greet(z, members):
    barrier = pltpu.get_barrier_semaphore()
    for device in members:
        pl.semaphore_signal(barrier, inc=1, device_id=(z, device), device_id_type=MESH)
    pl.semaphore_wait(barrier, len(members))


def remote(src, dst, send, recv, device):
    return pltpu.make_async_remote_copy(
        src_ref=src, dst_ref=dst, send_sem=send, recv_sem=recv, device_id=device, device_id_type=MESH
    )


def note_copies(z, me, peers, note, notes, send, recv):
    return [
        remote(note, notes.at[me], send.at[n], recv.at[n], (z, d)) for n, d in enumerate(peers)
    ]


def gather_kernel(with_note, with_swap, *refs):
    refs = list(refs)
    x_ref = refs.pop(0)
    note = refs.pop(0) if with_note else None
    swap = refs.pop(0) if with_swap else None
    o_ref = refs.pop(0)
    notes = refs.pop(0) if with_note else None
    swapped = refs.pop(0) if with_swap else None
    local, send, recv = refs[:3]
    refs = refs[3:]
    z, y, x, core = place()
    me, mate = member(y, x, core), member(y, x, 1 - core)
    on_x, on_y, across = member(y, 1 - x, core), member(1 - y, x, core), member(1 - y, 1 - x, core)
    peers = plane_peers(y, x, core)
    greet(z, peers)
    half = x_ref.shape[0] // 2
    low, high = pl.ds(0, half), pl.ds(half, half)

    def own(part, n, device):
        return remote(x_ref.at[part], o_ref.at[me, part], send.at[n], recv.at[n], (z, device))

    def pass_on(block, part, n, device):
        ref = o_ref.at[block, part]
        return remote(ref, ref, send.at[n], recv.at[n], (z, device))

    keep = pltpu.make_async_copy(x_ref, o_ref.at[me], local.at[0])
    first = [own(low, 0, on_y), own(high, 1, on_x), own(high, 2, on_y), own(low, 3, on_x)]
    mine = remote(x_ref, o_ref.at[me], send.at[4], recv.at[4], (z, mate))
    extra = []
    if with_note:
        extra += note_copies(z, me, peers, note, notes, refs[0], refs[1])
        refs = refs[2:]
    if with_swap:
        extra += [
            remote(swap.at[d], swapped.at[me], refs[0].at[n], refs[1].at[n], (z, d))
            for n, d in enumerate(peers)
        ]
        keep_swap = pltpu.make_async_copy(swap.at[me], swapped.at[me], local.at[1])
        keep_swap.start()
    for copy in first + extra:
        copy.start()
    mine.start()
    keep.start()
    if with_note:
        notes[me] = note[...]
    first[0].wait_recv()
    relay_x = pass_on(on_y, low, 5, on_x)
    relay_x.start()
    first[1].wait_recv()
    relay_y = pass_on(on_x, high, 6, on_y)
    relay_y.start()
    first[2].wait_recv()
    y_mate = remote(o_ref.at[on_y], o_ref.at[on_y], send.at[7], recv.at[7], (z, mate))
    y_mate.start()
    first[3].wait_recv()
    x_mate = remote(o_ref.at[on_x], o_ref.at[on_x], send.at[8], recv.at[8], (z, mate))
    x_mate.start()
    relay_x.wait_recv()
    low_mate = pass_on(across, low, 9, mate)
    low_mate.start()
    relay_y.wait_recv()
    high_mate = pass_on(across, high, 10, mate)
    high_mate.start()
    keep.wait()
    if with_swap:
        keep_swap.wait()
    for copy in (mine, y_mate, x_mate, low_mate, high_mate, *extra):
        copy.wait_recv()
    for copy in (*first, mine, relay_x, relay_y, y_mate, x_mate, low_mate, high_mate, *extra):
        copy.wait_send()


def plane_gather(value, number, note=None, swap=None):
    rows, width = value.shape
    ins, in_specs = [value], [ANY]
    outs, out_specs = [jax.ShapeDtypeStruct((8, rows, width), value.dtype)], [ANY]
    scratch = [pltpu.SemaphoreType.DMA((n,)) for n in (2, 11, 11)]
    if note is not None:
        ins.append(note)
        in_specs.append(VMEM)
        outs.append(jax.ShapeDtypeStruct((8, *note.shape), note.dtype))
        out_specs.append(VMEM)
        scratch += [pltpu.SemaphoreType.DMA((7,)) for _ in range(2)]
    if swap is not None:
        ins.append(swap)
        in_specs.append(ANY)
        outs.append(jax.ShapeDtypeStruct(swap.shape, swap.dtype))
        out_specs.append(ANY)
        scratch += [pltpu.SemaphoreType.DMA((7,)) for _ in range(2)]
    gathered, *rest = pl.pallas_call(
        functools.partial(gather_kernel, note is not None, swap is not None),
        out_shape=outs,
        in_specs=in_specs,
        out_specs=out_specs,
        scratch_shapes=scratch,
        compiler_params=pltpu.CompilerParams(collective_id=number, has_side_effects=True),
        cost_estimate=pl.CostEstimate(flops=0, bytes_accessed=160 * rows * width, transcendentals=0),
        name=f"plane_gather_{number}",
    )(*ins)
    return (gathered.reshape(8 * rows, width), *rest)


def swap_kernel(with_note, *refs):
    refs = list(refs)
    x_ref = refs.pop(0)
    note = refs.pop(0) if with_note else None
    o_ref = refs.pop(0)
    notes = refs.pop(0) if with_note else None
    local, send, recv = refs[:3]
    z, y, x, core = place()
    me = member(y, x, core)
    peers = plane_peers(y, x, core)
    greet(z, peers)
    keep = pltpu.make_async_copy(x_ref.at[me], o_ref.at[me], local)
    copies = [remote(x_ref.at[d], o_ref.at[me], send.at[n], recv.at[n], (z, d)) for n, d in enumerate(peers)]
    if with_note:
        copies += note_copies(z, me, peers, note, notes, refs[3], refs[4])
    for copy in copies:
        copy.start()
    keep.start()
    if with_note:
        notes[me] = note[...]
    keep.wait()
    for copy in copies:
        copy.wait()


def plane_swap(value, number, note=None):
    ins, in_specs = [value], [ANY]
    outs, out_specs = [jax.ShapeDtypeStruct(value.shape, value.dtype)], [ANY]
    scratch = [pltpu.SemaphoreType.DMA] + [pltpu.SemaphoreType.DMA((7,)) for _ in range(2)]
    if note is not None:
        ins.append(note)
        in_specs.append(VMEM)
        outs.append(jax.ShapeDtypeStruct((8, *note.shape), note.dtype))
        out_specs.append(VMEM)
        scratch += [pltpu.SemaphoreType.DMA((7,)) for _ in range(2)]
    return pl.pallas_call(
        functools.partial(swap_kernel, note is not None),
        out_shape=outs,
        in_specs=in_specs,
        out_specs=out_specs,
        scratch_shapes=scratch,
        compiler_params=pltpu.CompilerParams(collective_id=number, has_side_effects=True),
        cost_estimate=pl.CostEstimate(flops=0, bytes_accessed=40 * value.size, transcendentals=0),
        name=f"plane_swap_{number}",
    )(*ins)


def scatter_kernel(pairs, flip, mixing, side, tile, *refs):
    refs = list(refs)
    lefts = [refs.pop(0) for _ in range(pairs)]
    rights = [refs.pop(0) for _ in range(pairs)]
    squares = refs.pop(0) if mixing else None
    side_left = refs.pop(0) if side else None
    side_rights = [refs.pop(0) for _ in range(side)]
    o_ref = refs.pop(0)
    scale_ref = refs.pop(0) if mixing else None
    side_outs = [refs.pop(0) for _ in range(side)]
    to_mate, from_mate, stage, from_x, from_y, s_mate, r_mate, s_x, r_x, s_y, r_y = refs[:11]
    z, y, x, core = place()
    rows, width = o_ref.shape
    half = width // 2
    me, mate = member(y, x, core), member(y, x, 1 - core)
    on_x, on_y = member(y, 1 - x, core), member(1 - y, x, core)
    peers = plane_peers(y, x, core)
    greet(z, peers)
    left_cols, right_cols = pl.ds(0, half), pl.ds(half, half)

    if mixing:
        all_squares, columns, s_note, r_note = refs[11:]
        notes = note_copies(z, me, peers, squares, all_squares, s_note, r_note)
        for copy in notes:
            copy.start()
        all_squares[me] = squares[...]
        for copy in notes:
            copy.wait_recv()
        scale = lax.rsqrt(jnp.sum(all_squares[...], axis=0) / width + EPS)
        scale_ref[...] = scale
        columns[...] = jnp.transpose(scale)

    def target(i, c):
        return member(other(y, 1 - i % 2), other(x, 1 - i // 2), c)

    def left_rows(left, block):
        here = pl.ds(pl.multiple_of(block * rows, rows), rows)
        if not mixing:
            return left[here, :]
        deep = left.shape[1] // 2
        spot = lax.broadcasted_iota(jnp.int32, columns.shape, 1) == block
        column = jnp.sum(jnp.where(spot, columns[...], 0.0), axis=1, keepdims=True)
        return (left[here, :deep] * column * left[here, deep:]).astype(jnp.bfloat16)

    def each_tile(block, use):
        parts = [left_rows(left, block) for left in lefts] if mixing else None

        @pl.loop(0, width // tile)
        def _(t):
            cols = pl.ds(pl.multiple_of(t * tile, tile), tile)
            total = None
            for n, right in enumerate(rights):
                part = parts[n] if mixing else left_rows(lefts[n], block)
                term = matmul_nt(part, right[cols, :]) if flip else matmul(part, right[:, cols])
                total = term if total is None else total + term
            use(cols, total)

    def mate_copy(i):
        return remote(to_mate.at[i], from_mate.at[i], s_mate.at[i], r_mate.at[i], (z, mate))

    def send_x(i, n):
        return remote(stage.at[i, :, right_cols if n == 2 else left_cols], from_x.at[n], s_x.at[n], r_x.at[n], (z, on_x))

    def send_y(i, n):
        return remote(stage.at[i, :, left_cols if n == 2 else right_cols], from_y.at[n], s_y.at[n], r_y.at[n], (z, on_y))

    for i in range(4):

        def give(cols, total, i=i):
            to_mate[i, :, cols] = total.astype(jnp.bfloat16)

        def add(cols, total, i=i):
            total = total + from_mate[i, :, cols].astype(jnp.float32)
            if i < 3:
                stage[i, :, cols] = total.astype(jnp.bfloat16)
            else:
                o_ref[:, cols] = total

        each_tile(target(i, 1 - core), give)
        mate_copy(i).start()
        mate_copy(i).wait_recv()
        each_tile(target(i, core), add)
        if i == 0:
            send_x(0, 0).start()
            send_y(0, 0).start()
        if i == 1:
            send_x(1, 1).start()
        if i == 2:
            send_y(2, 1).start()

    def side_tiles(start, stop):
        size = 256

        @pl.loop(start, stop)
        def _(t):
            cols = pl.ds(pl.multiple_of(t * size, size), size)
            for right, out in zip(side_rights, side_outs):
                out[cols, :] = matmul_tn(side_left[:, cols], right[...]).astype(out.dtype)

    steps = side_left.shape[1] // 256 if side else 0
    if side:
        side_tiles(0, steps // 2)
    send_y(0, 0).wait_recv()
    stage[1, :, right_cols] = (
        stage[1, :, right_cols].astype(jnp.float32) + from_y[0].astype(jnp.float32)
    ).astype(jnp.bfloat16)
    send_x(1, 2).start()
    send_x(0, 0).wait_recv()
    stage[2, :, left_cols] = (
        stage[2, :, left_cols].astype(jnp.float32) + from_x[0].astype(jnp.float32)
    ).astype(jnp.bfloat16)
    send_y(2, 2).start()
    if side:
        side_tiles(steps // 2, steps)
    send_x(1, 1).wait_recv()
    o_ref[:, left_cols] += from_x[1].astype(jnp.float32)
    send_y(2, 1).wait_recv()
    o_ref[:, right_cols] += from_y[1].astype(jnp.float32)
    send_x(1, 2).wait_recv()
    o_ref[:, right_cols] += from_x[2].astype(jnp.float32)
    send_y(2, 2).wait_recv()
    o_ref[:, left_cols] += from_y[2].astype(jnp.float32)
    for i in range(4):
        mate_copy(i).wait_send()
    for copy in (send_x(0, 0), send_x(1, 1), send_x(1, 2), send_y(0, 0), send_y(2, 1), send_y(2, 2)):
        copy.wait_send()
    if mixing:
        for copy in notes:
            copy.wait_send()


def plane_scatter(lefts, rights, flip, number, squares=None, side=None):
    mixing = squares is not None
    side_left, side_rights = side or (None, ())
    rows = lefts[0].shape[0] // 8
    width = rights[0].shape[0 if flip else 1]
    depth = sum(left.shape[1] for left in lefts)
    ins = [*lefts, *rights]
    outs = [jax.ShapeDtypeStruct((rows, width), jnp.float32)]
    scratch = [pltpu.VMEM((n, rows, width), jnp.bfloat16) for n in (4, 4, 3)]
    scratch += [pltpu.VMEM((3, rows, width // 2), jnp.bfloat16) for _ in range(2)]
    scratch += [pltpu.SemaphoreType.DMA((n,)) for n in (4, 4, 3, 3, 3, 3)]
    if mixing:
        ins.append(squares)
        outs.append(jax.ShapeDtypeStruct(squares.shape, jnp.float32))
        scratch += [
            pltpu.VMEM((8, *squares.shape), jnp.float32),
            pltpu.VMEM(squares.shape[::-1], jnp.float32),
            pltpu.SemaphoreType.DMA((7,)),
            pltpu.SemaphoreType.DMA((7,)),
        ]
    if side:
        ins += [side_left, *side_rights]
        outs += [jax.ShapeDtypeStruct((side_left.shape[1], r.shape[1]), jnp.bfloat16) for r in side_rights]
    flops = 16 * rows * width * depth + sum(2 * side_left.size * r.shape[1] for r in side_rights)
    return pl.pallas_call(
        functools.partial(scatter_kernel, len(lefts), flip, mixing, len(side_rights), 512),
        out_shape=outs,
        in_specs=[VMEM] * len(ins),
        out_specs=[VMEM] * len(outs),
        scratch_shapes=scratch,
        compiler_params=pltpu.CompilerParams(
            collective_id=number, has_side_effects=True, vmem_limit_bytes=VMEM_BYTES
        ),
        cost_estimate=pl.CostEstimate(
            flops=flops, bytes_accessed=250 * rows * width, transcendentals=0
        ),
        name=f"plane_scatter_{number}",
    )(*ins)


def dot_fine(left, right, dims):
    high = right.astype(jnp.bfloat16)
    low = (right - high.astype(jnp.float32)).astype(jnp.bfloat16)
    product = functools.partial(
        lax.dot_general, dimension_numbers=(dims, ((), ())), preferred_element_type=jnp.float32
    )
    return product(left, high) + product(left, low)


NN, NT, TN = ((1,), (0,)), ((1,), (1,)), ((0,), (0,))


def block_tables(count, rate, rows):
    spot = lax.broadcasted_iota(jnp.int32, (rows, 1), 0)
    live = spot < count
    behind = jnp.where(live, jnp.exp(-rate * spot.astype(jnp.float32)), 0.0)
    ahead = jnp.where(live, jnp.exp(-rate * (count - spot).astype(jnp.float32)), 0.0)
    fade = jnp.exp(jnp.full((1, HEAD_DIM), -rate * count.astype(jnp.float32), jnp.float32))
    return live, behind, ahead, fade


def fill_decay(base, rates):
    heads, rows, _ = base.shape
    gap = lax.broadcasted_iota(jnp.int32, (rows, rows), 0) - lax.broadcasted_iota(jnp.int32, (rows, rows), 1)
    far = jnp.maximum(gap, 0).astype(jnp.float32)
    for t in range(heads):
        base[t] = jnp.where(gap >= 0, jnp.exp(-rates[t] * far), 0.0)


def mix_kernel(counts, rates, hidden, weight, pre, attn_gate, qkv, entering, squares, base, state):
    b = pl.program_id(0)
    rows = hidden.shape[0]
    wide = weight.shape[1] // 4

    @pl.when(b == 0)
    def _():
        fill_decay(base, rates)
        state[...] = jnp.zeros_like(state)

    count = counts[b]
    out = matmul(hidden[...], weight[...])
    pre[...] = out[:, : 2 * wide]
    gate = out[:, 3 * wide :]
    query = jax.nn.silu(out[:, :wide]).astype(jnp.bfloat16)
    keys = jax.nn.silu(out[:, wide : 2 * wide]).astype(jnp.bfloat16)
    value = out[:, 2 * wide : 3 * wide].astype(jnp.bfloat16)
    qkv[:, :wide] = query
    qkv[:, wide : 2 * wide] = keys
    qkv[:, 2 * wide :] = value
    attn_gate[:, wide:] = gate
    entering[0] = state[...]
    total = jnp.zeros((8, rows), jnp.float32)
    for t in range(state.shape[0]):
        at = slice(t * HEAD_DIM, (t + 1) * HEAD_DIM)
        q, k, v = query[:, at], keys[:, at], value[:, at]
        live, behind, ahead, fade = block_tables(count, rates[t], rows)
        mask = jnp.where(live, base[t], 0.0)
        probs = (matmul_nt(q, k) * mask).astype(jnp.bfloat16)
        attn = matmul(probs, v) + behind * dot_fine(q, state[t], NN)
        attn_gate[:, at] = attn
        total += lax.dot_general(
            jnp.ones((8, HEAD_DIM), jnp.float32), attn * attn, (NT, ((), ())), precision=HIGH,
            preferred_element_type=jnp.float32,
        )
        local = dot_fine(k, v.astype(jnp.float32) * ahead, TN)
        state[t] = jnp.where(count < rows, 0.0, fade * state[t] + local)
    squares[pl.ds(b, 1), :] = total[:1]


def mix_heads(counts, rates, hidden, weight):
    rows = hidden.shape[0] // 8
    wide = weight.shape[1] // 4
    heads = wide // HEAD_DIM
    f32 = jnp.float32

    def by_block(width):
        return pl.BlockSpec((rows, width), lambda b: (b, 0))

    def whole(*shape):
        return pl.BlockSpec(shape, lambda b: (0,) * len(shape))

    return pl.pallas_call(
        mix_kernel,
        grid=(8,),
        out_shape=[
            jax.ShapeDtypeStruct((8 * rows, 2 * wide), f32),
            jax.ShapeDtypeStruct((8 * rows, 2 * wide), f32),
            jax.ShapeDtypeStruct((8 * rows, 3 * wide), jnp.bfloat16),
            jax.ShapeDtypeStruct((8, heads, HEAD_DIM, HEAD_DIM), f32),
            jax.ShapeDtypeStruct((8, rows), f32),
        ],
        in_specs=[SMEM, SMEM, by_block(hidden.shape[1]), whole(*weight.shape)],
        out_specs=[
            by_block(2 * wide),
            by_block(2 * wide),
            by_block(3 * wide),
            pl.BlockSpec((1, heads, HEAD_DIM, HEAD_DIM), lambda b: (b, 0, 0, 0)),
            whole(8, rows),
        ],
        scratch_shapes=[pltpu.VMEM((heads, rows, rows), f32), pltpu.VMEM((heads, HEAD_DIM, HEAD_DIM), f32)],
        compiler_params=pltpu.CompilerParams(
            dimension_semantics=("arbitrary",), vmem_limit_bytes=VMEM_BYTES
        ),
        cost_estimate=pl.CostEstimate(
            flops=2 * hidden.size * weight.shape[1], bytes_accessed=4 * hidden.size, transcendentals=0
        ),
        name="mix_heads",
    )(counts, rates, hidden, weight)


def unmix_kernel(
    counts, rates, low, weight, pre, attn_gate, qkv, entering, scale, inner, grads, out_term, base, state, total
):
    step = pl.program_id(0)
    b = pl.num_programs(0) - 1 - step
    rows, width = low.shape
    wide = weight.shape[0]

    @pl.when(step == 0)
    def _():
        fill_decay(base, rates)
        state[...] = jnp.zeros_like(state)
        total[...] = jnp.zeros_like(total)

    count = counts[b]

    def column(ref):
        here = lax.broadcasted_iota(jnp.int32, (8, rows), 0) == b
        turned = jnp.transpose(jnp.where(here, ref[...], 0.0))
        return jnp.sum(turned, axis=1, keepdims=True)

    factor, inside = column(scale), column(inner)
    attn, gate = attn_gate[:, :wide], attn_gate[:, wide:]
    normal = attn * factor
    grad = matmul_nt(low[...], weight[...])
    grads[:, 3 * wide :] = (grad * normal).astype(jnp.bfloat16)
    grad_attn = (factor * grad * gate - normal * factor * inside * (1.0 / width)).astype(jnp.bfloat16)
    total[...] += matmul_tn((normal * gate).astype(jnp.bfloat16), low[...])
    for t in range(state.shape[0]):
        at = slice(t * HEAD_DIM, (t + 1) * HEAD_DIM)
        q, k, v = (qkv[:, i * wide + t * HEAD_DIM : i * wide + (t + 1) * HEAD_DIM] for i in range(3))
        g = grad_attn[:, at]
        live, behind, ahead, fade = block_tables(count, rates[t], rows)
        mask = jnp.where(live, base[t], 0.0)
        probs = (matmul_nt(q, k) * mask).astype(jnp.bfloat16)
        raw = (matmul_nt(g, v) * mask).astype(jnp.bfloat16)
        leaving = jnp.where(count < rows, 0.0, state[t])
        grad_q = matmul(raw, k) + behind * dot_fine(g, entering[0, t], NT)
        grad_k = matmul_tn(raw, q) + ahead * dot_fine(v, leaving, NT)
        grad_v = matmul_tn(probs, g) + ahead * dot_fine(k, leaving, NN)
        state[t] = dot_fine(q, g.astype(jnp.float32) * behind, TN) + fade * leaving
        grads[:, at] = (grad_q * silu_slope(pre[:, at])).astype(jnp.bfloat16)
        after = slice(wide + t * HEAD_DIM, wide + (t + 1) * HEAD_DIM)
        grads[:, after] = (grad_k * silu_slope(pre[:, after])).astype(jnp.bfloat16)
        grads[:, 2 * wide + t * HEAD_DIM : 2 * wide + (t + 1) * HEAD_DIM] = grad_v.astype(jnp.bfloat16)

    @pl.when(step == pl.num_programs(0) - 1)
    def _():
        out_term[...] = total[...].astype(jnp.bfloat16)


def unmix_heads(counts, rates, low, weight, pre, attn_gate, qkv, entering, scale, inner):
    rows, width = low.shape[0] // 8, low.shape[1]
    wide = weight.shape[0]
    heads = wide // HEAD_DIM
    f32 = jnp.float32

    def by_block(columns):
        return pl.BlockSpec((rows, columns), lambda s: (7 - s, 0))

    def whole(*shape):
        return pl.BlockSpec(shape, lambda s: (0,) * len(shape))

    return pl.pallas_call(
        unmix_kernel,
        grid=(8,),
        out_shape=[
            jax.ShapeDtypeStruct((8 * rows, 4 * wide), jnp.bfloat16),
            jax.ShapeDtypeStruct((wide, width), jnp.bfloat16),
        ],
        in_specs=[
            SMEM,
            SMEM,
            by_block(width),
            whole(wide, width),
            by_block(2 * wide),
            by_block(2 * wide),
            by_block(3 * wide),
            pl.BlockSpec((1, heads, HEAD_DIM, HEAD_DIM), lambda s: (7 - s, 0, 0, 0)),
            whole(8, rows),
            whole(8, rows),
        ],
        out_specs=[by_block(4 * wide), whole(wide, width)],
        scratch_shapes=[
            pltpu.VMEM((heads, rows, rows), f32),
            pltpu.VMEM((heads, HEAD_DIM, HEAD_DIM), f32),
            pltpu.VMEM((wide, width), f32),
        ],
        compiler_params=pltpu.CompilerParams(
            dimension_semantics=("arbitrary",), vmem_limit_bytes=VMEM_BYTES
        ),
        cost_estimate=pl.CostEstimate(
            flops=4 * low.size * wide, bytes_accessed=6 * low.size, transcendentals=0
        ),
        name="unmix_heads",
    )(counts, rates, low, weight, pre, attn_gate, qkv, entering, scale, inner)


def after(value, *others):
    return lax.optimization_barrier((value, *others))[0]


def fast_plan(
    tokens,
    block_counts,
    decay_rate,
    query_weight,
    key_weight,
    value_weight,
    gate_weight,
    out_weight,
    first_weight,
    second_weight,
    down_weight,
    cotangent,
):
    rows, width = tokens.shape
    nz = lax.axis_size("dp")
    nf = lax.axis_size("fsdp")
    chips = nf // 2
    plane = lax.axis_index("fsdp")
    chip, core = plane // 2, plane % 2
    bf = jnp.bfloat16
    half = HEADS // nf
    own = half * HEAD_DIM
    units = first_weight.shape[1] // nf
    own_heads = chips * (half * core + jnp.arange(half)) + chip

    def columns(weight):
        r = weight.shape[0]
        w = weight.reshape(r, 2, half, chips, HEAD_DIM).transpose(3, 1, 0, 2, 4)
        return w.reshape(nf, r, own)

    def columns_ff(weight):
        r, n = weight.shape
        return weight.reshape(r, nz, nf, n // (nz * nf)).transpose(2, 0, 1, 3).reshape(nf, r, n // nf)

    def along(weight):
        weight = weight.reshape(-1, weight.shape[-1])
        return lax.all_gather(weight, "dp", axis=0, tiled=True)

    swap = [(i, i ^ 1) for i in range(nf)]

    def cross(x):
        keep = lax.dynamic_slice_in_dim(x, core * half, half, 0)
        send = lax.dynamic_slice_in_dim(x, (1 - core) * half, half, 0)
        got = lax.ppermute(send, "fsdp", swap)
        return jnp.stack([jnp.where(core == 0, keep, got), jnp.where(core == 0, got, keep)], axis=1)

    def uncross(x):
        keep = lax.dynamic_index_in_dim(x, core, 1, False)
        send = lax.dynamic_index_in_dim(x, 1 - core, 1, False)
        got = lax.ppermute(send, "fsdp", swap)
        return jnp.concatenate([jnp.where(core == 0, keep, got), jnp.where(core == 0, got, keep)], axis=0)

    heads_weight = jnp.concatenate(
        [columns(w) for w in (query_weight, key_weight, value_weight, gate_weight)], axis=-1
    )
    note = jnp.broadcast_to(block_counts, (8, 128))
    heads_weight, counts = plane_swap(heads_weight, 0, note)
    counts = counts[:, 0, 0]
    w_heads = along(heads_weight)
    rates = decay_rate[own_heads]
    inputs = tokens.astype(jnp.float32)
    in_normed, in_scale = normed(inputs)
    units_weight = jnp.concatenate([columns_ff(first_weight), columns_ff(second_weight)], axis=-1)
    units_weight = after(units_weight, heads_weight)
    hidden, units_weight = plane_gather(in_normed.astype(bf), 1, swap=units_weight)
    wo = lax.all_gather(after(out_weight, hidden), "dp", axis=0)
    (cot,) = plane_gather(after(cotangent, hidden), 2)
    w_units = along(after(units_weight, cot))
    wd = along(after(down_weight, cot))

    pre, attn_gate, qkv, entering, squares = mix_heads(counts, rates, hidden, w_heads)
    wo = cross(after(wo, squares)).reshape(own, width)
    out_own, scale = plane_scatter([attn_gate], [wo], False, 3, squares=squares)
    middle = inputs + out_own
    mid_normed, mid_scale = normed(middle)
    (mid,) = plane_gather(mid_normed.astype(bf), 4)
    w1, w2 = w_units[:, :units], w_units[:, units:]
    first, second = matmul(mid, w1), matmul(mid, w2)
    product = (first * second).astype(bf)

    down_term = matmul_tn(product, cot).astype(bf)
    grad_product = matmul_nt(cot, wd)
    grad_first = (grad_product * second).astype(bf)
    grad_second = (grad_product * first).astype(bf)
    grad_first, grad_second, down_term = lax.optimization_barrier((grad_first, grad_second, down_term))
    down_sum = lax.psum_scatter(down_term, "dp", scatter_dimension=0, tiled=True)
    grad_mid, first_term, second_term = plane_scatter(
        [grad_first, grad_second], [w1, w2], True, 5, side=(mid, (grad_first, grad_second))
    )
    units_sum = lax.psum_scatter(
        jnp.concatenate([first_term, second_term], axis=-1), "dp", scatter_dimension=0, tiled=True
    )
    grad_middle = cotangent.astype(jnp.float32) + norm_back(middle, mid_scale, grad_mid)
    low = grad_middle.astype(bf)
    inner = jnp.sum(low.astype(jnp.float32) * out_own, axis=-1)
    note = jnp.pad(inner.reshape(-1, 128), ((0, 8 - rows // 128), (0, 0)))
    low, inner = plane_gather(low, 6, note=note)
    inner = inner[:, : rows // 128].reshape(nf, rows)
    grad_heads, out_term = unmix_heads(
        counts, rates, low, wo, pre, attn_gate, qkv, entering, scale, inner
    )
    out_term = uncross(out_term.reshape(half, 2, -1, width))
    out_sum = lax.psum_scatter(out_term, "dp", scatter_dimension=0, tiled=False)
    heads_term = matmul_tn(hidden, grad_heads).astype(bf)
    heads_sum = lax.psum_scatter(heads_term, "dp", scatter_dimension=0, tiled=True)
    (grad_hidden,) = plane_scatter([after(grad_heads, heads_term)], [w_heads], True, 7)
    tokens_grad = grad_middle + norm_back(inputs, in_scale, grad_hidden)
    (down_own,) = plane_scatter([after(product, grad_hidden)], [wd], False, 8)
    block_out = (middle + down_own).astype(bf)

    def columns_back(t):
        r = t.shape[1]
        t = t.reshape(chips, 2, r, half, HEAD_DIM).transpose(2, 1, 3, 0, 4)
        return t.reshape(r, width).astype(jnp.float32)

    def columns_ff_back(t):
        r, n = t.shape[1:]
        t = t.reshape(nf, r, nz, n // nz).transpose(1, 2, 0, 3)
        return t.reshape(r, n * nf).astype(jnp.float32)

    down_grad = down_sum.astype(jnp.float32)
    units_sum = after(units_sum, down_grad)
    (units_grad,) = plane_swap(units_sum.reshape(nf, -1, 2 * units), 9)
    first_grad = columns_ff_back(units_grad[..., :units])
    second_grad = columns_ff_back(units_grad[..., units:])
    out_grad = after(out_sum, units_grad).astype(jnp.float32)
    heads_sum = after(heads_sum, out_grad)
    (heads_grad,) = plane_swap(heads_sum.reshape(nf, -1, 4 * own), 10)
    grads = [columns_back(heads_grad[..., i * own : (i + 1) * own]) for i in range(4)]
    return (block_out, tokens_grad, *grads, out_grad, first_grad, second_grad, down_grad)


def fits(mesh):
    return mesh.shape["dp"] == 4 and mesh.shape["fsdp"] == 8


def solution(mesh):
    return jax.shard_map(
        fast_plan if fits(mesh) else shards,
        mesh=mesh,
        in_specs=(
            P(("dp", "fsdp"), None),
            P("dp", "fsdp"),
            P(),
            P(("dp", "fsdp"), None),
            P(("dp", "fsdp"), None),
            P(("dp", "fsdp"), None),
            P(("dp", "fsdp"), None),
            P(("dp", "fsdp"), None),
            P(("dp", "fsdp"), None),
            P(("dp", "fsdp"), None),
            P(("dp", "fsdp"), None),
            P(("dp", "fsdp"), None),
        ),
        out_specs=(
            P(("dp", "fsdp"), None),
            P(("dp", "fsdp"), None),
            P(("dp", "fsdp"), None),
            P(("dp", "fsdp"), None),
            P(("dp", "fsdp"), None),
            P(("dp", "fsdp"), None),
            P(("dp", "fsdp"), None),
            P(("dp", "fsdp"), None),
            P(("dp", "fsdp"), None),
            P(("dp", "fsdp"), None),
        ),
        check_vma=False,
    )
```

```python
import functools

import jax
import jax.numpy as jnp
from jax import lax
from jax.experimental import pallas as pl
from jax.experimental.pallas import tpu as pltpu
from jax.sharding import PartitionSpec as P

HEADS = 16
HEAD_DIM = 128


EPS = 1e-06
HIGH = lax.Precision.HIGHEST


def carried_in(part, axis, combine, identity):
    place = lax.axis_index(axis)
    gathered = jax.tree.map(lambda a: lax.all_gather(a, axis), part)
    state = jax.tree.map(lambda a, e: jnp.zeros_like(a) + jnp.asarray(e, a.dtype), part, identity)

    def carried_one(lap, state):
        return combine(
            state, jax.tree.map(lambda a: lax.dynamic_index_in_dim(a, lap, 0, False), gathered)
        )

    return lax.fori_loop(0, place, carried_one, state)


def prefix_2(value, axis, join, neutral):
    count = lax.axis_size(axis)
    place = lax.axis_index(axis)
    ahead = count - 1 - place
    gathered = jax.tree.map(
        lambda a, kind: lax.all_gather(a.astype(kind), axis), value, (jnp.bfloat16, jnp.bfloat16)
    )
    state = jax.tree.map(lambda a, e: jnp.zeros_like(a) + jnp.asarray(e, a.dtype), value, neutral)

    def prefix_one(lap, state):
        source = count - 1 - lap
        return join(
            state,
            jax.tree.map(
                lambda a, own: lax.dynamic_index_in_dim(a, source, 0, False).astype(own.dtype),
                gathered,
                value,
            ),
        )

    return lax.fori_loop(0, ahead, prefix_one, state)


def normed(value):
    scale = lax.rsqrt(jnp.mean(value * value, axis=-1, keepdims=True) + EPS)
    return (value * scale, scale)


def norm_back(value, scale, grad):
    inner = jnp.mean(grad * value, axis=-1, keepdims=True)
    return scale * (grad - value * scale * scale * inner)


def silu_slope(value):
    sig = jax.nn.sigmoid(value)
    return sig * (1.0 + value * (1.0 - sig))


def chain_step(earlier, later):
    e_fade, e_state = earlier
    l_fade, l_state = later
    return (l_fade * e_fade, l_fade[:, None, None] * e_state + l_state)


def matmul(left, right):
    return jnp.dot(left, right, preferred_element_type=jnp.float32)


def matmul_tn(left, right):
    return lax.dot_general(
        left, right, (((0,), (0,)), ((), ())), preferred_element_type=jnp.float32
    )


def matmul_nt(left, right):
    return lax.dot_general(
        left, right, (((1,), (1,)), ((), ())), preferred_element_type=jnp.float32
    )


def decay_tables(count, rates, rows):
    pos = lax.iota(jnp.int32, rows)
    live = pos < count
    keep = (pos[:, None] >= pos[None, :]) & live[:, None] & live[None, :]
    spacing = jnp.where(keep, (pos[:, None] - pos[None, :]).astype(jnp.float32), 0.0)
    mask = jnp.where(keep[None], jnp.exp(-rates[:, None, None] * spacing[None]), 0.0)
    ahead = jnp.where(
        live[:, None], jnp.exp(-rates[None, :] * (count - pos)[:, None].astype(jnp.float32)), 0.0
    )
    behind = jnp.where(
        live[:, None], jnp.exp(-rates[None, :] * pos[:, None].astype(jnp.float32)), 0.0
    )
    fade = jnp.exp(-rates * count.astype(jnp.float32))
    return (mask, ahead, behind, fade)


def shards(
    tokens,
    block_counts,
    decay_rate,
    query_weight,
    key_weight,
    value_weight,
    gate_weight,
    out_weight,
    first_weight,
    second_weight,
    down_weight,
    cotangent,
):
    rows = tokens.shape[0]
    gathered = (
        lax.all_gather(query_weight, ("dp", "fsdp"), axis=0, tiled=True),
        lax.all_gather(key_weight, ("dp", "fsdp"), axis=0, tiled=True),
        lax.all_gather(value_weight, ("dp", "fsdp"), axis=0, tiled=True),
        lax.all_gather(gate_weight, ("dp", "fsdp"), axis=0, tiled=True),
        lax.all_gather(out_weight, ("dp", "fsdp"), axis=0, tiled=True),
        lax.all_gather(first_weight, ("dp", "fsdp"), axis=0, tiled=True),
        lax.all_gather(second_weight, ("dp", "fsdp"), axis=0, tiled=True),
        lax.all_gather(down_weight, ("dp", "fsdp"), axis=0, tiled=True),
    )
    w_query, w_key, w_value, w_gate, w_out, w_first, w_second, w_down = gathered
    count = block_counts[0, 0]
    closes = count < rows
    mask, ahead, behind, fade = decay_tables(count, decay_rate, rows)
    passing = jnp.where(closes, 0.0, fade)
    inputs = tokens.astype(jnp.float32)
    in_normed, in_scale = normed(inputs)
    hidden = in_normed.astype(jnp.bfloat16)
    q_pre = matmul(hidden, w_query)
    k_pre = matmul(hidden, w_key)
    value = matmul(hidden, w_value).astype(jnp.bfloat16)
    gate = matmul(hidden, w_gate)
    query = jax.nn.silu(q_pre).astype(jnp.bfloat16)
    keys = jax.nn.silu(k_pre).astype(jnp.bfloat16)
    query_heads = query.reshape(rows, HEADS, HEAD_DIM)
    key_heads = keys.reshape(rows, HEADS, HEAD_DIM)
    value_heads = value.reshape(rows, HEADS, HEAD_DIM)
    query_wide = query_heads.astype(jnp.float32)
    key_wide = key_heads.astype(jnp.float32)
    value_ahead = value_heads.astype(jnp.float32) * ahead[:, :, None]
    raw = jnp.einsum("ihe,jhe->hij", query_heads, key_heads, preferred_element_type=jnp.float32)
    probs = (raw * mask).astype(jnp.bfloat16)
    intra = jnp.einsum("hij,jhe->ihe", probs, value_heads, preferred_element_type=jnp.float32)
    local = jnp.einsum("jhe,jhf->hef", key_wide, value_ahead, precision=HIGH)
    local_sent = jnp.where(closes, 0.0, local)
    prefix = carried_in(
        (passing, local_sent), "fsdp", chain_step, (jnp.ones_like(fade), jnp.zeros_like(local))
    )
    entering = prefix[1]
    inter = behind[:, :, None] * jnp.einsum("ihe,hef->ihf", query_wide, entering, precision=HIGH)
    attn = (intra + inter).reshape(rows, HEADS * HEAD_DIM)
    attn_normed, attn_scale = normed(attn)
    mixed = (attn_normed * gate).astype(jnp.bfloat16)
    middle = inputs + matmul(mixed, w_out)
    mid_normed, mid_scale = normed(middle)
    mid = mid_normed.astype(jnp.bfloat16)
    first = matmul(mid, w_first)
    second = matmul(mid, w_second)
    product = (first * second).astype(jnp.bfloat16)
    block_out = (middle + matmul(product, w_down)).astype(jnp.bfloat16)
    w_first, w_second, w_down = (
        lax.all_gather(first_weight, ("dp", "fsdp"), axis=0, tiled=True),
        lax.all_gather(second_weight, ("dp", "fsdp"), axis=0, tiled=True),
        lax.all_gather(down_weight, ("dp", "fsdp"), axis=0, tiled=True),
    )
    grad_product = matmul_nt(cotangent, w_down)
    grad_first = (grad_product * second).astype(jnp.bfloat16)
    grad_second = (grad_product * first).astype(jnp.bfloat16)
    grad_mid = matmul_nt(grad_first, w_first) + matmul_nt(grad_second, w_second)
    grad_middle = cotangent.astype(jnp.float32) + norm_back(middle, mid_scale, grad_mid)

    def scattered(left, right, after):
        left, _ = lax.optimization_barrier((left, after))
        term = matmul_tn(left, right)
        return lax.psum_scatter(term, ("dp", "fsdp"), scatter_dimension=0, tiled=True)

    down_grad = scattered(product, cotangent, grad_middle)
    first_grad = scattered(mid, grad_first, down_grad)
    second_grad = scattered(mid, grad_second, first_grad)
    grad_middle, _ = lax.optimization_barrier((grad_middle, second_grad))
    w_query, w_key, w_value, w_gate, w_out = (
        lax.all_gather(query_weight, ("dp", "fsdp"), axis=0, tiled=True),
        lax.all_gather(key_weight, ("dp", "fsdp"), axis=0, tiled=True),
        lax.all_gather(value_weight, ("dp", "fsdp"), axis=0, tiled=True),
        lax.all_gather(gate_weight, ("dp", "fsdp"), axis=0, tiled=True),
        lax.all_gather(out_weight, ("dp", "fsdp"), axis=0, tiled=True),
    )
    grad_mid_low = grad_middle.astype(jnp.bfloat16)
    out_term = matmul_tn(mixed, grad_mid_low)
    grad_mixed = matmul_nt(grad_mid_low, w_out)
    grad_gate = (grad_mixed * attn_normed).astype(jnp.bfloat16)
    grad_attn = norm_back(attn, attn_scale, grad_mixed * gate).astype(jnp.bfloat16)
    grad_heads = grad_attn.reshape(rows, HEADS, HEAD_DIM)
    grad_heads_wide = grad_heads.astype(jnp.float32) * behind[:, :, None]
    grad_probs = jnp.einsum(
        "ihe,jhe->hij", grad_heads, value_heads, preferred_element_type=jnp.float32
    )
    grad_raw = (grad_probs * mask).astype(jnp.bfloat16)
    grad_entering = jnp.einsum("ihe,ihf->hef", query_wide, grad_heads_wide, precision=HIGH)
    suffix = prefix_2(
        (passing, grad_entering),
        "fsdp",
        chain_step,
        (jnp.ones_like(fade), jnp.zeros_like(grad_entering)),
    )
    grad_leaving = jnp.where(closes, 0.0, suffix[1])
    grad_query = jnp.einsum("hij,jhe->ihe", grad_raw, key_heads, preferred_element_type=jnp.float32)
    grad_query = grad_query + jnp.einsum("ihf,hef->ihe", grad_heads_wide, entering, precision=HIGH)
    grad_keys = jnp.einsum(
        "hij,ihe->jhe", grad_raw, query_heads, preferred_element_type=jnp.float32
    )
    grad_keys = grad_keys + jnp.einsum("hef,jhf->jhe", grad_leaving, value_ahead, precision=HIGH)
    grad_value = jnp.einsum("hij,ihe->jhe", probs, grad_heads, preferred_element_type=jnp.float32)
    grad_value = grad_value + ahead[:, :, None] * jnp.einsum(
        "hef,jhe->jhf", grad_leaving, key_wide, precision=HIGH
    )
    width = HEADS * HEAD_DIM
    grad_q_pre = (grad_query.reshape(rows, width) * silu_slope(q_pre)).astype(jnp.bfloat16)
    grad_k_pre = (grad_keys.reshape(rows, width) * silu_slope(k_pre)).astype(jnp.bfloat16)
    grad_v = grad_value.reshape(rows, width).astype(jnp.bfloat16)
    query_term = matmul_tn(hidden, grad_q_pre)
    key_term = matmul_tn(hidden, grad_k_pre)
    value_term = matmul_tn(hidden, grad_v)
    gate_term = matmul_tn(hidden, grad_gate)
    grad_hidden = matmul_nt(grad_q_pre, w_query) + matmul_nt(grad_k_pre, w_key)
    grad_hidden = grad_hidden + matmul_nt(grad_v, w_value) + matmul_nt(grad_gate, w_gate)
    tokens_grad = grad_middle + norm_back(inputs, in_scale, grad_hidden)
    query_grad, key_grad, value_grad, gate_grad, out_grad = (
        lax.psum_scatter(query_term, ("dp", "fsdp"), scatter_dimension=0, tiled=True),
        lax.psum_scatter(key_term, ("dp", "fsdp"), scatter_dimension=0, tiled=True),
        lax.psum_scatter(value_term, ("dp", "fsdp"), scatter_dimension=0, tiled=True),
        lax.psum_scatter(gate_term, ("dp", "fsdp"), scatter_dimension=0, tiled=True),
        lax.psum_scatter(out_term, ("dp", "fsdp"), scatter_dimension=0, tiled=True),
    )
    return (
        block_out,
        tokens_grad,
        query_grad,
        key_grad,
        value_grad,
        gate_grad,
        out_grad,
        first_grad,
        second_grad,
        down_grad,
    )


MESH = pl.DeviceIdType.MESH
VMEM_BYTES = 60 * 2**20
ANY = pl.BlockSpec(memory_space=pl.ANY)
VMEM = pl.BlockSpec(memory_space=pltpu.VMEM)
SMEM = pl.BlockSpec(memory_space=pltpu.SMEM)


def place():
    plane = lax.axis_index("fsdp")
    return lax.axis_index("dp"), plane // 4, (plane // 2) % 2, plane % 2


def other(i, way):
    return i + way - 2 * i * way


def member(y, x, core):
    return (y * 2 + x) * 2 + core


def plane_peers(y, x, core):
    ways = [(dy, dx, dc) for dy in (1, 0) for dx in (1, 0) for dc in (0, 1) if dy + dx + dc]
    return [member(other(y, dy), other(x, dx), other(core, dc)) for dy, dx, dc in ways]


def greet(z, members):
    barrier = pltpu.get_barrier_semaphore()
    for device in members:
        pl.semaphore_signal(barrier, inc=1, device_id=(z, device), device_id_type=MESH)
    pl.semaphore_wait(barrier, len(members))


def remote(src, dst, send, recv, device):
    return pltpu.make_async_remote_copy(
        src_ref=src, dst_ref=dst, send_sem=send, recv_sem=recv, device_id=device, device_id_type=MESH
    )


def note_copies(z, me, peers, note, notes, send, recv):
    return [
        remote(note, notes.at[me], send.at[n], recv.at[n], (z, d)) for n, d in enumerate(peers)
    ]


def pack_columns(spots, weights, stages):
    for f, n, src, m, dst, wide in spots:
        stages[m][f, :, dst : dst + wide] = weights[n][:, src : src + wide]


def unpack_columns(spots, stages, grads):
    for f, n, src, m, dst, wide in spots:
        grads[n][:, src : src + wide] = stages[m][f, :, dst : dst + wide].astype(jnp.float32)


def gather_kernel(with_note, spots, *refs):
    refs = list(refs)
    x_ref = refs.pop(0)
    note = refs.pop(0) if with_note else None
    weights = [refs.pop(0) for _ in range(2)] if spots else []
    o_ref = refs.pop(0)
    notes = refs.pop(0) if with_note else None
    swapped = refs.pop(0) if spots else None
    local, send, recv = refs[:3]
    refs = refs[3:]
    z, y, x, core = place()
    me, mate = member(y, x, core), member(y, x, 1 - core)
    on_x, on_y, across = member(y, 1 - x, core), member(1 - y, x, core), member(1 - y, 1 - x, core)
    peers = plane_peers(y, x, core)
    greet(z, peers)
    half = x_ref.shape[0] // 2
    low, high = pl.ds(0, half), pl.ds(half, half)

    def own(part, n, device):
        return remote(x_ref.at[part], o_ref.at[me, part], send.at[n], recv.at[n], (z, device))

    def pass_on(block, part, n, device):
        ref = o_ref.at[block, part]
        return remote(ref, ref, send.at[n], recv.at[n], (z, device))

    keep = pltpu.make_async_copy(x_ref, o_ref.at[me], local.at[0])
    first = [own(low, 0, on_y), own(high, 1, on_x), own(high, 2, on_y), own(low, 3, on_x)]
    mine = remote(x_ref, o_ref.at[me], send.at[4], recv.at[4], (z, mate))
    extra = []
    if with_note:
        extra += note_copies(z, me, peers, note, notes, refs[0], refs[1])
        refs = refs[2:]
    for copy in first + extra:
        copy.start()
    mine.start()
    keep.start()
    if spots:
        swap = refs[0]
        pack_columns(spots, weights, [swap])
        moves = [
            remote(swap.at[d], swapped.at[me], refs[1].at[n], refs[2].at[n], (z, d))
            for n, d in enumerate(peers)
        ]
        keep_swap = pltpu.make_async_copy(swap.at[me], swapped.at[me], local.at[1])
        keep_swap.start()
        for copy in moves:
            copy.start()
        extra += moves
    if with_note:
        notes[me] = note[...]
    first[0].wait_recv()
    relay_x = pass_on(on_y, low, 5, on_x)
    relay_x.start()
    first[1].wait_recv()
    relay_y = pass_on(on_x, high, 6, on_y)
    relay_y.start()
    first[2].wait_recv()
    y_mate = remote(o_ref.at[on_y], o_ref.at[on_y], send.at[7], recv.at[7], (z, mate))
    y_mate.start()
    first[3].wait_recv()
    x_mate = remote(o_ref.at[on_x], o_ref.at[on_x], send.at[8], recv.at[8], (z, mate))
    x_mate.start()
    relay_x.wait_recv()
    low_mate = pass_on(across, low, 9, mate)
    low_mate.start()
    relay_y.wait_recv()
    high_mate = pass_on(across, high, 10, mate)
    high_mate.start()
    keep.wait()
    if spots:
        keep_swap.wait()
    for copy in (mine, y_mate, x_mate, low_mate, high_mate, *extra):
        copy.wait_recv()
    for copy in (*first, mine, relay_x, relay_y, y_mate, x_mate, low_mate, high_mate, *extra):
        copy.wait_send()


def plane_gather(value, number, note=None, weights=(), spots=(), shape=None):
    rows, width = value.shape
    ins, in_specs = [value], [ANY]
    outs, out_specs = [jax.ShapeDtypeStruct((8, rows, width), value.dtype)], [ANY]
    scratch = [pltpu.SemaphoreType.DMA((n,)) for n in (2, 11, 11)]
    if note is not None:
        ins.append(note)
        in_specs.append(VMEM)
        outs.append(jax.ShapeDtypeStruct((8, *note.shape), note.dtype))
        out_specs.append(VMEM)
        scratch += [pltpu.SemaphoreType.DMA((7,)) for _ in range(2)]
    if spots:
        ins += weights
        in_specs += [VMEM] * 2
        outs.append(jax.ShapeDtypeStruct(shape, weights[0].dtype))
        out_specs.append(ANY)
        scratch += [pltpu.VMEM(shape, weights[0].dtype)]
        scratch += [pltpu.SemaphoreType.DMA((7,)) for _ in range(2)]
    gathered, *rest = pl.pallas_call(
        functools.partial(gather_kernel, note is not None, spots),
        out_shape=outs,
        in_specs=in_specs,
        out_specs=out_specs,
        scratch_shapes=scratch,
        compiler_params=pltpu.CompilerParams(
            collective_id=number, has_side_effects=True, vmem_limit_bytes=VMEM_BYTES
        ),
        cost_estimate=pl.CostEstimate(flops=0, bytes_accessed=2**20, transcendentals=0),
        name=f"plane_gather_{number}",
    )(*ins)
    return (gathered.reshape(8 * rows, width), *rest)


def spread_kernel(spots, *refs):
    *weights, note, o_ref, notes, stage, local, send, recv, s_note, r_note = refs
    z, y, x, core = place()
    me = member(y, x, core)
    peers = plane_peers(y, x, core)
    pack_columns(spots, weights, [stage])
    greet(z, peers)
    keep = pltpu.make_async_copy(stage.at[me], o_ref.at[me], local)
    copies = [remote(stage.at[d], o_ref.at[me], send.at[n], recv.at[n], (z, d)) for n, d in enumerate(peers)]
    copies += note_copies(z, me, peers, note, notes, s_note, r_note)
    for copy in copies:
        copy.start()
    keep.start()
    notes[me] = note[...]
    keep.wait()
    for copy in copies:
        copy.wait()


def plane_spread(weights, spots, shape, note, number):
    return pl.pallas_call(
        functools.partial(spread_kernel, spots),
        out_shape=[
            jax.ShapeDtypeStruct(shape, weights[0].dtype),
            jax.ShapeDtypeStruct((8, *note.shape), note.dtype),
        ],
        in_specs=[VMEM] * (len(weights) + 1),
        out_specs=[ANY, VMEM],
        scratch_shapes=[pltpu.VMEM(shape, weights[0].dtype), pltpu.SemaphoreType.DMA]
        + [pltpu.SemaphoreType.DMA((7,)) for _ in range(4)],
        compiler_params=pltpu.CompilerParams(
            collective_id=number, has_side_effects=True, vmem_limit_bytes=VMEM_BYTES
        ),
        cost_estimate=pl.CostEstimate(flops=0, bytes_accessed=2**20, transcendentals=0),
        name=f"plane_spread_{number}",
    )(*weights, note)


def collect_kernel(count, *refs):
    sums, stages = refs[:count], refs[count : 2 * count]
    local, send, recv = refs[2 * count :]
    z, y, x, core = place()
    me = member(y, x, core)
    peers = plane_peers(y, x, core)
    greet(z, peers)
    copies = []
    for m, (total, stage) in enumerate(zip(sums, stages)):
        rows = stage.shape[1]

        def part(d, total=total, rows=rows):
            return total.at[pl.ds(pl.multiple_of(d * rows, rows), rows)]

        copies.append(pltpu.make_async_copy(part(me), stage.at[me], local.at[m]))
        copies += [
            remote(part(d), stage.at[me], send.at[m, n], recv.at[m, n], (z, d)) for n, d in enumerate(peers)
        ]
    for copy in copies:
        copy.start()
    for copy in copies:
        copy.wait()


def unpack_kernel(spots, count, *refs):
    unpack_columns(spots, refs[:count], refs[count:])


def plane_collect(sums, spots, columns, outputs, number):
    rows = sums[0].shape[0] // 8
    stages = pl.pallas_call(
        functools.partial(collect_kernel, len(sums)),
        out_shape=[jax.ShapeDtypeStruct((8, rows, t.shape[1]), t.dtype) for t in sums],
        in_specs=[ANY] * len(sums),
        out_specs=[ANY] * len(sums),
        scratch_shapes=[pltpu.SemaphoreType.DMA((len(sums),))]
        + [pltpu.SemaphoreType.DMA((len(sums), 7)) for _ in range(2)],
        compiler_params=pltpu.CompilerParams(collective_id=number, has_side_effects=True),
        cost_estimate=pl.CostEstimate(flops=0, bytes_accessed=2**20, transcendentals=0),
        name=f"plane_collect_{number}",
    )(*sums)
    return pl.pallas_call(
        functools.partial(unpack_kernel, spots, len(sums)),
        out_shape=[jax.ShapeDtypeStruct((rows, columns), jnp.float32) for _ in range(outputs)],
        in_specs=[VMEM] * len(sums),
        out_specs=[VMEM] * outputs,
        compiler_params=pltpu.CompilerParams(vmem_limit_bytes=VMEM_BYTES),
        name=f"unpack_{number}",
    )(*stages)


def scatter_steps(spot, lefts, rights, flip, left_rows, o_ref, buffers):
    to_mate, from_mate, stage, from_x, from_y, s_mate, r_mate, s_x, r_x, s_y, r_y = buffers
    z, y, x, core = spot
    rows, width = o_ref.shape
    tile = 512
    mate = member(y, x, 1 - core)
    on_x, on_y = member(y, 1 - x, core), member(1 - y, x, core)
    left_cols, right_cols = pl.ds(0, width // 2), pl.ds(width // 2, width // 2)

    def target(i, c):
        return member(other(y, 1 - i % 2), other(x, 1 - i // 2), c)

    def each_tile(block, use):
        parts = [left_rows(left, block) for left in lefts] if left_rows else None
        here = pl.ds(pl.multiple_of(block * rows, rows), rows)

        @pl.loop(0, width // tile)
        def _(t):
            cols = pl.ds(pl.multiple_of(t * tile, tile), tile)
            total = None
            for n, right in enumerate(rights):
                part = parts[n] if left_rows else lefts[n][here, :]
                term = matmul_nt(part, right[cols, :]) if flip else matmul(part, right[:, cols])
                total = term if total is None else total + term
            use(cols, total)

    def mate_copy(i):
        return remote(to_mate.at[i], from_mate.at[i], s_mate.at[i], r_mate.at[i], (z, mate))

    def send_x(i, n):
        cols = right_cols if n == 2 else left_cols
        return remote(stage.at[i, :, cols], from_x.at[n], s_x.at[n], r_x.at[n], (z, on_x))

    def send_y(i, n):
        cols = left_cols if n == 2 else right_cols
        return remote(stage.at[i, :, cols], from_y.at[n], s_y.at[n], r_y.at[n], (z, on_y))

    def give(i):
        def use(cols, total):
            to_mate[i, :, cols] = total.astype(jnp.bfloat16)

        each_tile(target(i, 1 - core), use)
        mate_copy(i).start()

    def add(i):
        def use(cols, total):
            total = total + from_mate[i, :, cols].astype(jnp.float32)
            if i < 3:
                stage[i, :, cols] = total.astype(jnp.bfloat16)
            else:
                o_ref[:, cols] = total

        mate_copy(i).wait_recv()
        each_tile(target(i, core), use)
        if i == 0:
            send_x(0, 0).start()
            send_y(0, 0).start()
        if i == 1:
            send_x(1, 1).start()
        if i == 2:
            send_y(2, 1).start()

    def begin():
        give(0)
        for i in range(4):
            if i < 3:
                give(i + 1)
            add(i)

    def relay():
        send_y(0, 0).wait_recv()
        stage[1, :, right_cols] = (
            stage[1, :, right_cols].astype(jnp.float32) + from_y[0].astype(jnp.float32)
        ).astype(jnp.bfloat16)
        send_x(1, 2).start()
        send_x(0, 0).wait_recv()
        stage[2, :, left_cols] = (
            stage[2, :, left_cols].astype(jnp.float32) + from_x[0].astype(jnp.float32)
        ).astype(jnp.bfloat16)
        send_y(2, 2).start()

    def finish():
        send_x(1, 1).wait_recv()
        o_ref[:, left_cols] += from_x[1].astype(jnp.float32)
        send_y(2, 1).wait_recv()
        o_ref[:, right_cols] += from_y[1].astype(jnp.float32)
        send_x(1, 2).wait_recv()
        o_ref[:, right_cols] += from_x[2].astype(jnp.float32)
        send_y(2, 2).wait_recv()
        o_ref[:, left_cols] += from_y[2].astype(jnp.float32)

    def drain():
        for i in range(4):
            mate_copy(i).wait_send()
        for copy in (send_x(0, 0), send_x(1, 1), send_x(1, 2), send_y(0, 0), send_y(2, 1), send_y(2, 2)):
            copy.wait_send()

    return begin, relay, finish, drain


def scatter_buffers(rows, width):
    shapes = [pltpu.VMEM((n, rows, width), jnp.bfloat16) for n in (4, 4, 3)]
    shapes += [pltpu.VMEM((3, rows, width // 2), jnp.bfloat16) for _ in range(2)]
    return shapes + [pltpu.SemaphoreType.DMA((n,)) for n in (4, 4, 3, 3, 3, 3)]


BUFFERS = 11


def scatter_kernel(flip, mixing, cut, *refs):
    refs = list(refs)
    left, right = refs.pop(0), refs.pop(0)
    squares = refs.pop(0) if mixing else None
    side = refs.pop(0) if cut else None
    o_ref = refs.pop(0)
    scale_ref = refs.pop(0) if mixing else None
    side_out = refs.pop(0) if cut else None
    buffers = [refs.pop(0) for _ in range(BUFFERS)]
    spot = z, y, x, core = place()
    rows, width = o_ref.shape
    me = member(y, x, core)
    peers = plane_peers(y, x, core)
    left_rows = None
    if cut:
        side_here, s_side = refs
        fetch = pltpu.make_async_copy(side, side_here, s_side)
        fetch.start()
    greet(z, peers)

    if mixing:
        all_squares, columns, s_note, r_note = refs
        notes = note_copies(z, me, peers, squares, all_squares, s_note, r_note)
        for copy in notes:
            copy.start()
        all_squares[me] = squares[...]
        for copy in notes:
            copy.wait_recv()
        scale = lax.rsqrt(jnp.sum(all_squares[...], axis=0) / width + EPS)
        scale_ref[...] = scale
        columns[...] = jnp.transpose(scale)

        def left_rows(left, block):
            here = pl.ds(pl.multiple_of(block * rows, rows), rows)
            deep = left.shape[1] // 2
            one = lax.broadcasted_iota(jnp.int32, columns.shape, 1) == block
            column = jnp.sum(jnp.where(one, columns[...], 0.0), axis=1, keepdims=True)
            return (left[here, :deep] * column * left[here, deep:]).astype(jnp.bfloat16)

    begin, relay, finish, drain = scatter_steps(spot, [left], [right], flip, left_rows, o_ref, buffers)
    begin()
    if cut:
        fetch.wait()
        tiles = side.shape[1] // SIDE
        side_tiles(0, tiles // 2, side_here, left, slice(cut, None), side_out)
    relay()
    if cut:
        side_tiles(tiles // 2, tiles, side_here, left, slice(cut, None), side_out)
    finish()
    drain()
    if mixing:
        for copy in notes:
            copy.wait_send()


SIDE = 256


def side_tiles(start, stop, left, right, columns, out):
    @pl.loop(start, stop)
    def _(t):
        cols = pl.ds(pl.multiple_of(t * SIDE, SIDE), SIDE)
        out[cols, :] = matmul_tn(left[:, cols], right[:, columns]).astype(out.dtype)


def plane_scatter(left, right, flip, number, squares=None, side=None, cut=0):
    mixing = squares is not None
    rows = left.shape[0] // 8
    width = right.shape[0 if flip else 1]
    ins, in_specs = [left, right], [VMEM] * 2
    outs = [jax.ShapeDtypeStruct((rows, width), jnp.float32)]
    scratch = scatter_buffers(rows, width)
    if mixing:
        ins.append(squares)
        in_specs.append(VMEM)
        outs.append(jax.ShapeDtypeStruct(squares.shape, jnp.float32))
        scratch += [
            pltpu.VMEM((8, *squares.shape), jnp.float32),
            pltpu.VMEM(squares.shape[::-1], jnp.float32),
            pltpu.SemaphoreType.DMA((7,)),
            pltpu.SemaphoreType.DMA((7,)),
        ]
    if cut:
        ins.append(side)
        in_specs.append(ANY)
        outs.append(jax.ShapeDtypeStruct((side.shape[1], left.shape[1] - cut), jnp.bfloat16))
        scratch += [pltpu.VMEM(side.shape, side.dtype), pltpu.SemaphoreType.DMA]
    return pl.pallas_call(
        functools.partial(scatter_kernel, flip, mixing, cut),
        out_shape=outs,
        in_specs=in_specs,
        out_specs=[VMEM] * len(outs),
        scratch_shapes=scratch,
        compiler_params=pltpu.CompilerParams(
            collective_id=number, has_side_effects=True, vmem_limit_bytes=VMEM_BYTES
        ),
        cost_estimate=pl.CostEstimate(flops=0, bytes_accessed=2**20, transcendentals=0),
        name=f"plane_scatter_{number}",
    )(*ins)


def units_kernel(mid, weight, both, product):
    units = product.shape[1]
    out = matmul(mid[...], weight[...])
    both[...] = out
    product[...] = (out[:, :units] * out[:, units:]).astype(jnp.bfloat16)


def units_forward(mid, weight):
    rows, wide = mid.shape[0] // 8, weight.shape[1]
    return pl.pallas_call(
        units_kernel,
        grid=(8,),
        out_shape=[
            jax.ShapeDtypeStruct((8 * rows, wide), jnp.float32),
            jax.ShapeDtypeStruct((8 * rows, wide // 2), jnp.bfloat16),
        ],
        in_specs=[
            pl.BlockSpec((rows, mid.shape[1]), lambda b: (b, 0)),
            pl.BlockSpec(weight.shape, lambda b: (0, 0)),
        ],
        out_specs=[
            pl.BlockSpec((rows, wide), lambda b: (b, 0)),
            pl.BlockSpec((rows, wide // 2), lambda b: (b, 0)),
        ],
        compiler_params=pltpu.CompilerParams(
            dimension_semantics=("arbitrary",), vmem_limit_bytes=VMEM_BYTES
        ),
        cost_estimate=pl.CostEstimate(flops=2 * mid.size * wide, bytes_accessed=2**24, transcendentals=0),
        name="units_forward",
    )(mid, weight)


def units_back_kernel(
    cut, product, weight, cot, both, mid, o_ref, grads, term, cot_here, both_here, mid_here, s_mid, s_block, *buffers
):
    spot = z, y, x, core = place()
    rows = o_ref.shape[0]
    units = product.shape[1]
    fetch_mid = pltpu.make_async_copy(mid, mid_here, s_mid)

    def fetch(b, slot):
        here = pl.ds(pl.multiple_of(b * rows, rows), rows)
        return [
            pltpu.make_async_copy(cot.at[here], cot_here.at[slot], s_block.at[slot, 0]),
            pltpu.make_async_copy(both.at[here], both_here.at[slot], s_block.at[slot, 1]),
        ]

    for copy in fetch(0, 0):
        copy.start()
    fetch_mid.start()
    greet(z, plane_peers(y, x, core))
    begin, relay, finish, drain = scatter_steps(spot, [product], [weight], False, None, o_ref, buffers)
    begin()

    @pl.loop(0, 8)
    def _(b):
        slot = b % 2
        for copy in fetch(b, slot):
            copy.wait()

        @pl.when(b < 7)
        def _():
            for copy in fetch(b + 1, 1 - slot):
                copy.start()

        here = pl.ds(pl.multiple_of(b * rows, rows), rows)
        grad = matmul_nt(cot_here[slot], weight[...])
        pair = both_here[slot]
        grads[here, :units] = (grad * pair[:, units:]).astype(jnp.bfloat16)
        grads[here, units:] = (grad * pair[:, :units]).astype(jnp.bfloat16)

    relay()
    fetch_mid.wait()
    side_tiles(0, mid.shape[1] // SIDE, mid_here, grads, slice(0, cut), term)
    finish()
    drain()


def units_back(product, weight, cot, both, mid, cut, number):
    rows, width = product.shape[0] // 8, weight.shape[1]
    wide = both.shape[1]
    bf = jnp.bfloat16
    return pl.pallas_call(
        functools.partial(units_back_kernel, cut),
        out_shape=[
            jax.ShapeDtypeStruct((rows, width), jnp.float32),
            jax.ShapeDtypeStruct((8 * rows, wide), bf),
            jax.ShapeDtypeStruct((mid.shape[1], cut), bf),
        ],
        in_specs=[VMEM, VMEM, ANY, ANY, ANY],
        out_specs=[VMEM] * 3,
        scratch_shapes=[
            pltpu.VMEM((2, rows, width), bf),
            pltpu.VMEM((2, rows, wide), jnp.float32),
            pltpu.VMEM(mid.shape, bf),
            pltpu.SemaphoreType.DMA,
            pltpu.SemaphoreType.DMA((2, 2)),
        ]
        + scatter_buffers(rows, width),
        compiler_params=pltpu.CompilerParams(
            collective_id=number, has_side_effects=True, vmem_limit_bytes=VMEM_BYTES
        ),
        cost_estimate=pl.CostEstimate(flops=0, bytes_accessed=2**20, transcendentals=0),
        name=f"units_back_{number}",
    )(product, weight, cot, both, mid)


def dot_fine(left, right, dims):
    high = right.astype(jnp.bfloat16)
    low = (right - high.astype(jnp.float32)).astype(jnp.bfloat16)
    product = functools.partial(
        lax.dot_general, dimension_numbers=(dims, ((), ())), preferred_element_type=jnp.float32
    )
    return product(left, high) + product(left, low)


NN, NT, TN = ((1,), (0,)), ((1,), (1,)), ((0,), (0,))


def block_tables(count, rate, rows):
    spot = lax.broadcasted_iota(jnp.int32, (rows, 1), 0)
    live = spot < count
    behind = jnp.where(live, jnp.exp(-rate * spot.astype(jnp.float32)), 0.0)
    ahead = jnp.where(live, jnp.exp(-rate * (count - spot).astype(jnp.float32)), 0.0)
    fade = jnp.exp(jnp.full((1, HEAD_DIM), -rate * count.astype(jnp.float32), jnp.float32))
    return live, behind, ahead, fade


def fill_decay(base, rates):
    heads, rows, _ = base.shape
    gap = lax.broadcasted_iota(jnp.int32, (rows, rows), 0) - lax.broadcasted_iota(jnp.int32, (rows, rows), 1)
    far = jnp.maximum(gap, 0).astype(jnp.float32)
    for t in range(heads):
        base[t] = jnp.where(gap >= 0, jnp.exp(-rates[t] * far), 0.0)


def mix_kernel(counts, rates, hidden, weight, pre, attn_gate, qkv, entering, squares, base, state):
    b = pl.program_id(0)
    rows = hidden.shape[0]
    wide = weight.shape[1] // 4

    @pl.when(b == 0)
    def _():
        fill_decay(base, rates)
        state[...] = jnp.zeros_like(state)

    count = counts[b]
    out = matmul(hidden[...], weight[...])
    pre[...] = out[:, : 2 * wide]
    gate = out[:, 3 * wide :]
    query = jax.nn.silu(out[:, :wide]).astype(jnp.bfloat16)
    keys = jax.nn.silu(out[:, wide : 2 * wide]).astype(jnp.bfloat16)
    value = out[:, 2 * wide : 3 * wide].astype(jnp.bfloat16)
    qkv[:, :wide] = query
    qkv[:, wide : 2 * wide] = keys
    qkv[:, 2 * wide :] = value
    attn_gate[:, wide:] = gate
    entering[0] = state[...]
    total = jnp.zeros((8, rows), jnp.float32)
    for t in range(state.shape[0]):
        at = slice(t * HEAD_DIM, (t + 1) * HEAD_DIM)
        q, k, v = query[:, at], keys[:, at], value[:, at]
        live, behind, ahead, fade = block_tables(count, rates[t], rows)
        mask = jnp.where(live, base[t], 0.0)
        probs = (matmul_nt(q, k) * mask).astype(jnp.bfloat16)
        attn = matmul(probs, v) + behind * dot_fine(q, state[t], NN)
        attn_gate[:, at] = attn
        total += lax.dot_general(
            jnp.ones((8, HEAD_DIM), jnp.float32), attn * attn, (NT, ((), ())), precision=HIGH,
            preferred_element_type=jnp.float32,
        )
        local = dot_fine(k, v.astype(jnp.float32) * ahead, TN)
        state[t] = jnp.where(count < rows, 0.0, fade * state[t] + local)
    squares[pl.ds(b, 1), :] = total[:1]


def mix_heads(counts, rates, hidden, weight):
    rows = hidden.shape[0] // 8
    wide = weight.shape[1] // 4
    heads = wide // HEAD_DIM
    f32 = jnp.float32

    def by_block(width):
        return pl.BlockSpec((rows, width), lambda b: (b, 0))

    def whole(*shape):
        return pl.BlockSpec(shape, lambda b: (0,) * len(shape))

    return pl.pallas_call(
        mix_kernel,
        grid=(8,),
        out_shape=[
            jax.ShapeDtypeStruct((8 * rows, 2 * wide), f32),
            jax.ShapeDtypeStruct((8 * rows, 2 * wide), f32),
            jax.ShapeDtypeStruct((8 * rows, 3 * wide), jnp.bfloat16),
            jax.ShapeDtypeStruct((8, heads, HEAD_DIM, HEAD_DIM), f32),
            jax.ShapeDtypeStruct((8, rows), f32),
        ],
        in_specs=[SMEM, SMEM, by_block(hidden.shape[1]), whole(*weight.shape)],
        out_specs=[
            by_block(2 * wide),
            by_block(2 * wide),
            by_block(3 * wide),
            pl.BlockSpec((1, heads, HEAD_DIM, HEAD_DIM), lambda b: (b, 0, 0, 0)),
            whole(8, rows),
        ],
        scratch_shapes=[pltpu.VMEM((heads, rows, rows), f32), pltpu.VMEM((heads, HEAD_DIM, HEAD_DIM), f32)],
        compiler_params=pltpu.CompilerParams(
            dimension_semantics=("arbitrary",), vmem_limit_bytes=VMEM_BYTES
        ),
        cost_estimate=pl.CostEstimate(
            flops=2 * hidden.size * weight.shape[1], bytes_accessed=4 * hidden.size, transcendentals=0
        ),
        name="mix_heads",
    )(counts, rates, hidden, weight)


def unmix_kernel(
    counts, rates, low, weight, pre, attn_gate, qkv, entering, scale, inner, grads, out_term, base, state, total
):
    step = pl.program_id(0)
    b = pl.num_programs(0) - 1 - step
    rows, width = low.shape
    wide = weight.shape[0]

    @pl.when(step == 0)
    def _():
        fill_decay(base, rates)
        state[...] = jnp.zeros_like(state)
        total[...] = jnp.zeros_like(total)

    count = counts[b]

    def column(ref):
        here = lax.broadcasted_iota(jnp.int32, (8, rows), 0) == b
        turned = jnp.transpose(jnp.where(here, ref[...], 0.0))
        return jnp.sum(turned, axis=1, keepdims=True)

    factor, inside = column(scale), column(inner)
    attn, gate = attn_gate[:, :wide], attn_gate[:, wide:]
    normal = attn * factor
    grad = matmul_nt(low[...], weight[...])
    grads[:, 3 * wide :] = (grad * normal).astype(jnp.bfloat16)
    grad_attn = (factor * grad * gate - normal * factor * inside * (1.0 / width)).astype(jnp.bfloat16)
    total[...] += matmul_tn((normal * gate).astype(jnp.bfloat16), low[...])
    for t in range(state.shape[0]):
        at = slice(t * HEAD_DIM, (t + 1) * HEAD_DIM)
        q, k, v = (qkv[:, i * wide + t * HEAD_DIM : i * wide + (t + 1) * HEAD_DIM] for i in range(3))
        g = grad_attn[:, at]
        live, behind, ahead, fade = block_tables(count, rates[t], rows)
        mask = jnp.where(live, base[t], 0.0)
        probs = (matmul_nt(q, k) * mask).astype(jnp.bfloat16)
        raw = (matmul_nt(g, v) * mask).astype(jnp.bfloat16)
        leaving = jnp.where(count < rows, 0.0, state[t])
        grad_q = matmul(raw, k) + behind * dot_fine(g, entering[0, t], NT)
        grad_k = matmul_tn(raw, q) + ahead * dot_fine(v, leaving, NT)
        grad_v = matmul_tn(probs, g) + ahead * dot_fine(k, leaving, NN)
        state[t] = dot_fine(q, g.astype(jnp.float32) * behind, TN) + fade * leaving
        grads[:, at] = (grad_q * silu_slope(pre[:, at])).astype(jnp.bfloat16)
        after = slice(wide + t * HEAD_DIM, wide + (t + 1) * HEAD_DIM)
        grads[:, after] = (grad_k * silu_slope(pre[:, after])).astype(jnp.bfloat16)
        grads[:, 2 * wide + t * HEAD_DIM : 2 * wide + (t + 1) * HEAD_DIM] = grad_v.astype(jnp.bfloat16)

    @pl.when(step == pl.num_programs(0) - 1)
    def _():
        out_term[...] = total[...].astype(jnp.bfloat16)


def unmix_heads(counts, rates, low, weight, pre, attn_gate, qkv, entering, scale, inner):
    rows, width = low.shape[0] // 8, low.shape[1]
    wide = weight.shape[0]
    heads = wide // HEAD_DIM
    f32 = jnp.float32

    def by_block(columns):
        return pl.BlockSpec((rows, columns), lambda s: (7 - s, 0))

    def whole(*shape):
        return pl.BlockSpec(shape, lambda s: (0,) * len(shape))

    return pl.pallas_call(
        unmix_kernel,
        grid=(8,),
        out_shape=[
            jax.ShapeDtypeStruct((8 * rows, 4 * wide), jnp.bfloat16),
            jax.ShapeDtypeStruct((wide, width), jnp.bfloat16),
        ],
        in_specs=[
            SMEM,
            SMEM,
            by_block(width),
            whole(wide, width),
            by_block(2 * wide),
            by_block(2 * wide),
            by_block(3 * wide),
            pl.BlockSpec((1, heads, HEAD_DIM, HEAD_DIM), lambda s: (7 - s, 0, 0, 0)),
            whole(8, rows),
            whole(8, rows),
        ],
        out_specs=[by_block(4 * wide), whole(wide, width)],
        scratch_shapes=[
            pltpu.VMEM((heads, rows, rows), f32),
            pltpu.VMEM((heads, HEAD_DIM, HEAD_DIM), f32),
            pltpu.VMEM((wide, width), f32),
        ],
        compiler_params=pltpu.CompilerParams(
            dimension_semantics=("arbitrary",), vmem_limit_bytes=VMEM_BYTES
        ),
        cost_estimate=pl.CostEstimate(
            flops=4 * low.size * wide, bytes_accessed=6 * low.size, transcendentals=0
        ),
        name="unmix_heads",
    )(counts, rates, low, weight, pre, attn_gate, qkv, entering, scale, inner)


def after(value, *others):
    return lax.optimization_barrier((value, *others))[0]


def fast_plan(
    tokens,
    block_counts,
    decay_rate,
    query_weight,
    key_weight,
    value_weight,
    gate_weight,
    out_weight,
    first_weight,
    second_weight,
    down_weight,
    cotangent,
):
    rows, width = tokens.shape
    nz = lax.axis_size("dp")
    nf = lax.axis_size("fsdp")
    chips = nf // 2
    plane = lax.axis_index("fsdp")
    chip, core = plane // 2, plane % 2
    bf = jnp.bfloat16
    half = HEADS // nf
    own = half * HEAD_DIM
    units = first_weight.shape[1] // nf
    own_heads = chips * (half * core + jnp.arange(half)) + chip

    head_spots = tuple(
        (2 * c + k, n, HEAD_DIM * (chips * (half * k + t) + c), 0, n * own + t * HEAD_DIM, HEAD_DIM)
        for c in range(chips) for k in range(2) for n in range(4) for t in range(half)
    )
    run = units // nz
    unit_spots = tuple(
        (f, n, run * (nf * g + f), 0, n * units + g * run, run)
        for f in range(nf) for n in range(2) for g in range(nz)
    )
    cut = 2 * units // 256 * 128
    unit_back = []
    for f, n, src, _, dst, wide in unit_spots:
        here = min(max(cut - dst, 0), wide)
        if here:
            unit_back.append((f, n, src, 0, dst, here))
        if here < wide:
            unit_back.append((f, n, src + here, 1, dst + here - cut, wide - here))

    def along(weight):
        weight = weight.reshape(-1, weight.shape[-1])
        return lax.all_gather(weight, "dp", axis=0, tiled=True)

    swap = [(i, i ^ 1) for i in range(nf)]

    def cross(x):
        keep = lax.dynamic_slice_in_dim(x, core * half, half, 0)
        send = lax.dynamic_slice_in_dim(x, (1 - core) * half, half, 0)
        got = lax.ppermute(send, "fsdp", swap)
        return jnp.stack([jnp.where(core == 0, keep, got), jnp.where(core == 0, got, keep)], axis=1)

    def uncross(x):
        keep = lax.dynamic_index_in_dim(x, core, 1, False)
        send = lax.dynamic_index_in_dim(x, 1 - core, 1, False)
        got = lax.ppermute(send, "fsdp", swap)
        return jnp.concatenate([jnp.where(core == 0, keep, got), jnp.where(core == 0, got, keep)], axis=0)

    wo = cross(lax.all_gather(out_weight, "dp", axis=0)).reshape(own, width)
    note = jnp.broadcast_to(block_counts, (8, 128))
    shape = (nf, query_weight.shape[0], 4 * own)
    weights = (query_weight, key_weight, value_weight, gate_weight)
    heads_weight, counts = plane_spread(weights, head_spots, shape, note, 0)
    counts = counts[:, 0, 0]
    w_heads = after(along(heads_weight), wo)
    rates = decay_rate[own_heads]
    inputs = tokens.astype(jnp.float32)
    in_normed, in_scale = normed(inputs)
    shape = (nf, first_weight.shape[0], 2 * units)
    low, _ = lax.optimization_barrier((in_normed.astype(bf), heads_weight))
    hidden, units_weight = plane_gather(low, 1, weights=(first_weight, second_weight), spots=unit_spots, shape=shape)
    (cot,) = plane_gather(after(cotangent, hidden), 2)
    w_units = along(units_weight)
    wd = along(after(down_weight, cot))

    pre, attn_gate, qkv, entering, squares = mix_heads(counts, rates, hidden, w_heads)
    out_own, scale = plane_scatter(attn_gate, wo, False, 3, squares=squares)
    middle = inputs + out_own
    mid_normed, mid_scale = normed(middle)
    (mid,) = plane_gather(mid_normed.astype(bf), 4)
    both, product = units_forward(mid, w_units)
    down_term = matmul_tn(product, cot).astype(bf)
    wd = after(wd, down_term)
    down_sum = lax.psum_scatter(down_term, "dp", scatter_dimension=0, tiled=True)
    down_own, grad_units, low_term = units_back(product, wd, cot, both, mid, cut, 5)
    block_out = (middle + down_own).astype(bf)
    low_sum = lax.psum_scatter(low_term, "dp", scatter_dimension=0, tiled=True)
    grad_mid, high_term = plane_scatter(after(grad_units, down_sum), w_units, True, 6, side=mid, cut=cut)
    high_sum = lax.psum_scatter(high_term, "dp", scatter_dimension=0, tiled=True)
    grad_middle = cotangent.astype(jnp.float32) + norm_back(middle, mid_scale, grad_mid)
    low = grad_middle.astype(bf)
    inner = jnp.sum(low.astype(jnp.float32) * out_own, axis=-1)
    note = jnp.pad(inner.reshape(-1, 128), ((0, 8 - rows // 128), (0, 0)))
    low, inner = plane_gather(after(low, low_sum), 7, note=note)
    inner = inner[:, : rows // 128].reshape(nf, rows)
    grad_heads, out_term = unmix_heads(
        counts, rates, low, wo, pre, attn_gate, qkv, entering, scale, inner
    )
    heads_term = matmul_tn(hidden, grad_heads).astype(bf)
    heads_sum = lax.psum_scatter(heads_term, "dp", scatter_dimension=0, tiled=True)
    out_term = uncross(after(out_term, heads_term).reshape(half, 2, -1, width))
    out_sum = lax.psum_scatter(out_term, "dp", scatter_dimension=0, tiled=False)
    (grad_hidden,) = plane_scatter(after(grad_heads, out_term), w_heads, True, 8)
    tokens_grad = grad_middle + norm_back(inputs, in_scale, grad_hidden)
    down_grad = down_sum.astype(jnp.float32)
    sums = lax.optimization_barrier((low_sum, high_sum, down_grad, grad_hidden))[:2]
    first_grad, second_grad = plane_collect(sums, unit_back, nf * units, 2, 9)
    heads_sum = after(heads_sum, first_grad)
    grads = plane_collect([heads_sum], head_spots, width, 4, 10)
    out_grad = after(out_sum, *grads).astype(jnp.float32)
    return (block_out, tokens_grad, *grads, out_grad, first_grad, second_grad, down_grad)


def fits(mesh):
    return mesh.shape["dp"] == 4 and mesh.shape["fsdp"] == 8


def solution(mesh):
    return jax.shard_map(
        fast_plan if fits(mesh) else shards,
        mesh=mesh,
        in_specs=(
            P(("dp", "fsdp"), None),
            P("dp", "fsdp"),
            P(),
            P(("dp", "fsdp"), None),
            P(("dp", "fsdp"), None),
            P(("dp", "fsdp"), None),
            P(("dp", "fsdp"), None),
            P(("dp", "fsdp"), None),
            P(("dp", "fsdp"), None),
            P(("dp", "fsdp"), None),
            P(("dp", "fsdp"), None),
            P(("dp", "fsdp"), None),
        ),
        out_specs=(
            P(("dp", "fsdp"), None),
            P(("dp", "fsdp"), None),
            P(("dp", "fsdp"), None),
            P(("dp", "fsdp"), None),
            P(("dp", "fsdp"), None),
            P(("dp", "fsdp"), None),
            P(("dp", "fsdp"), None),
            P(("dp", "fsdp"), None),
            P(("dp", "fsdp"), None),
            P(("dp", "fsdp"), None),
        ),
        check_vma=False,
    )
```

```python
import functools

import jax
import jax.numpy as jnp
from jax import lax
from jax.experimental import pallas as pl
from jax.experimental.pallas import tpu as pltpu
from jax.sharding import PartitionSpec as P

HEADS = 16
HEAD_DIM = 128


EPS = 1e-06
HIGH = lax.Precision.HIGHEST


def carried_in(part, axis, combine, identity):
    place = lax.axis_index(axis)
    gathered = jax.tree.map(lambda a: lax.all_gather(a, axis), part)
    state = jax.tree.map(lambda a, e: jnp.zeros_like(a) + jnp.asarray(e, a.dtype), part, identity)

    def carried_one(lap, state):
        return combine(
            state, jax.tree.map(lambda a: lax.dynamic_index_in_dim(a, lap, 0, False), gathered)
        )

    return lax.fori_loop(0, place, carried_one, state)


def prefix_2(value, axis, join, neutral):
    count = lax.axis_size(axis)
    place = lax.axis_index(axis)
    ahead = count - 1 - place
    gathered = jax.tree.map(
        lambda a, kind: lax.all_gather(a.astype(kind), axis), value, (jnp.bfloat16, jnp.bfloat16)
    )
    state = jax.tree.map(lambda a, e: jnp.zeros_like(a) + jnp.asarray(e, a.dtype), value, neutral)

    def prefix_one(lap, state):
        source = count - 1 - lap
        return join(
            state,
            jax.tree.map(
                lambda a, own: lax.dynamic_index_in_dim(a, source, 0, False).astype(own.dtype),
                gathered,
                value,
            ),
        )

    return lax.fori_loop(0, ahead, prefix_one, state)


def normed(value):
    scale = lax.rsqrt(jnp.mean(value * value, axis=-1, keepdims=True) + EPS)
    return (value * scale, scale)


def norm_back(value, scale, grad):
    inner = jnp.mean(grad * value, axis=-1, keepdims=True)
    return scale * (grad - value * scale * scale * inner)


def silu_slope(value):
    sig = jax.nn.sigmoid(value)
    return sig * (1.0 + value * (1.0 - sig))


def chain_step(earlier, later):
    e_fade, e_state = earlier
    l_fade, l_state = later
    return (l_fade * e_fade, l_fade[:, None, None] * e_state + l_state)


def matmul(left, right):
    return jnp.dot(left, right, preferred_element_type=jnp.float32)


def matmul_tn(left, right):
    return lax.dot_general(
        left, right, (((0,), (0,)), ((), ())), preferred_element_type=jnp.float32
    )


def matmul_nt(left, right):
    return lax.dot_general(
        left, right, (((1,), (1,)), ((), ())), preferred_element_type=jnp.float32
    )


def decay_tables(count, rates, rows):
    pos = lax.iota(jnp.int32, rows)
    live = pos < count
    keep = (pos[:, None] >= pos[None, :]) & live[:, None] & live[None, :]
    spacing = jnp.where(keep, (pos[:, None] - pos[None, :]).astype(jnp.float32), 0.0)
    mask = jnp.where(keep[None], jnp.exp(-rates[:, None, None] * spacing[None]), 0.0)
    ahead = jnp.where(
        live[:, None], jnp.exp(-rates[None, :] * (count - pos)[:, None].astype(jnp.float32)), 0.0
    )
    behind = jnp.where(
        live[:, None], jnp.exp(-rates[None, :] * pos[:, None].astype(jnp.float32)), 0.0
    )
    fade = jnp.exp(-rates * count.astype(jnp.float32))
    return (mask, ahead, behind, fade)


def shards(
    tokens,
    block_counts,
    decay_rate,
    query_weight,
    key_weight,
    value_weight,
    gate_weight,
    out_weight,
    first_weight,
    second_weight,
    down_weight,
    cotangent,
):
    rows = tokens.shape[0]
    gathered = (
        lax.all_gather(query_weight, ("dp", "fsdp"), axis=0, tiled=True),
        lax.all_gather(key_weight, ("dp", "fsdp"), axis=0, tiled=True),
        lax.all_gather(value_weight, ("dp", "fsdp"), axis=0, tiled=True),
        lax.all_gather(gate_weight, ("dp", "fsdp"), axis=0, tiled=True),
        lax.all_gather(out_weight, ("dp", "fsdp"), axis=0, tiled=True),
        lax.all_gather(first_weight, ("dp", "fsdp"), axis=0, tiled=True),
        lax.all_gather(second_weight, ("dp", "fsdp"), axis=0, tiled=True),
        lax.all_gather(down_weight, ("dp", "fsdp"), axis=0, tiled=True),
    )
    w_query, w_key, w_value, w_gate, w_out, w_first, w_second, w_down = gathered
    count = block_counts[0, 0]
    closes = count < rows
    mask, ahead, behind, fade = decay_tables(count, decay_rate, rows)
    passing = jnp.where(closes, 0.0, fade)
    inputs = tokens.astype(jnp.float32)
    in_normed, in_scale = normed(inputs)
    hidden = in_normed.astype(jnp.bfloat16)
    q_pre = matmul(hidden, w_query)
    k_pre = matmul(hidden, w_key)
    value = matmul(hidden, w_value).astype(jnp.bfloat16)
    gate = matmul(hidden, w_gate)
    query = jax.nn.silu(q_pre).astype(jnp.bfloat16)
    keys = jax.nn.silu(k_pre).astype(jnp.bfloat16)
    query_heads = query.reshape(rows, HEADS, HEAD_DIM)
    key_heads = keys.reshape(rows, HEADS, HEAD_DIM)
    value_heads = value.reshape(rows, HEADS, HEAD_DIM)
    query_wide = query_heads.astype(jnp.float32)
    key_wide = key_heads.astype(jnp.float32)
    value_ahead = value_heads.astype(jnp.float32) * ahead[:, :, None]
    raw = jnp.einsum("ihe,jhe->hij", query_heads, key_heads, preferred_element_type=jnp.float32)
    probs = (raw * mask).astype(jnp.bfloat16)
    intra = jnp.einsum("hij,jhe->ihe", probs, value_heads, preferred_element_type=jnp.float32)
    local = jnp.einsum("jhe,jhf->hef", key_wide, value_ahead, precision=HIGH)
    local_sent = jnp.where(closes, 0.0, local)
    prefix = carried_in(
        (passing, local_sent), "fsdp", chain_step, (jnp.ones_like(fade), jnp.zeros_like(local))
    )
    entering = prefix[1]
    inter = behind[:, :, None] * jnp.einsum("ihe,hef->ihf", query_wide, entering, precision=HIGH)
    attn = (intra + inter).reshape(rows, HEADS * HEAD_DIM)
    attn_normed, attn_scale = normed(attn)
    mixed = (attn_normed * gate).astype(jnp.bfloat16)
    middle = inputs + matmul(mixed, w_out)
    mid_normed, mid_scale = normed(middle)
    mid = mid_normed.astype(jnp.bfloat16)
    first = matmul(mid, w_first)
    second = matmul(mid, w_second)
    product = (first * second).astype(jnp.bfloat16)
    block_out = (middle + matmul(product, w_down)).astype(jnp.bfloat16)
    w_first, w_second, w_down = (
        lax.all_gather(first_weight, ("dp", "fsdp"), axis=0, tiled=True),
        lax.all_gather(second_weight, ("dp", "fsdp"), axis=0, tiled=True),
        lax.all_gather(down_weight, ("dp", "fsdp"), axis=0, tiled=True),
    )
    grad_product = matmul_nt(cotangent, w_down)
    grad_first = (grad_product * second).astype(jnp.bfloat16)
    grad_second = (grad_product * first).astype(jnp.bfloat16)
    grad_mid = matmul_nt(grad_first, w_first) + matmul_nt(grad_second, w_second)
    grad_middle = cotangent.astype(jnp.float32) + norm_back(middle, mid_scale, grad_mid)

    def scattered(left, right, after):
        left, _ = lax.optimization_barrier((left, after))
        term = matmul_tn(left, right)
        return lax.psum_scatter(term, ("dp", "fsdp"), scatter_dimension=0, tiled=True)

    down_grad = scattered(product, cotangent, grad_middle)
    first_grad = scattered(mid, grad_first, down_grad)
    second_grad = scattered(mid, grad_second, first_grad)
    grad_middle, _ = lax.optimization_barrier((grad_middle, second_grad))
    w_query, w_key, w_value, w_gate, w_out = (
        lax.all_gather(query_weight, ("dp", "fsdp"), axis=0, tiled=True),
        lax.all_gather(key_weight, ("dp", "fsdp"), axis=0, tiled=True),
        lax.all_gather(value_weight, ("dp", "fsdp"), axis=0, tiled=True),
        lax.all_gather(gate_weight, ("dp", "fsdp"), axis=0, tiled=True),
        lax.all_gather(out_weight, ("dp", "fsdp"), axis=0, tiled=True),
    )
    grad_mid_low = grad_middle.astype(jnp.bfloat16)
    out_term = matmul_tn(mixed, grad_mid_low)
    grad_mixed = matmul_nt(grad_mid_low, w_out)
    grad_gate = (grad_mixed * attn_normed).astype(jnp.bfloat16)
    grad_attn = norm_back(attn, attn_scale, grad_mixed * gate).astype(jnp.bfloat16)
    grad_heads = grad_attn.reshape(rows, HEADS, HEAD_DIM)
    grad_heads_wide = grad_heads.astype(jnp.float32) * behind[:, :, None]
    grad_probs = jnp.einsum(
        "ihe,jhe->hij", grad_heads, value_heads, preferred_element_type=jnp.float32
    )
    grad_raw = (grad_probs * mask).astype(jnp.bfloat16)
    grad_entering = jnp.einsum("ihe,ihf->hef", query_wide, grad_heads_wide, precision=HIGH)
    suffix = prefix_2(
        (passing, grad_entering),
        "fsdp",
        chain_step,
        (jnp.ones_like(fade), jnp.zeros_like(grad_entering)),
    )
    grad_leaving = jnp.where(closes, 0.0, suffix[1])
    grad_query = jnp.einsum("hij,jhe->ihe", grad_raw, key_heads, preferred_element_type=jnp.float32)
    grad_query = grad_query + jnp.einsum("ihf,hef->ihe", grad_heads_wide, entering, precision=HIGH)
    grad_keys = jnp.einsum(
        "hij,ihe->jhe", grad_raw, query_heads, preferred_element_type=jnp.float32
    )
    grad_keys = grad_keys + jnp.einsum("hef,jhf->jhe", grad_leaving, value_ahead, precision=HIGH)
    grad_value = jnp.einsum("hij,ihe->jhe", probs, grad_heads, preferred_element_type=jnp.float32)
    grad_value = grad_value + ahead[:, :, None] * jnp.einsum(
        "hef,jhe->jhf", grad_leaving, key_wide, precision=HIGH
    )
    width = HEADS * HEAD_DIM
    grad_q_pre = (grad_query.reshape(rows, width) * silu_slope(q_pre)).astype(jnp.bfloat16)
    grad_k_pre = (grad_keys.reshape(rows, width) * silu_slope(k_pre)).astype(jnp.bfloat16)
    grad_v = grad_value.reshape(rows, width).astype(jnp.bfloat16)
    query_term = matmul_tn(hidden, grad_q_pre)
    key_term = matmul_tn(hidden, grad_k_pre)
    value_term = matmul_tn(hidden, grad_v)
    gate_term = matmul_tn(hidden, grad_gate)
    grad_hidden = matmul_nt(grad_q_pre, w_query) + matmul_nt(grad_k_pre, w_key)
    grad_hidden = grad_hidden + matmul_nt(grad_v, w_value) + matmul_nt(grad_gate, w_gate)
    tokens_grad = grad_middle + norm_back(inputs, in_scale, grad_hidden)
    query_grad, key_grad, value_grad, gate_grad, out_grad = (
        lax.psum_scatter(query_term, ("dp", "fsdp"), scatter_dimension=0, tiled=True),
        lax.psum_scatter(key_term, ("dp", "fsdp"), scatter_dimension=0, tiled=True),
        lax.psum_scatter(value_term, ("dp", "fsdp"), scatter_dimension=0, tiled=True),
        lax.psum_scatter(gate_term, ("dp", "fsdp"), scatter_dimension=0, tiled=True),
        lax.psum_scatter(out_term, ("dp", "fsdp"), scatter_dimension=0, tiled=True),
    )
    return (
        block_out,
        tokens_grad,
        query_grad,
        key_grad,
        value_grad,
        gate_grad,
        out_grad,
        first_grad,
        second_grad,
        down_grad,
    )


MESH = pl.DeviceIdType.MESH
VMEM_BYTES = 60 * 2**20
ANY = pl.BlockSpec(memory_space=pl.ANY)
VMEM = pl.BlockSpec(memory_space=pltpu.VMEM)
SMEM = pl.BlockSpec(memory_space=pltpu.SMEM)


def place():
    plane = lax.axis_index("fsdp")
    return lax.axis_index("dp"), plane // 4, (plane // 2) % 2, plane % 2


def other(i, way):
    return i + way - 2 * i * way


def member(y, x, core):
    return (y * 2 + x) * 2 + core


def plane_peers(y, x, core):
    ways = [(dy, dx, dc) for dy in (1, 0) for dx in (1, 0) for dc in (0, 1) if dy + dx + dc]
    return [member(other(y, dy), other(x, dx), other(core, dc)) for dy, dx, dc in ways]


def greet(devices):
    barrier = pltpu.get_barrier_semaphore()
    for device in devices:
        pl.semaphore_signal(barrier, inc=1, device_id=device, device_id_type=MESH)
    pl.semaphore_wait(barrier, len(devices))


def remote(src, dst, send, recv, device):
    return pltpu.make_async_remote_copy(
        src_ref=src, dst_ref=dst, send_sem=send, recv_sem=recv, device_id=device, device_id_type=MESH
    )


def note_copies(z, me, peers, note, notes, send, recv):
    return [
        remote(note, notes.at[me], send.at[n], recv.at[n], (z, d)) for n, d in enumerate(peers)
    ]


def pack_columns(spots, weights, stages):
    for f, n, src, m, dst, wide in spots:
        stages[m][f, :, dst : dst + wide] = weights[n][:, src : src + wide]


def unpack_columns(spots, stages, grads):
    for f, n, src, m, dst, wide in spots:
        grads[n][:, src : src + wide] = stages[m][f, :, dst : dst + wide].astype(jnp.float32)


def gather_steps(spot, x_ref, o_ref, local, send, recv):
    z, y, x, core = spot
    me, mate = member(y, x, core), member(y, x, 1 - core)
    on_x, on_y, across = member(y, 1 - x, core), member(1 - y, x, core), member(1 - y, 1 - x, core)
    half = x_ref.shape[0] // 2
    low, high = pl.ds(0, half), pl.ds(half, half)

    def own(part, n, device):
        return remote(x_ref.at[part], o_ref.at[me, part], send.at[n], recv.at[n], (z, device))

    def pass_on(block, part, n, device):
        ref = o_ref.at[block, part]
        return remote(ref, ref, send.at[n], recv.at[n], (z, device))

    keep = pltpu.make_async_copy(x_ref, o_ref.at[me], local)
    first = [own(low, 0, on_y), own(high, 1, on_x), own(high, 2, on_y), own(low, 3, on_x)]
    mine = remote(x_ref, o_ref.at[me], send.at[4], recv.at[4], (z, mate))
    relay_x = pass_on(on_y, low, 5, on_x)
    relay_y = pass_on(on_x, high, 6, on_y)
    y_mate = remote(o_ref.at[on_y], o_ref.at[on_y], send.at[7], recv.at[7], (z, mate))
    x_mate = remote(o_ref.at[on_x], o_ref.at[on_x], send.at[8], recv.at[8], (z, mate))
    low_mate = pass_on(across, low, 9, mate)
    high_mate = pass_on(across, high, 10, mate)

    def begin():
        for copy in (*first, mine, keep):
            copy.start()

    def relay():
        first[0].wait_recv()
        relay_x.start()
        first[1].wait_recv()
        relay_y.start()
        first[2].wait_recv()
        y_mate.start()
        first[3].wait_recv()
        x_mate.start()

    def finish():
        relay_x.wait_recv()
        low_mate.start()
        relay_y.wait_recv()
        high_mate.start()
        keep.wait()
        for copy in (mine, y_mate, x_mate, low_mate, high_mate):
            copy.wait_recv()
        for copy in (*first, mine, relay_x, relay_y, y_mate, x_mate, low_mate, high_mate):
            copy.wait_send()

    return begin, relay, finish


GATHER_SEMAPHORES = [pltpu.SemaphoreType.DMA, pltpu.SemaphoreType.DMA((11,)), pltpu.SemaphoreType.DMA((11,))]


def gather_kernel(spots, *refs):
    if spots:
        x_ref, *weights, o_ref, swapped, local, send, recv, swap, keep_sem, s_swap, r_swap = refs
    else:
        x_ref, o_ref, local, send, recv = refs
    spot = z, y, x, core = place()
    me = member(y, x, core)
    peers = plane_peers(y, x, core)
    greet([(z, d) for d in peers])
    begin, relay, finish = gather_steps(spot, x_ref, o_ref, local, send, recv)
    begin()
    if spots:
        pack_columns(spots, weights, [swap])
        moves = [
            remote(swap.at[d], swapped.at[me], s_swap.at[n], r_swap.at[n], (z, d)) for n, d in enumerate(peers)
        ]
        moves.append(pltpu.make_async_copy(swap.at[me], swapped.at[me], keep_sem))
        for copy in moves:
            copy.start()
    relay()
    finish()
    if spots:
        for copy in moves:
            copy.wait()


def plane_gather(value, number, weights=(), spots=(), shape=None):
    rows, width = value.shape
    outs, out_specs = [jax.ShapeDtypeStruct((8, rows, width), value.dtype)], [ANY]
    scratch = list(GATHER_SEMAPHORES)
    if spots:
        outs.append(jax.ShapeDtypeStruct(shape, weights[0].dtype))
        out_specs.append(ANY)
        scratch += [pltpu.VMEM(shape, weights[0].dtype), pltpu.SemaphoreType.DMA]
        scratch += [pltpu.SemaphoreType.DMA((7,)) for _ in range(2)]
    gathered, *rest = pl.pallas_call(
        functools.partial(gather_kernel, spots),
        out_shape=outs,
        in_specs=[ANY] + [VMEM] * len(weights),
        out_specs=out_specs,
        scratch_shapes=scratch,
        compiler_params=pltpu.CompilerParams(
            collective_id=number, has_side_effects=True, vmem_limit_bytes=VMEM_BYTES
        ),
        cost_estimate=pl.CostEstimate(flops=0, bytes_accessed=2**20, transcendentals=0),
        name=f"plane_gather_{number}",
    )(value, *weights)
    return (gathered.reshape(8 * rows, width), *rest)


def spread_kernel(spots, *refs):
    *weights, note, o_ref, notes, stage, local, send, recv, s_note, r_note = refs
    z, y, x, core = place()
    me = member(y, x, core)
    peers = plane_peers(y, x, core)
    pack_columns(spots, weights, [stage])
    greet([(z, d) for d in peers])
    keep = pltpu.make_async_copy(stage.at[me], o_ref.at[me], local)
    copies = [remote(stage.at[d], o_ref.at[me], send.at[n], recv.at[n], (z, d)) for n, d in enumerate(peers)]
    copies += note_copies(z, me, peers, note, notes, s_note, r_note)
    for copy in copies:
        copy.start()
    keep.start()
    notes[me] = note[...]
    keep.wait()
    for copy in copies:
        copy.wait()


def plane_spread(weights, spots, shape, note, number):
    return pl.pallas_call(
        functools.partial(spread_kernel, spots),
        out_shape=[
            jax.ShapeDtypeStruct(shape, weights[0].dtype),
            jax.ShapeDtypeStruct((8, *note.shape), note.dtype),
        ],
        in_specs=[VMEM] * (len(weights) + 1),
        out_specs=[ANY, VMEM],
        scratch_shapes=[pltpu.VMEM(shape, weights[0].dtype), pltpu.SemaphoreType.DMA]
        + [pltpu.SemaphoreType.DMA((7,)) for _ in range(4)],
        compiler_params=pltpu.CompilerParams(
            collective_id=number, has_side_effects=True, vmem_limit_bytes=VMEM_BYTES
        ),
        cost_estimate=pl.CostEstimate(flops=0, bytes_accessed=2**20, transcendentals=0),
        name=f"plane_spread_{number}",
    )(*weights, note)


def collect_copies(z, me, peers, total, stage, local, send, recv):
    rows = stage.shape[1]

    def part(d):
        return total.at[pl.ds(pl.multiple_of(d * rows, rows), rows)]

    return [pltpu.make_async_copy(part(me), stage.at[me], local)] + [
        remote(part(d), stage.at[me], send.at[n], recv.at[n], (z, d)) for n, d in enumerate(peers)
    ]


COLLECT_SEMAPHORES = [pltpu.SemaphoreType.DMA] + [pltpu.SemaphoreType.DMA((7,)) for _ in range(2)]


def collect_kernel(total, stage, *sems):
    z, y, x, core = place()
    peers = plane_peers(y, x, core)
    greet([(z, d) for d in peers])
    copies = collect_copies(z, member(y, x, core), peers, total, stage, *sems)
    for copy in copies:
        copy.start()
    for copy in copies:
        copy.wait()


def plane_collect(total, number):
    rows = total.shape[0] // 8
    return pl.pallas_call(
        collect_kernel,
        out_shape=jax.ShapeDtypeStruct((8, rows, total.shape[1]), total.dtype),
        in_specs=[ANY],
        out_specs=ANY,
        scratch_shapes=COLLECT_SEMAPHORES,
        compiler_params=pltpu.CompilerParams(collective_id=number, has_side_effects=True),
        cost_estimate=pl.CostEstimate(flops=0, bytes_accessed=2**20, transcendentals=0),
        name=f"plane_collect_{number}",
    )(total)


def unpack_kernel(spots, stage, *grads):
    unpack_columns(spots, [stage], grads)


def unpack(stage, spots, columns, outputs):
    return pl.pallas_call(
        functools.partial(unpack_kernel, spots),
        out_shape=[jax.ShapeDtypeStruct((stage.shape[1], columns), jnp.float32) for _ in range(outputs)],
        in_specs=[VMEM],
        out_specs=[VMEM] * outputs,
        compiler_params=pltpu.CompilerParams(vmem_limit_bytes=VMEM_BYTES),
        name=f"unpack_{outputs}",
    )(stage)


def scatter_steps(spot, lefts, rights, flip, left_rows, o_ref, buffers):
    to_mate, from_mate, stage, from_x, from_y, s_mate, r_mate, s_x, r_x, s_y, r_y = buffers
    z, y, x, core = spot
    rows, width = o_ref.shape
    tile = 512
    mate = member(y, x, 1 - core)
    on_x, on_y = member(y, 1 - x, core), member(1 - y, x, core)
    left_cols, right_cols = pl.ds(0, width // 2), pl.ds(width // 2, width // 2)

    def target(i, c):
        return member(other(y, 1 - i % 2), other(x, 1 - i // 2), c)

    def each_tile(block, use):
        parts = [left_rows(left, block) for left in lefts] if left_rows else None
        here = pl.ds(pl.multiple_of(block * rows, rows), rows)

        @pl.loop(0, width // tile)
        def _(t):
            cols = pl.ds(pl.multiple_of(t * tile, tile), tile)
            total = None
            for n, right in enumerate(rights):
                part = parts[n] if left_rows else lefts[n][here, :]
                term = matmul_nt(part, right[cols, :]) if flip else matmul(part, right[:, cols])
                total = term if total is None else total + term
            use(cols, total)

    def mate_copy(i):
        return remote(to_mate.at[i], from_mate.at[i], s_mate.at[i], r_mate.at[i], (z, mate))

    def send_x(i, n):
        cols = right_cols if n == 2 else left_cols
        return remote(stage.at[i, :, cols], from_x.at[n], s_x.at[n], r_x.at[n], (z, on_x))

    def send_y(i, n):
        cols = left_cols if n == 2 else right_cols
        return remote(stage.at[i, :, cols], from_y.at[n], s_y.at[n], r_y.at[n], (z, on_y))

    def give(i):
        def use(cols, total):
            to_mate[i, :, cols] = total.astype(jnp.bfloat16)

        each_tile(target(i, 1 - core), use)
        mate_copy(i).start()

    def add(i):
        def use(cols, total):
            total = total + from_mate[i, :, cols].astype(jnp.float32)
            if i < 3:
                stage[i, :, cols] = total.astype(jnp.bfloat16)
            else:
                o_ref[:, cols] = total

        mate_copy(i).wait_recv()
        each_tile(target(i, core), use)
        if i == 0:
            send_x(0, 0).start()
            send_y(0, 0).start()
        if i == 1:
            send_x(1, 1).start()
        if i == 2:
            send_y(2, 1).start()

    def begin():
        give(0)
        for i in range(4):
            if i < 3:
                give(i + 1)
            add(i)

    def relay():
        send_y(0, 0).wait_recv()
        stage[1, :, right_cols] = (
            stage[1, :, right_cols].astype(jnp.float32) + from_y[0].astype(jnp.float32)
        ).astype(jnp.bfloat16)
        send_x(1, 2).start()
        send_x(0, 0).wait_recv()
        stage[2, :, left_cols] = (
            stage[2, :, left_cols].astype(jnp.float32) + from_x[0].astype(jnp.float32)
        ).astype(jnp.bfloat16)
        send_y(2, 2).start()

    def finish():
        send_x(1, 1).wait_recv()
        o_ref[:, left_cols] += from_x[1].astype(jnp.float32)
        send_y(2, 1).wait_recv()
        o_ref[:, right_cols] += from_y[1].astype(jnp.float32)
        send_x(1, 2).wait_recv()
        o_ref[:, right_cols] += from_x[2].astype(jnp.float32)
        send_y(2, 2).wait_recv()
        o_ref[:, left_cols] += from_y[2].astype(jnp.float32)

    def drain():
        for i in range(4):
            mate_copy(i).wait_send()
        for copy in (send_x(0, 0), send_x(1, 1), send_x(1, 2), send_y(0, 0), send_y(2, 1), send_y(2, 2)):
            copy.wait_send()

    return begin, relay, finish, drain


def scatter_buffers(rows, width):
    shapes = [pltpu.VMEM((n, rows, width), jnp.bfloat16) for n in (4, 4, 3)]
    shapes += [pltpu.VMEM((3, rows, width // 2), jnp.bfloat16) for _ in range(2)]
    return shapes + [pltpu.SemaphoreType.DMA((n,)) for n in (4, 4, 3, 3, 3, 3)]


BUFFERS = 11


def turn_mid_kernel(
    left, right, squares, tokens, middle, mid_out, scale_ref, all_squares, columns, s_note, r_note, mid, total, *rest
):
    buffers, sems = rest[:BUFFERS], rest[BUFFERS:]
    spot = z, y, x, core = place()
    rows, width = middle.shape
    me = member(y, x, core)
    peers = plane_peers(y, x, core)
    greet([(z, d) for d in peers])
    notes = note_copies(z, me, peers, squares, all_squares, s_note, r_note)
    for copy in notes:
        copy.start()
    all_squares[me] = squares[...]
    for copy in notes:
        copy.wait_recv()
    scale = lax.rsqrt(jnp.sum(all_squares[...], axis=0) / width + EPS)
    scale_ref[...] = scale
    columns[...] = jnp.transpose(scale)

    def left_rows(left, block):
        here = pl.ds(pl.multiple_of(block * rows, rows), rows)
        deep = left.shape[1] // 2
        one = lax.broadcasted_iota(jnp.int32, columns.shape, 1) == block
        column = jnp.sum(jnp.where(one, columns[...], 0.0), axis=1, keepdims=True)
        return (left[here, :deep] * column * left[here, deep:]).astype(jnp.bfloat16)

    begin, relay, finish, drain = scatter_steps(spot, [left], [right], False, left_rows, total, buffers)
    begin()
    relay()
    finish()
    value = tokens[...].astype(jnp.float32) + total[...]
    middle[...] = value
    mid[...] = normed(value)[0].astype(jnp.bfloat16)
    begin, relay, finish = gather_steps(spot, mid, mid_out, *sems)
    begin()
    drain()
    for copy in notes:
        copy.wait_send()
    relay()
    finish()


def turn_mid(left, right, squares, tokens, number):
    rows, width = tokens.shape
    f32, bf = jnp.float32, tokens.dtype
    middle, mid, scale = pl.pallas_call(
        turn_mid_kernel,
        out_shape=[
            jax.ShapeDtypeStruct((rows, width), f32),
            jax.ShapeDtypeStruct((8, rows, width), bf),
            jax.ShapeDtypeStruct(squares.shape, f32),
        ],
        in_specs=[VMEM] * 4,
        out_specs=[VMEM, ANY, VMEM],
        scratch_shapes=[
            pltpu.VMEM((8, *squares.shape), f32),
            pltpu.VMEM(squares.shape[::-1], f32),
            pltpu.SemaphoreType.DMA((7,)),
            pltpu.SemaphoreType.DMA((7,)),
            pltpu.VMEM((rows, width), bf),
            pltpu.VMEM((rows, width), f32),
        ]
        + scatter_buffers(rows, width)
        + GATHER_SEMAPHORES,
        compiler_params=pltpu.CompilerParams(
            collective_id=number, has_side_effects=True, vmem_limit_bytes=VMEM_BYTES
        ),
        cost_estimate=pl.CostEstimate(flops=0, bytes_accessed=2**20, transcendentals=0),
        name=f"turn_mid_{number}",
    )(left, right, squares, tokens)
    return middle, mid.reshape(8 * rows, width), scale


def turn_back_kernel(
    left, right, middle, tokens, cot, grad_middle, low_out, inners, inner, s_note, r_note, low, total, *rest
):
    buffers, sems = rest[:BUFFERS], rest[BUFFERS:]
    spot = z, y, x, core = place()
    rows, width = middle.shape
    me = member(y, x, core)
    peers = plane_peers(y, x, core)
    greet([(z, d) for d in peers])
    begin, relay, finish, drain = scatter_steps(spot, [left], [right], True, None, total, buffers)
    begin()
    relay()
    finish()
    value = middle[...]
    grad = cot[...].astype(jnp.float32) + norm_back(value, normed(value)[1], total[...])
    grad_middle[...] = grad
    low[...] = grad.astype(jnp.bfloat16)
    begin, relay, finish = gather_steps(spot, low, low_out, *sems)
    begin()
    added = value - tokens[...].astype(jnp.float32)
    inner[...] = lax.dot_general(
        jnp.ones((8, width), jnp.float32), low[...].astype(jnp.float32) * added, (NT, ((), ())), precision=HIGH,
        preferred_element_type=jnp.float32,
    )
    notes = note_copies(z, me, peers, inner, inners, s_note, r_note)
    for copy in notes:
        copy.start()
    inners[me] = inner[...]
    drain()
    relay()
    finish()
    for copy in notes:
        copy.wait()


def turn_back(left, right, middle, tokens, cot, number):
    rows, width = tokens.shape
    f32, bf = jnp.float32, tokens.dtype
    grad_middle, low, inner = pl.pallas_call(
        turn_back_kernel,
        out_shape=[
            jax.ShapeDtypeStruct((rows, width), f32),
            jax.ShapeDtypeStruct((8, rows, width), bf),
            jax.ShapeDtypeStruct((8, 8, rows), f32),
        ],
        in_specs=[VMEM] * 5,
        out_specs=[VMEM, ANY, VMEM],
        scratch_shapes=[
            pltpu.VMEM((8, rows), f32),
            pltpu.SemaphoreType.DMA((7,)),
            pltpu.SemaphoreType.DMA((7,)),
            pltpu.VMEM((rows, width), bf),
            pltpu.VMEM((rows, width), f32),
        ]
        + scatter_buffers(rows, width)
        + GATHER_SEMAPHORES,
        compiler_params=pltpu.CompilerParams(
            collective_id=number, has_side_effects=True, vmem_limit_bytes=VMEM_BYTES
        ),
        cost_estimate=pl.CostEstimate(flops=0, bytes_accessed=2**20, transcendentals=0),
        name=f"turn_back_{number}",
    )(left, right, middle, tokens, cot)
    return grad_middle, low.reshape(8 * rows, width), inner[:, 0]


def tail_kernel(left, right, units, o_ref, stage, *rest):
    buffers, sems = rest[:BUFFERS], rest[BUFFERS:]
    spot = z, y, x, core = place()
    peers = plane_peers(y, x, core)
    greet([(z, d) for d in peers])
    copies = collect_copies(z, member(y, x, core), peers, units, stage, *sems)
    begin, relay, finish, drain = scatter_steps(spot, [left], [right], True, None, o_ref, buffers)
    begin()
    for copy in copies:
        copy.start()
    relay()
    finish()
    drain()
    for copy in copies:
        copy.wait()


def plane_tail(left, right, units, number):
    rows, width = left.shape[0] // 8, right.shape[0]
    return pl.pallas_call(
        tail_kernel,
        out_shape=[
            jax.ShapeDtypeStruct((rows, width), jnp.float32),
            jax.ShapeDtypeStruct((8, units.shape[0] // 8, units.shape[1]), units.dtype),
        ],
        in_specs=[VMEM, VMEM, ANY],
        out_specs=[VMEM, ANY],
        scratch_shapes=scatter_buffers(rows, width) + COLLECT_SEMAPHORES,
        compiler_params=pltpu.CompilerParams(
            collective_id=number, has_side_effects=True, vmem_limit_bytes=VMEM_BYTES
        ),
        cost_estimate=pl.CostEstimate(flops=0, bytes_accessed=2**20, transcendentals=0),
        name=f"plane_tail_{number}",
    )(left, right, units)


SIDE = 256


def side_tiles(left, right, out):
    @pl.loop(0, left.shape[1] // SIDE)
    def _(t):
        cols = pl.ds(pl.multiple_of(t * SIDE, SIDE), SIDE)
        out[cols, :] = matmul_tn(left[:, cols], right[...]).astype(out.dtype)


def units_kernel(mid, weight, both, product):
    units = product.shape[1]
    out = matmul(mid[...], weight[...])
    both[...] = out
    product[...] = (out[:, :units] * out[:, units:]).astype(jnp.bfloat16)


def units_forward(mid, weight):
    rows, wide = mid.shape[0] // 8, weight.shape[1]
    return pl.pallas_call(
        units_kernel,
        grid=(8,),
        out_shape=[
            jax.ShapeDtypeStruct((8 * rows, wide), jnp.float32),
            jax.ShapeDtypeStruct((8 * rows, wide // 2), jnp.bfloat16),
        ],
        in_specs=[
            pl.BlockSpec((rows, mid.shape[1]), lambda b: (b, 0)),
            pl.BlockSpec(weight.shape, lambda b: (0, 0)),
        ],
        out_specs=[
            pl.BlockSpec((rows, wide), lambda b: (b, 0)),
            pl.BlockSpec((rows, wide // 2), lambda b: (b, 0)),
        ],
        compiler_params=pltpu.CompilerParams(
            dimension_semantics=("arbitrary",), vmem_limit_bytes=VMEM_BYTES
        ),
        cost_estimate=pl.CostEstimate(flops=2 * mid.size * wide, bytes_accessed=2**24, transcendentals=0),
        name="units_forward",
    )(mid, weight)


def units_back_kernel(weight, cot, both, mid, grads, term, whole):
    step = pl.program_id(0)
    rows = cot.shape[0]
    units = weight.shape[0]

    @pl.when(step < 8)
    def _():
        grad = matmul_nt(cot[...], weight[...])
        pair = both[...]
        here = pl.ds(pl.multiple_of(step * rows, rows), rows)
        left = (grad * pair[:, units:]).astype(jnp.bfloat16)
        right = (grad * pair[:, :units]).astype(jnp.bfloat16)
        grads[:, :units] = left
        grads[:, units:] = right
        whole[here, :units] = left
        whole[here, units:] = right

    @pl.when(step >= 8)
    def _():
        term[...] = matmul_tn(mid[...], whole[...]).astype(term.dtype)


def units_back(weight, cot, both, mid):
    rows, width = cot.shape[0] // 8, cot.shape[1]
    wide = both.shape[1]
    tile = width // 8
    bf = jnp.bfloat16
    return pl.pallas_call(
        units_back_kernel,
        grid=(16,),
        out_shape=[
            jax.ShapeDtypeStruct((8 * rows, wide), bf),
            jax.ShapeDtypeStruct((width, wide), bf),
        ],
        in_specs=[
            pl.BlockSpec(weight.shape, lambda s: (0, 0)),
            pl.BlockSpec((rows, width), lambda s: (jnp.minimum(s, 7), 0)),
            pl.BlockSpec((rows, wide), lambda s: (jnp.minimum(s, 7), 0)),
            pl.BlockSpec((8 * rows, tile), lambda s: (0, jnp.maximum(s - 8, 0))),
        ],
        out_specs=[
            pl.BlockSpec((rows, wide), lambda s: (jnp.minimum(s, 7), 0)),
            pl.BlockSpec((tile, wide), lambda s: (jnp.maximum(s - 8, 0), 0)),
        ],
        scratch_shapes=[pltpu.VMEM((8 * rows, wide), bf)],
        compiler_params=pltpu.CompilerParams(
            dimension_semantics=("arbitrary",), vmem_limit_bytes=VMEM_BYTES
        ),
        cost_estimate=pl.CostEstimate(
            flops=2 * cot.size * wide * 3 // 2, bytes_accessed=2**25, transcendentals=0
        ),
        name="units_back",
    )(weight, cot, both, mid)


def dot_fine(left, right, dims):
    high = right.astype(jnp.bfloat16)
    low = (right - high.astype(jnp.float32)).astype(jnp.bfloat16)
    product = functools.partial(
        lax.dot_general, dimension_numbers=(dims, ((), ())), preferred_element_type=jnp.float32
    )
    return product(left, high) + product(left, low)


NN, NT, TN = ((1,), (0,)), ((1,), (1,)), ((0,), (0,))


def block_tables(count, rate, rows):
    spot = lax.broadcasted_iota(jnp.int32, (rows, 1), 0)
    live = spot < count
    behind = jnp.where(live, jnp.exp(-rate * spot.astype(jnp.float32)), 0.0)
    ahead = jnp.where(live, jnp.exp(-rate * (count - spot).astype(jnp.float32)), 0.0)
    fade = jnp.exp(jnp.full((1, HEAD_DIM), -rate * count.astype(jnp.float32), jnp.float32))
    return live, behind, ahead, fade


def fill_decay(base, rates):
    heads, rows, _ = base.shape
    gap = lax.broadcasted_iota(jnp.int32, (rows, rows), 0) - lax.broadcasted_iota(jnp.int32, (rows, rows), 1)
    far = jnp.maximum(gap, 0).astype(jnp.float32)
    for t in range(heads):
        base[t] = jnp.where(gap >= 0, jnp.exp(-rates[t] * far), 0.0)


def own_rates(decay, heads):
    _, y, x, core = place()
    return [decay[4 * (heads * core + t) + 2 * y + x] for t in range(heads)]


def mix_kernel(counts, decay, hidden, weight, pre, attn_gate, qkv, entering, squares, base, state):
    b = pl.program_id(0)
    rows = hidden.shape[0]
    wide = weight.shape[1] // 4
    rates = own_rates(decay, state.shape[0])

    @pl.when(b == 0)
    def _():
        fill_decay(base, rates)
        state[...] = jnp.zeros_like(state)

    count = counts[b, 0]
    out = matmul(hidden[...], weight[...])
    pre[...] = out[:, : 2 * wide]
    gate = out[:, 3 * wide :]
    query = jax.nn.silu(out[:, :wide]).astype(jnp.bfloat16)
    keys = jax.nn.silu(out[:, wide : 2 * wide]).astype(jnp.bfloat16)
    value = out[:, 2 * wide : 3 * wide].astype(jnp.bfloat16)
    qkv[:, :wide] = query
    qkv[:, wide : 2 * wide] = keys
    qkv[:, 2 * wide :] = value
    attn_gate[:, wide:] = gate
    entering[0] = state[...]
    total = jnp.zeros((8, rows), jnp.float32)
    for t in range(state.shape[0]):
        at = slice(t * HEAD_DIM, (t + 1) * HEAD_DIM)
        q, k, v = query[:, at], keys[:, at], value[:, at]
        live, behind, ahead, fade = block_tables(count, rates[t], rows)
        mask = jnp.where(live, base[t], 0.0)
        probs = (matmul_nt(q, k) * mask).astype(jnp.bfloat16)
        attn = matmul(probs, v) + behind * dot_fine(q, state[t], NN)
        attn_gate[:, at] = attn
        total += lax.dot_general(
            jnp.ones((8, HEAD_DIM), jnp.float32), attn * attn, (NT, ((), ())), precision=HIGH,
            preferred_element_type=jnp.float32,
        )
        local = dot_fine(k, v.astype(jnp.float32) * ahead, TN)
        state[t] = jnp.where(count < rows, 0.0, fade * state[t] + local)
    squares[pl.ds(b, 1), :] = total[:1]


def mix_heads(counts, rates, hidden, weight):
    rows = hidden.shape[0] // 8
    wide = weight.shape[1] // 4
    heads = wide // HEAD_DIM
    f32 = jnp.float32

    def by_block(width):
        return pl.BlockSpec((rows, width), lambda b: (b, 0))

    def whole(*shape):
        return pl.BlockSpec(shape, lambda b: (0,) * len(shape))

    return pl.pallas_call(
        mix_kernel,
        grid=(8,),
        out_shape=[
            jax.ShapeDtypeStruct((8 * rows, 2 * wide), f32),
            jax.ShapeDtypeStruct((8 * rows, 2 * wide), f32),
            jax.ShapeDtypeStruct((8 * rows, 3 * wide), jnp.bfloat16),
            jax.ShapeDtypeStruct((8, heads, HEAD_DIM, HEAD_DIM), f32),
            jax.ShapeDtypeStruct((8, rows), f32),
        ],
        in_specs=[SMEM, SMEM, by_block(hidden.shape[1]), whole(*weight.shape)],
        out_specs=[
            by_block(2 * wide),
            by_block(2 * wide),
            by_block(3 * wide),
            pl.BlockSpec((1, heads, HEAD_DIM, HEAD_DIM), lambda b: (b, 0, 0, 0)),
            whole(8, rows),
        ],
        scratch_shapes=[pltpu.VMEM((heads, rows, rows), f32), pltpu.VMEM((heads, HEAD_DIM, HEAD_DIM), f32)],
        compiler_params=pltpu.CompilerParams(
            dimension_semantics=("arbitrary",), vmem_limit_bytes=VMEM_BYTES
        ),
        cost_estimate=pl.CostEstimate(
            flops=2 * hidden.size * weight.shape[1], bytes_accessed=4 * hidden.size, transcendentals=0
        ),
        name="mix_heads",
    )(counts, rates, hidden, weight)


def unmix_kernel(
    counts, decay, low, weight, pre, attn_gate, qkv, entering, scale, inner, product, down, hidden,
    grads_out, out_term, term_out, down_out,
    base, state, total, product_here, down_here, hidden_here, grads, term, down_own, s_in, s_out, *buffers
):
    step = pl.program_id(0)
    steps = pl.num_programs(0)
    b = steps - 1 - step
    rows, width = low.shape
    wide = weight.shape[0]
    rates = own_rates(decay, state.shape[0])
    spot = z, y, x, core = place()
    fetch = [
        pltpu.make_async_copy(src, dst, s_in.at[n])
        for n, (src, dst) in enumerate(((product, product_here), (down, down_here), (hidden, hidden_here)))
    ]
    leave = [
        pltpu.make_async_copy(src, dst, s_out.at[n])
        for n, (src, dst) in enumerate(((grads, grads_out), (term, term_out), (down_own, down_out)))
    ]
    begin, relay, finish, drain = scatter_steps(
        spot, [product_here], [down_here], False, None, down_own, buffers
    )

    @pl.when(step == 0)
    def _():
        for copy in fetch:
            copy.start()
        greet([(z, d) for d in plane_peers(y, x, core)])
        fill_decay(base, rates)
        state[...] = jnp.zeros_like(state)
        total[...] = jnp.zeros_like(total)
        fetch[0].wait()
        fetch[1].wait()
        begin()

    count = counts[b, 0]

    def column(ref):
        here = lax.broadcasted_iota(jnp.int32, (8, rows), 0) == b
        turned = jnp.transpose(jnp.where(here, ref[...], 0.0))
        return jnp.sum(turned, axis=1, keepdims=True)

    here = pl.ds(pl.multiple_of(b * rows, rows), rows)
    factor, inside = column(scale), column(inner)
    attn, gate = attn_gate[:, :wide], attn_gate[:, wide:]
    normal = attn * factor
    grad = matmul_nt(low[...], weight[...])
    grads[here, 3 * wide :] = (grad * normal).astype(jnp.bfloat16)
    grad_attn = (factor * grad * gate - normal * factor * inside * (1.0 / width)).astype(jnp.bfloat16)
    total[...] += matmul_tn((normal * gate).astype(jnp.bfloat16), low[...])
    for t in range(state.shape[0]):
        at = slice(t * HEAD_DIM, (t + 1) * HEAD_DIM)
        q, k, v = (qkv[:, i * wide + t * HEAD_DIM : i * wide + (t + 1) * HEAD_DIM] for i in range(3))
        g = grad_attn[:, at]
        live, behind, ahead, fade = block_tables(count, rates[t], rows)
        mask = jnp.where(live, base[t], 0.0)
        probs = (matmul_nt(q, k) * mask).astype(jnp.bfloat16)
        raw = (matmul_nt(g, v) * mask).astype(jnp.bfloat16)
        leaving = jnp.where(count < rows, 0.0, state[t])
        grad_q = matmul(raw, k) + behind * dot_fine(g, entering[0, t], NT)
        grad_k = matmul_tn(raw, q) + ahead * dot_fine(v, leaving, NT)
        grad_v = matmul_tn(probs, g) + ahead * dot_fine(k, leaving, NN)
        state[t] = dot_fine(q, g.astype(jnp.float32) * behind, TN) + fade * leaving
        grads[here, at] = (grad_q * silu_slope(pre[:, at])).astype(jnp.bfloat16)
        after = slice(wide + t * HEAD_DIM, wide + (t + 1) * HEAD_DIM)
        grads[here, after] = (grad_k * silu_slope(pre[:, after])).astype(jnp.bfloat16)
        grads[here, 2 * wide + t * HEAD_DIM : 2 * wide + (t + 1) * HEAD_DIM] = grad_v.astype(jnp.bfloat16)

    @pl.when(step == 2)
    def _():
        relay()

    @pl.when(step == steps - 1)
    def _():
        leave[0].start()
        out_term[...] = total[...].astype(jnp.bfloat16)
        fetch[2].wait()
        side_tiles(hidden_here, grads, term)
        leave[1].start()
        finish()
        leave[2].start()
        drain()
        for copy in leave:
            copy.wait()


def unmix_heads(counts, decay, low, weight, pre, attn_gate, qkv, entering, scale, inner, product, down, hidden, number):
    rows, width = low.shape[0] // 8, low.shape[1]
    wide = weight.shape[0]
    heads = wide // HEAD_DIM
    f32, bf = jnp.float32, jnp.bfloat16

    def by_block(columns):
        return pl.BlockSpec((rows, columns), lambda s: (7 - s, 0))

    def whole(*shape):
        return pl.BlockSpec(shape, lambda s: (0,) * len(shape))

    return pl.pallas_call(
        unmix_kernel,
        grid=(8,),
        out_shape=[
            jax.ShapeDtypeStruct((8 * rows, 4 * wide), bf),
            jax.ShapeDtypeStruct((wide, width), bf),
            jax.ShapeDtypeStruct((hidden.shape[1], 4 * wide), bf),
            jax.ShapeDtypeStruct((rows, width), f32),
        ],
        in_specs=[
            SMEM,
            SMEM,
            by_block(width),
            whole(wide, width),
            by_block(2 * wide),
            by_block(2 * wide),
            by_block(3 * wide),
            pl.BlockSpec((1, heads, HEAD_DIM, HEAD_DIM), lambda s: (7 - s, 0, 0, 0)),
            whole(8, rows),
            whole(8, rows),
            ANY,
            ANY,
            ANY,
        ],
        out_specs=[ANY, whole(wide, width), ANY, ANY],
        scratch_shapes=[
            pltpu.VMEM((heads, rows, rows), f32),
            pltpu.VMEM((heads, HEAD_DIM, HEAD_DIM), f32),
            pltpu.VMEM((wide, width), f32),
            pltpu.VMEM(product.shape, bf),
            pltpu.VMEM(down.shape, bf),
            pltpu.VMEM(hidden.shape, bf),
            pltpu.VMEM((8 * rows, 4 * wide), bf),
            pltpu.VMEM((hidden.shape[1], 4 * wide), bf),
            pltpu.VMEM((rows, width), f32),
            pltpu.SemaphoreType.DMA((3,)),
            pltpu.SemaphoreType.DMA((3,)),
        ]
        + scatter_buffers(rows, width),
        compiler_params=pltpu.CompilerParams(
            collective_id=number,
            has_side_effects=True,
            dimension_semantics=("arbitrary",),
            vmem_limit_bytes=VMEM_BYTES,
        ),
        cost_estimate=pl.CostEstimate(flops=0, bytes_accessed=2**20, transcendentals=0),
        name="unmix_heads",
    )(counts, decay, low, weight, pre, attn_gate, qkv, entering, scale, inner, product, down, hidden)


def after(value, *others):
    return lax.optimization_barrier((value, *others))[0]


def fast_plan(
    tokens,
    block_counts,
    decay_rate,
    query_weight,
    key_weight,
    value_weight,
    gate_weight,
    out_weight,
    first_weight,
    second_weight,
    down_weight,
    cotangent,
):
    rows, width = tokens.shape
    nz = lax.axis_size("dp")
    nf = lax.axis_size("fsdp")
    chips = nf // 2
    plane = lax.axis_index("fsdp")
    core = plane % 2
    bf = jnp.bfloat16
    half = HEADS // nf
    own = half * HEAD_DIM
    units = first_weight.shape[1] // nf

    head_spots = tuple(
        (2 * c + k, n, HEAD_DIM * (chips * (half * k + t) + c), 0, n * own + t * HEAD_DIM, HEAD_DIM)
        for c in range(chips) for k in range(2) for n in range(4) for t in range(half)
    )
    run = units // nz
    unit_spots = tuple(
        (f, n, run * (nf * g + f), 0, n * units + g * run, run)
        for f in range(nf) for n in range(2) for g in range(nz)
    )
    def along(weight):
        weight = weight.reshape(-1, weight.shape[-1])
        return lax.all_gather(weight, "dp", axis=0, tiled=True)

    swap = [(i, i ^ 1) for i in range(nf)]

    def cross(x):
        keep = lax.dynamic_slice_in_dim(x, core * half, half, 0)
        send = lax.dynamic_slice_in_dim(x, (1 - core) * half, half, 0)
        got = lax.ppermute(send, "fsdp", swap)
        return jnp.stack([jnp.where(core == 0, keep, got), jnp.where(core == 0, got, keep)], axis=1)

    def uncross(x):
        keep = lax.dynamic_index_in_dim(x, core, 1, False)
        send = lax.dynamic_index_in_dim(x, 1 - core, 1, False)
        got = lax.ppermute(send, "fsdp", swap)
        return jnp.concatenate([jnp.where(core == 0, keep, got), jnp.where(core == 0, got, keep)], axis=0)

    wo = cross(lax.all_gather(out_weight, "dp", axis=0)).reshape(own, width)
    note = jnp.broadcast_to(block_counts, (8, 128))
    shape = (nf, query_weight.shape[0], 4 * own)
    weights = (query_weight, key_weight, value_weight, gate_weight)
    heads_weight, counts = plane_spread(weights, head_spots, shape, note, 0)
    counts = counts[:, 0]
    w_heads = after(along(heads_weight), wo)
    inputs = tokens.astype(jnp.float32)
    in_normed, in_scale = normed(inputs)
    shape = (nf, first_weight.shape[0], 2 * units)
    low, _ = lax.optimization_barrier((in_normed.astype(bf), heads_weight))
    hidden, units_weight = plane_gather(low, 1, (first_weight, second_weight), unit_spots, shape)
    (cot,) = plane_gather(after(cotangent, hidden), 6)
    w_units = along(units_weight)
    wd = along(after(down_weight, cot))

    pre, attn_gate, qkv, entering, squares = mix_heads(counts, decay_rate, hidden, w_heads)
    middle, mid, scale = turn_mid(attn_gate, wo, squares, tokens, 2)
    both, product = units_forward(mid, w_units)
    down_term = matmul_tn(product, cot).astype(bf)
    wd = after(wd, down_term)
    down_sum = lax.psum_scatter(down_term, "dp", scatter_dimension=0, tiled=True)
    grad_units, units_term = units_back(wd, cot, both, mid)
    units_sum = lax.psum_scatter(units_term, "dp", scatter_dimension=0, tiled=True)
    grad_middle, low, inner = turn_back(grad_units, w_units, middle, tokens, cotangent, 3)
    grad_heads, out_term, heads_term, down_own = unmix_heads(
        counts, decay_rate, after(low, down_sum), wo, pre, attn_gate, qkv, entering, scale, inner, product, wd, hidden, 4
    )
    block_out = (middle + down_own).astype(bf)
    heads_sum = lax.psum_scatter(heads_term, "dp", scatter_dimension=0, tiled=True)
    out_term = uncross(out_term.reshape(half, 2, -1, width))
    out_sum = lax.psum_scatter(out_term, "dp", scatter_dimension=0, tiled=False)
    grad_hidden, units_grad = plane_tail(after(grad_heads, out_term), w_heads, units_sum, 5)
    tokens_grad = grad_middle + norm_back(inputs, in_scale, grad_hidden)
    down_grad = down_sum.astype(jnp.float32)
    first_grad, second_grad = unpack(units_grad, unit_spots, nf * units, 2)
    heads_sum = after(heads_sum, first_grad, grad_hidden)
    heads_grad = plane_collect(heads_sum, 7)
    grads = unpack(heads_grad, head_spots, width, 4)
    out_grad = after(out_sum, *grads).astype(jnp.float32)
    return (block_out, tokens_grad, *grads, out_grad, first_grad, second_grad, down_grad)


def fits(mesh):
    return mesh.shape["dp"] == 4 and mesh.shape["fsdp"] == 8


def solution(mesh):
    return jax.shard_map(
        fast_plan if fits(mesh) else shards,
        mesh=mesh,
        in_specs=(
            P(("dp", "fsdp"), None),
            P("dp", "fsdp"),
            P(),
            P(("dp", "fsdp"), None),
            P(("dp", "fsdp"), None),
            P(("dp", "fsdp"), None),
            P(("dp", "fsdp"), None),
            P(("dp", "fsdp"), None),
            P(("dp", "fsdp"), None),
            P(("dp", "fsdp"), None),
            P(("dp", "fsdp"), None),
            P(("dp", "fsdp"), None),
        ),
        out_specs=(
            P(("dp", "fsdp"), None),
            P(("dp", "fsdp"), None),
            P(("dp", "fsdp"), None),
            P(("dp", "fsdp"), None),
            P(("dp", "fsdp"), None),
            P(("dp", "fsdp"), None),
            P(("dp", "fsdp"), None),
            P(("dp", "fsdp"), None),
            P(("dp", "fsdp"), None),
            P(("dp", "fsdp"), None),
        ),
        check_vma=False,
    )
```

```python
import functools

import jax
import jax.numpy as jnp
from jax import lax
from jax.experimental import pallas as pl
from jax.experimental.pallas import tpu as pltpu
from jax.sharding import PartitionSpec as P

HEADS = 16
HEAD_DIM = 128


EPS = 1e-06
HIGH = lax.Precision.HIGHEST


def carried_in(part, axis, combine, identity):
    place = lax.axis_index(axis)
    gathered = jax.tree.map(lambda a: lax.all_gather(a, axis), part)
    state = jax.tree.map(lambda a, e: jnp.zeros_like(a) + jnp.asarray(e, a.dtype), part, identity)

    def carried_one(lap, state):
        return combine(
            state, jax.tree.map(lambda a: lax.dynamic_index_in_dim(a, lap, 0, False), gathered)
        )

    return lax.fori_loop(0, place, carried_one, state)


def prefix_2(value, axis, join, neutral):
    count = lax.axis_size(axis)
    place = lax.axis_index(axis)
    ahead = count - 1 - place
    gathered = jax.tree.map(
        lambda a, kind: lax.all_gather(a.astype(kind), axis), value, (jnp.bfloat16, jnp.bfloat16)
    )
    state = jax.tree.map(lambda a, e: jnp.zeros_like(a) + jnp.asarray(e, a.dtype), value, neutral)

    def prefix_one(lap, state):
        source = count - 1 - lap
        return join(
            state,
            jax.tree.map(
                lambda a, own: lax.dynamic_index_in_dim(a, source, 0, False).astype(own.dtype),
                gathered,
                value,
            ),
        )

    return lax.fori_loop(0, ahead, prefix_one, state)


def normed(value):
    scale = lax.rsqrt(jnp.mean(value * value, axis=-1, keepdims=True) + EPS)
    return (value * scale, scale)


def norm_back(value, scale, grad):
    inner = jnp.mean(grad * value, axis=-1, keepdims=True)
    return scale * (grad - value * scale * scale * inner)


def silu_slope(value):
    sig = jax.nn.sigmoid(value)
    return sig * (1.0 + value * (1.0 - sig))


def chain_step(earlier, later):
    e_fade, e_state = earlier
    l_fade, l_state = later
    return (l_fade * e_fade, l_fade[:, None, None] * e_state + l_state)


def matmul(left, right):
    return jnp.dot(left, right, preferred_element_type=jnp.float32)


def matmul_tn(left, right):
    return lax.dot_general(
        left, right, (((0,), (0,)), ((), ())), preferred_element_type=jnp.float32
    )


def matmul_nt(left, right):
    return lax.dot_general(
        left, right, (((1,), (1,)), ((), ())), preferred_element_type=jnp.float32
    )


def decay_tables(count, rates, rows):
    pos = lax.iota(jnp.int32, rows)
    live = pos < count
    keep = (pos[:, None] >= pos[None, :]) & live[:, None] & live[None, :]
    spacing = jnp.where(keep, (pos[:, None] - pos[None, :]).astype(jnp.float32), 0.0)
    mask = jnp.where(keep[None], jnp.exp(-rates[:, None, None] * spacing[None]), 0.0)
    ahead = jnp.where(
        live[:, None], jnp.exp(-rates[None, :] * (count - pos)[:, None].astype(jnp.float32)), 0.0
    )
    behind = jnp.where(
        live[:, None], jnp.exp(-rates[None, :] * pos[:, None].astype(jnp.float32)), 0.0
    )
    fade = jnp.exp(-rates * count.astype(jnp.float32))
    return (mask, ahead, behind, fade)


def shards(
    tokens,
    block_counts,
    decay_rate,
    query_weight,
    key_weight,
    value_weight,
    gate_weight,
    out_weight,
    first_weight,
    second_weight,
    down_weight,
    cotangent,
):
    rows = tokens.shape[0]
    gathered = (
        lax.all_gather(query_weight, ("dp", "fsdp"), axis=0, tiled=True),
        lax.all_gather(key_weight, ("dp", "fsdp"), axis=0, tiled=True),
        lax.all_gather(value_weight, ("dp", "fsdp"), axis=0, tiled=True),
        lax.all_gather(gate_weight, ("dp", "fsdp"), axis=0, tiled=True),
        lax.all_gather(out_weight, ("dp", "fsdp"), axis=0, tiled=True),
        lax.all_gather(first_weight, ("dp", "fsdp"), axis=0, tiled=True),
        lax.all_gather(second_weight, ("dp", "fsdp"), axis=0, tiled=True),
        lax.all_gather(down_weight, ("dp", "fsdp"), axis=0, tiled=True),
    )
    w_query, w_key, w_value, w_gate, w_out, w_first, w_second, w_down = gathered
    count = block_counts[0, 0]
    closes = count < rows
    mask, ahead, behind, fade = decay_tables(count, decay_rate, rows)
    passing = jnp.where(closes, 0.0, fade)
    inputs = tokens.astype(jnp.float32)
    in_normed, in_scale = normed(inputs)
    hidden = in_normed.astype(jnp.bfloat16)
    q_pre = matmul(hidden, w_query)
    k_pre = matmul(hidden, w_key)
    value = matmul(hidden, w_value).astype(jnp.bfloat16)
    gate = matmul(hidden, w_gate)
    query = jax.nn.silu(q_pre).astype(jnp.bfloat16)
    keys = jax.nn.silu(k_pre).astype(jnp.bfloat16)
    query_heads = query.reshape(rows, HEADS, HEAD_DIM)
    key_heads = keys.reshape(rows, HEADS, HEAD_DIM)
    value_heads = value.reshape(rows, HEADS, HEAD_DIM)
    query_wide = query_heads.astype(jnp.float32)
    key_wide = key_heads.astype(jnp.float32)
    value_ahead = value_heads.astype(jnp.float32) * ahead[:, :, None]
    raw = jnp.einsum("ihe,jhe->hij", query_heads, key_heads, preferred_element_type=jnp.float32)
    probs = (raw * mask).astype(jnp.bfloat16)
    intra = jnp.einsum("hij,jhe->ihe", probs, value_heads, preferred_element_type=jnp.float32)
    local = jnp.einsum("jhe,jhf->hef", key_wide, value_ahead, precision=HIGH)
    local_sent = jnp.where(closes, 0.0, local)
    prefix = carried_in(
        (passing, local_sent), "fsdp", chain_step, (jnp.ones_like(fade), jnp.zeros_like(local))
    )
    entering = prefix[1]
    inter = behind[:, :, None] * jnp.einsum("ihe,hef->ihf", query_wide, entering, precision=HIGH)
    attn = (intra + inter).reshape(rows, HEADS * HEAD_DIM)
    attn_normed, attn_scale = normed(attn)
    mixed = (attn_normed * gate).astype(jnp.bfloat16)
    middle = inputs + matmul(mixed, w_out)
    mid_normed, mid_scale = normed(middle)
    mid = mid_normed.astype(jnp.bfloat16)
    first = matmul(mid, w_first)
    second = matmul(mid, w_second)
    product = (first * second).astype(jnp.bfloat16)
    block_out = (middle + matmul(product, w_down)).astype(jnp.bfloat16)
    w_first, w_second, w_down = (
        lax.all_gather(first_weight, ("dp", "fsdp"), axis=0, tiled=True),
        lax.all_gather(second_weight, ("dp", "fsdp"), axis=0, tiled=True),
        lax.all_gather(down_weight, ("dp", "fsdp"), axis=0, tiled=True),
    )
    grad_product = matmul_nt(cotangent, w_down)
    grad_first = (grad_product * second).astype(jnp.bfloat16)
    grad_second = (grad_product * first).astype(jnp.bfloat16)
    grad_mid = matmul_nt(grad_first, w_first) + matmul_nt(grad_second, w_second)
    grad_middle = cotangent.astype(jnp.float32) + norm_back(middle, mid_scale, grad_mid)

    def scattered(left, right, after):
        left, _ = lax.optimization_barrier((left, after))
        term = matmul_tn(left, right)
        return lax.psum_scatter(term, ("dp", "fsdp"), scatter_dimension=0, tiled=True)

    down_grad = scattered(product, cotangent, grad_middle)
    first_grad = scattered(mid, grad_first, down_grad)
    second_grad = scattered(mid, grad_second, first_grad)
    grad_middle, _ = lax.optimization_barrier((grad_middle, second_grad))
    w_query, w_key, w_value, w_gate, w_out = (
        lax.all_gather(query_weight, ("dp", "fsdp"), axis=0, tiled=True),
        lax.all_gather(key_weight, ("dp", "fsdp"), axis=0, tiled=True),
        lax.all_gather(value_weight, ("dp", "fsdp"), axis=0, tiled=True),
        lax.all_gather(gate_weight, ("dp", "fsdp"), axis=0, tiled=True),
        lax.all_gather(out_weight, ("dp", "fsdp"), axis=0, tiled=True),
    )
    grad_mid_low = grad_middle.astype(jnp.bfloat16)
    out_term = matmul_tn(mixed, grad_mid_low)
    grad_mixed = matmul_nt(grad_mid_low, w_out)
    grad_gate = (grad_mixed * attn_normed).astype(jnp.bfloat16)
    grad_attn = norm_back(attn, attn_scale, grad_mixed * gate).astype(jnp.bfloat16)
    grad_heads = grad_attn.reshape(rows, HEADS, HEAD_DIM)
    grad_heads_wide = grad_heads.astype(jnp.float32) * behind[:, :, None]
    grad_probs = jnp.einsum(
        "ihe,jhe->hij", grad_heads, value_heads, preferred_element_type=jnp.float32
    )
    grad_raw = (grad_probs * mask).astype(jnp.bfloat16)
    grad_entering = jnp.einsum("ihe,ihf->hef", query_wide, grad_heads_wide, precision=HIGH)
    suffix = prefix_2(
        (passing, grad_entering),
        "fsdp",
        chain_step,
        (jnp.ones_like(fade), jnp.zeros_like(grad_entering)),
    )
    grad_leaving = jnp.where(closes, 0.0, suffix[1])
    grad_query = jnp.einsum("hij,jhe->ihe", grad_raw, key_heads, preferred_element_type=jnp.float32)
    grad_query = grad_query + jnp.einsum("ihf,hef->ihe", grad_heads_wide, entering, precision=HIGH)
    grad_keys = jnp.einsum(
        "hij,ihe->jhe", grad_raw, query_heads, preferred_element_type=jnp.float32
    )
    grad_keys = grad_keys + jnp.einsum("hef,jhf->jhe", grad_leaving, value_ahead, precision=HIGH)
    grad_value = jnp.einsum("hij,ihe->jhe", probs, grad_heads, preferred_element_type=jnp.float32)
    grad_value = grad_value + ahead[:, :, None] * jnp.einsum(
        "hef,jhe->jhf", grad_leaving, key_wide, precision=HIGH
    )
    width = HEADS * HEAD_DIM
    grad_q_pre = (grad_query.reshape(rows, width) * silu_slope(q_pre)).astype(jnp.bfloat16)
    grad_k_pre = (grad_keys.reshape(rows, width) * silu_slope(k_pre)).astype(jnp.bfloat16)
    grad_v = grad_value.reshape(rows, width).astype(jnp.bfloat16)
    query_term = matmul_tn(hidden, grad_q_pre)
    key_term = matmul_tn(hidden, grad_k_pre)
    value_term = matmul_tn(hidden, grad_v)
    gate_term = matmul_tn(hidden, grad_gate)
    grad_hidden = matmul_nt(grad_q_pre, w_query) + matmul_nt(grad_k_pre, w_key)
    grad_hidden = grad_hidden + matmul_nt(grad_v, w_value) + matmul_nt(grad_gate, w_gate)
    tokens_grad = grad_middle + norm_back(inputs, in_scale, grad_hidden)
    query_grad, key_grad, value_grad, gate_grad, out_grad = (
        lax.psum_scatter(query_term, ("dp", "fsdp"), scatter_dimension=0, tiled=True),
        lax.psum_scatter(key_term, ("dp", "fsdp"), scatter_dimension=0, tiled=True),
        lax.psum_scatter(value_term, ("dp", "fsdp"), scatter_dimension=0, tiled=True),
        lax.psum_scatter(gate_term, ("dp", "fsdp"), scatter_dimension=0, tiled=True),
        lax.psum_scatter(out_term, ("dp", "fsdp"), scatter_dimension=0, tiled=True),
    )
    return (
        block_out,
        tokens_grad,
        query_grad,
        key_grad,
        value_grad,
        gate_grad,
        out_grad,
        first_grad,
        second_grad,
        down_grad,
    )


MESH = pl.DeviceIdType.MESH
VMEM_BYTES = 60 * 2**20
ANY = pl.BlockSpec(memory_space=pl.ANY)
VMEM = pl.BlockSpec(memory_space=pltpu.VMEM)
SMEM = pl.BlockSpec(memory_space=pltpu.SMEM)


def place():
    plane = lax.axis_index("fsdp")
    return lax.axis_index("dp"), plane // 4, (plane // 2) % 2, plane % 2


def other(i, way):
    return i + way - 2 * i * way


def member(y, x, core):
    return (y * 2 + x) * 2 + core


def plane_peers(y, x, core):
    ways = [(dy, dx, dc) for dy in (1, 0) for dx in (1, 0) for dc in (0, 1) if dy + dx + dc]
    return [member(other(y, dy), other(x, dx), other(core, dc)) for dy, dx, dc in ways]


def greet(devices):
    barrier = pltpu.get_barrier_semaphore()
    for device in devices:
        pl.semaphore_signal(barrier, inc=1, device_id=device, device_id_type=MESH)
    pl.semaphore_wait(barrier, len(devices))


def remote(src, dst, send, recv, device):
    return pltpu.make_async_remote_copy(
        src_ref=src, dst_ref=dst, send_sem=send, recv_sem=recv, device_id=device, device_id_type=MESH
    )


def note_copies(z, me, peers, note, notes, send, recv):
    return [
        remote(note, notes.at[me], send.at[n], recv.at[n], (z, d)) for n, d in enumerate(peers)
    ]


def pack_columns(spots, weights, stages):
    for f, n, src, m, dst, wide in spots:
        stages[m][f, :, dst : dst + wide] = weights[n][:, src : src + wide]


def unpack_columns(spots, stages, grads):
    for f, n, src, m, dst, wide in spots:
        grads[n][:, src : src + wide] = stages[m][f, :, dst : dst + wide].astype(jnp.float32)


def gather_steps(spot, x_ref, o_ref, local, send, recv, first_row=0, rows=None):
    z, y, x, core = spot
    me, mate = member(y, x, core), member(y, x, 1 - core)
    on_x, on_y, across = member(y, 1 - x, core), member(1 - y, x, core), member(1 - y, 1 - x, core)
    rows = rows or x_ref.shape[0]
    half = rows // 2
    both = pl.ds(first_row, rows)
    low, high = pl.ds(first_row, half), pl.ds(first_row + half, half)

    def own(part, n, device):
        return remote(x_ref.at[part], o_ref.at[me, part], send.at[n], recv.at[n], (z, device))

    def pass_on(block, part, n, device):
        ref = o_ref.at[block, part]
        return remote(ref, ref, send.at[n], recv.at[n], (z, device))

    keep = pltpu.make_async_copy(x_ref.at[both], o_ref.at[me, both], local)
    first = [own(low, 0, on_y), own(high, 1, on_x), own(high, 2, on_y), own(low, 3, on_x)]
    mine = own(both, 4, mate)
    relay_x = pass_on(on_y, low, 5, on_x)
    relay_y = pass_on(on_x, high, 6, on_y)
    y_mate = pass_on(on_y, both, 7, mate)
    x_mate = pass_on(on_x, both, 8, mate)
    low_mate = pass_on(across, low, 9, mate)
    high_mate = pass_on(across, high, 10, mate)

    def begin():
        for copy in (*first, mine, keep):
            copy.start()

    def relay():
        first[0].wait_recv()
        relay_x.start()
        first[1].wait_recv()
        relay_y.start()
        first[2].wait_recv()
        y_mate.start()
        first[3].wait_recv()
        x_mate.start()

    def finish():
        relay_x.wait_recv()
        low_mate.start()
        relay_y.wait_recv()
        high_mate.start()
        keep.wait()
        for copy in (mine, y_mate, x_mate, low_mate, high_mate):
            copy.wait_recv()
        for copy in (*first, mine, relay_x, relay_y, y_mate, x_mate, low_mate, high_mate):
            copy.wait_send()

    return begin, relay, finish


GATHER_SEMAPHORES = [pltpu.SemaphoreType.DMA, pltpu.SemaphoreType.DMA((11,)), pltpu.SemaphoreType.DMA((11,))]


def row_steps(spot, rows, held, local, send, recv):
    z, y, x, core = spot
    planes = held.shape[0]
    user = z // (planes // 2)
    slot = lax.rem(z, planes // 2) * 2 + core
    keep = pltpu.make_async_copy(rows, held.at[slot], local)
    mate = remote(rows, held.at[slot], send.at[0], recv.at[slot], (z, member(y, x, 1 - core)))
    far = [
        remote(rows, held.at[slot], send.at[n], recv.at[slot], (lax.rem(z + n, planes), member(y, x, user)))
        for n in range(1, planes)
    ]

    def begin():
        for copy in far:
            copy.start()

        @pl.when(user == core)
        def _():
            keep.start()

        @pl.when(user != core)
        def _():
            mate.start()

    def finish():
        for n in range(planes):
            own = (user == core) & (slot == n)

            @pl.when(own)
            def _():
                keep.wait()

            @pl.when(jnp.logical_not(own))
            def _(n=n):
                remote(rows, held.at[n], send.at[0], recv.at[n], (z, member(y, x, 1 - core))).wait_recv()

        for copy in far:
            copy.wait_send()

        @pl.when(user != core)
        def _():
            mate.wait_send()

    return begin, finish


def column_of_chips(spot):
    z, y, x, _ = spot
    planes = lax.axis_size("dp")
    return [(lax.rem(z + n, planes), member(y, x, c)) for n in range(1, planes) for c in (0, 1)]


def plane_line_steps(spot, ref, send, recv):
    z, y, x, core = spot
    me = member(y, x, core)
    middle = lax.rem((z + 1) // 2, 2)
    own_end = 3 * (z // 2)
    near = z // 2 + 1

    def move(part, n, plane):
        return remote(ref.at[part], ref.at[part], send.at[n], recv.at[part], (plane, me))

    first = move(z, 0, middle * (3 - own_end) + (1 - middle) * (3 - near))
    second = move(z, 1, middle * own_end + (1 - middle) * near)
    relay = move(3 - own_end, 2, own_end)
    across = move(z, 3, 3 - z)

    def begin():
        first.start()
        second.start()

    def service():
        @pl.when(middle == 1)
        def _():
            relay.wait_recv()
            relay.start()
            across.start()

    def finish():
        for part in range(4):
            taken = (middle == 1) & (part == 3 - own_end)

            @pl.when((part != z) & jnp.logical_not(taken))
            def _(part=part):
                remote(ref.at[part], ref.at[part], send.at[0], recv.at[part], (3 - z, me)).wait_recv()

        first.wait_send()
        second.wait_send()

        @pl.when(middle == 1)
        def _():
            relay.wait_send()
            across.wait_send()

    return begin, service, finish


def by_planes(left, slot, right):
    rows = right.shape[1]
    return sum(matmul(left[slot, :, g * rows : (g + 1) * rows], right[g]) for g in range(right.shape[0]))


def open_kernel(head_spots, unit_spots, *refs):
    refs = list(refs)
    tokens, cot, *heads = [refs.pop(0) for _ in range(6)]
    units, (rows, down, note, decay) = [refs.pop(0) for _ in range(2)], [refs.pop(0) for _ in range(4)]
    hidden, cots, weight, held, early, units_out, notes, pre, attn_gate, qkv, entering, squares = [
        refs.pop(0) for _ in range(12)
    ]
    stage, here, swap, own, block, pre_here, mix_here, qkv_here, entering_here, base, state = [
        refs.pop(0) for _ in range(11)
    ]
    s_swap, r_swap, s_note, r_note, s_units, r_units, s_line, r_line, s_early, r_early, s_rows, r_rows = [
        refs.pop(0) for _ in range(12)
    ]
    s_block, s_out, local = [refs.pop(0) for _ in range(3)]
    sems_hidden, sems_cot = refs[:3], refs[3:]
    spot = z, y, x, core = place()
    me = member(y, x, core)
    peers = plane_peers(y, x, core)
    size = tokens.shape[0]
    deep = stage.shape[1]
    wide = here.shape[2] // 4
    count_heads = state.shape[0]

    first = pltpu.make_async_copy(down.at[pl.ds(0, early.shape[1])], early.at[z], local.at[2])
    first.start()
    pack_columns(head_spots, heads, [stage])
    greet([(z, d) for d in peers] + column_of_chips(spot))
    mine = here.at[z, pl.ds(pl.multiple_of(me * deep, deep), deep)]
    swaps = [remote(stage.at[d], mine, s_swap.at[n], r_swap.at[n], (z, d)) for n, d in enumerate(peers)]
    swaps.append(pltpu.make_async_copy(stage.at[me], mine, local.at[0]))
    passing = note_copies(z, me, peers, note, notes, s_note, r_note)
    begin_rows, finish_rows = row_steps(spot, rows, held, local.at[1], s_rows, r_rows)
    begin_early, service_early, finish_early = plane_line_steps(spot, early, s_early, r_early)
    for copy in swaps + passing:
        copy.start()
    first.wait()
    begin_early()
    notes[me] = note[...]
    own[...] = normed(tokens[...].astype(jnp.float32))[0].astype(own.dtype)
    pack_columns(unit_spots, units, [swap])
    rates = own_rates(decay, count_heads)
    fill_decay(base, rates)
    state[...] = jnp.zeros_like(state)
    service_early()
    for copy in swaps:
        copy.wait()

    begin_line, service_line, finish_line = plane_line_steps(spot, here, s_line, r_line)
    begin_hidden, relay_hidden, finish_hidden = gather_steps(spot, own, hidden, *sems_hidden)
    begin_cot, relay_cot, finish_cot = gather_steps(spot, cot, cots, *sems_cot)
    moves = [
        remote(swap.at[d], units_out.at[me], s_units.at[n], r_units.at[n], (z, d)) for n, d in enumerate(peers)
    ]
    moves.append(pltpu.make_async_copy(swap.at[me], units_out.at[me], local.at[3]))
    begin_line()
    begin_hidden()
    for copy in moves:
        copy.start()
    relay_hidden()
    finish_early()
    service_line()
    finish_hidden()
    for copy in moves + passing:
        copy.wait()
    begin_cot()

    def fetch(b):
        return pltpu.make_async_copy(hidden.at[b], block.at[b % 2], s_block.at[b % 2])

    fetch(0).start()
    finish_line()
    keep_weight = pltpu.make_async_copy(here, weight, local.at[4])
    keep_weight.start()
    begin_rows()

    def block_rows(b):
        return pl.ds(pl.multiple_of(b * size, size), size)

    def outs(b):
        return [
            pltpu.make_async_copy(src.at[at], dst.at[at], s_out.at[n, b])
            for n, (src, dst, at) in enumerate((
                (pre_here, pre, block_rows(b)),
                (mix_here, attn_gate, block_rows(b)),
                (qkv_here, qkv, block_rows(b)),
                (entering_here, entering, b),
            ))
        ]

    def mix(b):
        fetch(b).wait()

        @pl.when(b < 7)
        def _():
            fetch(b + 1).start()

        at_rows = block_rows(b)
        count = notes[b, :1, :1]
        out = by_planes(block, b % 2, here)
        pre_here[at_rows, :] = out[:, : 2 * wide]
        query = jax.nn.silu(out[:, :wide]).astype(jnp.bfloat16)
        keys = jax.nn.silu(out[:, wide : 2 * wide]).astype(jnp.bfloat16)
        value = out[:, 2 * wide : 3 * wide].astype(jnp.bfloat16)
        qkv_here[at_rows, :wide] = query
        qkv_here[at_rows, wide : 2 * wide] = keys
        qkv_here[at_rows, 2 * wide :] = value
        mix_here[at_rows, wide:] = out[:, 3 * wide :]
        entering_here[b] = state[...]
        total = jnp.zeros((8, size), jnp.float32)
        for t in range(count_heads):
            at = slice(t * HEAD_DIM, (t + 1) * HEAD_DIM)
            q, k, v = query[:, at], keys[:, at], value[:, at]
            live, behind, ahead, fade = block_tables(count, rates[t], size)
            probs = (matmul_nt(q, k) * jnp.where(live, base[t], 0.0)).astype(jnp.bfloat16)
            attn = matmul(probs, v) + behind * dot_fine(q, state[t], NN)
            mix_here[at_rows, at] = attn
            total += lax.dot_general(
                jnp.ones((8, HEAD_DIM), jnp.float32), attn * attn, (NT, ((), ())), precision=HIGH,
                preferred_element_type=jnp.float32,
            )
            local_state = dot_fine(k, v.astype(jnp.float32) * ahead, TN)
            stays = jnp.where(count < size, 0.0, 1.0)
            state[t] = stays * (fade * state[t] + local_state)
        squares[pl.ds(b, 1), :] = total[:1]
        for copy in outs(b):
            copy.start()

    pl.loop(0, 4)(mix)
    relay_cot()
    pl.loop(4, 8)(mix)
    finish_rows()

    @pl.loop(0, 8)
    def _(b):
        for copy in outs(b):
            copy.wait()

    keep_weight.wait()
    finish_cot()


def open_attention(
    tokens, cot, heads, units, rows, down, note, decay, head_spots, unit_spots, columns, unit_columns, early, number
):
    size, width = tokens.shape
    deep = rows.shape[0]
    wide = columns // 4
    count = wide // HEAD_DIM
    f32, bf, dma = jnp.float32, tokens.dtype, pltpu.SemaphoreType.DMA
    outs = (
        ((8, size, width), bf),
        ((8, size, width), bf),
        ((4, 8 * deep, columns), bf),
        ((4, deep, width), bf),
        ((4, early, width), bf),
        ((8, deep, unit_columns), bf),
        ((8, *note.shape), note.dtype),
        ((8 * size, 2 * wide), f32),
        ((8 * size, 2 * wide), f32),
        ((8 * size, 3 * wide), bf),
        ((8, count, HEAD_DIM, HEAD_DIM), f32),
        ((8, size), f32),
    )
    return pl.pallas_call(
        functools.partial(open_kernel, head_spots, unit_spots),
        out_shape=[jax.ShapeDtypeStruct(*out) for out in outs],
        in_specs=[VMEM, ANY] + [VMEM] * 6 + [ANY, ANY, VMEM, SMEM],
        out_specs=[ANY] * 6 + [VMEM] + [ANY] * 4 + [VMEM],
        scratch_shapes=[
            pltpu.VMEM((8, deep, columns), bf),
            pltpu.VMEM((4, 8 * deep, columns), bf),
            pltpu.VMEM((8, deep, unit_columns), bf),
            pltpu.VMEM((size, width), bf),
            pltpu.VMEM((2, size, width), bf),
            pltpu.VMEM((8 * size, 2 * wide), f32),
            pltpu.VMEM((8 * size, 2 * wide), f32),
            pltpu.VMEM((8 * size, 3 * wide), bf),
            pltpu.VMEM((8, count, HEAD_DIM, HEAD_DIM), f32),
            pltpu.VMEM((count, size, size), f32),
            pltpu.VMEM((count, HEAD_DIM, HEAD_DIM), f32),
        ]
        + [dma((7,)) for _ in range(6)]
        + [dma((4,)) for _ in range(6)]
        + [dma((2,)), dma((4, 8)), dma((5,))]
        + GATHER_SEMAPHORES * 2,
        compiler_params=pltpu.CompilerParams(
            collective_id=number, has_side_effects=True, vmem_limit_bytes=VMEM_BYTES
        ),
        cost_estimate=pl.CostEstimate(flops=0, bytes_accessed=2**20, transcendentals=0),
        name=f"open_attention_{number}",
    )(tokens, cot, *heads, *units, rows, down, note, decay)


def collect_copies(z, me, peers, total, stage, local, send, recv):
    rows = stage.shape[1]

    def part(d):
        return total.at[pl.ds(pl.multiple_of(d * rows, rows), rows)]

    return [pltpu.make_async_copy(part(me), stage.at[me], local)] + [
        remote(part(d), stage.at[me], send.at[n], recv.at[n], (z, d)) for n, d in enumerate(peers)
    ]


COLLECT_SEMAPHORES = [pltpu.SemaphoreType.DMA] + [pltpu.SemaphoreType.DMA((7,)) for _ in range(2)]


def collect_kernel(total, stage, *sems):
    z, y, x, core = place()
    peers = plane_peers(y, x, core)
    greet([(z, d) for d in peers])
    copies = collect_copies(z, member(y, x, core), peers, total, stage, *sems)
    for copy in copies:
        copy.start()
    for copy in copies:
        copy.wait()


def plane_collect(total, number):
    rows = total.shape[0] // 8
    return pl.pallas_call(
        collect_kernel,
        out_shape=jax.ShapeDtypeStruct((8, rows, total.shape[1]), total.dtype),
        in_specs=[ANY],
        out_specs=ANY,
        scratch_shapes=COLLECT_SEMAPHORES,
        compiler_params=pltpu.CompilerParams(collective_id=number, has_side_effects=True),
        cost_estimate=pl.CostEstimate(flops=0, bytes_accessed=2**20, transcendentals=0),
        name=f"plane_collect_{number}",
    )(total)


def unpack_kernel(spots, stage, *grads):
    unpack_columns(spots, [stage], grads)


def unpack(stage, spots, columns, outputs):
    return pl.pallas_call(
        functools.partial(unpack_kernel, spots),
        out_shape=[jax.ShapeDtypeStruct((stage.shape[1], columns), jnp.float32) for _ in range(outputs)],
        in_specs=[VMEM],
        out_specs=[VMEM] * outputs,
        compiler_params=pltpu.CompilerParams(vmem_limit_bytes=VMEM_BYTES),
        name=f"unpack_{outputs}",
    )(stage)


def scatter_steps(spot, left, right_tile, left_rows, o_ref, buffers, parts=1):
    to_mate, from_mate, stage, from_x, from_y, s_mate, r_mate, s_x, r_x, s_y, r_y = buffers
    z, y, x, core = spot
    rows, width = o_ref.shape
    tile = width // 4
    mate = member(y, x, 1 - core)
    on_x, on_y = member(y, 1 - x, core), member(1 - y, x, core)
    left_cols, right_cols = pl.ds(0, width // 2), pl.ds(width // 2, width // 2)

    def target(i, c):
        return member(other(y, 1 - i % 2), other(x, 1 - i // 2), c)

    def each_tile(block, use):
        part = left_rows(left, block) if left_rows else None
        here = pl.ds(pl.multiple_of(block * rows, rows), rows)

        @pl.loop(0, width // tile)
        def _(t):
            cols = pl.ds(pl.multiple_of(t * tile, tile), tile)
            use(cols, right_tile(part if left_rows else left[here, :], t, cols))

    def mate_copy(i):
        return remote(to_mate.at[i], from_mate.at[i], s_mate.at[i], r_mate.at[i], (z, mate))

    def part_rows(h):
        return pl.ds(h * (rows // parts), rows // parts)

    def send_x(i, n, h):
        here, cols = part_rows(h), right_cols if n == 2 else left_cols
        return remote(
            stage.at[i, here, cols], from_x.at[n, here], s_x.at[n, h], r_x.at[n, h], (z, on_x)
        )

    def send_y(i, n, h):
        here, cols = part_rows(h), left_cols if n == 2 else right_cols
        return remote(
            stage.at[i, here, cols], from_y.at[n, here], s_y.at[n, h], r_y.at[n, h], (z, on_y)
        )

    def give(i):
        def use(cols, total):
            to_mate[i, :, cols] = total.astype(jnp.bfloat16)

        each_tile(target(i, 1 - core), use)
        mate_copy(i).start()

    def add(i):
        def use(cols, total):
            total = total + from_mate[i, :, cols].astype(jnp.float32)
            if i < 3:
                stage[i, :, cols] = total.astype(jnp.bfloat16)
            else:
                o_ref[:, cols] = total

        mate_copy(i).wait_recv()
        each_tile(target(i, core), use)
        if i == 0:
            send_x(0, 0, 0).start()
            send_y(0, 0, 0).start()
        if i == 1:
            send_x(1, 1, 0).start()
        if i == 2:
            send_y(2, 1, 0).start()

    def begin():
        give(0)
        for i in range(4):
            if i < 3:
                give(i + 1)
            add(i)

    def more(h):
        send_x(0, 0, h).start()
        send_y(0, 0, h).start()
        send_x(1, 1, h).start()
        send_y(2, 1, h).start()

    def relay(h=0):
        here = part_rows(h)
        send_y(0, 0, h).wait_recv()
        stage[1, here, right_cols] = (
            stage[1, here, right_cols].astype(jnp.float32) + from_y[0, here].astype(jnp.float32)
        ).astype(jnp.bfloat16)
        send_x(1, 2, h).start()
        send_x(0, 0, h).wait_recv()
        stage[2, here, left_cols] = (
            stage[2, here, left_cols].astype(jnp.float32) + from_x[0, here].astype(jnp.float32)
        ).astype(jnp.bfloat16)
        send_y(2, 2, h).start()

    def finish(h=0):
        here = part_rows(h)
        send_x(1, 1, h).wait_recv()
        o_ref[here, left_cols] += from_x[1, here].astype(jnp.float32)
        send_y(2, 1, h).wait_recv()
        o_ref[here, right_cols] += from_y[1, here].astype(jnp.float32)
        send_x(1, 2, h).wait_recv()
        o_ref[here, right_cols] += from_x[2, here].astype(jnp.float32)
        send_y(2, 2, h).wait_recv()
        o_ref[here, left_cols] += from_y[2, here].astype(jnp.float32)

    def drain():
        for i in range(4):
            mate_copy(i).wait_send()
        for h in range(parts):
            for i, n in ((0, 0), (1, 1), (1, 2)):
                send_x(i, n, h).wait_send()
            for i, n in ((0, 0), (2, 1), (2, 2)):
                send_y(i, n, h).wait_send()

    return begin, more, relay, finish, drain


def scatter_buffers(rows, width, parts=1):
    shapes = [pltpu.VMEM((n, rows, width), jnp.bfloat16) for n in (4, 4, 3)]
    shapes += [pltpu.VMEM((3, rows, width // 2), jnp.bfloat16) for _ in range(2)]
    shapes += [pltpu.SemaphoreType.DMA((4,)) for _ in range(2)]
    return shapes + [pltpu.SemaphoreType.DMA((3, parts)) for _ in range(4)]


BUFFERS = 11


def own_row_copies(spot, packed, held, local, send, recv):
    z, y, x, core = spot
    planes, deep, wide = packed.shape
    rows = held.shape[0] // planes
    parts = held.shape[1] // wide
    mate = (z, member(y, x, 1 - core))
    copies = []
    for t in range(planes // 2):
        for n in range(parts):
            i = t * parts + n
            source = pl.ds(deep - (parts - n) * rows, rows)
            here = held.at[
                pl.ds(pl.multiple_of((2 * t + core) * rows, rows), rows), pl.ds(n * wide, wide)
            ]
            keep = packed.at[planes // 2 * core + t, source]
            give = packed.at[planes // 2 * (1 - core) + t, source]
            copies.append(pltpu.make_async_copy(keep, here, local.at[i]))
            copies.append(remote(give, here, send.at[i], recv.at[i], mate))
    return copies


TURN_PARTS = 1


def turn(spot, left, right_tile, left_rows, total, buffers, use, value, value_out, sems, last=None):
    rows = value.shape[0] // TURN_PARTS
    begin, more, relay, finish, drain = scatter_steps(
        spot, left, right_tile, left_rows, total, buffers, TURN_PARTS
    )
    count = len(GATHER_SEMAPHORES)
    gathers = [
        gather_steps(spot, value, value_out, *sems[h * count : (h + 1) * count], h * rows, rows)
        for h in range(TURN_PARTS)
    ]
    begin()
    for h in range(TURN_PARTS):
        relay(h)
        if h + 1 < TURN_PARTS:
            more(h + 1)
        finish(h)
        use(pl.ds(h * rows, rows))
        gathers[h][0]()
    if last:
        last()
    drain()
    for _, pass_on, _ in gathers:
        pass_on()
    for _, _, end in gathers:
        end()


def turn_mid_kernel(
    left, right, squares, tokens, units, down, cot, middle, mid_out, scale_ref, weight, late, both, product, term,
    all_squares, columns, s_note, r_note, mid, total, here, block, both_here, product_here, cot_here, term_here,
    s_line, r_line, s_late, r_late, s_block, s_out, s_cot, s_term, local, *rest
):
    buffers, sems = rest[:BUFFERS], rest[BUFFERS:]
    spot = z, y, x, core = place()
    rows, width = middle.shape
    me = member(y, x, core)
    peers = plane_peers(y, x, core)
    wide = here.shape[2]
    tile = cot_here.shape[2]
    shard = pltpu.make_async_copy(units, here.at[z], local.at[0])
    shard.start()
    skip = down.shape[0] - late.shape[1]
    last = pltpu.make_async_copy(down.at[pl.ds(skip, late.shape[1])], late.at[z], local.at[1])
    last.start()
    greet([(z, d) for d in peers] + [(lax.rem(z + n, 4), me) for n in range(1, 4)])
    begin_line, service_line, finish_line = plane_line_steps(spot, here, s_line, r_line)
    begin_late, service_late, finish_late = plane_line_steps(spot, late, s_late, r_late)
    notes = note_copies(z, me, peers, squares, all_squares, s_note, r_note)
    for copy in notes:
        copy.start()
    all_squares[me] = squares[...]
    shard.wait()
    begin_line()
    for copy in notes:
        copy.wait_recv()
    scale = lax.rsqrt(jnp.sum(all_squares[...], axis=0) / width + EPS)
    scale_ref[...] = scale
    columns[...] = jnp.transpose(scale)

    def left_rows(left, block):
        here = pl.ds(pl.multiple_of(block * rows, rows), rows)
        deep = left.shape[1] // 2
        one = lax.broadcasted_iota(jnp.int32, columns.shape, 1) == block
        column = jnp.sum(jnp.where(one, columns[...], 0.0), axis=1, keepdims=True)
        return (left[here, :deep] * column * left[here, deep:]).astype(jnp.bfloat16)

    def right_tile(part, t, cols):
        return matmul(part, right[:, cols])

    begin, more, relay, finish, drain = scatter_steps(spot, left, right_tile, left_rows, total, buffers)
    begin()
    relay()
    finish()
    value = tokens[...].astype(jnp.float32) + total[...]
    middle[...] = value
    mid[...] = normed(value)[0].astype(jnp.bfloat16)
    begin, relay, finish = gather_steps(spot, mid, mid_out, *sems)
    begin()
    drain()
    for copy in notes:
        copy.wait_send()
    last.wait()
    service_line()
    relay()
    finish()

    def fetch(b):
        return pltpu.make_async_copy(mid_out.at[b], block.at[b % 2], s_block.at[b % 2])

    def outs(b):
        at = pl.ds(pl.multiple_of(b * rows, rows), rows)
        return [
            pltpu.make_async_copy(both_here.at[b % 2], both.at[at], s_out.at[0, b % 2]),
            pltpu.make_async_copy(product_here.at[at], product.at[at], s_out.at[1, b % 2]),
        ]

    def fetch_cot(t):
        cols = pl.ds(pl.multiple_of(t * tile, tile), tile)
        return pltpu.make_async_copy(cot.at[:, cols], cot_here.at[t % 2], s_cot.at[t % 2])

    def leave_term(t):
        cols = pl.ds(pl.multiple_of(t * tile, tile), tile)
        return pltpu.make_async_copy(term_here.at[:, :, cols], term.at[:, :, cols], s_term.at[t])

    fetch(0).start()
    finish_line()
    keep = pltpu.make_async_copy(here, weight, local.at[2])
    keep.start()
    begin_late()

    def forward(b):
        fetch(b).wait()

        @pl.when(b < 7)
        def _():
            fetch(b + 1).start()

        @pl.when(b > 1)
        def _():
            for copy in outs(b - 2):
                copy.wait()

        out = by_planes(block, b % 2, here)
        both_here[b % 2] = out
        at = pl.ds(pl.multiple_of(b * rows, rows), rows)
        product_here[at, :] = (out[:, : wide // 2] * out[:, wide // 2 :]).astype(jnp.bfloat16)
        for copy in outs(b):
            copy.start()

    pl.loop(0, 7)(forward)
    service_late()
    fetch_cot(0).start()
    pl.loop(7, 8)(forward)

    @pl.loop(0, width // tile)
    def _(t):
        fetch_cot(t).wait()

        @pl.when(t + 1 < width // tile)
        def _():
            fetch_cot(t + 1).start()

        cols = pl.ds(pl.multiple_of(t * tile, tile), tile)
        out = matmul_tn(product_here[...], cot_here[t % 2]).astype(term.dtype)
        for g in range(4):
            term_here[g, :skip, cols] = out[g * skip : (g + 1) * skip]
            start = 4 * skip + g * late.shape[1]
            term_here[g, skip:, cols] = out[start : start + late.shape[1]]
        leave_term(t).start()

    for b in (6, 7):
        for copy in outs(b):
            copy.wait()
    for t in range(width // tile):
        leave_term(t).wait()
    keep.wait()
    finish_late()


def turn_mid(left, right, squares, tokens, units, down, cot, late, number):
    rows, width = tokens.shape
    wide = units.shape[1]
    tile = width // 4
    f32, bf, dma = jnp.float32, tokens.dtype, pltpu.SemaphoreType.DMA
    outs = (
        ((rows, width), f32),
        ((8, rows, width), bf),
        (squares.shape, f32),
        ((4, *units.shape), bf),
        ((4, late, width), bf),
        ((8 * rows, wide), f32),
        ((8 * rows, wide // 2), bf),
        ((4, wide // 8, width), bf),
    )
    return pl.pallas_call(
        turn_mid_kernel,
        out_shape=[jax.ShapeDtypeStruct(*out) for out in outs],
        in_specs=[VMEM] * 4 + [ANY] * 3,
        out_specs=[VMEM, ANY, VMEM] + [ANY] * 5,
        scratch_shapes=[
            pltpu.VMEM((8, *squares.shape), f32),
            pltpu.VMEM(squares.shape[::-1], f32),
            dma((7,)),
            dma((7,)),
            pltpu.VMEM((rows, width), bf),
            pltpu.VMEM((rows, width), f32),
            pltpu.VMEM((4, *units.shape), bf),
            pltpu.VMEM((2, rows, width), bf),
            pltpu.VMEM((2, rows, wide), f32),
            pltpu.VMEM((8 * rows, wide // 2), bf),
            pltpu.VMEM((2, 8 * rows, tile), bf),
            pltpu.VMEM((4, wide // 8, width), bf),
        ]
        + [dma((4,)) for _ in range(4)]
        + [dma((2,)), dma((2, 2)), dma((2,)), dma((4,)), dma((3,))]
        + scatter_buffers(rows, width)
        + GATHER_SEMAPHORES,
        compiler_params=pltpu.CompilerParams(
            collective_id=number, has_side_effects=True, vmem_limit_bytes=VMEM_BYTES
        ),
        cost_estimate=pl.CostEstimate(flops=0, bytes_accessed=2**20, transcendentals=0),
        name=f"turn_mid_{number}",
    )(left, right, squares, tokens, units, down, cot)


def turn_back_kernel(
    left, right, middle, tokens, cot, grad_middle, low_out, inners, inner, s_note, r_note, low, total, *rest
):
    buffers, sems = rest[:BUFFERS], rest[BUFFERS:]
    spot = z, y, x, core = place()
    rows, width = middle.shape
    me = member(y, x, core)
    peers = plane_peers(y, x, core)
    greet([(z, d) for d in peers])

    def right_tile(part, t, cols):
        return matmul_nt(part, right[cols, :])

    def use(here):
        value = middle[here, :]
        grad = cot[here, :].astype(jnp.float32) + norm_back(value, normed(value)[1], total[here, :])
        grad_middle[here, :] = grad
        low[here, :] = grad.astype(jnp.bfloat16)

    def send_inner():
        added = middle[...] - tokens[...].astype(jnp.float32)
        inner[...] = lax.dot_general(
            jnp.ones((8, width), jnp.float32), low[...].astype(jnp.float32) * added, (NT, ((), ())),
            precision=HIGH, preferred_element_type=jnp.float32,
        )
        for copy in notes:
            copy.start()
        inners[me] = inner[...]

    notes = note_copies(z, me, peers, inner, inners, s_note, r_note)
    turn(spot, left, right_tile, None, total, buffers, use, low, low_out, sems, send_inner)
    for copy in notes:
        copy.wait()


def turn_back(left, right, middle, tokens, cot, number):
    rows, width = tokens.shape
    f32, bf = jnp.float32, tokens.dtype
    grad_middle, low, inner = pl.pallas_call(
        turn_back_kernel,
        out_shape=[
            jax.ShapeDtypeStruct((rows, width), f32),
            jax.ShapeDtypeStruct((8, rows, width), bf),
            jax.ShapeDtypeStruct((8, 8, rows), f32),
        ],
        in_specs=[VMEM] * 5,
        out_specs=[VMEM, ANY, VMEM],
        scratch_shapes=[
            pltpu.VMEM((8, rows), f32),
            pltpu.SemaphoreType.DMA((7,)),
            pltpu.SemaphoreType.DMA((7,)),
            pltpu.VMEM((rows, width), bf),
            pltpu.VMEM((rows, width), f32),
        ]
        + scatter_buffers(rows, width, TURN_PARTS)
        + GATHER_SEMAPHORES * TURN_PARTS,
        compiler_params=pltpu.CompilerParams(
            collective_id=number, has_side_effects=True, vmem_limit_bytes=VMEM_BYTES
        ),
        cost_estimate=pl.CostEstimate(flops=0, bytes_accessed=2**20, transcendentals=0),
        name=f"turn_back_{number}",
    )(left, right, middle, tokens, cot)
    return grad_middle, low.reshape(8 * rows, width), inner[:, 0]


def tail_kernel(left, right, units, o_ref, stage, *rest):
    buffers, sems = rest[:BUFFERS], rest[BUFFERS:]
    spot = z, y, x, core = place()
    peers = plane_peers(y, x, core)
    greet([(z, d) for d in peers])
    copies = collect_copies(z, member(y, x, core), peers, units, stage, *sems)

    def right_tile(part, t, cols):
        return matmul_nt(part, right[cols, :])

    begin, _, relay, finish, drain = scatter_steps(spot, left, right_tile, None, o_ref, buffers)
    begin()
    for copy in copies:
        copy.start()
    relay()
    finish()
    drain()
    for copy in copies:
        copy.wait()


def plane_tail(left, right, units, number):
    rows, width = left.shape[0] // 8, right.shape[0]
    return pl.pallas_call(
        tail_kernel,
        out_shape=[
            jax.ShapeDtypeStruct((rows, width), jnp.float32),
            jax.ShapeDtypeStruct((8, units.shape[0] // 8, units.shape[1]), units.dtype),
        ],
        in_specs=[VMEM, VMEM, ANY],
        out_specs=[VMEM, ANY],
        scratch_shapes=scatter_buffers(rows, width) + COLLECT_SEMAPHORES,
        compiler_params=pltpu.CompilerParams(
            collective_id=number, has_side_effects=True, vmem_limit_bytes=VMEM_BYTES
        ),
        cost_estimate=pl.CostEstimate(flops=0, bytes_accessed=2**20, transcendentals=0),
        name=f"plane_tail_{number}",
    )(left, right, units)


SIDE = 512


def side_tiles(left, right, out):
    @pl.loop(0, left.shape[1] // SIDE)
    def _(t):
        cols = pl.ds(pl.multiple_of(t * SIDE, SIDE), SIDE)
        out[cols, :] = matmul_tn(left[:, cols], right[...]).astype(out.dtype)


def units_back_kernel(early, late, cot, both, mid, grads, term, whole, weight):
    step = pl.program_id(0)
    rows = cot.shape[0]
    units = weight.shape[0]

    @pl.when(step == 0)
    def _():
        weight[: early.shape[0]] = early[...]
        weight[early.shape[0] :] = late[...]

    @pl.when(step < 4)
    def _():
        grad = matmul_nt(cot[...], weight[...])
        here = pl.ds(pl.multiple_of(step * rows, rows), rows)
        left = (grad * both[:, units:]).astype(jnp.bfloat16)
        right = (grad * both[:, :units]).astype(jnp.bfloat16)
        grads[:, :units] = left
        grads[:, units:] = right
        whole[here, :units] = left
        whole[here, units:] = right

    @pl.when(step >= 4)
    def _():
        term[...] = matmul_tn(mid[...], whole[...]).astype(term.dtype)


def units_back(early, late, cot, both, mid):
    height, width = cot.shape
    wide = both.shape[1]
    rows, tile = height // 4, width // 4
    bf = jnp.bfloat16
    return pl.pallas_call(
        units_back_kernel,
        grid=(8,),
        out_shape=[
            jax.ShapeDtypeStruct((height, wide), bf),
            jax.ShapeDtypeStruct((width, wide), bf),
        ],
        in_specs=[
            pl.BlockSpec(early.shape, lambda s: (0, 0)),
            pl.BlockSpec(late.shape, lambda s: (0, 0)),
            pl.BlockSpec((rows, width), lambda s: (jnp.minimum(s, 3), 0)),
            pl.BlockSpec((rows, wide), lambda s: (jnp.minimum(s, 3), 0)),
            pl.BlockSpec((height, tile), lambda s: (0, jnp.maximum(s - 4, 0))),
        ],
        out_specs=[
            pl.BlockSpec((rows, wide), lambda s: (jnp.minimum(s, 3), 0)),
            pl.BlockSpec((tile, wide), lambda s: (jnp.maximum(s - 4, 0), 0)),
        ],
        scratch_shapes=[pltpu.VMEM((height, wide), bf), pltpu.VMEM((wide // 2, width), bf)],
        compiler_params=pltpu.CompilerParams(
            dimension_semantics=("arbitrary",), vmem_limit_bytes=VMEM_BYTES
        ),
        cost_estimate=pl.CostEstimate(
            flops=2 * cot.size * wide * 3 // 2, bytes_accessed=2**25, transcendentals=0
        ),
        name="units_back",
    )(early, late, cot, both, mid)


def dot_fine(left, right, dims):
    high = right.astype(jnp.bfloat16)
    low = (right - high.astype(jnp.float32)).astype(jnp.bfloat16)
    product = functools.partial(
        lax.dot_general, dimension_numbers=(dims, ((), ())), preferred_element_type=jnp.float32
    )
    return product(left, high) + product(left, low)


NN, NT, TN = ((1,), (0,)), ((1,), (1,)), ((0,), (0,))


def block_tables(count, rate, rows):
    spot = lax.broadcasted_iota(jnp.int32, (rows, 1), 0)
    live = spot < count
    behind = jnp.where(live, jnp.exp(-rate * spot.astype(jnp.float32)), 0.0)
    ahead = jnp.where(live, jnp.exp(-rate * (count - spot).astype(jnp.float32)), 0.0)
    fade = jnp.exp(jnp.full((1, HEAD_DIM), -rate * count.astype(jnp.float32), jnp.float32))
    return live, behind, ahead, fade


def fill_decay(base, rates):
    heads, rows, _ = base.shape
    gap = lax.broadcasted_iota(jnp.int32, (rows, rows), 0) - lax.broadcasted_iota(jnp.int32, (rows, rows), 1)
    far = jnp.maximum(gap, 0).astype(jnp.float32)
    for t in range(heads):
        base[t] = jnp.where(gap >= 0, jnp.exp(-rates[t] * far), 0.0)


def own_rates(decay, heads):
    _, y, x, core = place()
    return [decay[4 * (heads * core + t) + 2 * y + x] for t in range(heads)]


def unmix_kernel(
    counts, decay, low, weight, pre, attn_gate, qkv, entering, scale, inner, product, early, late, hidden,
    grads_out, out_term, term_out, down_out,
    base, state, total, product_here, down_here, hidden_here, grads, term, down_own, s_in, s_out, *buffers
):
    step = pl.program_id(0)
    steps = pl.num_programs(0)
    b = steps - 1 - step
    rows, width = low.shape
    wide = weight.shape[0]
    rates = own_rates(decay, state.shape[0])
    spot = z, y, x, core = place()
    fetch = [
        pltpu.make_async_copy(src, dst, s_in.at[n])
        for n, (src, dst) in enumerate((
            (product, product_here),
            (early, down_here.at[pl.ds(0, early.shape[0])]),
            (late, down_here.at[pl.ds(early.shape[0], late.shape[0])]),
            (hidden, hidden_here),
        ))
    ]
    leave = [
        pltpu.make_async_copy(src, dst, s_out.at[n])
        for n, (src, dst) in enumerate(((grads, grads_out), (term, term_out), (down_own, down_out)))
    ]

    def right_tile(part, t, cols):
        return matmul(part, down_here[:, cols])

    begin, _, relay, finish, drain = scatter_steps(spot, product_here, right_tile, None, down_own, buffers)

    @pl.when(step == 0)
    def _():
        for copy in fetch:
            copy.start()
        greet([(z, d) for d in plane_peers(y, x, core)])
        fill_decay(base, rates)
        state[...] = jnp.zeros_like(state)
        total[...] = jnp.zeros_like(total)
        for copy in fetch[:3]:
            copy.wait()
        begin()

    count = counts[b, 0]

    def column(ref):
        here = lax.broadcasted_iota(jnp.int32, (8, rows), 0) == b
        turned = jnp.transpose(jnp.where(here, ref[...], 0.0))
        return jnp.sum(turned, axis=1, keepdims=True)

    here = pl.ds(pl.multiple_of(b * rows, rows), rows)
    factor, inside = column(scale), column(inner)
    attn, gate = attn_gate[:, :wide], attn_gate[:, wide:]
    normal = attn * factor
    grad = matmul_nt(low[...], weight[...])
    grads[here, 3 * wide :] = (grad * normal).astype(jnp.bfloat16)
    grad_attn = (factor * grad * gate - normal * factor * inside * (1.0 / width)).astype(jnp.bfloat16)
    total[...] += matmul_tn((normal * gate).astype(jnp.bfloat16), low[...])
    for t in range(state.shape[0]):
        at = slice(t * HEAD_DIM, (t + 1) * HEAD_DIM)
        q, k, v = (qkv[:, i * wide + t * HEAD_DIM : i * wide + (t + 1) * HEAD_DIM] for i in range(3))
        g = grad_attn[:, at]
        live, behind, ahead, fade = block_tables(count, rates[t], rows)
        mask = jnp.where(live, base[t], 0.0)
        probs = (matmul_nt(q, k) * mask).astype(jnp.bfloat16)
        raw = (matmul_nt(g, v) * mask).astype(jnp.bfloat16)
        leaving = jnp.where(count < rows, 0.0, state[t])
        grad_q = matmul(raw, k) + behind * dot_fine(g, entering[0, t], NT)
        grad_k = matmul_tn(raw, q) + ahead * dot_fine(v, leaving, NT)
        grad_v = matmul_tn(probs, g) + ahead * dot_fine(k, leaving, NN)
        state[t] = dot_fine(q, g.astype(jnp.float32) * behind, TN) + fade * leaving
        grads[here, at] = (grad_q * silu_slope(pre[:, at])).astype(jnp.bfloat16)
        after = slice(wide + t * HEAD_DIM, wide + (t + 1) * HEAD_DIM)
        grads[here, after] = (grad_k * silu_slope(pre[:, after])).astype(jnp.bfloat16)
        grads[here, 2 * wide + t * HEAD_DIM : 2 * wide + (t + 1) * HEAD_DIM] = grad_v.astype(jnp.bfloat16)

    @pl.when(step == 2)
    def _():
        relay()

    @pl.when(step == steps - 1)
    def _():
        leave[0].start()
        out_term[...] = total[...].astype(jnp.bfloat16)
        fetch[3].wait()
        side_tiles(hidden_here, grads, term)
        leave[1].start()
        finish()
        leave[2].start()
        drain()
        for copy in leave:
            copy.wait()


def unmix_heads(counts, decay, low, weight, pre, attn_gate, qkv, entering, scale, inner, product, early, late, hidden, number):
    rows, width = low.shape[0] // 8, low.shape[1]
    wide = weight.shape[0]
    heads = wide // HEAD_DIM
    f32, bf = jnp.float32, jnp.bfloat16

    def by_block(columns):
        return pl.BlockSpec((rows, columns), lambda s: (7 - s, 0))

    def whole(*shape):
        return pl.BlockSpec(shape, lambda s: (0,) * len(shape))

    return pl.pallas_call(
        unmix_kernel,
        grid=(8,),
        out_shape=[
            jax.ShapeDtypeStruct((8 * rows, 4 * wide), bf),
            jax.ShapeDtypeStruct((wide, width), bf),
            jax.ShapeDtypeStruct((hidden.shape[1], 4 * wide), bf),
            jax.ShapeDtypeStruct((rows, width), f32),
        ],
        in_specs=[
            SMEM,
            SMEM,
            by_block(width),
            whole(wide, width),
            by_block(2 * wide),
            by_block(2 * wide),
            by_block(3 * wide),
            pl.BlockSpec((1, heads, HEAD_DIM, HEAD_DIM), lambda s: (7 - s, 0, 0, 0)),
            whole(8, rows),
            whole(8, rows),
            ANY,
            ANY,
            ANY,
            ANY,
        ],
        out_specs=[ANY, whole(wide, width), ANY, ANY],
        scratch_shapes=[
            pltpu.VMEM((heads, rows, rows), f32),
            pltpu.VMEM((heads, HEAD_DIM, HEAD_DIM), f32),
            pltpu.VMEM((wide, width), f32),
            pltpu.VMEM(product.shape, bf),
            pltpu.VMEM((product.shape[1], width), bf),
            pltpu.VMEM(hidden.shape, bf),
            pltpu.VMEM((8 * rows, 4 * wide), bf),
            pltpu.VMEM((hidden.shape[1], 4 * wide), bf),
            pltpu.VMEM((rows, width), f32),
            pltpu.SemaphoreType.DMA((4,)),
            pltpu.SemaphoreType.DMA((3,)),
        ]
        + scatter_buffers(rows, width),
        compiler_params=pltpu.CompilerParams(
            collective_id=number,
            has_side_effects=True,
            dimension_semantics=("arbitrary",),
            vmem_limit_bytes=VMEM_BYTES,
        ),
        cost_estimate=pl.CostEstimate(flops=0, bytes_accessed=2**20, transcendentals=0),
        name="unmix_heads",
    )(counts, decay, low, weight, pre, attn_gate, qkv, entering, scale, inner, product, early, late, hidden)


def after(value, *others):
    return lax.optimization_barrier((value, *others))[0]


def fast_plan(
    tokens,
    block_counts,
    decay_rate,
    query_weight,
    key_weight,
    value_weight,
    gate_weight,
    out_weight,
    first_weight,
    second_weight,
    down_weight,
    cotangent,
):
    rows, width = tokens.shape
    nz = lax.axis_size("dp")
    nf = lax.axis_size("fsdp")
    chips = nf // 2
    plane = lax.axis_index("fsdp")
    core = plane % 2
    bf = jnp.bfloat16
    half = HEADS // nf
    own = half * HEAD_DIM
    units = first_weight.shape[1] // nf

    head_spots = tuple(
        (2 * c + k, n, HEAD_DIM * (chips * (half * k + t) + c), 0, n * own + t * HEAD_DIM, HEAD_DIM)
        for c in range(chips) for k in range(2) for n in range(4) for t in range(half)
    )
    run = units // nz
    early = 64
    unit_spots = tuple(
        (f, n, run * (nf * g + f) + skip, 0, n * units + nz * skip + g * wide, wide)
        for f in range(nf) for n in range(2) for g in range(nz) for skip, wide in ((0, early), (early, run - early))
    )
    swap = [(i, i ^ 1) for i in range(nf)]

    def uncross(x):
        keep = lax.dynamic_index_in_dim(x, core, 1, False)
        send = lax.dynamic_index_in_dim(x, 1 - core, 1, False)
        got = lax.ppermute(send, "fsdp", swap)
        return jnp.concatenate([jnp.where(core == 0, keep, got), jnp.where(core == 0, got, keep)], axis=0)

    note = jnp.broadcast_to(block_counts, (8, 128))
    hidden, cot, w_heads, wo, wd_early, w_units, counts, pre, attn_gate, qkv, entering, squares = open_attention(
        tokens, cotangent, (query_weight, key_weight, value_weight, gate_weight), (first_weight, second_weight),
        out_weight, down_weight, note, decay_rate, head_spots, unit_spots, 4 * own, 2 * units, early, 0,
    )
    hidden, cot, wo, wd_early = (a.reshape(-1, width) for a in (hidden, cot, wo, wd_early))
    w_heads = w_heads.reshape(-1, 4 * own)
    counts = counts[:, 0]
    middle, mid, scale, w_units, wd_late, both, product, down_term = turn_mid(
        attn_gate, wo, squares, tokens, w_units.reshape(-1, 2 * units), down_weight, cot, run - early, 2
    )
    down_term = down_term.reshape(units, width)
    mid, wd_late = mid.reshape(-1, width), wd_late.reshape(-1, width)
    w_units = w_units.reshape(-1, 2 * units)
    inputs = tokens.astype(jnp.float32)
    down_sum = lax.psum_scatter(down_term, "dp", scatter_dimension=0, tiled=True)
    grad_units, units_term = units_back(wd_early, wd_late, cot, both, mid)
    units_sum = lax.psum_scatter(units_term, "dp", scatter_dimension=0, tiled=True)
    grad_middle, low, inner = turn_back(grad_units, w_units, middle, tokens, cotangent, 3)
    grad_heads, out_term, heads_term, down_own = unmix_heads(
        counts, decay_rate, after(low, down_sum), wo, pre, attn_gate, qkv, entering, scale, inner, product, wd_early, wd_late, hidden, 4
    )
    block_out = (middle + down_own).astype(bf)
    heads_sum = lax.psum_scatter(heads_term, "dp", scatter_dimension=0, tiled=True)
    out_term = uncross(out_term.reshape(half, 2, -1, width))
    out_sum = lax.psum_scatter(out_term, "dp", scatter_dimension=0, tiled=False)
    grad_hidden, units_grad = plane_tail(after(grad_heads, out_term), w_heads, units_sum, 5)
    tokens_grad = grad_middle + norm_back(inputs, normed(inputs)[1], grad_hidden)
    down_grad = down_sum.astype(jnp.float32)
    first_grad, second_grad = unpack(units_grad, unit_spots, nf * units, 2)
    heads_sum = after(heads_sum, first_grad, grad_hidden)
    heads_grad = plane_collect(heads_sum, 7)
    grads = unpack(heads_grad, head_spots, width, 4)
    out_grad = after(out_sum, *grads).astype(jnp.float32)
    return (block_out, tokens_grad, *grads, out_grad, first_grad, second_grad, down_grad)


def fits(mesh):
    return mesh.shape["dp"] == 4 and mesh.shape["fsdp"] == 8


def solution(mesh):
    return jax.shard_map(
        fast_plan if fits(mesh) else shards,
        mesh=mesh,
        in_specs=(
            P(("dp", "fsdp"), None),
            P("dp", "fsdp"),
            P(),
            P(("dp", "fsdp"), None),
            P(("dp", "fsdp"), None),
            P(("dp", "fsdp"), None),
            P(("dp", "fsdp"), None),
            P(("dp", "fsdp"), None),
            P(("dp", "fsdp"), None),
            P(("dp", "fsdp"), None),
            P(("dp", "fsdp"), None),
            P(("dp", "fsdp"), None),
        ),
        out_specs=(
            P(("dp", "fsdp"), None),
            P(("dp", "fsdp"), None),
            P(("dp", "fsdp"), None),
            P(("dp", "fsdp"), None),
            P(("dp", "fsdp"), None),
            P(("dp", "fsdp"), None),
            P(("dp", "fsdp"), None),
            P(("dp", "fsdp"), None),
            P(("dp", "fsdp"), None),
            P(("dp", "fsdp"), None),
        ),
        check_vma=False,
    )
```

```python
import functools

import jax
import jax.numpy as jnp
from jax import lax
from jax.experimental import pallas as pl
from jax.experimental.pallas import tpu as pltpu
from jax.sharding import PartitionSpec as P

HEADS = 16
HEAD_DIM = 128


EPS = 1e-06
HIGH = lax.Precision.HIGHEST


def carried_in(part, axis, combine, identity):
    place = lax.axis_index(axis)
    gathered = jax.tree.map(lambda a: lax.all_gather(a, axis), part)
    state = jax.tree.map(lambda a, e: jnp.zeros_like(a) + jnp.asarray(e, a.dtype), part, identity)

    def carried_one(lap, state):
        return combine(
            state, jax.tree.map(lambda a: lax.dynamic_index_in_dim(a, lap, 0, False), gathered)
        )

    return lax.fori_loop(0, place, carried_one, state)


def prefix_2(value, axis, join, neutral):
    count = lax.axis_size(axis)
    place = lax.axis_index(axis)
    ahead = count - 1 - place
    gathered = jax.tree.map(
        lambda a, kind: lax.all_gather(a.astype(kind), axis), value, (jnp.bfloat16, jnp.bfloat16)
    )
    state = jax.tree.map(lambda a, e: jnp.zeros_like(a) + jnp.asarray(e, a.dtype), value, neutral)

    def prefix_one(lap, state):
        source = count - 1 - lap
        return join(
            state,
            jax.tree.map(
                lambda a, own: lax.dynamic_index_in_dim(a, source, 0, False).astype(own.dtype),
                gathered,
                value,
            ),
        )

    return lax.fori_loop(0, ahead, prefix_one, state)


def normed(value):
    scale = lax.rsqrt(jnp.mean(value * value, axis=-1, keepdims=True) + EPS)
    return (value * scale, scale)


def norm_back(value, scale, grad):
    inner = jnp.mean(grad * value, axis=-1, keepdims=True)
    return scale * (grad - value * scale * scale * inner)


def silu_slope(value):
    sig = jax.nn.sigmoid(value)
    return sig * (1.0 + value * (1.0 - sig))


def chain_step(earlier, later):
    e_fade, e_state = earlier
    l_fade, l_state = later
    return (l_fade * e_fade, l_fade[:, None, None] * e_state + l_state)


def matmul(left, right):
    return jnp.dot(left, right, preferred_element_type=jnp.float32)


def matmul_tn(left, right):
    return lax.dot_general(
        left, right, (((0,), (0,)), ((), ())), preferred_element_type=jnp.float32
    )


def matmul_nt(left, right):
    return lax.dot_general(
        left, right, (((1,), (1,)), ((), ())), preferred_element_type=jnp.float32
    )


def decay_tables(count, rates, rows):
    pos = lax.iota(jnp.int32, rows)
    live = pos < count
    keep = (pos[:, None] >= pos[None, :]) & live[:, None] & live[None, :]
    spacing = jnp.where(keep, (pos[:, None] - pos[None, :]).astype(jnp.float32), 0.0)
    mask = jnp.where(keep[None], jnp.exp(-rates[:, None, None] * spacing[None]), 0.0)
    ahead = jnp.where(
        live[:, None], jnp.exp(-rates[None, :] * (count - pos)[:, None].astype(jnp.float32)), 0.0
    )
    behind = jnp.where(
        live[:, None], jnp.exp(-rates[None, :] * pos[:, None].astype(jnp.float32)), 0.0
    )
    fade = jnp.exp(-rates * count.astype(jnp.float32))
    return (mask, ahead, behind, fade)


def shards(
    tokens,
    block_counts,
    decay_rate,
    query_weight,
    key_weight,
    value_weight,
    gate_weight,
    out_weight,
    first_weight,
    second_weight,
    down_weight,
    cotangent,
):
    rows = tokens.shape[0]
    gathered = (
        lax.all_gather(query_weight, ("dp", "fsdp"), axis=0, tiled=True),
        lax.all_gather(key_weight, ("dp", "fsdp"), axis=0, tiled=True),
        lax.all_gather(value_weight, ("dp", "fsdp"), axis=0, tiled=True),
        lax.all_gather(gate_weight, ("dp", "fsdp"), axis=0, tiled=True),
        lax.all_gather(out_weight, ("dp", "fsdp"), axis=0, tiled=True),
        lax.all_gather(first_weight, ("dp", "fsdp"), axis=0, tiled=True),
        lax.all_gather(second_weight, ("dp", "fsdp"), axis=0, tiled=True),
        lax.all_gather(down_weight, ("dp", "fsdp"), axis=0, tiled=True),
    )
    w_query, w_key, w_value, w_gate, w_out, w_first, w_second, w_down = gathered
    count = block_counts[0, 0]
    closes = count < rows
    mask, ahead, behind, fade = decay_tables(count, decay_rate, rows)
    passing = jnp.where(closes, 0.0, fade)
    inputs = tokens.astype(jnp.float32)
    in_normed, in_scale = normed(inputs)
    hidden = in_normed.astype(jnp.bfloat16)
    q_pre = matmul(hidden, w_query)
    k_pre = matmul(hidden, w_key)
    value = matmul(hidden, w_value).astype(jnp.bfloat16)
    gate = matmul(hidden, w_gate)
    query = jax.nn.silu(q_pre).astype(jnp.bfloat16)
    keys = jax.nn.silu(k_pre).astype(jnp.bfloat16)
    query_heads = query.reshape(rows, HEADS, HEAD_DIM)
    key_heads = keys.reshape(rows, HEADS, HEAD_DIM)
    value_heads = value.reshape(rows, HEADS, HEAD_DIM)
    query_wide = query_heads.astype(jnp.float32)
    key_wide = key_heads.astype(jnp.float32)
    value_ahead = value_heads.astype(jnp.float32) * ahead[:, :, None]
    raw = jnp.einsum("ihe,jhe->hij", query_heads, key_heads, preferred_element_type=jnp.float32)
    probs = (raw * mask).astype(jnp.bfloat16)
    intra = jnp.einsum("hij,jhe->ihe", probs, value_heads, preferred_element_type=jnp.float32)
    local = jnp.einsum("jhe,jhf->hef", key_wide, value_ahead, precision=HIGH)
    local_sent = jnp.where(closes, 0.0, local)
    prefix = carried_in(
        (passing, local_sent), "fsdp", chain_step, (jnp.ones_like(fade), jnp.zeros_like(local))
    )
    entering = prefix[1]
    inter = behind[:, :, None] * jnp.einsum("ihe,hef->ihf", query_wide, entering, precision=HIGH)
    attn = (intra + inter).reshape(rows, HEADS * HEAD_DIM)
    attn_normed, attn_scale = normed(attn)
    mixed = (attn_normed * gate).astype(jnp.bfloat16)
    middle = inputs + matmul(mixed, w_out)
    mid_normed, mid_scale = normed(middle)
    mid = mid_normed.astype(jnp.bfloat16)
    first = matmul(mid, w_first)
    second = matmul(mid, w_second)
    product = (first * second).astype(jnp.bfloat16)
    block_out = (middle + matmul(product, w_down)).astype(jnp.bfloat16)
    w_first, w_second, w_down = (
        lax.all_gather(first_weight, ("dp", "fsdp"), axis=0, tiled=True),
        lax.all_gather(second_weight, ("dp", "fsdp"), axis=0, tiled=True),
        lax.all_gather(down_weight, ("dp", "fsdp"), axis=0, tiled=True),
    )
    grad_product = matmul_nt(cotangent, w_down)
    grad_first = (grad_product * second).astype(jnp.bfloat16)
    grad_second = (grad_product * first).astype(jnp.bfloat16)
    grad_mid = matmul_nt(grad_first, w_first) + matmul_nt(grad_second, w_second)
    grad_middle = cotangent.astype(jnp.float32) + norm_back(middle, mid_scale, grad_mid)

    def scattered(left, right, after):
        left, _ = lax.optimization_barrier((left, after))
        term = matmul_tn(left, right)
        return lax.psum_scatter(term, ("dp", "fsdp"), scatter_dimension=0, tiled=True)

    down_grad = scattered(product, cotangent, grad_middle)
    first_grad = scattered(mid, grad_first, down_grad)
    second_grad = scattered(mid, grad_second, first_grad)
    grad_middle, _ = lax.optimization_barrier((grad_middle, second_grad))
    w_query, w_key, w_value, w_gate, w_out = (
        lax.all_gather(query_weight, ("dp", "fsdp"), axis=0, tiled=True),
        lax.all_gather(key_weight, ("dp", "fsdp"), axis=0, tiled=True),
        lax.all_gather(value_weight, ("dp", "fsdp"), axis=0, tiled=True),
        lax.all_gather(gate_weight, ("dp", "fsdp"), axis=0, tiled=True),
        lax.all_gather(out_weight, ("dp", "fsdp"), axis=0, tiled=True),
    )
    grad_mid_low = grad_middle.astype(jnp.bfloat16)
    out_term = matmul_tn(mixed, grad_mid_low)
    grad_mixed = matmul_nt(grad_mid_low, w_out)
    grad_gate = (grad_mixed * attn_normed).astype(jnp.bfloat16)
    grad_attn = norm_back(attn, attn_scale, grad_mixed * gate).astype(jnp.bfloat16)
    grad_heads = grad_attn.reshape(rows, HEADS, HEAD_DIM)
    grad_heads_wide = grad_heads.astype(jnp.float32) * behind[:, :, None]
    grad_probs = jnp.einsum(
        "ihe,jhe->hij", grad_heads, value_heads, preferred_element_type=jnp.float32
    )
    grad_raw = (grad_probs * mask).astype(jnp.bfloat16)
    grad_entering = jnp.einsum("ihe,ihf->hef", query_wide, grad_heads_wide, precision=HIGH)
    suffix = prefix_2(
        (passing, grad_entering),
        "fsdp",
        chain_step,
        (jnp.ones_like(fade), jnp.zeros_like(grad_entering)),
    )
    grad_leaving = jnp.where(closes, 0.0, suffix[1])
    grad_query = jnp.einsum("hij,jhe->ihe", grad_raw, key_heads, preferred_element_type=jnp.float32)
    grad_query = grad_query + jnp.einsum("ihf,hef->ihe", grad_heads_wide, entering, precision=HIGH)
    grad_keys = jnp.einsum(
        "hij,ihe->jhe", grad_raw, query_heads, preferred_element_type=jnp.float32
    )
    grad_keys = grad_keys + jnp.einsum("hef,jhf->jhe", grad_leaving, value_ahead, precision=HIGH)
    grad_value = jnp.einsum("hij,ihe->jhe", probs, grad_heads, preferred_element_type=jnp.float32)
    grad_value = grad_value + ahead[:, :, None] * jnp.einsum(
        "hef,jhe->jhf", grad_leaving, key_wide, precision=HIGH
    )
    width = HEADS * HEAD_DIM
    grad_q_pre = (grad_query.reshape(rows, width) * silu_slope(q_pre)).astype(jnp.bfloat16)
    grad_k_pre = (grad_keys.reshape(rows, width) * silu_slope(k_pre)).astype(jnp.bfloat16)
    grad_v = grad_value.reshape(rows, width).astype(jnp.bfloat16)
    query_term = matmul_tn(hidden, grad_q_pre)
    key_term = matmul_tn(hidden, grad_k_pre)
    value_term = matmul_tn(hidden, grad_v)
    gate_term = matmul_tn(hidden, grad_gate)
    grad_hidden = matmul_nt(grad_q_pre, w_query) + matmul_nt(grad_k_pre, w_key)
    grad_hidden = grad_hidden + matmul_nt(grad_v, w_value) + matmul_nt(grad_gate, w_gate)
    tokens_grad = grad_middle + norm_back(inputs, in_scale, grad_hidden)
    query_grad, key_grad, value_grad, gate_grad, out_grad = (
        lax.psum_scatter(query_term, ("dp", "fsdp"), scatter_dimension=0, tiled=True),
        lax.psum_scatter(key_term, ("dp", "fsdp"), scatter_dimension=0, tiled=True),
        lax.psum_scatter(value_term, ("dp", "fsdp"), scatter_dimension=0, tiled=True),
        lax.psum_scatter(gate_term, ("dp", "fsdp"), scatter_dimension=0, tiled=True),
        lax.psum_scatter(out_term, ("dp", "fsdp"), scatter_dimension=0, tiled=True),
    )
    return (
        block_out,
        tokens_grad,
        query_grad,
        key_grad,
        value_grad,
        gate_grad,
        out_grad,
        first_grad,
        second_grad,
        down_grad,
    )


MESH = pl.DeviceIdType.MESH
VMEM_BYTES = 60 * 2**20
ANY = pl.BlockSpec(memory_space=pl.ANY)
VMEM = pl.BlockSpec(memory_space=pltpu.VMEM)
SMEM = pl.BlockSpec(memory_space=pltpu.SMEM)


def place():
    plane = lax.axis_index("fsdp")
    return lax.axis_index("dp"), plane // 4, (plane // 2) % 2, plane % 2


def other(i, way):
    return i + way - 2 * i * way


def member(y, x, core):
    return (y * 2 + x) * 2 + core


def plane_peers(y, x, core):
    ways = [(dy, dx, dc) for dy in (1, 0) for dx in (1, 0) for dc in (0, 1) if dy + dx + dc]
    return [member(other(y, dy), other(x, dx), other(core, dc)) for dy, dx, dc in ways]


def greet(devices):
    barrier = pltpu.get_barrier_semaphore()
    for device in devices:
        pl.semaphore_signal(barrier, inc=1, device_id=device, device_id_type=MESH)
    pl.semaphore_wait(barrier, len(devices))


def remote(src, dst, send, recv, device):
    return pltpu.make_async_remote_copy(
        src_ref=src, dst_ref=dst, send_sem=send, recv_sem=recv, device_id=device, device_id_type=MESH
    )


def note_copies(z, me, peers, note, notes, send, recv):
    return [
        remote(note, notes.at[me], send.at[n], recv.at[n], (z, d)) for n, d in enumerate(peers)
    ]


def pack_columns(spots, weights, stages):
    for f, n, src, m, dst, wide in spots:
        stages[m][f, :, dst : dst + wide] = weights[n][:, src : src + wide]


def unpack_columns(spots, stages, grads):
    for f, n, src, m, dst, wide in spots:
        grads[n][:, src : src + wide] = stages[m][f, :, dst : dst + wide].astype(jnp.float32)


def gather_steps(spot, x_ref, o_ref, local, send, recv, first_row=0, rows=None):
    z, y, x, core = spot
    me, mate = member(y, x, core), member(y, x, 1 - core)
    on_x, on_y, across = member(y, 1 - x, core), member(1 - y, x, core), member(1 - y, 1 - x, core)
    rows = rows or x_ref.shape[0]
    half = rows // 2
    both = pl.ds(first_row, rows)
    low, high = pl.ds(first_row, half), pl.ds(first_row + half, half)

    def own(part, n, device):
        return remote(x_ref.at[part], o_ref.at[me, part], send.at[n], recv.at[n], (z, device))

    def pass_on(block, part, n, device):
        ref = o_ref.at[block, part]
        return remote(ref, ref, send.at[n], recv.at[n], (z, device))

    keep = pltpu.make_async_copy(x_ref.at[both], o_ref.at[me, both], local)
    first = [own(low, 0, on_y), own(high, 1, on_x), own(high, 2, on_y), own(low, 3, on_x)]
    mine = own(both, 4, mate)
    relay_x = pass_on(on_y, low, 5, on_x)
    relay_y = pass_on(on_x, high, 6, on_y)
    y_mate = pass_on(on_y, both, 7, mate)
    x_mate = pass_on(on_x, both, 8, mate)
    low_mate = pass_on(across, low, 9, mate)
    high_mate = pass_on(across, high, 10, mate)

    def begin():
        for copy in (*first, mine, keep):
            copy.start()

    def relay():
        first[0].wait_recv()
        relay_x.start()
        first[1].wait_recv()
        relay_y.start()
        first[2].wait_recv()
        y_mate.start()
        first[3].wait_recv()
        x_mate.start()

    def finish():
        relay_x.wait_recv()
        low_mate.start()
        relay_y.wait_recv()
        high_mate.start()
        keep.wait()
        for copy in (mine, y_mate, x_mate, low_mate, high_mate):
            copy.wait_recv()
        for copy in (*first, mine, relay_x, relay_y, y_mate, x_mate, low_mate, high_mate):
            copy.wait_send()

    return begin, relay, finish


GATHER_SEMAPHORES = [pltpu.SemaphoreType.DMA, pltpu.SemaphoreType.DMA((11,)), pltpu.SemaphoreType.DMA((11,))]


def column_of_chips(spot):
    z, y, x, _ = spot
    planes = lax.axis_size("dp")
    return [(lax.rem(z + n, planes), member(y, x, c)) for n in range(1, planes) for c in (0, 1)]


def plane_line_steps(spot, ref, send, recv):
    z, y, x, core = spot
    me = member(y, x, core)
    middle = lax.rem((z + 1) // 2, 2)
    own_end = 3 * (z // 2)
    near = z // 2 + 1

    def move(part, n, plane):
        return remote(ref.at[part], ref.at[part], send.at[n], recv.at[part], (plane, me))

    first = move(z, 0, middle * (3 - own_end) + (1 - middle) * (3 - near))
    second = move(z, 1, middle * own_end + (1 - middle) * near)
    relay = move(3 - own_end, 2, own_end)
    across = move(z, 3, 3 - z)

    def begin():
        first.start()
        second.start()

    def service():
        @pl.when(middle == 1)
        def _():
            relay.wait_recv()
            relay.start()
            across.start()

    def finish():
        for part in range(4):
            taken = (middle == 1) & (part == 3 - own_end)

            @pl.when((part != z) & jnp.logical_not(taken))
            def _(part=part):
                remote(ref.at[part], ref.at[part], send.at[0], recv.at[part], (3 - z, me)).wait_recv()

        first.wait_send()
        second.wait_send()

        @pl.when(middle == 1)
        def _():
            relay.wait_send()
            across.wait_send()

    return begin, service, finish


def by_planes(left, slot, right):
    rows = right.shape[1]
    return sum(matmul(left[slot, :, g * rows : (g + 1) * rows], right[g]) for g in range(right.shape[0]))


def open_kernel(head_spots, unit_spots, *refs):
    refs = list(refs)
    tokens, cot, *heads = [refs.pop(0) for _ in range(6)]
    units, (rows, down, note, decay) = [refs.pop(0) for _ in range(2)], [refs.pop(0) for _ in range(4)]
    hidden, cots, weight, held, early, units_out, notes, pre, attn_gate, qkv, entering, squares = [
        refs.pop(0) for _ in range(12)
    ]
    stage, here, swap, own, block, pre_here, mix_here, qkv_here, entering_here, base, state = [
        refs.pop(0) for _ in range(11)
    ]
    s_swap, r_swap, s_note, r_note, s_units, r_units, s_line, r_line, s_early, r_early, s_rows, r_rows = [
        refs.pop(0) for _ in range(12)
    ]
    s_next, r_next = [refs.pop(0) for _ in range(2)]
    s_block, s_out, local = [refs.pop(0) for _ in range(3)]
    sems_hidden, sems_cot = refs[:3], refs[3:]
    spot = z, y, x, core = place()
    me = member(y, x, core)
    peers = plane_peers(y, x, core)
    size = tokens.shape[0]
    deep = stage.shape[1]
    wide = here.shape[2] // 4
    count_heads = state.shape[0]

    first = pltpu.make_async_copy(down.at[pl.ds(0, early.shape[1])], early.at[z], local.at[2])
    first.start()
    pack_columns(head_spots, heads, [stage])
    greet([(z, d) for d in peers] + [(lax.rem(z + n, 4), me) for n in range(1, 4)])
    mine = pl.ds(pl.multiple_of(me * deep, deep), deep)
    columns = [pl.ds(h * 2 * wide, 2 * wide) for h in range(2)]
    swaps = []
    for h, cols in enumerate(columns):
        copies = [
            remote(stage.at[d, :, cols], here.at[z, mine, cols], s_swap.at[h, n], r_swap.at[h, n], (z, d))
            for n, d in enumerate(peers)
        ]
        copies.append(pltpu.make_async_copy(stage.at[me, :, cols], here.at[z, mine, cols], local.at[5 * h]))
        swaps.append(copies)
    passing = note_copies(z, me, peers, note, notes, s_note, r_note)
    begin_rows, service_rows, finish_rows = plane_line_steps(spot, held, s_rows, r_rows)
    keep_rows = pltpu.make_async_copy(rows, held.at[z], local.at[1])
    keep_rows.start()
    half = early.shape[1] // 2
    begin_early, service_early, finish_early = plane_line_steps(
        spot, early.at[:, pl.ds(0, half)], s_early, r_early
    )
    begin_next, service_next, finish_next = plane_line_steps(
        spot, early.at[:, pl.ds(half, half)], s_next, r_next
    )
    for copy in swaps[0] + swaps[1] + passing:
        copy.start()
    first.wait()
    begin_early()
    notes[me] = note[...]
    lines = [
        plane_line_steps(spot, here.at[:, :, cols], s_line.at[h], r_line.at[h]) for h, cols in enumerate(columns)
    ]
    own[...] = normed(tokens[...].astype(jnp.float32))[0].astype(own.dtype)
    for copy in swaps[0]:
        copy.wait()
    lines[0][0]()
    service_early()
    pack_columns(unit_spots, units, [swap])
    rates = own_rates(decay, count_heads)
    fill_decay(base, rates)
    state[...] = jnp.zeros_like(state)
    for copy in swaps[1]:
        copy.wait()
    lines[1][0]()
    begin_hidden, relay_hidden, finish_hidden = gather_steps(spot, own, hidden, *sems_hidden)
    begin_cot, relay_cot, finish_cot = gather_steps(spot, cot, cots, *sems_cot)
    moves = [
        remote(swap.at[d], units_out.at[me], s_units.at[n], r_units.at[n], (z, d)) for n, d in enumerate(peers)
    ]
    moves.append(pltpu.make_async_copy(swap.at[me], units_out.at[me], local.at[3]))
    begin_hidden()
    relay_hidden()
    for copy in moves:
        copy.start()
    begin_cot()
    finish_early()
    for _, service, _ in lines:
        service()
    finish_hidden()
    for copy in passing:
        copy.wait()

    def fetch(b):
        return pltpu.make_async_copy(hidden.at[b], block.at[b % 2], s_block.at[b % 2])

    fetch(0).start()
    for _, _, finish_line in lines:
        finish_line()
    keep_weight = pltpu.make_async_copy(here, weight, local.at[4])
    keep_weight.start()
    keep_rows.wait()
    begin_rows()
    begin_next()

    def block_rows(b):
        return pl.ds(pl.multiple_of(b * size, size), size)

    def outs(b):
        return [
            pltpu.make_async_copy(src.at[at], dst.at[at], s_out.at[n, b])
            for n, (src, dst, at) in enumerate((
                (pre_here, pre, block_rows(b)),
                (mix_here, attn_gate, block_rows(b)),
                (qkv_here, qkv, block_rows(b)),
                (entering_here, entering, b),
            ))
        ]

    def mix(b):
        fetch(b).wait()

        @pl.when(b < 7)
        def _():
            fetch(b + 1).start()

        at_rows = block_rows(b)
        count = notes[b, :1, :1]
        out = by_planes(block, b % 2, here)
        pre_here[at_rows, :] = out[:, : 2 * wide]
        query = jax.nn.silu(out[:, :wide]).astype(jnp.bfloat16)
        keys = jax.nn.silu(out[:, wide : 2 * wide]).astype(jnp.bfloat16)
        value = out[:, 2 * wide : 3 * wide].astype(jnp.bfloat16)
        qkv_here[at_rows, :wide] = query
        qkv_here[at_rows, wide : 2 * wide] = keys
        qkv_here[at_rows, 2 * wide :] = value
        mix_here[at_rows, wide:] = out[:, 3 * wide :]
        entering_here[b] = state[...]
        total = jnp.zeros((8, size), jnp.float32)
        for t in range(count_heads):
            at = slice(t * HEAD_DIM, (t + 1) * HEAD_DIM)
            q, k, v = query[:, at], keys[:, at], value[:, at]
            live, behind, ahead, fade = block_tables(count, rates[t], size)
            probs = (matmul_nt(q, k) * jnp.where(live, base[t], 0.0)).astype(jnp.bfloat16)
            attn = matmul(probs, v) + behind * dot_fine(q, state[t], NN)
            mix_here[at_rows, at] = attn
            total += lax.dot_general(
                jnp.ones((8, HEAD_DIM), jnp.float32), attn * attn, (NT, ((), ())), precision=HIGH,
                preferred_element_type=jnp.float32,
            )
            local_state = dot_fine(k, v.astype(jnp.float32) * ahead, TN)
            stays = jnp.where(count < size, 0.0, 1.0)
            state[t] = stays * (fade * state[t] + local_state)
        squares[pl.ds(b, 1), :] = total[:1]
        for copy in outs(b):
            copy.start()

    pl.loop(0, 5)(mix)
    relay_cot()
    service_rows()
    service_next()
    pl.loop(5, 8)(mix)
    finish_rows()
    finish_next()
    for copy in moves:
        copy.wait()

    @pl.loop(0, 8)
    def _(b):
        for copy in outs(b):
            copy.wait()

    keep_weight.wait()
    finish_cot()


def open_attention(
    tokens, cot, heads, units, rows, down, note, decay, head_spots, unit_spots, columns, unit_columns, early, number
):
    size, width = tokens.shape
    deep = rows.shape[0]
    wide = columns // 4
    count = wide // HEAD_DIM
    f32, bf, dma = jnp.float32, tokens.dtype, pltpu.SemaphoreType.DMA
    outs = (
        ((8, size, width), bf),
        ((8, size, width), bf),
        ((4, 8 * deep, columns), bf),
        ((4, deep, width), bf),
        ((4, early, width), bf),
        ((8, deep, unit_columns), bf),
        ((8, *note.shape), note.dtype),
        ((8 * size, 2 * wide), f32),
        ((8 * size, 2 * wide), f32),
        ((8 * size, 3 * wide), bf),
        ((8, count, HEAD_DIM, HEAD_DIM), f32),
        ((8, size), f32),
    )
    return pl.pallas_call(
        functools.partial(open_kernel, head_spots, unit_spots),
        out_shape=[jax.ShapeDtypeStruct(*out) for out in outs],
        in_specs=[VMEM, ANY] + [VMEM] * 6 + [ANY, ANY, VMEM, SMEM],
        out_specs=[ANY] * 6 + [VMEM] + [ANY] * 4 + [VMEM],
        scratch_shapes=[
            pltpu.VMEM((8, deep, columns), bf),
            pltpu.VMEM((4, 8 * deep, columns), bf),
            pltpu.VMEM((8, deep, unit_columns), bf),
            pltpu.VMEM((size, width), bf),
            pltpu.VMEM((2, size, width), bf),
            pltpu.VMEM((8 * size, 2 * wide), f32),
            pltpu.VMEM((8 * size, 2 * wide), f32),
            pltpu.VMEM((8 * size, 3 * wide), bf),
            pltpu.VMEM((8, count, HEAD_DIM, HEAD_DIM), f32),
            pltpu.VMEM((count, size, size), f32),
            pltpu.VMEM((count, HEAD_DIM, HEAD_DIM), f32),
        ]
        + [dma((2, 7)) for _ in range(2)]
        + [dma((7,)) for _ in range(4)]
        + [dma((2, 4)) for _ in range(2)]
        + [dma((4,)) for _ in range(6)]
        + [dma((2,)), dma((4, 8)), dma((6,))]
        + GATHER_SEMAPHORES * 2,
        compiler_params=pltpu.CompilerParams(
            collective_id=number, has_side_effects=True, vmem_limit_bytes=VMEM_BYTES
        ),
        cost_estimate=pl.CostEstimate(flops=0, bytes_accessed=2**20, transcendentals=0),
        name=f"open_attention_{number}",
    )(tokens, cot, *heads, *units, rows, down, note, decay)


def collect_copies(z, me, peers, total, stage, local, send, recv):
    rows = stage.shape[1]

    def part(d):
        return total.at[pl.ds(pl.multiple_of(d * rows, rows), rows)]

    return [pltpu.make_async_copy(part(me), stage.at[me], local)] + [
        remote(part(d), stage.at[me], send.at[n], recv.at[n], (z, d)) for n, d in enumerate(peers)
    ]


COLLECT_SEMAPHORES = [pltpu.SemaphoreType.DMA] + [pltpu.SemaphoreType.DMA((7,)) for _ in range(2)]


def collect_kernel(total, stage, *sems):
    z, y, x, core = place()
    peers = plane_peers(y, x, core)
    greet([(z, d) for d in peers])
    copies = collect_copies(z, member(y, x, core), peers, total, stage, *sems)
    for copy in copies:
        copy.start()
    for copy in copies:
        copy.wait()


def plane_collect(total, number):
    rows = total.shape[0] // 8
    return pl.pallas_call(
        collect_kernel,
        out_shape=jax.ShapeDtypeStruct((8, rows, total.shape[1]), total.dtype),
        in_specs=[ANY],
        out_specs=ANY,
        scratch_shapes=COLLECT_SEMAPHORES,
        compiler_params=pltpu.CompilerParams(collective_id=number, has_side_effects=True),
        cost_estimate=pl.CostEstimate(flops=0, bytes_accessed=2**20, transcendentals=0),
        name=f"plane_collect_{number}",
    )(total)


def unpack_kernel(spots, stage, *grads):
    unpack_columns(spots, [stage], grads)


def unpack(stage, spots, columns, outputs):
    return pl.pallas_call(
        functools.partial(unpack_kernel, spots),
        out_shape=[jax.ShapeDtypeStruct((stage.shape[1], columns), jnp.float32) for _ in range(outputs)],
        in_specs=[VMEM],
        out_specs=[VMEM] * outputs,
        compiler_params=pltpu.CompilerParams(vmem_limit_bytes=VMEM_BYTES),
        name=f"unpack_{outputs}",
    )(stage)


PIECES = 5


def scatter_steps(spot, left, right_tile, left_rows, o_ref, buffers):
    to_mate, from_mate, stage, from_x, from_y, s_mate, r_mate, s_x, r_x, s_y, r_y = buffers
    z, y, x, core = spot
    rows, width = o_ref.shape
    tile = width // 4
    mate = member(y, x, 1 - core)
    on_x, on_y = member(y, 1 - x, core), member(1 - y, x, core)
    left_cols, right_cols = pl.ds(0, width // 2), pl.ds(width // 2, width // 2)

    def target(i, c):
        return member(other(y, 1 - i % 2), other(x, 1 - i // 2), c)

    def each_tile(block, use):
        part = left_rows(left, block) if left_rows else None
        here = pl.ds(pl.multiple_of(block * rows, rows), rows)

        @pl.loop(0, width // tile)
        def _(t):
            cols = pl.ds(pl.multiple_of(t * tile, tile), tile)
            use(t, cols, right_tile(part if left_rows else left[here, :], t, cols))

    def mate_copy(i):
        return remote(to_mate.at[i], from_mate.at[i], s_mate.at[i], r_mate.at[i], (z, mate))

    def send_x(i, n):
        cols = right_cols if n == 2 else left_cols
        return remote(stage.at[i, :, cols], from_x.at[n], s_x.at[n], r_x.at[n], (z, on_x))

    def send_y(i, n):
        cols = left_cols if n == 2 else right_cols
        return remote(stage.at[i, :, cols], from_y.at[n], s_y.at[n], r_y.at[n], (z, on_y))

    def give(i):
        def use(t, cols, total):
            to_mate[i, :, cols] = total.astype(jnp.bfloat16)

        each_tile(target(i, 1 - core), use)
        mate_copy(i).start()

    def add(i):
        def use(t, cols, total):
            pl.when(t == 0)(mate_copy(i).wait_recv)
            total = total + from_mate[i, :, cols].astype(jnp.float32)
            if i < 3:
                stage[i, :, cols] = total.astype(jnp.bfloat16)
            else:
                o_ref[:, cols] = total
            if i == 0:
                pl.when(t == width // tile // 2 - 1)(send_x(0, 0).start)

        each_tile(target(i, core), use)
        if i == 0:
            send_y(0, 0).start()
        if i == 1:
            send_x(1, 1).start()
        if i == 2:
            send_y(2, 1).start()

    def piece(n):
        if n < 4:
            give(n)
        if n > 0:
            add(n - 1)

    def begin():
        for n in range(PIECES):
            piece(n)

    def relay():
        send_y(0, 0).wait_recv()
        stage[1, :, right_cols] = (
            stage[1, :, right_cols].astype(jnp.float32) + from_y[0].astype(jnp.float32)
        ).astype(jnp.bfloat16)
        send_x(1, 2).start()
        send_x(0, 0).wait_recv()
        stage[2, :, left_cols] = (
            stage[2, :, left_cols].astype(jnp.float32) + from_x[0].astype(jnp.float32)
        ).astype(jnp.bfloat16)
        send_y(2, 2).start()

    def finish():
        send_x(1, 1).wait_recv()
        o_ref[:, left_cols] += from_x[1].astype(jnp.float32)
        send_y(2, 1).wait_recv()
        o_ref[:, right_cols] += from_y[1].astype(jnp.float32)
        send_x(1, 2).wait_recv()
        o_ref[:, right_cols] += from_x[2].astype(jnp.float32)
        send_y(2, 2).wait_recv()
        o_ref[:, left_cols] += from_y[2].astype(jnp.float32)

    def drain():
        for i in range(4):
            mate_copy(i).wait_send()
        for copy in (send_x(0, 0), send_x(1, 1), send_x(1, 2), send_y(0, 0), send_y(2, 1), send_y(2, 2)):
            copy.wait_send()

    return begin, piece, relay, finish, drain


def scatter_buffers(rows, width):
    shapes = [pltpu.VMEM((n, rows, width), jnp.bfloat16) for n in (4, 4, 3)]
    shapes += [pltpu.VMEM((3, rows, width // 2), jnp.bfloat16) for _ in range(2)]
    return shapes + [pltpu.SemaphoreType.DMA((n,)) for n in (4, 4, 3, 3, 3, 3)]


BUFFERS = 11


def own_row_copies(spot, packed, held, local, send, recv):
    z, y, x, core = spot
    planes, deep, wide = packed.shape
    rows = held.shape[0] // planes
    parts = held.shape[1] // wide
    mate = (z, member(y, x, 1 - core))
    copies = []
    for t in range(planes // 2):
        for n in range(parts):
            i = t * parts + n
            source = pl.ds(deep - (parts - n) * rows, rows)
            here = held.at[
                pl.ds(pl.multiple_of((2 * t + core) * rows, rows), rows), pl.ds(n * wide, wide)
            ]
            keep = packed.at[planes // 2 * core + t, source]
            give = packed.at[planes // 2 * (1 - core) + t, source]
            copies.append(pltpu.make_async_copy(keep, here, local.at[i]))
            copies.append(remote(give, here, send.at[i], recv.at[i], mate))
    return copies


def own_row_copies(spot, held, right, local, send, recv):
    z, y, x, core = spot
    planes, rows, _ = held.shape
    half = planes // 2
    mate = (z, member(y, x, 1 - core))
    copies = []
    for t in range(half):
        here = right.at[pl.ds(pl.multiple_of((2 * t + core) * rows, rows), rows)]
        copies.append(pltpu.make_async_copy(held.at[half * core + t], here, local.at[t]))
        copies.append(remote(held.at[half * (1 - core) + t], here, send.at[t], recv.at[t], mate))
    return copies


def turn_mid_kernel(
    left, held, squares, tokens, units, down, cot, middle, mid_out, scale_ref, weight, late, both, product, term, right,
    all_squares, columns, s_note, r_note, mid, total, here, block, both_here, product_here, cot_here, term_here,
    s_line, r_line, s_late, r_late, s_block, s_out, s_cot, s_term, local, right_here, s_row, r_row, *rest
):
    buffers, sems = rest[:BUFFERS], rest[BUFFERS:]
    spot = z, y, x, core = place()
    rows, width = middle.shape
    me = member(y, x, core)
    peers = plane_peers(y, x, core)
    wide = here.shape[2]
    tile = cot_here.shape[2]
    shard = pltpu.make_async_copy(units, here.at[z], local.at[0])
    shard.start()
    skip = down.shape[0] - late.shape[1]
    last = pltpu.make_async_copy(down.at[pl.ds(skip, late.shape[1])], late.at[z], local.at[1])
    last.start()
    greet([(z, d) for d in peers] + [(lax.rem(z + n, 4), me) for n in range(1, 4)])
    begin_line, service_line, finish_line = plane_line_steps(spot, here, s_line, r_line)
    begin_late, service_late, finish_late = plane_line_steps(spot, late, s_late, r_late)
    notes = note_copies(z, me, peers, squares, all_squares, s_note, r_note)
    moves = own_row_copies(spot, held, right_here, local.at[pl.ds(3, 2)], s_row, r_row)
    for copy in notes + moves:
        copy.start()
    all_squares[me] = squares[...]
    shard.wait()
    begin_line()
    for copy in notes:
        copy.wait_recv()
    scale = lax.rsqrt(jnp.sum(all_squares[...], axis=0) / width + EPS)
    scale_ref[...] = scale
    columns[...] = jnp.transpose(scale)

    def left_rows(left, block):
        here = pl.ds(pl.multiple_of(block * rows, rows), rows)
        deep = left.shape[1] // 2
        one = lax.broadcasted_iota(jnp.int32, columns.shape, 1) == block
        column = jnp.sum(jnp.where(one, columns[...], 0.0), axis=1, keepdims=True)
        return (left[here, :deep] * column * left[here, deep:]).astype(jnp.bfloat16)

    for copy in moves:
        copy.wait()
    right[...] = right_here[...]

    def right_tile(part, t, cols):
        return matmul(part, right_here[:, cols])

    begin, _, relay, finish, drain = scatter_steps(spot, left, right_tile, left_rows, total, buffers)
    begin()
    relay()
    finish()
    value = tokens[...].astype(jnp.float32) + total[...]
    middle[...] = value
    mid[...] = normed(value)[0].astype(jnp.bfloat16)
    begin, relay, finish = gather_steps(spot, mid, mid_out, *sems)
    begin()
    drain()
    for copy in notes:
        copy.wait_send()
    last.wait()
    service_line()
    relay()
    finish()

    def fetch(b):
        return pltpu.make_async_copy(mid_out.at[b], block.at[b % 2], s_block.at[b % 2])

    def outs(b):
        at = pl.ds(pl.multiple_of(b * rows, rows), rows)
        return [
            pltpu.make_async_copy(both_here.at[b % 2], both.at[at], s_out.at[0, b % 2]),
            pltpu.make_async_copy(product_here.at[at], product.at[at], s_out.at[1, b % 2]),
        ]

    def fetch_cot(t):
        cols = pl.ds(pl.multiple_of(t * tile, tile), tile)
        return pltpu.make_async_copy(cot.at[:, cols], cot_here.at[t % 2], s_cot.at[t % 2])

    def leave_term(t):
        cols = pl.ds(pl.multiple_of(t * tile, tile), tile)
        return pltpu.make_async_copy(term_here.at[:, :, cols], term.at[:, :, cols], s_term.at[t])

    fetch(0).start()
    finish_line()
    keep = pltpu.make_async_copy(here, weight, local.at[2])
    keep.start()
    begin_late()

    def forward(b):
        fetch(b).wait()

        @pl.when(b < 7)
        def _():
            fetch(b + 1).start()

        @pl.when(b > 1)
        def _():
            for copy in outs(b - 2):
                copy.wait()

        out = by_planes(block, b % 2, here)
        both_here[b % 2] = out
        at = pl.ds(pl.multiple_of(b * rows, rows), rows)
        product_here[at, :] = (out[:, : wide // 2] * out[:, wide // 2 :]).astype(jnp.bfloat16)
        for copy in outs(b):
            copy.start()

    pl.loop(0, 7)(forward)
    service_late()
    fetch_cot(0).start()
    pl.loop(7, 8)(forward)

    @pl.loop(0, width // tile)
    def _(t):
        fetch_cot(t).wait()

        @pl.when(t + 1 < width // tile)
        def _():
            fetch_cot(t + 1).start()

        cols = pl.ds(pl.multiple_of(t * tile, tile), tile)
        out = matmul_tn(product_here[...], cot_here[t % 2]).astype(term.dtype)
        for g in range(4):
            term_here[g, :skip, cols] = out[g * skip : (g + 1) * skip]
            start = 4 * skip + g * late.shape[1]
            term_here[g, skip:, cols] = out[start : start + late.shape[1]]
        leave_term(t).start()

    for b in (6, 7):
        for copy in outs(b):
            copy.wait()
    for t in range(width // tile):
        leave_term(t).wait()
    keep.wait()
    finish_late()


def turn_mid(left, held, squares, tokens, units, down, cot, late, number):
    rows, width = tokens.shape
    wide = units.shape[1]
    tile = width // 4
    f32, bf, dma = jnp.float32, tokens.dtype, pltpu.SemaphoreType.DMA
    outs = (
        ((rows, width), f32),
        ((8, rows, width), bf),
        (squares.shape, f32),
        ((4, *units.shape), bf),
        ((4, late, width), bf),
        ((8 * rows, wide), f32),
        ((8 * rows, wide // 2), bf),
        ((4, wide // 8, width), bf),
        ((held.shape[0] * held.shape[1], width), bf),
    )
    return pl.pallas_call(
        turn_mid_kernel,
        out_shape=[jax.ShapeDtypeStruct(*out) for out in outs],
        in_specs=[VMEM, ANY, VMEM, VMEM] + [ANY] * 3,
        out_specs=[VMEM, ANY, VMEM] + [ANY] * 5 + [VMEM],
        scratch_shapes=[
            pltpu.VMEM((8, *squares.shape), f32),
            pltpu.VMEM(squares.shape[::-1], f32),
            dma((7,)),
            dma((7,)),
            pltpu.VMEM((rows, width), bf),
            pltpu.VMEM((rows, width), f32),
            pltpu.VMEM((4, *units.shape), bf),
            pltpu.VMEM((2, rows, width), bf),
            pltpu.VMEM((2, rows, wide), f32),
            pltpu.VMEM((8 * rows, wide // 2), bf),
            pltpu.VMEM((2, 8 * rows, tile), bf),
            pltpu.VMEM((4, wide // 8, width), bf),
        ]
        + [dma((4,)) for _ in range(4)]
        + [dma((2,)), dma((2, 2)), dma((2,)), dma((4,)), dma((5,))]
        + [pltpu.VMEM((held.shape[0] * held.shape[1], width), bf), dma((2,)), dma((2,))]
        + scatter_buffers(rows, width)
        + GATHER_SEMAPHORES,
        compiler_params=pltpu.CompilerParams(
            collective_id=number, has_side_effects=True, vmem_limit_bytes=VMEM_BYTES
        ),
        cost_estimate=pl.CostEstimate(flops=0, bytes_accessed=2**20, transcendentals=0),
        name=f"turn_mid_{number}",
    )(left, held, squares, tokens, units, down, cot)


def turn_back_kernel(
    left, right, middle, tokens, cot, grad_middle, low_out, inners,
    inner, s_note, r_note, low, total, left_here, right_here, middle_here, tokens_here, cot_here, s_left, s_in, *rest
):
    buffers, sems = rest[:BUFFERS], rest[BUFFERS:]
    spot = z, y, x, core = place()
    rows, width = grad_middle.shape
    me = member(y, x, core)
    peers = plane_peers(y, x, core)

    def fetch(block):
        here = pl.ds(pl.multiple_of(block * rows, rows), rows)
        return pltpu.make_async_copy(left.at[here], left_here.at[here], s_left.at[block])

    pairs = ((right, right_here), (middle, middle_here), (tokens, tokens_here), (cot, cot_here))
    whole = [pltpu.make_async_copy(src, dst, s_in.at[n]) for n, (src, dst) in enumerate(pairs)]
    whole[0].start()
    for way in range(4):
        for other_core in (1, 0):
            fetch(member(other(y, 1 - way % 2), other(x, 1 - way // 2), other(core, other_core))).start()
    for copy in whole[1:]:
        copy.start()
    greet([(z, d) for d in peers])
    whole[0].wait()

    def left_rows(left, block):
        fetch(block).wait()
        return left_here[pl.ds(pl.multiple_of(block * rows, rows), rows), :]

    def right_tile(part, t, cols):
        return matmul_nt(part, right_here[cols, :])

    begin, _, relay, finish, drain = scatter_steps(spot, left, right_tile, left_rows, total, buffers)
    begin()
    relay()
    finish()
    for copy in whole[1:]:
        copy.wait()
    value = middle_here[...]
    grad = cot_here[...].astype(jnp.float32) + norm_back(value, normed(value)[1], total[...])
    grad_middle[...] = grad
    low[...] = grad.astype(jnp.bfloat16)
    begin, relay, finish = gather_steps(spot, low, low_out, *sems)
    begin()
    added = value - tokens_here[...].astype(jnp.float32)
    inner[...] = lax.dot_general(
        jnp.ones((8, width), jnp.float32), low[...].astype(jnp.float32) * added, (NT, ((), ())), precision=HIGH,
        preferred_element_type=jnp.float32,
    )
    notes = note_copies(z, me, peers, inner, inners, s_note, r_note)
    for copy in notes:
        copy.start()
    inners[me] = inner[...]
    drain()
    relay()
    finish()
    for copy in notes:
        copy.wait()


def turn_back(left, right, middle, tokens, cot, number):
    rows, width = tokens.shape
    f32, bf = jnp.float32, tokens.dtype
    grad_middle, low, inner = pl.pallas_call(
        turn_back_kernel,
        out_shape=[
            jax.ShapeDtypeStruct((rows, width), f32),
            jax.ShapeDtypeStruct((8, rows, width), bf),
            jax.ShapeDtypeStruct((8, 8, rows), f32),
        ],
        in_specs=[ANY] * 5,
        out_specs=[VMEM, ANY, VMEM],
        scratch_shapes=[
            pltpu.VMEM((8, rows), f32),
            pltpu.SemaphoreType.DMA((7,)),
            pltpu.SemaphoreType.DMA((7,)),
            pltpu.VMEM((rows, width), bf),
            pltpu.VMEM((rows, width), f32),
            pltpu.VMEM(left.shape, bf),
            pltpu.VMEM(right.shape, bf),
            pltpu.VMEM((rows, width), f32),
            pltpu.VMEM((rows, width), bf),
            pltpu.VMEM((rows, width), bf),
            pltpu.SemaphoreType.DMA((8,)),
            pltpu.SemaphoreType.DMA((4,)),
        ]
        + scatter_buffers(rows, width)
        + GATHER_SEMAPHORES,
        compiler_params=pltpu.CompilerParams(
            collective_id=number, has_side_effects=True, vmem_limit_bytes=VMEM_BYTES
        ),
        cost_estimate=pl.CostEstimate(flops=0, bytes_accessed=2**20, transcendentals=0),
        name=f"turn_back_{number}",
    )(left, right, middle, tokens, cot)
    return grad_middle, low.reshape(8 * rows, width), inner


def tail_kernel(left, right, units, o_ref, stage, *rest):
    buffers, sems = rest[:BUFFERS], rest[BUFFERS:]
    spot = z, y, x, core = place()
    peers = plane_peers(y, x, core)
    greet([(z, d) for d in peers])
    copies = collect_copies(z, member(y, x, core), peers, units, stage, *sems)

    def right_tile(part, t, cols):
        return matmul_nt(part, right[cols, :])

    begin, _, relay, finish, drain = scatter_steps(spot, left, right_tile, None, o_ref, buffers)
    begin()
    for copy in copies:
        copy.start()
    relay()
    finish()
    drain()
    for copy in copies:
        copy.wait()


def plane_tail(left, right, units, number):
    rows, width = left.shape[0] // 8, right.shape[0]
    return pl.pallas_call(
        tail_kernel,
        out_shape=[
            jax.ShapeDtypeStruct((rows, width), jnp.float32),
            jax.ShapeDtypeStruct((8, units.shape[0] // 8, units.shape[1]), units.dtype),
        ],
        in_specs=[VMEM, VMEM, ANY],
        out_specs=[VMEM, ANY],
        scratch_shapes=scatter_buffers(rows, width) + COLLECT_SEMAPHORES,
        compiler_params=pltpu.CompilerParams(
            collective_id=number, has_side_effects=True, vmem_limit_bytes=VMEM_BYTES
        ),
        cost_estimate=pl.CostEstimate(flops=0, bytes_accessed=2**20, transcendentals=0),
        name=f"plane_tail_{number}",
    )(left, right, units)


SIDE = 512


def side_tiles(left, right, out):
    @pl.loop(0, left.shape[1] // SIDE)
    def _(t):
        cols = pl.ds(pl.multiple_of(t * SIDE, SIDE), SIDE)
        out[cols, :] = matmul_tn(left[:, cols], right[...]).astype(out.dtype)


def units_back_kernel(early, late, cot, both, mid, grads, term, whole, weight, sems):
    step = pl.program_id(0)
    rows = cot.shape[0]
    units = weight.shape[0]

    @pl.when(step == 0)
    def _():
        count = early.shape[0]
        parts = ((early, weight.at[pl.ds(0, count)]), (late, weight.at[pl.ds(count, late.shape[0])]))
        copies = [pltpu.make_async_copy(src, dst, sems.at[n]) for n, (src, dst) in enumerate(parts)]
        for copy in copies:
            copy.start()
        for copy in copies:
            copy.wait()

    @pl.when(step < 4)
    def _():
        grad = matmul_nt(cot[...], weight[...])
        here = pl.ds(pl.multiple_of(step * rows, rows), rows)
        left = (grad * both[:, units:]).astype(jnp.bfloat16)
        right = (grad * both[:, :units]).astype(jnp.bfloat16)
        grads[:, :units] = left
        grads[:, units:] = right
        whole[here, :units] = left
        whole[here, units:] = right

    @pl.when(step >= 4)
    def _():
        term[...] = matmul_tn(mid[...], whole[...]).astype(term.dtype)


def units_back(early, late, cot, both, mid):
    height, width = cot.shape
    wide = both.shape[1]
    rows, tile = height // 4, width // 4
    bf = jnp.bfloat16
    return pl.pallas_call(
        units_back_kernel,
        grid=(8,),
        out_shape=[
            jax.ShapeDtypeStruct((height, wide), bf),
            jax.ShapeDtypeStruct((width, wide), bf),
        ],
        in_specs=[
            ANY,
            ANY,
            pl.BlockSpec((rows, width), lambda s: (jnp.minimum(s, 3), 0)),
            pl.BlockSpec((rows, wide), lambda s: (jnp.minimum(s, 3), 0)),
            pl.BlockSpec((height, tile), lambda s: (0, jnp.maximum(s - 4, 0))),
        ],
        out_specs=[
            pl.BlockSpec((rows, wide), lambda s: (jnp.minimum(s, 3), 0)),
            pl.BlockSpec((tile, wide), lambda s: (jnp.maximum(s - 4, 0), 0)),
        ],
        scratch_shapes=[
            pltpu.VMEM((height, wide), bf),
            pltpu.VMEM((wide // 2, width), bf),
            pltpu.SemaphoreType.DMA((2,)),
        ],
        compiler_params=pltpu.CompilerParams(
            dimension_semantics=("arbitrary",), vmem_limit_bytes=VMEM_BYTES
        ),
        cost_estimate=pl.CostEstimate(
            flops=2 * cot.size * wide * 3 // 2, bytes_accessed=2**25, transcendentals=0
        ),
        name="units_back",
    )(early, late, cot, both, mid)


def dot_fine(left, right, dims):
    high = right.astype(jnp.bfloat16)
    low = (right - high.astype(jnp.float32)).astype(jnp.bfloat16)
    product = functools.partial(
        lax.dot_general, dimension_numbers=(dims, ((), ())), preferred_element_type=jnp.float32
    )
    return product(left, high) + product(left, low)


NN, NT, TN = ((1,), (0,)), ((1,), (1,)), ((0,), (0,))


def block_tables(count, rate, rows):
    spot = lax.broadcasted_iota(jnp.int32, (rows, 1), 0)
    live = spot < count
    behind = jnp.where(live, jnp.exp(-rate * spot.astype(jnp.float32)), 0.0)
    ahead = jnp.where(live, jnp.exp(-rate * (count - spot).astype(jnp.float32)), 0.0)
    fade = jnp.exp(jnp.full((1, HEAD_DIM), -rate * count.astype(jnp.float32), jnp.float32))
    return live, behind, ahead, fade


def fill_decay(base, rates):
    heads, rows, _ = base.shape
    gap = lax.broadcasted_iota(jnp.int32, (rows, rows), 0) - lax.broadcasted_iota(jnp.int32, (rows, rows), 1)
    far = jnp.maximum(gap, 0).astype(jnp.float32)
    for t in range(heads):
        base[t] = jnp.where(gap >= 0, jnp.exp(-rates[t] * far), 0.0)


def own_rates(decay, heads):
    _, y, x, core = place()
    return [decay[4 * (heads * core + t) + 2 * y + x] for t in range(heads)]


def unmix_kernel(
    counts, decay, low, weight, pre, attn_gate, qkv, entering, scale, inner, product, early, late, hidden,
    grads_out, out_term, term_out, down_out,
    base, state, total, product_here, down_here, hidden_here, grads, term, down_own, s_in, s_out, *buffers
):
    step = pl.program_id(0)
    steps = pl.num_programs(0)
    b = steps - 1 - step
    rows, width = low.shape
    wide = weight.shape[0]
    rates = own_rates(decay, state.shape[0])
    spot = z, y, x, core = place()
    fetch = [
        pltpu.make_async_copy(src, dst, s_in.at[n])
        for n, (src, dst) in enumerate((
            (product, product_here),
            (early, down_here.at[pl.ds(0, early.shape[0])]),
            (late, down_here.at[pl.ds(early.shape[0], late.shape[0])]),
            (hidden, hidden_here),
        ))
    ]
    leave = [
        pltpu.make_async_copy(src, dst, s_out.at[n])
        for n, (src, dst) in enumerate(((grads, grads_out), (term, term_out), (down_own, down_out)))
    ]

    def right_tile(part, t, cols):
        return matmul(part, down_here[:, cols])

    _, piece, relay, finish, drain = scatter_steps(spot, product_here, right_tile, None, down_own, buffers)

    @pl.when(step == 0)
    def _():
        for copy in fetch:
            copy.start()
        fill_decay(base, rates)
        state[...] = jnp.zeros_like(state)
        total[...] = jnp.zeros_like(total)
        greet([(z, d) for d in plane_peers(y, x, core)])
        for copy in fetch[:3]:
            copy.wait()

    for n in range(PIECES):
        pl.when(step == n // 2)(functools.partial(piece, n))

    count = counts[b, 0]

    def column(ref):
        here = lax.broadcasted_iota(jnp.int32, (8, rows), 0) == b
        turned = jnp.transpose(jnp.where(here, ref, 0.0))
        return jnp.sum(turned, axis=1, keepdims=True)

    here = pl.ds(pl.multiple_of(b * rows, rows), rows)
    factor, inside = column(scale[...]), column(inner[:, 0])
    attn, gate = attn_gate[:, :wide], attn_gate[:, wide:]
    normal = attn * factor
    grad = matmul_nt(low[...], weight[...])
    grads[here, 3 * wide :] = (grad * normal).astype(jnp.bfloat16)
    grad_attn = (factor * grad * gate - normal * factor * inside * (1.0 / width)).astype(jnp.bfloat16)
    total[...] += matmul_tn((normal * gate).astype(jnp.bfloat16), low[...])
    for t in range(state.shape[0]):
        at = slice(t * HEAD_DIM, (t + 1) * HEAD_DIM)
        q, k, v = (qkv[:, i * wide + t * HEAD_DIM : i * wide + (t + 1) * HEAD_DIM] for i in range(3))
        g = grad_attn[:, at]
        live, behind, ahead, fade = block_tables(count, rates[t], rows)
        mask = jnp.where(live, base[t], 0.0)
        probs = (matmul_nt(q, k) * mask).astype(jnp.bfloat16)
        raw = (matmul_nt(g, v) * mask).astype(jnp.bfloat16)
        leaving = jnp.where(count < rows, 0.0, state[t])
        grad_q = matmul(raw, k) + behind * dot_fine(g, entering[0, t], NT)
        grad_k = matmul_tn(raw, q) + ahead * dot_fine(v, leaving, NT)
        grad_v = matmul_tn(probs, g) + ahead * dot_fine(k, leaving, NN)
        state[t] = dot_fine(q, g.astype(jnp.float32) * behind, TN) + fade * leaving
        grads[here, at] = (grad_q * silu_slope(pre[:, at])).astype(jnp.bfloat16)
        after = slice(wide + t * HEAD_DIM, wide + (t + 1) * HEAD_DIM)
        grads[here, after] = (grad_k * silu_slope(pre[:, after])).astype(jnp.bfloat16)
        grads[here, 2 * wide + t * HEAD_DIM : 2 * wide + (t + 1) * HEAD_DIM] = grad_v.astype(jnp.bfloat16)

    @pl.when(step == 4)
    def _():
        relay()

    @pl.when(step == steps - 1)
    def _():
        leave[0].start()
        out_term[...] = total[...].astype(jnp.bfloat16)
        fetch[3].wait()
        side_tiles(hidden_here, grads, term)
        leave[1].start()
        finish()
        leave[2].start()
        drain()
        for copy in leave:
            copy.wait()


def unmix_heads(counts, decay, low, weight, pre, attn_gate, qkv, entering, scale, inner, product, early, late, hidden, number):
    rows, width = low.shape[0] // 8, low.shape[1]
    wide = weight.shape[0]
    heads = wide // HEAD_DIM
    f32, bf = jnp.float32, jnp.bfloat16

    def by_block(columns):
        return pl.BlockSpec((rows, columns), lambda s: (7 - s, 0))

    def whole(*shape):
        return pl.BlockSpec(shape, lambda s: (0,) * len(shape))

    return pl.pallas_call(
        unmix_kernel,
        grid=(8,),
        out_shape=[
            jax.ShapeDtypeStruct((8 * rows, 4 * wide), bf),
            jax.ShapeDtypeStruct((wide, width), bf),
            jax.ShapeDtypeStruct((hidden.shape[1], 4 * wide), bf),
            jax.ShapeDtypeStruct((rows, width), f32),
        ],
        in_specs=[
            SMEM,
            SMEM,
            by_block(width),
            whole(wide, width),
            by_block(2 * wide),
            by_block(2 * wide),
            by_block(3 * wide),
            pl.BlockSpec((1, heads, HEAD_DIM, HEAD_DIM), lambda s: (7 - s, 0, 0, 0)),
            whole(8, rows),
            whole(8, 8, rows),
            ANY,
            ANY,
            ANY,
            ANY,
        ],
        out_specs=[ANY, whole(wide, width), ANY, ANY],
        scratch_shapes=[
            pltpu.VMEM((heads, rows, rows), f32),
            pltpu.VMEM((heads, HEAD_DIM, HEAD_DIM), f32),
            pltpu.VMEM((wide, width), f32),
            pltpu.VMEM(product.shape, bf),
            pltpu.VMEM((product.shape[1], width), bf),
            pltpu.VMEM(hidden.shape, bf),
            pltpu.VMEM((8 * rows, 4 * wide), bf),
            pltpu.VMEM((hidden.shape[1], 4 * wide), bf),
            pltpu.VMEM((rows, width), f32),
            pltpu.SemaphoreType.DMA((4,)),
            pltpu.SemaphoreType.DMA((3,)),
        ]
        + scatter_buffers(rows, width),
        compiler_params=pltpu.CompilerParams(
            collective_id=number,
            has_side_effects=True,
            dimension_semantics=("arbitrary",),
            vmem_limit_bytes=VMEM_BYTES,
        ),
        cost_estimate=pl.CostEstimate(flops=0, bytes_accessed=2**20, transcendentals=0),
        name="unmix_heads",
    )(counts, decay, low, weight, pre, attn_gate, qkv, entering, scale, inner, product, early, late, hidden)


def after(value, *others):
    return lax.optimization_barrier((value, *others))[0]


def fast_plan(
    tokens,
    block_counts,
    decay_rate,
    query_weight,
    key_weight,
    value_weight,
    gate_weight,
    out_weight,
    first_weight,
    second_weight,
    down_weight,
    cotangent,
):
    rows, width = tokens.shape
    nz = lax.axis_size("dp")
    nf = lax.axis_size("fsdp")
    chips = nf // 2
    plane = lax.axis_index("fsdp")
    core = plane % 2
    bf = jnp.bfloat16
    half = HEADS // nf
    own = half * HEAD_DIM
    units = first_weight.shape[1] // nf

    head_spots = tuple(
        (2 * c + k, n, HEAD_DIM * (chips * (half * k + t) + c), 0, n * own + t * HEAD_DIM, HEAD_DIM)
        for c in range(chips) for k in range(2) for n in range(4) for t in range(half)
    )
    run = units // nz
    early = 64
    unit_spots = tuple(
        (f, n, run * (nf * g + f) + skip, 0, n * units + nz * skip + g * wide, wide)
        for f in range(nf) for n in range(2) for g in range(nz) for skip, wide in ((0, early), (early, run - early))
    )
    swap = [(i, i ^ 1) for i in range(nf)]

    def uncross(x):
        keep = lax.dynamic_index_in_dim(x, core, 1, False)
        send = lax.dynamic_index_in_dim(x, 1 - core, 1, False)
        got = lax.ppermute(send, "fsdp", swap)
        return jnp.concatenate([jnp.where(core == 0, keep, got), jnp.where(core == 0, got, keep)], axis=0)

    note = jnp.broadcast_to(block_counts, (8, 128))
    hidden, cot, w_heads, out_rows, wd_early, w_units, counts, pre, attn_gate, qkv, entering, squares = open_attention(
        tokens, cotangent, (query_weight, key_weight, value_weight, gate_weight), (first_weight, second_weight),
        out_weight, down_weight, note, decay_rate, head_spots, unit_spots, 4 * own, 2 * units, early, 0,
    )
    hidden, cot, wd_early = (a.reshape(-1, width) for a in (hidden, cot, wd_early))
    w_heads = w_heads.reshape(-1, 4 * own)
    counts = counts[:, 0]
    middle, mid, scale, w_units, wd_late, both, product, down_term, wo = turn_mid(
        attn_gate, out_rows, squares, tokens, w_units.reshape(-1, 2 * units), down_weight, cot, run - early, 2
    )
    down_term = down_term.reshape(units, width)
    mid, wd_late = mid.reshape(-1, width), wd_late.reshape(-1, width)
    w_units = w_units.reshape(-1, 2 * units)
    inputs = tokens.astype(jnp.float32)
    down_sum = lax.psum_scatter(down_term, "dp", scatter_dimension=0, tiled=True)
    grad_units, units_term = units_back(wd_early, wd_late, cot, both, mid)
    units_sum = lax.psum_scatter(units_term, "dp", scatter_dimension=0, tiled=True)
    grad_middle, low, inner = turn_back(grad_units, w_units, middle, tokens, cotangent, 3)
    grad_heads, out_term, heads_term, down_own = unmix_heads(
        counts, decay_rate, after(low, down_sum), wo, pre, attn_gate, qkv, entering, scale, inner, product, wd_early, wd_late, hidden, 4
    )
    block_out = (middle + down_own).astype(bf)
    heads_sum = lax.psum_scatter(heads_term, "dp", scatter_dimension=0, tiled=True)
    out_term = uncross(out_term.reshape(half, 2, -1, width))
    out_sum = lax.psum_scatter(out_term, "dp", scatter_dimension=0, tiled=False)
    grad_hidden, units_grad = plane_tail(after(grad_heads, out_term), w_heads, units_sum, 5)
    tokens_grad = grad_middle + norm_back(inputs, normed(inputs)[1], grad_hidden)
    down_grad = down_sum.astype(jnp.float32)
    first_grad, second_grad = unpack(units_grad, unit_spots, nf * units, 2)
    heads_sum = after(heads_sum, first_grad, grad_hidden)
    heads_grad = plane_collect(heads_sum, 7)
    grads = unpack(heads_grad, head_spots, width, 4)
    out_grad = after(out_sum, *grads).astype(jnp.float32)
    return (block_out, tokens_grad, *grads, out_grad, first_grad, second_grad, down_grad)


def fits(mesh):
    return mesh.shape["dp"] == 4 and mesh.shape["fsdp"] == 8


def solution(mesh):
    return jax.shard_map(
        fast_plan if fits(mesh) else shards,
        mesh=mesh,
        in_specs=(
            P(("dp", "fsdp"), None),
            P("dp", "fsdp"),
            P(),
            P(("dp", "fsdp"), None),
            P(("dp", "fsdp"), None),
            P(("dp", "fsdp"), None),
            P(("dp", "fsdp"), None),
            P(("dp", "fsdp"), None),
            P(("dp", "fsdp"), None),
            P(("dp", "fsdp"), None),
            P(("dp", "fsdp"), None),
            P(("dp", "fsdp"), None),
        ),
        out_specs=(
            P(("dp", "fsdp"), None),
            P(("dp", "fsdp"), None),
            P(("dp", "fsdp"), None),
            P(("dp", "fsdp"), None),
            P(("dp", "fsdp"), None),
            P(("dp", "fsdp"), None),
            P(("dp", "fsdp"), None),
            P(("dp", "fsdp"), None),
            P(("dp", "fsdp"), None),
            P(("dp", "fsdp"), None),
        ),
        check_vma=False,
    )
```

```python
import functools

import jax
import jax.numpy as jnp
from jax import lax
from jax.experimental import pallas as pl
from jax.experimental.pallas import tpu as pltpu
from jax.sharding import PartitionSpec as P

HEADS = 16
HEAD_DIM = 128


EPS = 1e-06
HIGH = lax.Precision.HIGHEST


def carried_in(part, axis, combine, identity):
    place = lax.axis_index(axis)
    gathered = jax.tree.map(lambda a: lax.all_gather(a, axis), part)
    state = jax.tree.map(lambda a, e: jnp.zeros_like(a) + jnp.asarray(e, a.dtype), part, identity)

    def carried_one(lap, state):
        return combine(
            state, jax.tree.map(lambda a: lax.dynamic_index_in_dim(a, lap, 0, False), gathered)
        )

    return lax.fori_loop(0, place, carried_one, state)


def prefix_2(value, axis, join, neutral):
    count = lax.axis_size(axis)
    place = lax.axis_index(axis)
    ahead = count - 1 - place
    gathered = jax.tree.map(
        lambda a, kind: lax.all_gather(a.astype(kind), axis), value, (jnp.bfloat16, jnp.bfloat16)
    )
    state = jax.tree.map(lambda a, e: jnp.zeros_like(a) + jnp.asarray(e, a.dtype), value, neutral)

    def prefix_one(lap, state):
        source = count - 1 - lap
        return join(
            state,
            jax.tree.map(
                lambda a, own: lax.dynamic_index_in_dim(a, source, 0, False).astype(own.dtype),
                gathered,
                value,
            ),
        )

    return lax.fori_loop(0, ahead, prefix_one, state)


def normed(value):
    scale = lax.rsqrt(jnp.mean(value * value, axis=-1, keepdims=True) + EPS)
    return (value * scale, scale)


def norm_back(value, scale, grad):
    inner = jnp.mean(grad * value, axis=-1, keepdims=True)
    return scale * (grad - value * scale * scale * inner)


def silu_slope(value):
    sig = jax.nn.sigmoid(value)
    return sig * (1.0 + value * (1.0 - sig))


def chain_step(earlier, later):
    e_fade, e_state = earlier
    l_fade, l_state = later
    return (l_fade * e_fade, l_fade[:, None, None] * e_state + l_state)


def matmul(left, right):
    return jnp.dot(left, right, preferred_element_type=jnp.float32)


def matmul_tn(left, right):
    return lax.dot_general(
        left, right, (((0,), (0,)), ((), ())), preferred_element_type=jnp.float32
    )


def matmul_nt(left, right):
    return lax.dot_general(
        left, right, (((1,), (1,)), ((), ())), preferred_element_type=jnp.float32
    )


def decay_tables(count, rates, rows):
    pos = lax.iota(jnp.int32, rows)
    live = pos < count
    keep = (pos[:, None] >= pos[None, :]) & live[:, None] & live[None, :]
    spacing = jnp.where(keep, (pos[:, None] - pos[None, :]).astype(jnp.float32), 0.0)
    mask = jnp.where(keep[None], jnp.exp(-rates[:, None, None] * spacing[None]), 0.0)
    ahead = jnp.where(
        live[:, None], jnp.exp(-rates[None, :] * (count - pos)[:, None].astype(jnp.float32)), 0.0
    )
    behind = jnp.where(
        live[:, None], jnp.exp(-rates[None, :] * pos[:, None].astype(jnp.float32)), 0.0
    )
    fade = jnp.exp(-rates * count.astype(jnp.float32))
    return (mask, ahead, behind, fade)


def shards(
    tokens,
    block_counts,
    decay_rate,
    query_weight,
    key_weight,
    value_weight,
    gate_weight,
    out_weight,
    first_weight,
    second_weight,
    down_weight,
    cotangent,
):
    rows = tokens.shape[0]
    gathered = (
        lax.all_gather(query_weight, ("dp", "fsdp"), axis=0, tiled=True),
        lax.all_gather(key_weight, ("dp", "fsdp"), axis=0, tiled=True),
        lax.all_gather(value_weight, ("dp", "fsdp"), axis=0, tiled=True),
        lax.all_gather(gate_weight, ("dp", "fsdp"), axis=0, tiled=True),
        lax.all_gather(out_weight, ("dp", "fsdp"), axis=0, tiled=True),
        lax.all_gather(first_weight, ("dp", "fsdp"), axis=0, tiled=True),
        lax.all_gather(second_weight, ("dp", "fsdp"), axis=0, tiled=True),
        lax.all_gather(down_weight, ("dp", "fsdp"), axis=0, tiled=True),
    )
    w_query, w_key, w_value, w_gate, w_out, w_first, w_second, w_down = gathered
    count = block_counts[0, 0]
    closes = count < rows
    mask, ahead, behind, fade = decay_tables(count, decay_rate, rows)
    passing = jnp.where(closes, 0.0, fade)
    inputs = tokens.astype(jnp.float32)
    in_normed, in_scale = normed(inputs)
    hidden = in_normed.astype(jnp.bfloat16)
    q_pre = matmul(hidden, w_query)
    k_pre = matmul(hidden, w_key)
    value = matmul(hidden, w_value).astype(jnp.bfloat16)
    gate = matmul(hidden, w_gate)
    query = jax.nn.silu(q_pre).astype(jnp.bfloat16)
    keys = jax.nn.silu(k_pre).astype(jnp.bfloat16)
    query_heads = query.reshape(rows, HEADS, HEAD_DIM)
    key_heads = keys.reshape(rows, HEADS, HEAD_DIM)
    value_heads = value.reshape(rows, HEADS, HEAD_DIM)
    query_wide = query_heads.astype(jnp.float32)
    key_wide = key_heads.astype(jnp.float32)
    value_ahead = value_heads.astype(jnp.float32) * ahead[:, :, None]
    raw = jnp.einsum("ihe,jhe->hij", query_heads, key_heads, preferred_element_type=jnp.float32)
    probs = (raw * mask).astype(jnp.bfloat16)
    intra = jnp.einsum("hij,jhe->ihe", probs, value_heads, preferred_element_type=jnp.float32)
    local = jnp.einsum("jhe,jhf->hef", key_wide, value_ahead, precision=HIGH)
    local_sent = jnp.where(closes, 0.0, local)
    prefix = carried_in(
        (passing, local_sent), "fsdp", chain_step, (jnp.ones_like(fade), jnp.zeros_like(local))
    )
    entering = prefix[1]
    inter = behind[:, :, None] * jnp.einsum("ihe,hef->ihf", query_wide, entering, precision=HIGH)
    attn = (intra + inter).reshape(rows, HEADS * HEAD_DIM)
    attn_normed, attn_scale = normed(attn)
    mixed = (attn_normed * gate).astype(jnp.bfloat16)
    middle = inputs + matmul(mixed, w_out)
    mid_normed, mid_scale = normed(middle)
    mid = mid_normed.astype(jnp.bfloat16)
    first = matmul(mid, w_first)
    second = matmul(mid, w_second)
    product = (first * second).astype(jnp.bfloat16)
    block_out = (middle + matmul(product, w_down)).astype(jnp.bfloat16)
    w_first, w_second, w_down = (
        lax.all_gather(first_weight, ("dp", "fsdp"), axis=0, tiled=True),
        lax.all_gather(second_weight, ("dp", "fsdp"), axis=0, tiled=True),
        lax.all_gather(down_weight, ("dp", "fsdp"), axis=0, tiled=True),
    )
    grad_product = matmul_nt(cotangent, w_down)
    grad_first = (grad_product * second).astype(jnp.bfloat16)
    grad_second = (grad_product * first).astype(jnp.bfloat16)
    grad_mid = matmul_nt(grad_first, w_first) + matmul_nt(grad_second, w_second)
    grad_middle = cotangent.astype(jnp.float32) + norm_back(middle, mid_scale, grad_mid)

    def scattered(left, right, after):
        left, _ = lax.optimization_barrier((left, after))
        term = matmul_tn(left, right)
        return lax.psum_scatter(term, ("dp", "fsdp"), scatter_dimension=0, tiled=True)

    down_grad = scattered(product, cotangent, grad_middle)
    first_grad = scattered(mid, grad_first, down_grad)
    second_grad = scattered(mid, grad_second, first_grad)
    grad_middle, _ = lax.optimization_barrier((grad_middle, second_grad))
    w_query, w_key, w_value, w_gate, w_out = (
        lax.all_gather(query_weight, ("dp", "fsdp"), axis=0, tiled=True),
        lax.all_gather(key_weight, ("dp", "fsdp"), axis=0, tiled=True),
        lax.all_gather(value_weight, ("dp", "fsdp"), axis=0, tiled=True),
        lax.all_gather(gate_weight, ("dp", "fsdp"), axis=0, tiled=True),
        lax.all_gather(out_weight, ("dp", "fsdp"), axis=0, tiled=True),
    )
    grad_mid_low = grad_middle.astype(jnp.bfloat16)
    out_term = matmul_tn(mixed, grad_mid_low)
    grad_mixed = matmul_nt(grad_mid_low, w_out)
    grad_gate = (grad_mixed * attn_normed).astype(jnp.bfloat16)
    grad_attn = norm_back(attn, attn_scale, grad_mixed * gate).astype(jnp.bfloat16)
    grad_heads = grad_attn.reshape(rows, HEADS, HEAD_DIM)
    grad_heads_wide = grad_heads.astype(jnp.float32) * behind[:, :, None]
    grad_probs = jnp.einsum(
        "ihe,jhe->hij", grad_heads, value_heads, preferred_element_type=jnp.float32
    )
    grad_raw = (grad_probs * mask).astype(jnp.bfloat16)
    grad_entering = jnp.einsum("ihe,ihf->hef", query_wide, grad_heads_wide, precision=HIGH)
    suffix = prefix_2(
        (passing, grad_entering),
        "fsdp",
        chain_step,
        (jnp.ones_like(fade), jnp.zeros_like(grad_entering)),
    )
    grad_leaving = jnp.where(closes, 0.0, suffix[1])
    grad_query = jnp.einsum("hij,jhe->ihe", grad_raw, key_heads, preferred_element_type=jnp.float32)
    grad_query = grad_query + jnp.einsum("ihf,hef->ihe", grad_heads_wide, entering, precision=HIGH)
    grad_keys = jnp.einsum(
        "hij,ihe->jhe", grad_raw, query_heads, preferred_element_type=jnp.float32
    )
    grad_keys = grad_keys + jnp.einsum("hef,jhf->jhe", grad_leaving, value_ahead, precision=HIGH)
    grad_value = jnp.einsum("hij,ihe->jhe", probs, grad_heads, preferred_element_type=jnp.float32)
    grad_value = grad_value + ahead[:, :, None] * jnp.einsum(
        "hef,jhe->jhf", grad_leaving, key_wide, precision=HIGH
    )
    width = HEADS * HEAD_DIM
    grad_q_pre = (grad_query.reshape(rows, width) * silu_slope(q_pre)).astype(jnp.bfloat16)
    grad_k_pre = (grad_keys.reshape(rows, width) * silu_slope(k_pre)).astype(jnp.bfloat16)
    grad_v = grad_value.reshape(rows, width).astype(jnp.bfloat16)
    query_term = matmul_tn(hidden, grad_q_pre)
    key_term = matmul_tn(hidden, grad_k_pre)
    value_term = matmul_tn(hidden, grad_v)
    gate_term = matmul_tn(hidden, grad_gate)
    grad_hidden = matmul_nt(grad_q_pre, w_query) + matmul_nt(grad_k_pre, w_key)
    grad_hidden = grad_hidden + matmul_nt(grad_v, w_value) + matmul_nt(grad_gate, w_gate)
    tokens_grad = grad_middle + norm_back(inputs, in_scale, grad_hidden)
    query_grad, key_grad, value_grad, gate_grad, out_grad = (
        lax.psum_scatter(query_term, ("dp", "fsdp"), scatter_dimension=0, tiled=True),
        lax.psum_scatter(key_term, ("dp", "fsdp"), scatter_dimension=0, tiled=True),
        lax.psum_scatter(value_term, ("dp", "fsdp"), scatter_dimension=0, tiled=True),
        lax.psum_scatter(gate_term, ("dp", "fsdp"), scatter_dimension=0, tiled=True),
        lax.psum_scatter(out_term, ("dp", "fsdp"), scatter_dimension=0, tiled=True),
    )
    return (
        block_out,
        tokens_grad,
        query_grad,
        key_grad,
        value_grad,
        gate_grad,
        out_grad,
        first_grad,
        second_grad,
        down_grad,
    )


MESH = pl.DeviceIdType.MESH
VMEM_BYTES = 60 * 2**20
ANY = pl.BlockSpec(memory_space=pl.ANY)
VMEM = pl.BlockSpec(memory_space=pltpu.VMEM)
SMEM = pl.BlockSpec(memory_space=pltpu.SMEM)


def place():
    plane = lax.axis_index("fsdp")
    return lax.axis_index("dp"), plane // 4, (plane // 2) % 2, plane % 2


def other(i, way):
    return i + way - 2 * i * way


def member(y, x, core):
    return (y * 2 + x) * 2 + core


def plane_peers(y, x, core):
    ways = [(dy, dx, dc) for dy in (1, 0) for dx in (1, 0) for dc in (0, 1) if dy + dx + dc]
    return [member(other(y, dy), other(x, dx), other(core, dc)) for dy, dx, dc in ways]


def greet(devices):
    barrier = pltpu.get_barrier_semaphore()
    for device in devices:
        pl.semaphore_signal(barrier, inc=1, device_id=device, device_id_type=MESH)
    pl.semaphore_wait(barrier, len(devices))


def remote(src, dst, send, recv, device):
    return pltpu.make_async_remote_copy(
        src_ref=src, dst_ref=dst, send_sem=send, recv_sem=recv, device_id=device, device_id_type=MESH
    )


def note_copies(z, me, peers, note, notes, send, recv):
    return [
        remote(note, notes.at[me], send.at[n], recv.at[n], (z, d)) for n, d in enumerate(peers)
    ]


def pack_columns(spots, weights, stages):
    for f, n, src, m, dst, wide in spots:
        stages[m][f, :, dst : dst + wide] = weights[n][:, src : src + wide]


def unpack_columns(spots, stages, grads):
    for f, n, src, m, dst, wide in spots:
        grads[n][:, src : src + wide] = stages[m][f, :, dst : dst + wide].astype(jnp.float32)


def gather_steps(spot, x_ref, o_ref, local, send, recv, first_row=0, rows=None):
    z, y, x, core = spot
    me, mate = member(y, x, core), member(y, x, 1 - core)
    on_x, on_y, across = member(y, 1 - x, core), member(1 - y, x, core), member(1 - y, 1 - x, core)
    rows = rows or x_ref.shape[0]
    half = rows // 2
    both = pl.ds(first_row, rows)
    low, high = pl.ds(first_row, half), pl.ds(first_row + half, half)

    def own(part, n, device):
        return remote(x_ref.at[part], o_ref.at[me, part], send.at[n], recv.at[n], (z, device))

    def pass_on(block, part, n, device):
        ref = o_ref.at[block, part]
        return remote(ref, ref, send.at[n], recv.at[n], (z, device))

    keep = pltpu.make_async_copy(x_ref.at[both], o_ref.at[me, both], local)
    first = [own(low, 0, on_y), own(high, 1, on_x), own(high, 2, on_y), own(low, 3, on_x)]
    mine = own(both, 4, mate)
    relay_x = pass_on(on_y, low, 5, on_x)
    relay_y = pass_on(on_x, high, 6, on_y)
    y_mate = pass_on(on_y, both, 7, mate)
    x_mate = pass_on(on_x, both, 8, mate)
    low_mate = pass_on(across, low, 9, mate)
    high_mate = pass_on(across, high, 10, mate)

    def begin():
        for copy in (*first, mine, keep):
            copy.start()

    def relay():
        first[0].wait_recv()
        relay_x.start()
        first[1].wait_recv()
        relay_y.start()
        first[2].wait_recv()
        y_mate.start()
        first[3].wait_recv()
        x_mate.start()

    def finish():
        relay_x.wait_recv()
        low_mate.start()
        relay_y.wait_recv()
        high_mate.start()
        keep.wait()
        for copy in (mine, y_mate, x_mate, low_mate, high_mate):
            copy.wait_recv()
        for copy in (*first, mine, relay_x, relay_y, y_mate, x_mate, low_mate, high_mate):
            copy.wait_send()

    return begin, relay, finish


GATHER_SEMAPHORES = [pltpu.SemaphoreType.DMA, pltpu.SemaphoreType.DMA((11,)), pltpu.SemaphoreType.DMA((11,))]


def column_of_chips(spot):
    z, y, x, _ = spot
    planes = lax.axis_size("dp")
    return [(lax.rem(z + n, planes), member(y, x, c)) for n in range(1, planes) for c in (0, 1)]


def plane_line_steps(spot, ref, send, recv, source=None):
    z, y, x, core = spot
    me = member(y, x, core)
    middle = lax.rem((z + 1) // 2, 2)
    own_end = 3 * (z // 2)
    near = z // 2 + 1

    def move(part, n, plane, source=None):
        here = ref.at[part]
        return remote(here if source is None else source, here, send.at[n], recv.at[part], (plane, me))

    first = move(z, 0, middle * (3 - own_end) + (1 - middle) * (3 - near), source)
    second = move(z, 1, middle * own_end + (1 - middle) * near, source)
    relay = move(3 - own_end, 2, own_end)
    across = move(z, 3, 3 - z, source)

    def begin():
        first.start()
        second.start()

    def service():
        @pl.when(middle == 1)
        def _():
            relay.wait_recv()
            relay.start()
            across.start()

    def finish():
        for part in range(4):
            taken = (middle == 1) & (part == 3 - own_end)

            @pl.when((part != z) & jnp.logical_not(taken))
            def _(part=part):
                remote(ref.at[part], ref.at[part], send.at[0], recv.at[part], (3 - z, me)).wait_recv()

        first.wait_send()
        second.wait_send()

        @pl.when(middle == 1)
        def _():
            relay.wait_send()
            across.wait_send()

    return begin, service, finish


def by_planes(left, slot, right):
    rows = right.shape[1]
    return sum(matmul(left[slot, :, g * rows : (g + 1) * rows], right[g]) for g in range(right.shape[0]))


def open_kernel(head_spots, unit_spots, *refs):
    refs = list(refs)
    tokens, cot, *heads = [refs.pop(0) for _ in range(6)]
    units, (rows, down, note, decay) = [refs.pop(0) for _ in range(2)], [refs.pop(0) for _ in range(4)]
    hidden, cots, weight, held, early, units_out, notes, pre, attn_gate, qkv, entering, squares = [
        refs.pop(0) for _ in range(12)
    ]
    stage, here, swap, own, block, pre_here, mix_here, qkv_here, entering_here, base, state = [
        refs.pop(0) for _ in range(11)
    ]
    s_swap, r_swap, s_note, r_note, s_units, r_units, s_line, r_line, s_early, r_early, s_rows, r_rows = [
        refs.pop(0) for _ in range(12)
    ]
    s_next, r_next = [refs.pop(0) for _ in range(2)]
    s_block, s_out, local = [refs.pop(0) for _ in range(3)]
    sems_hidden, sems_cot = refs[:3], refs[3:]
    spot = z, y, x, core = place()
    me = member(y, x, core)
    peers = plane_peers(y, x, core)
    size = tokens.shape[0]
    deep = stage.shape[1]
    wide = here.shape[2] // 4
    count_heads = state.shape[0]

    first = pltpu.make_async_copy(down.at[pl.ds(0, early.shape[1])], early.at[z], local.at[2])
    first.start()
    pack_columns(head_spots, heads, [stage])
    greet([(z, d) for d in peers] + [(lax.rem(z + n, 4), me) for n in range(1, 4)])
    mine = pl.ds(pl.multiple_of(me * deep, deep), deep)
    columns = [pl.ds(h * 2 * wide, 2 * wide) for h in range(2)]
    swaps = []
    for h, cols in enumerate(columns):
        copies = [
            remote(stage.at[d, :, cols], here.at[z, mine, cols], s_swap.at[h, n], r_swap.at[h, n], (z, d))
            for n, d in enumerate(peers)
        ]
        copies.append(pltpu.make_async_copy(stage.at[me, :, cols], here.at[z, mine, cols], local.at[5 * h]))
        swaps.append(copies)
    passing = note_copies(z, me, peers, note, notes, s_note, r_note)
    begin_rows, service_rows, finish_rows = plane_line_steps(spot, held, s_rows, r_rows)
    keep_rows = pltpu.make_async_copy(rows, held.at[z], local.at[1])
    keep_rows.start()
    half = early.shape[1] // 2
    begin_early, service_early, finish_early = plane_line_steps(
        spot, early.at[:, pl.ds(0, half)], s_early, r_early
    )
    begin_next, service_next, finish_next = plane_line_steps(
        spot, early.at[:, pl.ds(half, half)], s_next, r_next
    )
    for copy in swaps[0] + swaps[1] + passing:
        copy.start()
    first.wait()
    begin_early()
    notes[me] = note[...]
    lines = [
        plane_line_steps(spot, here.at[:, :, cols], s_line.at[h], r_line.at[h]) for h, cols in enumerate(columns)
    ]
    own[...] = normed(tokens[...].astype(jnp.float32))[0].astype(own.dtype)
    for copy in swaps[0]:
        copy.wait()
    lines[0][0]()
    service_early()
    pack_columns(unit_spots, units, [swap])
    rates = own_rates(decay, count_heads)
    fill_decay(base, rates)
    state[...] = jnp.zeros_like(state)
    for copy in swaps[1]:
        copy.wait()
    lines[1][0]()
    begin_hidden, relay_hidden, finish_hidden = gather_steps(spot, own, hidden, *sems_hidden)
    begin_cot, relay_cot, finish_cot = gather_steps(spot, cot, cots, *sems_cot)
    moves = [
        remote(swap.at[d], units_out.at[me], s_units.at[n], r_units.at[n], (z, d)) for n, d in enumerate(peers)
    ]
    moves.append(pltpu.make_async_copy(swap.at[me], units_out.at[me], local.at[3]))
    begin_hidden()
    relay_hidden()
    for copy in moves:
        copy.start()
    begin_cot()
    finish_early()
    for _, service, _ in lines:
        service()
    finish_hidden()
    for copy in passing:
        copy.wait()

    def fetch(b):
        return pltpu.make_async_copy(hidden.at[b], block.at[b % 2], s_block.at[b % 2])

    fetch(0).start()
    for _, _, finish_line in lines:
        finish_line()
    keep_weight = pltpu.make_async_copy(here, weight, local.at[4])
    keep_weight.start()
    keep_rows.wait()
    begin_rows()
    begin_next()

    def block_rows(b):
        return pl.ds(pl.multiple_of(b * size, size), size)

    def outs(b):
        return [
            pltpu.make_async_copy(src.at[at], dst.at[at], s_out.at[n, b])
            for n, (src, dst, at) in enumerate((
                (pre_here, pre, block_rows(b)),
                (mix_here, attn_gate, block_rows(b)),
                (qkv_here, qkv, block_rows(b)),
                (entering_here, entering, b),
            ))
        ]

    def mix(b):
        fetch(b).wait()

        @pl.when(b < 7)
        def _():
            fetch(b + 1).start()

        at_rows = block_rows(b)
        count = notes[b, :1, :1]
        out = by_planes(block, b % 2, here)
        pre_here[at_rows, :] = out[:, : 2 * wide]
        query = jax.nn.silu(out[:, :wide]).astype(jnp.bfloat16)
        keys = jax.nn.silu(out[:, wide : 2 * wide]).astype(jnp.bfloat16)
        value = out[:, 2 * wide : 3 * wide].astype(jnp.bfloat16)
        qkv_here[at_rows, :wide] = query
        qkv_here[at_rows, wide : 2 * wide] = keys
        qkv_here[at_rows, 2 * wide :] = value
        mix_here[at_rows, wide:] = out[:, 3 * wide :]
        entering_here[b] = state[...]
        total = jnp.zeros((8, size), jnp.float32)
        for t in range(count_heads):
            at = slice(t * HEAD_DIM, (t + 1) * HEAD_DIM)
            q, k, v = query[:, at], keys[:, at], value[:, at]
            live, behind, ahead, fade = block_tables(count, rates[t], size)
            probs = (matmul_nt(q, k) * jnp.where(live, base[t], 0.0)).astype(jnp.bfloat16)
            attn = matmul(probs, v) + behind * dot_fine(q, state[t], NN)
            mix_here[at_rows, at] = attn
            total += lax.dot_general(
                jnp.ones((8, HEAD_DIM), jnp.float32), attn * attn, (NT, ((), ())), precision=HIGH,
                preferred_element_type=jnp.float32,
            )
            local_state = dot_fine(k, v.astype(jnp.float32) * ahead, TN)
            stays = jnp.where(count < size, 0.0, 1.0)
            state[t] = stays * (fade * state[t] + local_state)
        squares[pl.ds(b, 1), :] = total[:1]
        for copy in outs(b):
            copy.start()

    pl.loop(0, 5)(mix)
    relay_cot()
    service_rows()
    service_next()
    pl.loop(5, 8)(mix)
    finish_rows()
    finish_next()
    for copy in moves:
        copy.wait()

    @pl.loop(0, 8)
    def _(b):
        for copy in outs(b):
            copy.wait()

    keep_weight.wait()
    finish_cot()


def open_attention(
    tokens, cot, heads, units, rows, down, note, decay, head_spots, unit_spots, columns, unit_columns, early, number
):
    size, width = tokens.shape
    deep = rows.shape[0]
    wide = columns // 4
    count = wide // HEAD_DIM
    f32, bf, dma = jnp.float32, tokens.dtype, pltpu.SemaphoreType.DMA
    outs = (
        ((8, size, width), bf),
        ((8, size, width), bf),
        ((4, 8 * deep, columns), bf),
        ((4, deep, width), bf),
        ((4, early, width), bf),
        ((8, deep, unit_columns), bf),
        ((8, *note.shape), note.dtype),
        ((8 * size, 2 * wide), f32),
        ((8 * size, 2 * wide), f32),
        ((8 * size, 3 * wide), bf),
        ((8, count, HEAD_DIM, HEAD_DIM), f32),
        ((8, size), f32),
    )
    return pl.pallas_call(
        functools.partial(open_kernel, head_spots, unit_spots),
        out_shape=[jax.ShapeDtypeStruct(*out) for out in outs],
        in_specs=[VMEM, ANY] + [VMEM] * 6 + [ANY, ANY, VMEM, SMEM],
        out_specs=[ANY] * 6 + [VMEM] + [ANY] * 4 + [VMEM],
        scratch_shapes=[
            pltpu.VMEM((8, deep, columns), bf),
            pltpu.VMEM((4, 8 * deep, columns), bf),
            pltpu.VMEM((8, deep, unit_columns), bf),
            pltpu.VMEM((size, width), bf),
            pltpu.VMEM((2, size, width), bf),
            pltpu.VMEM((8 * size, 2 * wide), f32),
            pltpu.VMEM((8 * size, 2 * wide), f32),
            pltpu.VMEM((8 * size, 3 * wide), bf),
            pltpu.VMEM((8, count, HEAD_DIM, HEAD_DIM), f32),
            pltpu.VMEM((count, size, size), f32),
            pltpu.VMEM((count, HEAD_DIM, HEAD_DIM), f32),
        ]
        + [dma((2, 7)) for _ in range(2)]
        + [dma((7,)) for _ in range(4)]
        + [dma((2, 4)) for _ in range(2)]
        + [dma((4,)) for _ in range(6)]
        + [dma((2,)), dma((4, 8)), dma((6,))]
        + GATHER_SEMAPHORES * 2,
        compiler_params=pltpu.CompilerParams(
            collective_id=number, has_side_effects=True, vmem_limit_bytes=VMEM_BYTES
        ),
        cost_estimate=pl.CostEstimate(flops=0, bytes_accessed=2**20, transcendentals=0),
        name=f"open_attention_{number}",
    )(tokens, cot, *heads, *units, rows, down, note, decay)


def collect_copies(z, me, peers, total, stage, local, send, recv):
    rows = stage.shape[1]

    def part(d):
        return total.at[pl.ds(pl.multiple_of(d * rows, rows), rows)]

    return [pltpu.make_async_copy(part(me), stage.at[me], local)] + [
        remote(part(d), stage.at[me], send.at[n], recv.at[n], (z, d)) for n, d in enumerate(peers)
    ]


COLLECT_SEMAPHORES = [pltpu.SemaphoreType.DMA] + [pltpu.SemaphoreType.DMA((7,)) for _ in range(2)]


def collect_kernel(total, stage, *sems):
    z, y, x, core = place()
    peers = plane_peers(y, x, core)
    greet([(z, d) for d in peers])
    copies = collect_copies(z, member(y, x, core), peers, total, stage, *sems)
    for copy in copies:
        copy.start()
    for copy in copies:
        copy.wait()


def plane_collect(total, number):
    rows = total.shape[0] // 8
    return pl.pallas_call(
        collect_kernel,
        out_shape=jax.ShapeDtypeStruct((8, rows, total.shape[1]), total.dtype),
        in_specs=[ANY],
        out_specs=ANY,
        scratch_shapes=COLLECT_SEMAPHORES,
        compiler_params=pltpu.CompilerParams(collective_id=number, has_side_effects=True),
        cost_estimate=pl.CostEstimate(flops=0, bytes_accessed=2**20, transcendentals=0),
        name=f"plane_collect_{number}",
    )(total)


def unpack_kernel(spots, stage, *grads):
    unpack_columns(spots, [stage], grads)


def unpack(stage, spots, columns, outputs):
    return pl.pallas_call(
        functools.partial(unpack_kernel, spots),
        out_shape=[jax.ShapeDtypeStruct((stage.shape[1], columns), jnp.float32) for _ in range(outputs)],
        in_specs=[VMEM],
        out_specs=[VMEM] * outputs,
        compiler_params=pltpu.CompilerParams(vmem_limit_bytes=VMEM_BYTES),
        name=f"unpack_{outputs}",
    )(stage)


PIECES = 5


def scatter_steps(spot, left, right_tile, left_rows, o_ref, buffers):
    to_mate, from_mate, stage, from_x, from_y, s_mate, r_mate, s_x, r_x, s_y, r_y = buffers
    z, y, x, core = spot
    rows, width = o_ref.shape
    tile = width // 4
    mate = member(y, x, 1 - core)
    on_x, on_y = member(y, 1 - x, core), member(1 - y, x, core)
    left_cols, right_cols = pl.ds(0, width // 2), pl.ds(width // 2, width // 2)

    def target(i, c):
        return member(other(y, 1 - i % 2), other(x, 1 - i // 2), c)

    def each_tile(block, use):
        part = left_rows(left, block) if left_rows else None
        here = pl.ds(pl.multiple_of(block * rows, rows), rows)

        @pl.loop(0, width // tile)
        def _(t):
            cols = pl.ds(pl.multiple_of(t * tile, tile), tile)
            use(t, cols, right_tile(part if left_rows else left[here, :], t, cols))

    def mate_copy(i):
        return remote(to_mate.at[i], from_mate.at[i], s_mate.at[i], r_mate.at[i], (z, mate))

    def send_x(i, n):
        cols = right_cols if n == 2 else left_cols
        return remote(stage.at[i, :, cols], from_x.at[n], s_x.at[n], r_x.at[n], (z, on_x))

    def send_y(i, n):
        cols = left_cols if n == 2 else right_cols
        return remote(stage.at[i, :, cols], from_y.at[n], s_y.at[n], r_y.at[n], (z, on_y))

    def give(i):
        def use(t, cols, total):
            to_mate[i, :, cols] = total.astype(jnp.bfloat16)

        each_tile(target(i, 1 - core), use)
        mate_copy(i).start()

    def add(i):
        def use(t, cols, total):
            pl.when(t == 0)(mate_copy(i).wait_recv)
            total = total + from_mate[i, :, cols].astype(jnp.float32)
            if i < 3:
                stage[i, :, cols] = total.astype(jnp.bfloat16)
            else:
                o_ref[:, cols] = total
            if i == 0:
                pl.when(t == width // tile // 2 - 1)(send_x(0, 0).start)

        each_tile(target(i, core), use)
        if i == 0:
            send_y(0, 0).start()
        if i == 1:
            send_x(1, 1).start()
        if i == 2:
            send_y(2, 1).start()

    def piece(n):
        if n < 4:
            give(n)
        if n > 0:
            add(n - 1)

    def begin():
        for n in range(PIECES):
            piece(n)

    def relay():
        send_y(0, 0).wait_recv()
        stage[1, :, right_cols] = (
            stage[1, :, right_cols].astype(jnp.float32) + from_y[0].astype(jnp.float32)
        ).astype(jnp.bfloat16)
        send_x(1, 2).start()
        send_x(0, 0).wait_recv()
        stage[2, :, left_cols] = (
            stage[2, :, left_cols].astype(jnp.float32) + from_x[0].astype(jnp.float32)
        ).astype(jnp.bfloat16)
        send_y(2, 2).start()

    def finish():
        send_x(1, 1).wait_recv()
        o_ref[:, left_cols] += from_x[1].astype(jnp.float32)
        send_y(2, 1).wait_recv()
        o_ref[:, right_cols] += from_y[1].astype(jnp.float32)
        send_x(1, 2).wait_recv()
        o_ref[:, right_cols] += from_x[2].astype(jnp.float32)
        send_y(2, 2).wait_recv()
        o_ref[:, left_cols] += from_y[2].astype(jnp.float32)

    def drain():
        for i in range(4):
            mate_copy(i).wait_send()
        for copy in (send_x(0, 0), send_x(1, 1), send_x(1, 2), send_y(0, 0), send_y(2, 1), send_y(2, 2)):
            copy.wait_send()

    return begin, piece, relay, finish, drain


def scatter_buffers(rows, width):
    shapes = [pltpu.VMEM((n, rows, width), jnp.bfloat16) for n in (4, 4, 3)]
    shapes += [pltpu.VMEM((3, rows, width // 2), jnp.bfloat16) for _ in range(2)]
    return shapes + [pltpu.SemaphoreType.DMA((n,)) for n in (4, 4, 3, 3, 3, 3)]


BUFFERS = 11


def own_row_copies(spot, packed, held, local, send, recv):
    z, y, x, core = spot
    planes, deep, wide = packed.shape
    rows = held.shape[0] // planes
    parts = held.shape[1] // wide
    mate = (z, member(y, x, 1 - core))
    copies = []
    for t in range(planes // 2):
        for n in range(parts):
            i = t * parts + n
            source = pl.ds(deep - (parts - n) * rows, rows)
            here = held.at[
                pl.ds(pl.multiple_of((2 * t + core) * rows, rows), rows), pl.ds(n * wide, wide)
            ]
            keep = packed.at[planes // 2 * core + t, source]
            give = packed.at[planes // 2 * (1 - core) + t, source]
            copies.append(pltpu.make_async_copy(keep, here, local.at[i]))
            copies.append(remote(give, here, send.at[i], recv.at[i], mate))
    return copies


def own_row_copies(spot, held, right, local, send, recv):
    z, y, x, core = spot
    planes, rows, _ = held.shape
    half = planes // 2
    mate = (z, member(y, x, 1 - core))
    copies = []
    for t in range(half):
        here = right.at[pl.ds(pl.multiple_of((2 * t + core) * rows, rows), rows)]
        copies.append(pltpu.make_async_copy(held.at[half * core + t], here, local.at[t]))
        copies.append(remote(held.at[half * (1 - core) + t], here, send.at[t], recv.at[t], mate))
    return copies


def turn_mid_kernel(
    left_in, held, squares, tokens, units, down, cot, middle, mid_out, scale_ref, weight, late, both, product, term, right,
    all_squares, columns, s_note, r_note, mid, total, here, block, both_here, product_here, cot_here, term_here,
    s_line, r_line, s_late, r_late, s_block, s_out, s_cot, s_term, local, right_here, s_row, r_row, left, *rest
):
    buffers, sems = rest[:BUFFERS], rest[BUFFERS:]
    spot = z, y, x, core = place()
    rows, width = middle.shape
    me = member(y, x, core)
    peers = plane_peers(y, x, core)
    wide = here.shape[2]
    tile = cot_here.shape[2]
    shard = pltpu.make_async_copy(units, here.at[z], local.at[0])
    shard.start()
    fetch_left = pltpu.make_async_copy(left_in, left, local.at[5])
    skip = down.shape[0] - late.shape[1]
    last = pltpu.make_async_copy(down.at[pl.ds(skip, late.shape[1])], late.at[z], local.at[1])
    greet([(z, d) for d in peers] + [(lax.rem(z + n, 4), me) for n in range(1, 4)])
    begin_line, service_line, finish_line = plane_line_steps(spot, here, s_line, r_line, units)
    begin_line()
    fetch_left.start()
    last.start()
    begin_late, service_late, finish_late = plane_line_steps(spot, late, s_late, r_late)
    notes = note_copies(z, me, peers, squares, all_squares, s_note, r_note)
    moves = own_row_copies(spot, held, right_here, local.at[pl.ds(3, 2)], s_row, r_row)
    for copy in notes + moves:
        copy.start()
    all_squares[me] = squares[...]
    shard.wait()
    for copy in notes:
        copy.wait_recv()
    scale = lax.rsqrt(jnp.sum(all_squares[...], axis=0) / width + EPS)
    scale_ref[...] = scale
    columns[...] = jnp.transpose(scale)

    def left_rows(left, block):
        here = pl.ds(pl.multiple_of(block * rows, rows), rows)
        deep = left.shape[1] // 2
        one = lax.broadcasted_iota(jnp.int32, columns.shape, 1) == block
        column = jnp.sum(jnp.where(one, columns[...], 0.0), axis=1, keepdims=True)
        return (left[here, :deep] * column * left[here, deep:]).astype(jnp.bfloat16)

    for copy in moves:
        copy.wait()
    right[...] = right_here[...]
    fetch_left.wait()

    def right_tile(part, t, cols):
        return matmul(part, right_here[:, cols])

    begin, _, relay, finish, drain = scatter_steps(spot, left, right_tile, left_rows, total, buffers)
    begin()
    relay()
    finish()
    value = tokens[...].astype(jnp.float32) + total[...]
    middle[...] = value
    mid[...] = normed(value)[0].astype(jnp.bfloat16)
    begin, relay, finish = gather_steps(spot, mid, mid_out, *sems)
    begin()
    drain()
    for copy in notes:
        copy.wait_send()
    last.wait()
    service_line()
    relay()
    finish()

    def fetch(b):
        return pltpu.make_async_copy(mid_out.at[b], block.at[b % 2], s_block.at[b % 2])

    def outs(b):
        at = pl.ds(pl.multiple_of(b * rows, rows), rows)
        return [
            pltpu.make_async_copy(both_here.at[b % 2], both.at[at], s_out.at[0, b % 2]),
            pltpu.make_async_copy(product_here.at[at], product.at[at], s_out.at[1, b % 2]),
        ]

    def fetch_cot(t):
        cols = pl.ds(pl.multiple_of(t * tile, tile), tile)
        return pltpu.make_async_copy(cot.at[:, cols], cot_here.at[t % 2], s_cot.at[t % 2])

    def leave_term(t):
        cols = pl.ds(pl.multiple_of(t * tile, tile), tile)
        return pltpu.make_async_copy(term_here.at[:, :, cols], term.at[:, :, cols], s_term.at[t])

    fetch(0).start()
    finish_line()
    keep = pltpu.make_async_copy(here, weight, local.at[2])
    keep.start()
    begin_late()

    def forward(b):
        fetch(b).wait()

        @pl.when(b < 7)
        def _():
            fetch(b + 1).start()

        @pl.when(b > 1)
        def _():
            for copy in outs(b - 2):
                copy.wait()

        out = by_planes(block, b % 2, here)
        both_here[b % 2] = out
        at = pl.ds(pl.multiple_of(b * rows, rows), rows)
        product_here[at, :] = (out[:, : wide // 2] * out[:, wide // 2 :]).astype(jnp.bfloat16)
        for copy in outs(b):
            copy.start()

    pl.loop(0, 7)(forward)
    service_late()
    fetch_cot(0).start()
    pl.loop(7, 8)(forward)

    @pl.loop(0, width // tile)
    def _(t):
        fetch_cot(t).wait()

        @pl.when(t + 1 < width // tile)
        def _():
            fetch_cot(t + 1).start()

        cols = pl.ds(pl.multiple_of(t * tile, tile), tile)
        out = matmul_tn(product_here[...], cot_here[t % 2]).astype(term.dtype)
        for g in range(4):
            term_here[g, :skip, cols] = out[g * skip : (g + 1) * skip]
            start = 4 * skip + g * late.shape[1]
            term_here[g, skip:, cols] = out[start : start + late.shape[1]]
        leave_term(t).start()

    for b in (6, 7):
        for copy in outs(b):
            copy.wait()
    for t in range(width // tile):
        leave_term(t).wait()
    keep.wait()
    finish_late()


def turn_mid(left, held, squares, tokens, units, down, cot, late, number):
    rows, width = tokens.shape
    wide = units.shape[1]
    tile = width // 4
    f32, bf, dma = jnp.float32, tokens.dtype, pltpu.SemaphoreType.DMA
    outs = (
        ((rows, width), f32),
        ((8, rows, width), bf),
        (squares.shape, f32),
        ((4, *units.shape), bf),
        ((4, late, width), bf),
        ((8 * rows, wide), f32),
        ((8 * rows, wide // 2), bf),
        ((4, wide // 8, width), bf),
        ((held.shape[0] * held.shape[1], width), bf),
    )
    return pl.pallas_call(
        turn_mid_kernel,
        out_shape=[jax.ShapeDtypeStruct(*out) for out in outs],
        in_specs=[ANY, ANY, VMEM, VMEM] + [ANY] * 3,
        out_specs=[VMEM, ANY, VMEM] + [ANY] * 5 + [VMEM],
        scratch_shapes=[
            pltpu.VMEM((8, *squares.shape), f32),
            pltpu.VMEM(squares.shape[::-1], f32),
            dma((7,)),
            dma((7,)),
            pltpu.VMEM((rows, width), bf),
            pltpu.VMEM((rows, width), f32),
            pltpu.VMEM((4, *units.shape), bf),
            pltpu.VMEM((2, rows, width), bf),
            pltpu.VMEM((2, rows, wide), f32),
            pltpu.VMEM((8 * rows, wide // 2), bf),
            pltpu.VMEM((2, 8 * rows, tile), bf),
            pltpu.VMEM((4, wide // 8, width), bf),
        ]
        + [dma((4,)) for _ in range(4)]
        + [dma((2,)), dma((2, 2)), dma((2,)), dma((4,)), dma((6,))]
        + [pltpu.VMEM((held.shape[0] * held.shape[1], width), bf), dma((2,)), dma((2,))]
        + [pltpu.VMEM(left.shape, f32)]
        + scatter_buffers(rows, width)
        + GATHER_SEMAPHORES,
        compiler_params=pltpu.CompilerParams(
            collective_id=number, has_side_effects=True, vmem_limit_bytes=VMEM_BYTES
        ),
        cost_estimate=pl.CostEstimate(flops=0, bytes_accessed=2**20, transcendentals=0),
        name=f"turn_mid_{number}",
    )(left, held, squares, tokens, units, down, cot)


def turn_back_kernel(
    left, right, middle, tokens, cot, grad_middle, low_out, inners,
    inner, s_note, r_note, low, total, left_here, right_here, middle_here, tokens_here, cot_here, s_left, s_in, *rest
):
    buffers, sems = rest[:BUFFERS], rest[BUFFERS:]
    spot = z, y, x, core = place()
    rows, width = grad_middle.shape
    me = member(y, x, core)
    peers = plane_peers(y, x, core)

    def fetch(block):
        here = pl.ds(pl.multiple_of(block * rows, rows), rows)
        return pltpu.make_async_copy(left.at[here], left_here.at[here], s_left.at[block])

    pairs = ((right, right_here), (middle, middle_here), (tokens, tokens_here), (cot, cot_here))
    whole = [pltpu.make_async_copy(src, dst, s_in.at[n]) for n, (src, dst) in enumerate(pairs)]
    blocks = [
        fetch(member(other(y, 1 - way % 2), other(x, 1 - way // 2), other(core, other_core)))
        for way in range(4) for other_core in (1, 0)
    ]
    for copy in blocks[:1] + whole[:1] + blocks[1:3]:
        copy.start()
    greet([(z, d) for d in peers])
    whole[0].wait()
    for copy in blocks[3:] + whole[1:]:
        copy.start()

    def left_rows(left, block):
        fetch(block).wait()
        return left_here[pl.ds(pl.multiple_of(block * rows, rows), rows), :]

    def right_tile(part, t, cols):
        return matmul_nt(part, right_here[cols, :])

    begin, _, relay, finish, drain = scatter_steps(spot, left, right_tile, left_rows, total, buffers)
    begin()
    relay()
    finish()
    for copy in whole[1:]:
        copy.wait()
    value = middle_here[...]
    grad = cot_here[...].astype(jnp.float32) + norm_back(value, normed(value)[1], total[...])
    grad_middle[...] = grad
    low[...] = grad.astype(jnp.bfloat16)
    begin, relay, finish = gather_steps(spot, low, low_out, *sems)
    begin()
    added = value - tokens_here[...].astype(jnp.float32)
    inner[...] = lax.dot_general(
        jnp.ones((8, width), jnp.float32), low[...].astype(jnp.float32) * added, (NT, ((), ())), precision=HIGH,
        preferred_element_type=jnp.float32,
    )
    notes = note_copies(z, me, peers, inner, inners, s_note, r_note)
    for copy in notes:
        copy.start()
    inners[me] = inner[...]
    drain()
    relay()
    finish()
    for copy in notes:
        copy.wait()


def turn_back(left, right, middle, tokens, cot, number):
    rows, width = tokens.shape
    f32, bf = jnp.float32, tokens.dtype
    grad_middle, low, inner = pl.pallas_call(
        turn_back_kernel,
        out_shape=[
            jax.ShapeDtypeStruct((rows, width), f32),
            jax.ShapeDtypeStruct((8, rows, width), bf),
            jax.ShapeDtypeStruct((8, 8, rows), f32),
        ],
        in_specs=[ANY] * 5,
        out_specs=[VMEM, ANY, VMEM],
        scratch_shapes=[
            pltpu.VMEM((8, rows), f32),
            pltpu.SemaphoreType.DMA((7,)),
            pltpu.SemaphoreType.DMA((7,)),
            pltpu.VMEM((rows, width), bf),
            pltpu.VMEM((rows, width), f32),
            pltpu.VMEM(left.shape, bf),
            pltpu.VMEM(right.shape, bf),
            pltpu.VMEM((rows, width), f32),
            pltpu.VMEM((rows, width), bf),
            pltpu.VMEM((rows, width), bf),
            pltpu.SemaphoreType.DMA((8,)),
            pltpu.SemaphoreType.DMA((4,)),
        ]
        + scatter_buffers(rows, width)
        + GATHER_SEMAPHORES,
        compiler_params=pltpu.CompilerParams(
            collective_id=number, has_side_effects=True, vmem_limit_bytes=VMEM_BYTES
        ),
        cost_estimate=pl.CostEstimate(flops=0, bytes_accessed=2**20, transcendentals=0),
        name=f"turn_back_{number}",
    )(left, right, middle, tokens, cot)
    return grad_middle, low.reshape(8 * rows, width), inner


def tail_kernel(left, right, units, o_ref, stage, *rest):
    buffers, sems = rest[:BUFFERS], rest[BUFFERS:]
    spot = z, y, x, core = place()
    peers = plane_peers(y, x, core)
    greet([(z, d) for d in peers])
    copies = collect_copies(z, member(y, x, core), peers, units, stage, *sems)

    def right_tile(part, t, cols):
        return matmul_nt(part, right[cols, :])

    begin, _, relay, finish, drain = scatter_steps(spot, left, right_tile, None, o_ref, buffers)
    begin()
    for copy in copies:
        copy.start()
    relay()
    finish()
    drain()
    for copy in copies:
        copy.wait()


def plane_tail(left, right, units, number):
    rows, width = left.shape[0] // 8, right.shape[0]
    return pl.pallas_call(
        tail_kernel,
        out_shape=[
            jax.ShapeDtypeStruct((rows, width), jnp.float32),
            jax.ShapeDtypeStruct((8, units.shape[0] // 8, units.shape[1]), units.dtype),
        ],
        in_specs=[VMEM, VMEM, ANY],
        out_specs=[VMEM, ANY],
        scratch_shapes=scatter_buffers(rows, width) + COLLECT_SEMAPHORES,
        compiler_params=pltpu.CompilerParams(
            collective_id=number, has_side_effects=True, vmem_limit_bytes=VMEM_BYTES
        ),
        cost_estimate=pl.CostEstimate(flops=0, bytes_accessed=2**20, transcendentals=0),
        name=f"plane_tail_{number}",
    )(left, right, units)


SIDE = 512


def side_tiles(left, right, out):
    @pl.loop(0, left.shape[1] // SIDE)
    def _(t):
        cols = pl.ds(pl.multiple_of(t * SIDE, SIDE), SIDE)
        out[cols, :] = matmul_tn(left[:, cols], right[...]).astype(out.dtype)


def units_back_kernel(early, late, cot, both, mid, grads, term, whole, weight, sems):
    step = pl.program_id(0)
    rows = cot.shape[0]
    units = weight.shape[0]

    @pl.when(step == 0)
    def _():
        count = early.shape[0]
        parts = ((early, weight.at[pl.ds(0, count)]), (late, weight.at[pl.ds(count, late.shape[0])]))
        copies = [pltpu.make_async_copy(src, dst, sems.at[n]) for n, (src, dst) in enumerate(parts)]
        for copy in copies:
            copy.start()
        for copy in copies:
            copy.wait()

    @pl.when(step < 4)
    def _():
        grad = matmul_nt(cot[...], weight[...])
        here = pl.ds(pl.multiple_of(step * rows, rows), rows)
        left = (grad * both[:, units:]).astype(jnp.bfloat16)
        right = (grad * both[:, :units]).astype(jnp.bfloat16)
        grads[:, :units] = left
        grads[:, units:] = right
        whole[here, :units] = left
        whole[here, units:] = right

    @pl.when(step >= 4)
    def _():
        term[...] = matmul_tn(mid[...], whole[...]).astype(term.dtype)


def units_back(early, late, cot, both, mid):
    height, width = cot.shape
    wide = both.shape[1]
    rows, tile = height // 4, width // 4
    bf = jnp.bfloat16
    return pl.pallas_call(
        units_back_kernel,
        grid=(8,),
        out_shape=[
            jax.ShapeDtypeStruct((height, wide), bf),
            jax.ShapeDtypeStruct((width, wide), bf),
        ],
        in_specs=[
            ANY,
            ANY,
            pl.BlockSpec((rows, width), lambda s: (jnp.minimum(s, 3), 0)),
            pl.BlockSpec((rows, wide), lambda s: (jnp.minimum(s, 3), 0)),
            pl.BlockSpec((height, tile), lambda s: (0, jnp.maximum(s - 4, 0))),
        ],
        out_specs=[
            pl.BlockSpec((rows, wide), lambda s: (jnp.minimum(s, 3), 0)),
            pl.BlockSpec((tile, wide), lambda s: (jnp.maximum(s - 4, 0), 0)),
        ],
        scratch_shapes=[
            pltpu.VMEM((height, wide), bf),
            pltpu.VMEM((wide // 2, width), bf),
            pltpu.SemaphoreType.DMA((2,)),
        ],
        compiler_params=pltpu.CompilerParams(
            dimension_semantics=("arbitrary",), vmem_limit_bytes=VMEM_BYTES
        ),
        cost_estimate=pl.CostEstimate(
            flops=2 * cot.size * wide * 3 // 2, bytes_accessed=2**25, transcendentals=0
        ),
        name="units_back",
    )(early, late, cot, both, mid)


def dot_fine(left, right, dims):
    high = right.astype(jnp.bfloat16)
    low = (right - high.astype(jnp.float32)).astype(jnp.bfloat16)
    product = functools.partial(
        lax.dot_general, dimension_numbers=(dims, ((), ())), preferred_element_type=jnp.float32
    )
    return product(left, high) + product(left, low)


NN, NT, TN = ((1,), (0,)), ((1,), (1,)), ((0,), (0,))


def block_tables(count, rate, rows):
    spot = lax.broadcasted_iota(jnp.int32, (rows, 1), 0)
    live = spot < count
    behind = jnp.where(live, jnp.exp(-rate * spot.astype(jnp.float32)), 0.0)
    ahead = jnp.where(live, jnp.exp(-rate * (count - spot).astype(jnp.float32)), 0.0)
    fade = jnp.exp(jnp.full((1, HEAD_DIM), -rate * count.astype(jnp.float32), jnp.float32))
    return live, behind, ahead, fade


def fill_decay(base, rates):
    heads, rows, _ = base.shape
    gap = lax.broadcasted_iota(jnp.int32, (rows, rows), 0) - lax.broadcasted_iota(jnp.int32, (rows, rows), 1)
    far = jnp.maximum(gap, 0).astype(jnp.float32)
    for t in range(heads):
        base[t] = jnp.where(gap >= 0, jnp.exp(-rates[t] * far), 0.0)


def own_rates(decay, heads):
    _, y, x, core = place()
    return [decay[4 * (heads * core + t) + 2 * y + x] for t in range(heads)]


def unmix_kernel(
    counts, decay, low, weight, pre, attn_gate, qkv, entering, scale, inner, product, early, late, hidden,
    grads_out, out_term, term_out, down_out,
    base, state, total, product_here, down_here, hidden_here, grads, term, down_own, s_in, s_out, *buffers
):
    step = pl.program_id(0)
    steps = pl.num_programs(0)
    b = steps - 1 - step
    rows, width = low.shape
    wide = weight.shape[0]
    rates = own_rates(decay, state.shape[0])
    spot = z, y, x, core = place()
    fetch = [
        pltpu.make_async_copy(src, dst, s_in.at[n])
        for n, (src, dst) in enumerate((
            (product, product_here),
            (early, down_here.at[pl.ds(0, early.shape[0])]),
            (late, down_here.at[pl.ds(early.shape[0], late.shape[0])]),
            (hidden, hidden_here),
        ))
    ]
    leave = [
        pltpu.make_async_copy(src, dst, s_out.at[n])
        for n, (src, dst) in enumerate(((grads, grads_out), (term, term_out), (down_own, down_out)))
    ]

    def right_tile(part, t, cols):
        return matmul(part, down_here[:, cols])

    _, piece, relay, finish, drain = scatter_steps(spot, product_here, right_tile, None, down_own, buffers)

    @pl.when(step == 0)
    def _():
        for copy in fetch[:3]:
            copy.start()
        fill_decay(base, rates)
        state[...] = jnp.zeros_like(state)
        total[...] = jnp.zeros_like(total)
        greet([(z, d) for d in plane_peers(y, x, core)])
        for copy in fetch[:3]:
            copy.wait()

    for n in range(PIECES):
        pl.when(step == n // 2)(functools.partial(piece, n))
    pl.when(step == 1)(fetch[3].start)

    count = counts[b, 0]

    def column(ref):
        here = lax.broadcasted_iota(jnp.int32, (8, rows), 0) == b
        turned = jnp.transpose(jnp.where(here, ref, 0.0))
        return jnp.sum(turned, axis=1, keepdims=True)

    here = pl.ds(pl.multiple_of(b * rows, rows), rows)
    factor, inside = column(scale[...]), column(inner[:, 0])
    attn, gate = attn_gate[:, :wide], attn_gate[:, wide:]
    normal = attn * factor
    grad = matmul_nt(low[...], weight[...])
    grads[here, 3 * wide :] = (grad * normal).astype(jnp.bfloat16)
    grad_attn = (factor * grad * gate - normal * factor * inside * (1.0 / width)).astype(jnp.bfloat16)
    total[...] += matmul_tn((normal * gate).astype(jnp.bfloat16), low[...])
    for t in range(state.shape[0]):
        at = slice(t * HEAD_DIM, (t + 1) * HEAD_DIM)
        q, k, v = (qkv[:, i * wide + t * HEAD_DIM : i * wide + (t + 1) * HEAD_DIM] for i in range(3))
        g = grad_attn[:, at]
        live, behind, ahead, fade = block_tables(count, rates[t], rows)
        mask = jnp.where(live, base[t], 0.0)
        probs = (matmul_nt(q, k) * mask).astype(jnp.bfloat16)
        raw = (matmul_nt(g, v) * mask).astype(jnp.bfloat16)
        leaving = jnp.where(count < rows, 0.0, state[t])
        grad_q = matmul(raw, k) + behind * dot_fine(g, entering[0, t], NT)
        grad_k = matmul_tn(raw, q) + ahead * dot_fine(v, leaving, NT)
        grad_v = matmul_tn(probs, g) + ahead * dot_fine(k, leaving, NN)
        state[t] = dot_fine(q, g.astype(jnp.float32) * behind, TN) + fade * leaving
        grads[here, at] = (grad_q * silu_slope(pre[:, at])).astype(jnp.bfloat16)
        after = slice(wide + t * HEAD_DIM, wide + (t + 1) * HEAD_DIM)
        grads[here, after] = (grad_k * silu_slope(pre[:, after])).astype(jnp.bfloat16)
        grads[here, 2 * wide + t * HEAD_DIM : 2 * wide + (t + 1) * HEAD_DIM] = grad_v.astype(jnp.bfloat16)

    @pl.when(step == 4)
    def _():
        relay()

    @pl.when(step == steps - 1)
    def _():
        leave[0].start()
        out_term[...] = total[...].astype(jnp.bfloat16)
        fetch[3].wait()
        side_tiles(hidden_here, grads, term)
        leave[1].start()
        finish()
        leave[2].start()
        drain()
        for copy in leave:
            copy.wait()


def unmix_heads(counts, decay, low, weight, pre, attn_gate, qkv, entering, scale, inner, product, early, late, hidden, number):
    rows, width = low.shape[0] // 8, low.shape[1]
    wide = weight.shape[0]
    heads = wide // HEAD_DIM
    f32, bf = jnp.float32, jnp.bfloat16

    def by_block(columns):
        return pl.BlockSpec((rows, columns), lambda s: (7 - s, 0))

    def whole(*shape):
        return pl.BlockSpec(shape, lambda s: (0,) * len(shape))

    return pl.pallas_call(
        unmix_kernel,
        grid=(8,),
        out_shape=[
            jax.ShapeDtypeStruct((8 * rows, 4 * wide), bf),
            jax.ShapeDtypeStruct((wide, width), bf),
            jax.ShapeDtypeStruct((hidden.shape[1], 4 * wide), bf),
            jax.ShapeDtypeStruct((rows, width), f32),
        ],
        in_specs=[
            SMEM,
            SMEM,
            by_block(width),
            whole(wide, width),
            by_block(2 * wide),
            by_block(2 * wide),
            by_block(3 * wide),
            pl.BlockSpec((1, heads, HEAD_DIM, HEAD_DIM), lambda s: (7 - s, 0, 0, 0)),
            whole(8, rows),
            whole(8, 8, rows),
            ANY,
            ANY,
            ANY,
            ANY,
        ],
        out_specs=[ANY, whole(wide, width), ANY, ANY],
        scratch_shapes=[
            pltpu.VMEM((heads, rows, rows), f32),
            pltpu.VMEM((heads, HEAD_DIM, HEAD_DIM), f32),
            pltpu.VMEM((wide, width), f32),
            pltpu.VMEM(product.shape, bf),
            pltpu.VMEM((product.shape[1], width), bf),
            pltpu.VMEM(hidden.shape, bf),
            pltpu.VMEM((8 * rows, 4 * wide), bf),
            pltpu.VMEM((hidden.shape[1], 4 * wide), bf),
            pltpu.VMEM((rows, width), f32),
            pltpu.SemaphoreType.DMA((4,)),
            pltpu.SemaphoreType.DMA((3,)),
        ]
        + scatter_buffers(rows, width),
        compiler_params=pltpu.CompilerParams(
            collective_id=number,
            has_side_effects=True,
            dimension_semantics=("arbitrary",),
            vmem_limit_bytes=VMEM_BYTES,
        ),
        cost_estimate=pl.CostEstimate(flops=0, bytes_accessed=2**20, transcendentals=0),
        name="unmix_heads",
    )(counts, decay, low, weight, pre, attn_gate, qkv, entering, scale, inner, product, early, late, hidden)


def after(value, *others):
    return lax.optimization_barrier((value, *others))[0]


def fast_plan(
    tokens,
    block_counts,
    decay_rate,
    query_weight,
    key_weight,
    value_weight,
    gate_weight,
    out_weight,
    first_weight,
    second_weight,
    down_weight,
    cotangent,
):
    rows, width = tokens.shape
    nz = lax.axis_size("dp")
    nf = lax.axis_size("fsdp")
    chips = nf // 2
    plane = lax.axis_index("fsdp")
    core = plane % 2
    bf = jnp.bfloat16
    half = HEADS // nf
    own = half * HEAD_DIM
    units = first_weight.shape[1] // nf

    head_spots = tuple(
        (2 * c + k, n, HEAD_DIM * (chips * (half * k + t) + c), 0, n * own + t * HEAD_DIM, HEAD_DIM)
        for c in range(chips) for k in range(2) for n in range(4) for t in range(half)
    )
    run = units // nz
    early = 64
    unit_spots = tuple(
        (f, n, run * (nf * g + f) + skip, 0, n * units + nz * skip + g * wide, wide)
        for f in range(nf) for n in range(2) for g in range(nz) for skip, wide in ((0, early), (early, run - early))
    )
    swap = [(i, i ^ 1) for i in range(nf)]

    def uncross(x):
        keep = lax.dynamic_index_in_dim(x, core, 1, False)
        send = lax.dynamic_index_in_dim(x, 1 - core, 1, False)
        got = lax.ppermute(send, "fsdp", swap)
        return jnp.concatenate([jnp.where(core == 0, keep, got), jnp.where(core == 0, got, keep)], axis=0)

    note = jnp.broadcast_to(block_counts, (8, 128))
    hidden, cot, w_heads, out_rows, wd_early, w_units, counts, pre, attn_gate, qkv, entering, squares = open_attention(
        tokens, cotangent, (query_weight, key_weight, value_weight, gate_weight), (first_weight, second_weight),
        out_weight, down_weight, note, decay_rate, head_spots, unit_spots, 4 * own, 2 * units, early, 0,
    )
    hidden, cot, wd_early = (a.reshape(-1, width) for a in (hidden, cot, wd_early))
    w_heads = w_heads.reshape(-1, 4 * own)
    counts = counts[:, 0]
    middle, mid, scale, w_units, wd_late, both, product, down_term, wo = turn_mid(
        attn_gate, out_rows, squares, tokens, w_units.reshape(-1, 2 * units), down_weight, cot, run - early, 2
    )
    down_term = down_term.reshape(units, width)
    mid, wd_late = mid.reshape(-1, width), wd_late.reshape(-1, width)
    w_units = w_units.reshape(-1, 2 * units)
    inputs = tokens.astype(jnp.float32)
    down_sum = lax.psum_scatter(down_term, "dp", scatter_dimension=0, tiled=True)
    grad_units, units_term = units_back(wd_early, wd_late, cot, both, mid)
    units_sum = lax.psum_scatter(units_term, "dp", scatter_dimension=0, tiled=True)
    grad_middle, low, inner = turn_back(grad_units, w_units, middle, tokens, cotangent, 3)
    grad_heads, out_term, heads_term, down_own = unmix_heads(
        counts, decay_rate, after(low, down_sum), wo, pre, attn_gate, qkv, entering, scale, inner, product, wd_early, wd_late, hidden, 4
    )
    block_out = (middle + down_own).astype(bf)
    heads_sum = lax.psum_scatter(heads_term, "dp", scatter_dimension=0, tiled=True)
    out_term = uncross(out_term.reshape(half, 2, -1, width))
    out_sum = lax.psum_scatter(out_term, "dp", scatter_dimension=0, tiled=False)
    grad_hidden, units_grad = plane_tail(after(grad_heads, out_term), w_heads, units_sum, 5)
    tokens_grad = grad_middle + norm_back(inputs, normed(inputs)[1], grad_hidden)
    down_grad = down_sum.astype(jnp.float32)
    first_grad, second_grad = unpack(units_grad, unit_spots, nf * units, 2)
    heads_sum = after(heads_sum, first_grad, grad_hidden)
    heads_grad = plane_collect(heads_sum, 7)
    grads = unpack(heads_grad, head_spots, width, 4)
    out_grad = after(out_sum, *grads).astype(jnp.float32)
    return (block_out, tokens_grad, *grads, out_grad, first_grad, second_grad, down_grad)


def fits(mesh):
    return mesh.shape["dp"] == 4 and mesh.shape["fsdp"] == 8


def solution(mesh):
    return jax.shard_map(
        fast_plan if fits(mesh) else shards,
        mesh=mesh,
        in_specs=(
            P(("dp", "fsdp"), None),
            P("dp", "fsdp"),
            P(),
            P(("dp", "fsdp"), None),
            P(("dp", "fsdp"), None),
            P(("dp", "fsdp"), None),
            P(("dp", "fsdp"), None),
            P(("dp", "fsdp"), None),
            P(("dp", "fsdp"), None),
            P(("dp", "fsdp"), None),
            P(("dp", "fsdp"), None),
            P(("dp", "fsdp"), None),
        ),
        out_specs=(
            P(("dp", "fsdp"), None),
            P(("dp", "fsdp"), None),
            P(("dp", "fsdp"), None),
            P(("dp", "fsdp"), None),
            P(("dp", "fsdp"), None),
            P(("dp", "fsdp"), None),
            P(("dp", "fsdp"), None),
            P(("dp", "fsdp"), None),
            P(("dp", "fsdp"), None),
            P(("dp", "fsdp"), None),
        ),
        check_vma=False,
    )
```

```python
import functools

import jax
import jax.numpy as jnp
from jax import lax
from jax.experimental import pallas as pl
from jax.experimental.pallas import tpu as pltpu
from jax.sharding import PartitionSpec as P

HEADS = 16
HEAD_DIM = 128


EPS = 1e-06
HIGH = lax.Precision.HIGHEST


def carried_in(part, axis, combine, identity):
    place = lax.axis_index(axis)
    gathered = jax.tree.map(lambda a: lax.all_gather(a, axis), part)
    state = jax.tree.map(lambda a, e: jnp.zeros_like(a) + jnp.asarray(e, a.dtype), part, identity)

    def carried_one(lap, state):
        return combine(
            state, jax.tree.map(lambda a: lax.dynamic_index_in_dim(a, lap, 0, False), gathered)
        )

    return lax.fori_loop(0, place, carried_one, state)


def prefix_2(value, axis, join, neutral):
    count = lax.axis_size(axis)
    place = lax.axis_index(axis)
    ahead = count - 1 - place
    gathered = jax.tree.map(
        lambda a, kind: lax.all_gather(a.astype(kind), axis), value, (jnp.bfloat16, jnp.bfloat16)
    )
    state = jax.tree.map(lambda a, e: jnp.zeros_like(a) + jnp.asarray(e, a.dtype), value, neutral)

    def prefix_one(lap, state):
        source = count - 1 - lap
        return join(
            state,
            jax.tree.map(
                lambda a, own: lax.dynamic_index_in_dim(a, source, 0, False).astype(own.dtype),
                gathered,
                value,
            ),
        )

    return lax.fori_loop(0, ahead, prefix_one, state)


def normed(value):
    scale = lax.rsqrt(jnp.mean(value * value, axis=-1, keepdims=True) + EPS)
    return (value * scale, scale)


def norm_back(value, scale, grad):
    inner = jnp.mean(grad * value, axis=-1, keepdims=True)
    return scale * (grad - value * scale * scale * inner)


def silu_slope(value):
    sig = jax.nn.sigmoid(value)
    return sig * (1.0 + value * (1.0 - sig))


def chain_step(earlier, later):
    e_fade, e_state = earlier
    l_fade, l_state = later
    return (l_fade * e_fade, l_fade[:, None, None] * e_state + l_state)


def matmul(left, right):
    return jnp.dot(left, right, preferred_element_type=jnp.float32)


def matmul_tn(left, right):
    return lax.dot_general(
        left, right, (((0,), (0,)), ((), ())), preferred_element_type=jnp.float32
    )


def matmul_nt(left, right):
    return lax.dot_general(
        left, right, (((1,), (1,)), ((), ())), preferred_element_type=jnp.float32
    )


def decay_tables(count, rates, rows):
    pos = lax.iota(jnp.int32, rows)
    live = pos < count
    keep = (pos[:, None] >= pos[None, :]) & live[:, None] & live[None, :]
    spacing = jnp.where(keep, (pos[:, None] - pos[None, :]).astype(jnp.float32), 0.0)
    mask = jnp.where(keep[None], jnp.exp(-rates[:, None, None] * spacing[None]), 0.0)
    ahead = jnp.where(
        live[:, None], jnp.exp(-rates[None, :] * (count - pos)[:, None].astype(jnp.float32)), 0.0
    )
    behind = jnp.where(
        live[:, None], jnp.exp(-rates[None, :] * pos[:, None].astype(jnp.float32)), 0.0
    )
    fade = jnp.exp(-rates * count.astype(jnp.float32))
    return (mask, ahead, behind, fade)


def shards(
    tokens,
    block_counts,
    decay_rate,
    query_weight,
    key_weight,
    value_weight,
    gate_weight,
    out_weight,
    first_weight,
    second_weight,
    down_weight,
    cotangent,
):
    rows = tokens.shape[0]
    gathered = (
        lax.all_gather(query_weight, ("dp", "fsdp"), axis=0, tiled=True),
        lax.all_gather(key_weight, ("dp", "fsdp"), axis=0, tiled=True),
        lax.all_gather(value_weight, ("dp", "fsdp"), axis=0, tiled=True),
        lax.all_gather(gate_weight, ("dp", "fsdp"), axis=0, tiled=True),
        lax.all_gather(out_weight, ("dp", "fsdp"), axis=0, tiled=True),
        lax.all_gather(first_weight, ("dp", "fsdp"), axis=0, tiled=True),
        lax.all_gather(second_weight, ("dp", "fsdp"), axis=0, tiled=True),
        lax.all_gather(down_weight, ("dp", "fsdp"), axis=0, tiled=True),
    )
    w_query, w_key, w_value, w_gate, w_out, w_first, w_second, w_down = gathered
    count = block_counts[0, 0]
    closes = count < rows
    mask, ahead, behind, fade = decay_tables(count, decay_rate, rows)
    passing = jnp.where(closes, 0.0, fade)
    inputs = tokens.astype(jnp.float32)
    in_normed, in_scale = normed(inputs)
    hidden = in_normed.astype(jnp.bfloat16)
    q_pre = matmul(hidden, w_query)
    k_pre = matmul(hidden, w_key)
    value = matmul(hidden, w_value).astype(jnp.bfloat16)
    gate = matmul(hidden, w_gate)
    query = jax.nn.silu(q_pre).astype(jnp.bfloat16)
    keys = jax.nn.silu(k_pre).astype(jnp.bfloat16)
    query_heads = query.reshape(rows, HEADS, HEAD_DIM)
    key_heads = keys.reshape(rows, HEADS, HEAD_DIM)
    value_heads = value.reshape(rows, HEADS, HEAD_DIM)
    query_wide = query_heads.astype(jnp.float32)
    key_wide = key_heads.astype(jnp.float32)
    value_ahead = value_heads.astype(jnp.float32) * ahead[:, :, None]
    raw = jnp.einsum("ihe,jhe->hij", query_heads, key_heads, preferred_element_type=jnp.float32)
    probs = (raw * mask).astype(jnp.bfloat16)
    intra = jnp.einsum("hij,jhe->ihe", probs, value_heads, preferred_element_type=jnp.float32)
    local = jnp.einsum("jhe,jhf->hef", key_wide, value_ahead, precision=HIGH)
    local_sent = jnp.where(closes, 0.0, local)
    prefix = carried_in(
        (passing, local_sent), "fsdp", chain_step, (jnp.ones_like(fade), jnp.zeros_like(local))
    )
    entering = prefix[1]
    inter = behind[:, :, None] * jnp.einsum("ihe,hef->ihf", query_wide, entering, precision=HIGH)
    attn = (intra + inter).reshape(rows, HEADS * HEAD_DIM)
    attn_normed, attn_scale = normed(attn)
    mixed = (attn_normed * gate).astype(jnp.bfloat16)
    middle = inputs + matmul(mixed, w_out)
    mid_normed, mid_scale = normed(middle)
    mid = mid_normed.astype(jnp.bfloat16)
    first = matmul(mid, w_first)
    second = matmul(mid, w_second)
    product = (first * second).astype(jnp.bfloat16)
    block_out = (middle + matmul(product, w_down)).astype(jnp.bfloat16)
    w_first, w_second, w_down = (
        lax.all_gather(first_weight, ("dp", "fsdp"), axis=0, tiled=True),
        lax.all_gather(second_weight, ("dp", "fsdp"), axis=0, tiled=True),
        lax.all_gather(down_weight, ("dp", "fsdp"), axis=0, tiled=True),
    )
    grad_product = matmul_nt(cotangent, w_down)
    grad_first = (grad_product * second).astype(jnp.bfloat16)
    grad_second = (grad_product * first).astype(jnp.bfloat16)
    grad_mid = matmul_nt(grad_first, w_first) + matmul_nt(grad_second, w_second)
    grad_middle = cotangent.astype(jnp.float32) + norm_back(middle, mid_scale, grad_mid)

    def scattered(left, right, after):
        left, _ = lax.optimization_barrier((left, after))
        term = matmul_tn(left, right)
        return lax.psum_scatter(term, ("dp", "fsdp"), scatter_dimension=0, tiled=True)

    down_grad = scattered(product, cotangent, grad_middle)
    first_grad = scattered(mid, grad_first, down_grad)
    second_grad = scattered(mid, grad_second, first_grad)
    grad_middle, _ = lax.optimization_barrier((grad_middle, second_grad))
    w_query, w_key, w_value, w_gate, w_out = (
        lax.all_gather(query_weight, ("dp", "fsdp"), axis=0, tiled=True),
        lax.all_gather(key_weight, ("dp", "fsdp"), axis=0, tiled=True),
        lax.all_gather(value_weight, ("dp", "fsdp"), axis=0, tiled=True),
        lax.all_gather(gate_weight, ("dp", "fsdp"), axis=0, tiled=True),
        lax.all_gather(out_weight, ("dp", "fsdp"), axis=0, tiled=True),
    )
    grad_mid_low = grad_middle.astype(jnp.bfloat16)
    out_term = matmul_tn(mixed, grad_mid_low)
    grad_mixed = matmul_nt(grad_mid_low, w_out)
    grad_gate = (grad_mixed * attn_normed).astype(jnp.bfloat16)
    grad_attn = norm_back(attn, attn_scale, grad_mixed * gate).astype(jnp.bfloat16)
    grad_heads = grad_attn.reshape(rows, HEADS, HEAD_DIM)
    grad_heads_wide = grad_heads.astype(jnp.float32) * behind[:, :, None]
    grad_probs = jnp.einsum(
        "ihe,jhe->hij", grad_heads, value_heads, preferred_element_type=jnp.float32
    )
    grad_raw = (grad_probs * mask).astype(jnp.bfloat16)
    grad_entering = jnp.einsum("ihe,ihf->hef", query_wide, grad_heads_wide, precision=HIGH)
    suffix = prefix_2(
        (passing, grad_entering),
        "fsdp",
        chain_step,
        (jnp.ones_like(fade), jnp.zeros_like(grad_entering)),
    )
    grad_leaving = jnp.where(closes, 0.0, suffix[1])
    grad_query = jnp.einsum("hij,jhe->ihe", grad_raw, key_heads, preferred_element_type=jnp.float32)
    grad_query = grad_query + jnp.einsum("ihf,hef->ihe", grad_heads_wide, entering, precision=HIGH)
    grad_keys = jnp.einsum(
        "hij,ihe->jhe", grad_raw, query_heads, preferred_element_type=jnp.float32
    )
    grad_keys = grad_keys + jnp.einsum("hef,jhf->jhe", grad_leaving, value_ahead, precision=HIGH)
    grad_value = jnp.einsum("hij,ihe->jhe", probs, grad_heads, preferred_element_type=jnp.float32)
    grad_value = grad_value + ahead[:, :, None] * jnp.einsum(
        "hef,jhe->jhf", grad_leaving, key_wide, precision=HIGH
    )
    width = HEADS * HEAD_DIM
    grad_q_pre = (grad_query.reshape(rows, width) * silu_slope(q_pre)).astype(jnp.bfloat16)
    grad_k_pre = (grad_keys.reshape(rows, width) * silu_slope(k_pre)).astype(jnp.bfloat16)
    grad_v = grad_value.reshape(rows, width).astype(jnp.bfloat16)
    query_term = matmul_tn(hidden, grad_q_pre)
    key_term = matmul_tn(hidden, grad_k_pre)
    value_term = matmul_tn(hidden, grad_v)
    gate_term = matmul_tn(hidden, grad_gate)
    grad_hidden = matmul_nt(grad_q_pre, w_query) + matmul_nt(grad_k_pre, w_key)
    grad_hidden = grad_hidden + matmul_nt(grad_v, w_value) + matmul_nt(grad_gate, w_gate)
    tokens_grad = grad_middle + norm_back(inputs, in_scale, grad_hidden)
    query_grad, key_grad, value_grad, gate_grad, out_grad = (
        lax.psum_scatter(query_term, ("dp", "fsdp"), scatter_dimension=0, tiled=True),
        lax.psum_scatter(key_term, ("dp", "fsdp"), scatter_dimension=0, tiled=True),
        lax.psum_scatter(value_term, ("dp", "fsdp"), scatter_dimension=0, tiled=True),
        lax.psum_scatter(gate_term, ("dp", "fsdp"), scatter_dimension=0, tiled=True),
        lax.psum_scatter(out_term, ("dp", "fsdp"), scatter_dimension=0, tiled=True),
    )
    return (
        block_out,
        tokens_grad,
        query_grad,
        key_grad,
        value_grad,
        gate_grad,
        out_grad,
        first_grad,
        second_grad,
        down_grad,
    )


MESH = pl.DeviceIdType.MESH
VMEM_BYTES = 60 * 2**20
ANY = pl.BlockSpec(memory_space=pl.ANY)
VMEM = pl.BlockSpec(memory_space=pltpu.VMEM)
SMEM = pl.BlockSpec(memory_space=pltpu.SMEM)


def place():
    plane = lax.axis_index("fsdp")
    return lax.axis_index("dp"), plane // 4, (plane // 2) % 2, plane % 2


def other(i, way):
    return i + way - 2 * i * way


def member(y, x, core):
    return (y * 2 + x) * 2 + core


def plane_peers(y, x, core):
    ways = [(dy, dx, dc) for dy in (1, 0) for dx in (1, 0) for dc in (0, 1) if dy + dx + dc]
    return [member(other(y, dy), other(x, dx), other(core, dc)) for dy, dx, dc in ways]


def greet(devices):
    barrier = pltpu.get_barrier_semaphore()
    for device in devices:
        pl.semaphore_signal(barrier, inc=1, device_id=device, device_id_type=MESH)
    pl.semaphore_wait(barrier, len(devices))


def remote(src, dst, send, recv, device):
    return pltpu.make_async_remote_copy(
        src_ref=src, dst_ref=dst, send_sem=send, recv_sem=recv, device_id=device, device_id_type=MESH
    )


def note_copies(z, me, peers, note, notes, send, recv):
    return [
        remote(note, notes.at[me], send.at[n], recv.at[n], (z, d)) for n, d in enumerate(peers)
    ]


def pack_columns(spots, weights, stages):
    for f, n, src, m, dst, wide in spots:
        stages[m][f, :, dst : dst + wide] = weights[n][:, src : src + wide]


def unpack_columns(spots, stages, grads):
    for f, n, src, m, dst, wide in spots:
        grads[n][:, src : src + wide] = stages[m][f, :, dst : dst + wide].astype(jnp.float32)


def gather_steps(spot, x_ref, o_ref, local, send, recv, first_row=0, rows=None):
    z, y, x, core = spot
    me, mate = member(y, x, core), member(y, x, 1 - core)
    on_x, on_y, across = member(y, 1 - x, core), member(1 - y, x, core), member(1 - y, 1 - x, core)
    rows = rows or x_ref.shape[0]
    half = rows // 2
    both = pl.ds(first_row, rows)
    low, high = pl.ds(first_row, half), pl.ds(first_row + half, half)

    def own(part, n, device):
        return remote(x_ref.at[part], o_ref.at[me, part], send.at[n], recv.at[n], (z, device))

    def pass_on(block, part, n, device):
        ref = o_ref.at[block, part]
        return remote(ref, ref, send.at[n], recv.at[n], (z, device))

    keep = pltpu.make_async_copy(x_ref.at[both], o_ref.at[me, both], local)
    first = [own(low, 0, on_y), own(high, 1, on_x), own(high, 2, on_y), own(low, 3, on_x)]
    mine = own(both, 4, mate)
    relay_x = pass_on(on_y, low, 5, on_x)
    relay_y = pass_on(on_x, high, 6, on_y)
    y_mate = pass_on(on_y, both, 7, mate)
    x_mate = pass_on(on_x, both, 8, mate)
    low_mate = pass_on(across, low, 9, mate)
    high_mate = pass_on(across, high, 10, mate)

    def begin():
        for copy in (*first, mine, keep):
            copy.start()

    def relay():
        first[0].wait_recv()
        relay_x.start()
        first[1].wait_recv()
        relay_y.start()
        first[2].wait_recv()
        y_mate.start()
        first[3].wait_recv()
        x_mate.start()

    def finish():
        relay_x.wait_recv()
        low_mate.start()
        relay_y.wait_recv()
        high_mate.start()
        keep.wait()
        for copy in (mine, y_mate, x_mate, low_mate, high_mate):
            copy.wait_recv()
        for copy in (*first, mine, relay_x, relay_y, y_mate, x_mate, low_mate, high_mate):
            copy.wait_send()

    return begin, relay, finish


GATHER_SEMAPHORES = [pltpu.SemaphoreType.DMA, pltpu.SemaphoreType.DMA((11,)), pltpu.SemaphoreType.DMA((11,))]


def column_of_chips(spot):
    z, y, x, _ = spot
    planes = lax.axis_size("dp")
    return [(lax.rem(z + n, planes), member(y, x, c)) for n in range(1, planes) for c in (0, 1)]


def plane_line_steps(spot, ref, send, recv, source=None):
    z, y, x, core = spot
    me = member(y, x, core)
    middle = lax.rem((z + 1) // 2, 2)
    own_end = 3 * (z // 2)
    near = z // 2 + 1

    def move(part, n, plane, source=None):
        here = ref.at[part]
        return remote(here if source is None else source, here, send.at[n], recv.at[part], (plane, me))

    first = move(z, 0, middle * (3 - own_end) + (1 - middle) * (3 - near), source)
    second = move(z, 1, middle * own_end + (1 - middle) * near, source)
    relay = move(3 - own_end, 2, own_end)
    across = move(z, 3, 3 - z, source)

    def begin():
        first.start()
        second.start()

    def service():
        @pl.when(middle == 1)
        def _():
            relay.wait_recv()
            relay.start()
            across.start()

    def finish():
        for part in range(4):
            taken = (middle == 1) & (part == 3 - own_end)

            @pl.when((part != z) & jnp.logical_not(taken))
            def _(part=part):
                remote(ref.at[part], ref.at[part], send.at[0], recv.at[part], (3 - z, me)).wait_recv()

        first.wait_send()
        second.wait_send()

        @pl.when(middle == 1)
        def _():
            relay.wait_send()
            across.wait_send()

    return begin, service, finish


def by_planes(left, slot, right):
    rows = right.shape[1]
    return sum(matmul(left[slot, :, g * rows : (g + 1) * rows], right[g]) for g in range(right.shape[0]))


def open_kernel(head_spots, unit_spots, *refs):
    refs = list(refs)
    tokens, cot, *heads = [refs.pop(0) for _ in range(6)]
    units, (rows, down, note, decay) = [refs.pop(0) for _ in range(2)], [refs.pop(0) for _ in range(4)]
    hidden, cots, weight, held, early, units_out, notes, pre, attn_gate, qkv, entering, squares = [
        refs.pop(0) for _ in range(12)
    ]
    stage, here, swap, own, block, pre_here, mix_here, qkv_here, entering_here, base, state = [
        refs.pop(0) for _ in range(11)
    ]
    s_swap, r_swap, s_note, r_note, s_units, r_units, s_line, r_line, s_early, r_early, s_rows, r_rows = [
        refs.pop(0) for _ in range(12)
    ]
    s_next, r_next = [refs.pop(0) for _ in range(2)]
    s_block, s_out, local = [refs.pop(0) for _ in range(3)]
    sems_hidden, sems_cot = refs[:3], refs[3:]
    spot = z, y, x, core = place()
    me = member(y, x, core)
    peers = plane_peers(y, x, core)
    size = tokens.shape[0]
    deep = stage.shape[1]
    wide = here.shape[2] // 4
    count_heads = state.shape[0]

    first = pltpu.make_async_copy(down.at[pl.ds(0, early.shape[1])], early.at[z], local.at[2])
    first.start()
    pack_columns(head_spots, heads, [stage])
    greet([(z, d) for d in peers] + [(lax.rem(z + n, 4), me) for n in range(1, 4)])
    mine = pl.ds(pl.multiple_of(me * deep, deep), deep)
    columns = [pl.ds(h * 2 * wide, 2 * wide) for h in range(2)]
    swaps = []
    for h, cols in enumerate(columns):
        copies = [
            remote(stage.at[d, :, cols], here.at[z, mine, cols], s_swap.at[h, n], r_swap.at[h, n], (z, d))
            for n, d in enumerate(peers)
        ]
        copies.append(pltpu.make_async_copy(stage.at[me, :, cols], here.at[z, mine, cols], local.at[5 * h]))
        swaps.append(copies)
    passing = note_copies(z, me, peers, note, notes, s_note, r_note)
    begin_rows, service_rows, finish_rows = plane_line_steps(spot, held, s_rows, r_rows)
    keep_rows = pltpu.make_async_copy(rows, held.at[z], local.at[1])
    keep_rows.start()
    half = early.shape[1] // 2
    begin_early, service_early, finish_early = plane_line_steps(
        spot, early.at[:, pl.ds(0, half)], s_early, r_early
    )
    begin_next, service_next, finish_next = plane_line_steps(
        spot, early.at[:, pl.ds(half, half)], s_next, r_next
    )
    for copy in swaps[0] + swaps[1] + passing:
        copy.start()
    first.wait()
    begin_early()
    notes[me] = note[...]
    lines = [
        plane_line_steps(spot, here.at[:, :, cols], s_line.at[h], r_line.at[h]) for h, cols in enumerate(columns)
    ]
    own[...] = normed(tokens[...].astype(jnp.float32))[0].astype(own.dtype)
    for copy in swaps[0]:
        copy.wait()
    lines[0][0]()
    service_early()
    pack_columns(unit_spots, units, [swap])
    rates = own_rates(decay, count_heads)
    fill_decay(base, rates)
    state[...] = jnp.zeros_like(state)
    for copy in swaps[1]:
        copy.wait()
    lines[1][0]()
    begin_hidden, relay_hidden, finish_hidden = gather_steps(spot, own, hidden, *sems_hidden)
    begin_cot, relay_cot, finish_cot = gather_steps(spot, cot, cots, *sems_cot)
    moves = [
        remote(swap.at[d], units_out.at[me], s_units.at[n], r_units.at[n], (z, d)) for n, d in enumerate(peers)
    ]
    moves.append(pltpu.make_async_copy(swap.at[me], units_out.at[me], local.at[3]))
    begin_hidden()
    relay_hidden()
    for copy in moves:
        copy.start()
    begin_cot()
    finish_early()
    for _, service, _ in lines:
        service()
    finish_hidden()
    for copy in passing:
        copy.wait()

    def fetch(b):
        return pltpu.make_async_copy(hidden.at[b], block.at[b % 2], s_block.at[b % 2])

    fetch(0).start()
    for _, _, finish_line in lines:
        finish_line()
    keep_weight = pltpu.make_async_copy(here, weight, local.at[4])
    keep_weight.start()
    keep_rows.wait()
    begin_rows()
    begin_next()

    def block_rows(b):
        return pl.ds(pl.multiple_of(b * size, size), size)

    def outs(b):
        return [
            pltpu.make_async_copy(src.at[at], dst.at[at], s_out.at[n, b])
            for n, (src, dst, at) in enumerate((
                (pre_here, pre, block_rows(b)),
                (mix_here, attn_gate, block_rows(b)),
                (qkv_here, qkv, block_rows(b)),
                (entering_here, entering, b),
            ))
        ]

    def mix(b):
        fetch(b).wait()

        @pl.when(b < 7)
        def _():
            fetch(b + 1).start()

        at_rows = block_rows(b)
        count = notes[b, :1, :1]
        out = by_planes(block, b % 2, here)
        pre_here[at_rows, :] = out[:, : 2 * wide]
        query = jax.nn.silu(out[:, :wide]).astype(jnp.bfloat16)
        keys = jax.nn.silu(out[:, wide : 2 * wide]).astype(jnp.bfloat16)
        value = out[:, 2 * wide : 3 * wide].astype(jnp.bfloat16)
        qkv_here[at_rows, :wide] = query
        qkv_here[at_rows, wide : 2 * wide] = keys
        qkv_here[at_rows, 2 * wide :] = value
        mix_here[at_rows, wide:] = out[:, 3 * wide :]
        entering_here[b] = state[...]
        total = jnp.zeros((8, size), jnp.float32)
        for t in range(count_heads):
            at = slice(t * HEAD_DIM, (t + 1) * HEAD_DIM)
            q, k, v = query[:, at], keys[:, at], value[:, at]
            live, behind, ahead, fade = block_tables(count, rates[t], size)
            probs = (matmul_nt(q, k) * jnp.where(live, base[t], 0.0)).astype(jnp.bfloat16)
            attn = matmul(probs, v) + behind * dot_fine(q, state[t], NN)
            mix_here[at_rows, at] = attn
            total += lax.dot_general(
                jnp.ones((8, HEAD_DIM), jnp.float32), attn * attn, (NT, ((), ())), precision=HIGH,
                preferred_element_type=jnp.float32,
            )
            local_state = dot_fine(k, v.astype(jnp.float32) * ahead, TN)
            stays = jnp.where(count < size, 0.0, 1.0)
            state[t] = stays * (fade * state[t] + local_state)
        squares[pl.ds(b, 1), :] = total[:1]
        for copy in outs(b):
            copy.start()

    pl.loop(0, 5)(mix)
    relay_cot()
    service_rows()
    service_next()
    pl.loop(5, 8)(mix)
    finish_rows()
    finish_next()
    for copy in moves:
        copy.wait()

    @pl.loop(0, 8)
    def _(b):
        for copy in outs(b):
            copy.wait()

    keep_weight.wait()
    finish_cot()


def open_attention(
    tokens, cot, heads, units, rows, down, note, decay, head_spots, unit_spots, columns, unit_columns, early, number
):
    size, width = tokens.shape
    deep = rows.shape[0]
    wide = columns // 4
    count = wide // HEAD_DIM
    f32, bf, dma = jnp.float32, tokens.dtype, pltpu.SemaphoreType.DMA
    outs = (
        ((8, size, width), bf),
        ((8, size, width), bf),
        ((4, 8 * deep, columns), bf),
        ((4, deep, width), bf),
        ((4, early, width), bf),
        ((8, deep, unit_columns), bf),
        ((8, *note.shape), note.dtype),
        ((8 * size, 2 * wide), f32),
        ((8 * size, 2 * wide), f32),
        ((8 * size, 3 * wide), bf),
        ((8, count, HEAD_DIM, HEAD_DIM), f32),
        ((8, size), f32),
    )
    return pl.pallas_call(
        functools.partial(open_kernel, head_spots, unit_spots),
        out_shape=[jax.ShapeDtypeStruct(*out) for out in outs],
        in_specs=[VMEM, ANY] + [VMEM] * 6 + [ANY, ANY, VMEM, SMEM],
        out_specs=[ANY] * 6 + [VMEM] + [ANY] * 4 + [VMEM],
        scratch_shapes=[
            pltpu.VMEM((8, deep, columns), bf),
            pltpu.VMEM((4, 8 * deep, columns), bf),
            pltpu.VMEM((8, deep, unit_columns), bf),
            pltpu.VMEM((size, width), bf),
            pltpu.VMEM((2, size, width), bf),
            pltpu.VMEM((8 * size, 2 * wide), f32),
            pltpu.VMEM((8 * size, 2 * wide), f32),
            pltpu.VMEM((8 * size, 3 * wide), bf),
            pltpu.VMEM((8, count, HEAD_DIM, HEAD_DIM), f32),
            pltpu.VMEM((count, size, size), f32),
            pltpu.VMEM((count, HEAD_DIM, HEAD_DIM), f32),
        ]
        + [dma((2, 7)) for _ in range(2)]
        + [dma((7,)) for _ in range(4)]
        + [dma((2, 4)) for _ in range(2)]
        + [dma((4,)) for _ in range(6)]
        + [dma((2,)), dma((4, 8)), dma((6,))]
        + GATHER_SEMAPHORES * 2,
        compiler_params=pltpu.CompilerParams(
            collective_id=number, has_side_effects=True, vmem_limit_bytes=VMEM_BYTES
        ),
        cost_estimate=pl.CostEstimate(flops=0, bytes_accessed=2**20, transcendentals=0),
        name=f"open_attention_{number}",
    )(tokens, cot, *heads, *units, rows, down, note, decay)


def collect_copies(z, me, peers, total, stage, local, send, recv):
    rows = stage.shape[1]

    def part(d):
        return total.at[pl.ds(pl.multiple_of(d * rows, rows), rows)]

    return [pltpu.make_async_copy(part(me), stage.at[me], local)] + [
        remote(part(d), stage.at[me], send.at[n], recv.at[n], (z, d)) for n, d in enumerate(peers)
    ]


COLLECT_SEMAPHORES = [pltpu.SemaphoreType.DMA] + [pltpu.SemaphoreType.DMA((7,)) for _ in range(2)]


def collect_kernel(total, stage, *sems):
    z, y, x, core = place()
    peers = plane_peers(y, x, core)
    greet([(z, d) for d in peers])
    copies = collect_copies(z, member(y, x, core), peers, total, stage, *sems)
    for copy in copies:
        copy.start()
    for copy in copies:
        copy.wait()


def plane_collect(total, number):
    rows = total.shape[0] // 8
    return pl.pallas_call(
        collect_kernel,
        out_shape=jax.ShapeDtypeStruct((8, rows, total.shape[1]), total.dtype),
        in_specs=[ANY],
        out_specs=ANY,
        scratch_shapes=COLLECT_SEMAPHORES,
        compiler_params=pltpu.CompilerParams(collective_id=number, has_side_effects=True),
        cost_estimate=pl.CostEstimate(flops=0, bytes_accessed=2**20, transcendentals=0),
        name=f"plane_collect_{number}",
    )(total)


def unpack_kernel(spots, stage, *grads):
    unpack_columns(spots, [stage], grads)


def unpack(stage, spots, columns, outputs):
    return pl.pallas_call(
        functools.partial(unpack_kernel, spots),
        out_shape=[jax.ShapeDtypeStruct((stage.shape[1], columns), jnp.float32) for _ in range(outputs)],
        in_specs=[VMEM],
        out_specs=[VMEM] * outputs,
        compiler_params=pltpu.CompilerParams(vmem_limit_bytes=VMEM_BYTES),
        name=f"unpack_{outputs}",
    )(stage)


PIECES = 5


def scatter_steps(spot, left, right_tile, left_rows, o_ref, buffers):
    to_mate, from_mate, stage, from_x, from_y, s_mate, r_mate, s_x, r_x, s_y, r_y = buffers
    z, y, x, core = spot
    rows, width = o_ref.shape
    tile = width // 4
    mate = member(y, x, 1 - core)
    on_x, on_y = member(y, 1 - x, core), member(1 - y, x, core)
    left_cols, right_cols = pl.ds(0, width // 2), pl.ds(width // 2, width // 2)

    def target(i, c):
        return member(other(y, 1 - i % 2), other(x, 1 - i // 2), c)

    def each_tile(block, use):
        part = left_rows(left, block) if left_rows else None
        here = pl.ds(pl.multiple_of(block * rows, rows), rows)

        @pl.loop(0, width // tile)
        def _(t):
            cols = pl.ds(pl.multiple_of(t * tile, tile), tile)
            use(t, cols, right_tile(part if left_rows else left[here, :], t, cols))

    def mate_copy(i):
        return remote(to_mate.at[i], from_mate.at[i], s_mate.at[i], r_mate.at[i], (z, mate))

    def send_x(i, n):
        cols = right_cols if n == 2 else left_cols
        return remote(stage.at[i, :, cols], from_x.at[n], s_x.at[n], r_x.at[n], (z, on_x))

    def send_y(i, n):
        cols = left_cols if n == 2 else right_cols
        return remote(stage.at[i, :, cols], from_y.at[n], s_y.at[n], r_y.at[n], (z, on_y))

    def give(i):
        def use(t, cols, total):
            to_mate[i, :, cols] = total.astype(jnp.bfloat16)

        each_tile(target(i, 1 - core), use)
        mate_copy(i).start()

    def add(i):
        def use(t, cols, total):
            pl.when(t == 0)(mate_copy(i).wait_recv)
            total = total + from_mate[i, :, cols].astype(jnp.float32)
            if i < 3:
                stage[i, :, cols] = total.astype(jnp.bfloat16)
            else:
                o_ref[:, cols] = total
            if i == 0:
                pl.when(t == width // tile // 2 - 1)(send_x(0, 0).start)

        each_tile(target(i, core), use)
        if i == 0:
            send_y(0, 0).start()
        if i == 1:
            send_x(1, 1).start()
        if i == 2:
            send_y(2, 1).start()

    def piece(n):
        if n < 4:
            give(n)
        if n > 0:
            add(n - 1)

    def begin():
        for n in range(PIECES):
            piece(n)

    def relay():
        send_y(0, 0).wait_recv()
        stage[1, :, right_cols] = (
            stage[1, :, right_cols].astype(jnp.float32) + from_y[0].astype(jnp.float32)
        ).astype(jnp.bfloat16)
        send_x(1, 2).start()
        send_x(0, 0).wait_recv()
        stage[2, :, left_cols] = (
            stage[2, :, left_cols].astype(jnp.float32) + from_x[0].astype(jnp.float32)
        ).astype(jnp.bfloat16)
        send_y(2, 2).start()

    def finish():
        send_x(1, 1).wait_recv()
        o_ref[:, left_cols] += from_x[1].astype(jnp.float32)
        send_y(2, 1).wait_recv()
        o_ref[:, right_cols] += from_y[1].astype(jnp.float32)
        send_x(1, 2).wait_recv()
        o_ref[:, right_cols] += from_x[2].astype(jnp.float32)
        send_y(2, 2).wait_recv()
        o_ref[:, left_cols] += from_y[2].astype(jnp.float32)

    def drain():
        for i in range(4):
            mate_copy(i).wait_send()
        for copy in (send_x(0, 0), send_x(1, 1), send_x(1, 2), send_y(0, 0), send_y(2, 1), send_y(2, 2)):
            copy.wait_send()

    return begin, piece, relay, finish, drain


def scatter_buffers(rows, width):
    shapes = [pltpu.VMEM((n, rows, width), jnp.bfloat16) for n in (4, 4, 3)]
    shapes += [pltpu.VMEM((3, rows, width // 2), jnp.bfloat16) for _ in range(2)]
    return shapes + [pltpu.SemaphoreType.DMA((n,)) for n in (4, 4, 3, 3, 3, 3)]


BUFFERS = 11


def own_row_copies(spot, packed, held, local, send, recv):
    z, y, x, core = spot
    planes, deep, wide = packed.shape
    rows = held.shape[0] // planes
    parts = held.shape[1] // wide
    mate = (z, member(y, x, 1 - core))
    copies = []
    for t in range(planes // 2):
        for n in range(parts):
            i = t * parts + n
            source = pl.ds(deep - (parts - n) * rows, rows)
            here = held.at[
                pl.ds(pl.multiple_of((2 * t + core) * rows, rows), rows), pl.ds(n * wide, wide)
            ]
            keep = packed.at[planes // 2 * core + t, source]
            give = packed.at[planes // 2 * (1 - core) + t, source]
            copies.append(pltpu.make_async_copy(keep, here, local.at[i]))
            copies.append(remote(give, here, send.at[i], recv.at[i], mate))
    return copies


def own_row_copies(spot, held, right, local, send, recv):
    z, y, x, core = spot
    planes, rows, _ = held.shape
    half = planes // 2
    mate = (z, member(y, x, 1 - core))
    copies = []
    for t in range(half):
        here = right.at[pl.ds(pl.multiple_of((2 * t + core) * rows, rows), rows)]
        copies.append(pltpu.make_async_copy(held.at[half * core + t], here, local.at[t]))
        copies.append(remote(held.at[half * (1 - core) + t], here, send.at[t], recv.at[t], mate))
    return copies


def turn_mid_kernel(
    left_in, held, squares, tokens, units, down, cot, middle, mid_out, scale_ref, weight, late, both, product, term, right,
    all_squares, columns, s_note, r_note, mid, total, here, block, both_here, product_here, cot_here, term_here,
    s_line, r_line, s_late, r_late, s_block, s_out, s_cot, s_term, local, right_here, s_row, r_row, left, *rest
):
    buffers, sems = rest[:BUFFERS], rest[BUFFERS:]
    spot = z, y, x, core = place()
    rows, width = middle.shape
    me = member(y, x, core)
    peers = plane_peers(y, x, core)
    wide = here.shape[2]
    tile = cot_here.shape[2]
    shard = pltpu.make_async_copy(units, here.at[z], local.at[0])
    shard.start()
    fetch_left = pltpu.make_async_copy(left_in, left, local.at[5])
    skip = down.shape[0] - late.shape[1]
    last = pltpu.make_async_copy(down.at[pl.ds(skip, late.shape[1])], late.at[z], local.at[1])
    greet([(z, d) for d in peers] + [(lax.rem(z + n, 4), me) for n in range(1, 4)])
    begin_line, service_line, finish_line = plane_line_steps(spot, here, s_line, r_line, units)
    begin_line()
    fetch_left.start()
    last.start()
    begin_late, service_late, finish_late = plane_line_steps(spot, late, s_late, r_late)
    notes = note_copies(z, me, peers, squares, all_squares, s_note, r_note)
    moves = own_row_copies(spot, held, right_here, local.at[pl.ds(3, 2)], s_row, r_row)
    for copy in notes + moves:
        copy.start()
    all_squares[me] = squares[...]
    shard.wait()
    for copy in notes:
        copy.wait_recv()
    scale = lax.rsqrt(jnp.sum(all_squares[...], axis=0) / width + EPS)
    scale_ref[...] = scale
    columns[...] = jnp.transpose(scale)

    def left_rows(left, block):
        here = pl.ds(pl.multiple_of(block * rows, rows), rows)
        deep = left.shape[1] // 2
        one = lax.broadcasted_iota(jnp.int32, columns.shape, 1) == block
        column = jnp.sum(jnp.where(one, columns[...], 0.0), axis=1, keepdims=True)
        return (left[here, :deep] * column * left[here, deep:]).astype(jnp.bfloat16)

    for copy in moves:
        copy.wait()
    right[...] = right_here[...]
    fetch_left.wait()

    def right_tile(part, t, cols):
        return matmul(part, right_here[:, cols])

    begin, _, relay, finish, drain = scatter_steps(spot, left, right_tile, left_rows, total, buffers)
    begin()
    relay()
    finish()
    value = tokens[...].astype(jnp.float32) + total[...]
    middle[...] = value
    mid[...] = normed(value)[0].astype(jnp.bfloat16)
    begin, relay, finish = gather_steps(spot, mid, mid_out, *sems)
    begin()
    drain()
    for copy in notes:
        copy.wait_send()
    last.wait()
    service_line()
    relay()
    finish()

    def fetch(b):
        return pltpu.make_async_copy(mid_out.at[b], block.at[b % 2], s_block.at[b % 2])

    def outs(b):
        at = pl.ds(pl.multiple_of(b * rows, rows), rows)
        return [
            pltpu.make_async_copy(both_here.at[b % 2], both.at[at], s_out.at[0, b % 2]),
            pltpu.make_async_copy(product_here.at[at], product.at[at], s_out.at[1, b % 2]),
        ]

    def fetch_cot(t):
        cols = pl.ds(pl.multiple_of(t * tile, tile), tile)
        return pltpu.make_async_copy(cot.at[:, cols], cot_here.at[t % 2], s_cot.at[t % 2])

    def leave_term(t):
        cols = pl.ds(pl.multiple_of(t * tile, tile), tile)
        return pltpu.make_async_copy(term_here.at[:, :, cols], term.at[:, :, cols], s_term.at[t])

    fetch(0).start()
    finish_line()
    keep = pltpu.make_async_copy(here, weight, local.at[2])
    keep.start()
    begin_late()

    def forward(b):
        fetch(b).wait()

        @pl.when(b < 7)
        def _():
            fetch(b + 1).start()

        @pl.when(b > 1)
        def _():
            for copy in outs(b - 2):
                copy.wait()

        out = by_planes(block, b % 2, here)
        both_here[b % 2] = out.astype(both_here.dtype)
        at = pl.ds(pl.multiple_of(b * rows, rows), rows)
        product_here[at, :] = (out[:, : wide // 2] * out[:, wide // 2 :]).astype(jnp.bfloat16)
        for copy in outs(b):
            copy.start()

    pl.loop(0, 7)(forward)
    service_late()
    fetch_cot(0).start()
    pl.loop(7, 8)(forward)

    @pl.loop(0, width // tile)
    def _(t):
        fetch_cot(t).wait()

        @pl.when(t + 1 < width // tile)
        def _():
            fetch_cot(t + 1).start()

        cols = pl.ds(pl.multiple_of(t * tile, tile), tile)
        out = matmul_tn(product_here[...], cot_here[t % 2]).astype(term.dtype)
        for g in range(4):
            term_here[g, :skip, cols] = out[g * skip : (g + 1) * skip]
            start = 4 * skip + g * late.shape[1]
            term_here[g, skip:, cols] = out[start : start + late.shape[1]]
        leave_term(t).start()

    for b in (6, 7):
        for copy in outs(b):
            copy.wait()
    for t in range(width // tile):
        leave_term(t).wait()
    keep.wait()
    finish_late()


def turn_mid(left, held, squares, tokens, units, down, cot, late, number):
    rows, width = tokens.shape
    wide = units.shape[1]
    tile = width // 4
    f32, bf, dma = jnp.float32, tokens.dtype, pltpu.SemaphoreType.DMA
    outs = (
        ((rows, width), f32),
        ((8, rows, width), bf),
        (squares.shape, f32),
        ((4, *units.shape), bf),
        ((4, late, width), bf),
        ((8 * rows, wide), bf),
        ((8 * rows, wide // 2), bf),
        ((4, wide // 8, width), bf),
        ((held.shape[0] * held.shape[1], width), bf),
    )
    return pl.pallas_call(
        turn_mid_kernel,
        out_shape=[jax.ShapeDtypeStruct(*out) for out in outs],
        in_specs=[ANY, ANY, VMEM, VMEM] + [ANY] * 3,
        out_specs=[VMEM, ANY, VMEM] + [ANY] * 5 + [VMEM],
        scratch_shapes=[
            pltpu.VMEM((8, *squares.shape), f32),
            pltpu.VMEM(squares.shape[::-1], f32),
            dma((7,)),
            dma((7,)),
            pltpu.VMEM((rows, width), bf),
            pltpu.VMEM((rows, width), f32),
            pltpu.VMEM((4, *units.shape), bf),
            pltpu.VMEM((2, rows, width), bf),
            pltpu.VMEM((2, rows, wide), bf),
            pltpu.VMEM((8 * rows, wide // 2), bf),
            pltpu.VMEM((2, 8 * rows, tile), bf),
            pltpu.VMEM((4, wide // 8, width), bf),
        ]
        + [dma((4,)) for _ in range(4)]
        + [dma((2,)), dma((2, 2)), dma((2,)), dma((4,)), dma((6,))]
        + [pltpu.VMEM((held.shape[0] * held.shape[1], width), bf), dma((2,)), dma((2,))]
        + [pltpu.VMEM(left.shape, f32)]
        + scatter_buffers(rows, width)
        + GATHER_SEMAPHORES,
        compiler_params=pltpu.CompilerParams(
            collective_id=number, has_side_effects=True, vmem_limit_bytes=VMEM_BYTES
        ),
        cost_estimate=pl.CostEstimate(flops=0, bytes_accessed=2**20, transcendentals=0),
        name=f"turn_mid_{number}",
    )(left, held, squares, tokens, units, down, cot)


def turn_back_kernel(
    left, right, middle, tokens, cot, grad_middle, low_out, inners,
    inner, s_note, r_note, low, total, left_here, right_here, middle_here, tokens_here, cot_here, s_left, s_in, *rest
):
    buffers, sems = rest[:BUFFERS], rest[BUFFERS:]
    spot = z, y, x, core = place()
    rows, width = grad_middle.shape
    me = member(y, x, core)
    peers = plane_peers(y, x, core)

    def fetch(block):
        here = pl.ds(pl.multiple_of(block * rows, rows), rows)
        return pltpu.make_async_copy(left.at[here], left_here.at[here], s_left.at[block])

    pairs = ((right, right_here), (middle, middle_here), (tokens, tokens_here), (cot, cot_here))
    whole = [pltpu.make_async_copy(src, dst, s_in.at[n]) for n, (src, dst) in enumerate(pairs)]
    blocks = [
        fetch(member(other(y, 1 - way % 2), other(x, 1 - way // 2), other(core, other_core)))
        for way in range(4) for other_core in (1, 0)
    ]
    for copy in blocks[:1] + whole[:1] + blocks[1:3]:
        copy.start()
    greet([(z, d) for d in peers])
    whole[0].wait()
    for copy in blocks[3:] + whole[1:]:
        copy.start()

    def left_rows(left, block):
        fetch(block).wait()
        return left_here[pl.ds(pl.multiple_of(block * rows, rows), rows), :]

    def right_tile(part, t, cols):
        return matmul_nt(part, right_here[cols, :])

    begin, _, relay, finish, drain = scatter_steps(spot, left, right_tile, left_rows, total, buffers)
    begin()
    relay()
    finish()
    for copy in whole[1:]:
        copy.wait()
    value = middle_here[...]
    grad = cot_here[...].astype(jnp.float32) + norm_back(value, normed(value)[1], total[...])
    grad_middle[...] = grad
    low[...] = grad.astype(jnp.bfloat16)
    begin, relay, finish = gather_steps(spot, low, low_out, *sems)
    begin()
    added = value - tokens_here[...].astype(jnp.float32)
    inner[...] = lax.dot_general(
        jnp.ones((8, width), jnp.float32), low[...].astype(jnp.float32) * added, (NT, ((), ())), precision=HIGH,
        preferred_element_type=jnp.float32,
    )
    notes = note_copies(z, me, peers, inner, inners, s_note, r_note)
    for copy in notes:
        copy.start()
    inners[me] = inner[...]
    drain()
    relay()
    finish()
    for copy in notes:
        copy.wait()


def turn_back(left, right, middle, tokens, cot, number):
    rows, width = tokens.shape
    f32, bf = jnp.float32, tokens.dtype
    grad_middle, low, inner = pl.pallas_call(
        turn_back_kernel,
        out_shape=[
            jax.ShapeDtypeStruct((rows, width), f32),
            jax.ShapeDtypeStruct((8, rows, width), bf),
            jax.ShapeDtypeStruct((8, 8, rows), f32),
        ],
        in_specs=[ANY] * 5,
        out_specs=[VMEM, ANY, VMEM],
        scratch_shapes=[
            pltpu.VMEM((8, rows), f32),
            pltpu.SemaphoreType.DMA((7,)),
            pltpu.SemaphoreType.DMA((7,)),
            pltpu.VMEM((rows, width), bf),
            pltpu.VMEM((rows, width), f32),
            pltpu.VMEM(left.shape, bf),
            pltpu.VMEM(right.shape, bf),
            pltpu.VMEM((rows, width), f32),
            pltpu.VMEM((rows, width), bf),
            pltpu.VMEM((rows, width), bf),
            pltpu.SemaphoreType.DMA((8,)),
            pltpu.SemaphoreType.DMA((4,)),
        ]
        + scatter_buffers(rows, width)
        + GATHER_SEMAPHORES,
        compiler_params=pltpu.CompilerParams(
            collective_id=number, has_side_effects=True, vmem_limit_bytes=VMEM_BYTES
        ),
        cost_estimate=pl.CostEstimate(flops=0, bytes_accessed=2**20, transcendentals=0),
        name=f"turn_back_{number}",
    )(left, right, middle, tokens, cot)
    return grad_middle, low.reshape(8 * rows, width), inner


def tail_kernel(left, right, units, o_ref, stage, *rest):
    buffers, sems = rest[:BUFFERS], rest[BUFFERS:]
    spot = z, y, x, core = place()
    peers = plane_peers(y, x, core)
    greet([(z, d) for d in peers])
    copies = collect_copies(z, member(y, x, core), peers, units, stage, *sems)

    def right_tile(part, t, cols):
        return matmul_nt(part, right[cols, :])

    begin, _, relay, finish, drain = scatter_steps(spot, left, right_tile, None, o_ref, buffers)
    begin()
    for copy in copies:
        copy.start()
    relay()
    finish()
    drain()
    for copy in copies:
        copy.wait()


def plane_tail(left, right, units, number):
    rows, width = left.shape[0] // 8, right.shape[0]
    return pl.pallas_call(
        tail_kernel,
        out_shape=[
            jax.ShapeDtypeStruct((rows, width), jnp.float32),
            jax.ShapeDtypeStruct((8, units.shape[0] // 8, units.shape[1]), units.dtype),
        ],
        in_specs=[VMEM, VMEM, ANY],
        out_specs=[VMEM, ANY],
        scratch_shapes=scatter_buffers(rows, width) + COLLECT_SEMAPHORES,
        compiler_params=pltpu.CompilerParams(
            collective_id=number, has_side_effects=True, vmem_limit_bytes=VMEM_BYTES
        ),
        cost_estimate=pl.CostEstimate(flops=0, bytes_accessed=2**20, transcendentals=0),
        name=f"plane_tail_{number}",
    )(left, right, units)


SIDE = 512


def side_tiles(left, right, out, leave):
    @pl.loop(0, left.shape[1] // SIDE)
    def _(t):
        cols = pl.ds(pl.multiple_of(t * SIDE, SIDE), SIDE)
        out[cols, :] = matmul_tn(left[:, cols], right[...]).astype(out.dtype)
        leave(t).start()


def units_back_kernel(early, late, cot, both, mid, grads, term, whole, weight, sems):
    step = pl.program_id(0)
    rows = cot.shape[0]
    units = weight.shape[0]

    @pl.when(step == 0)
    def _():
        count = early.shape[0]
        parts = ((early, weight.at[pl.ds(0, count)]), (late, weight.at[pl.ds(count, late.shape[0])]))
        copies = [pltpu.make_async_copy(src, dst, sems.at[n]) for n, (src, dst) in enumerate(parts)]
        for copy in copies:
            copy.start()
        for copy in copies:
            copy.wait()

    @pl.when(step < 4)
    def _():
        grad = matmul_nt(cot[...], weight[...])
        here = pl.ds(pl.multiple_of(step * rows, rows), rows)
        pair = both[...].astype(jnp.float32)
        left = (grad * pair[:, units:]).astype(jnp.bfloat16)
        right = (grad * pair[:, :units]).astype(jnp.bfloat16)
        grads[:, :units] = left
        grads[:, units:] = right
        whole[here, :units] = left
        whole[here, units:] = right

    @pl.when(step >= 4)
    def _():
        term[...] = matmul_tn(mid[...], whole[...]).astype(term.dtype)


def units_back(early, late, cot, both, mid):
    height, width = cot.shape
    wide = both.shape[1]
    rows, tile = height // 4, width // 4
    bf = jnp.bfloat16
    return pl.pallas_call(
        units_back_kernel,
        grid=(8,),
        out_shape=[
            jax.ShapeDtypeStruct((height, wide), bf),
            jax.ShapeDtypeStruct((width, wide), bf),
        ],
        in_specs=[
            ANY,
            ANY,
            pl.BlockSpec((rows, width), lambda s: (jnp.minimum(s, 3), 0)),
            pl.BlockSpec((rows, wide), lambda s: (jnp.minimum(s, 3), 0)),
            pl.BlockSpec((height, tile), lambda s: (0, jnp.maximum(s - 4, 0))),
        ],
        out_specs=[
            pl.BlockSpec((rows, wide), lambda s: (jnp.minimum(s, 3), 0)),
            pl.BlockSpec((tile, wide), lambda s: (jnp.maximum(s - 4, 0), 0)),
        ],
        scratch_shapes=[
            pltpu.VMEM((height, wide), bf),
            pltpu.VMEM((wide // 2, width), bf),
            pltpu.SemaphoreType.DMA((2,)),
        ],
        compiler_params=pltpu.CompilerParams(
            dimension_semantics=("arbitrary",), vmem_limit_bytes=VMEM_BYTES
        ),
        cost_estimate=pl.CostEstimate(
            flops=2 * cot.size * wide * 3 // 2, bytes_accessed=2**25, transcendentals=0
        ),
        name="units_back",
    )(early, late, cot, both, mid)


def dot_fine(left, right, dims):
    high = right.astype(jnp.bfloat16)
    low = (right - high.astype(jnp.float32)).astype(jnp.bfloat16)
    product = functools.partial(
        lax.dot_general, dimension_numbers=(dims, ((), ())), preferred_element_type=jnp.float32
    )
    return product(left, high) + product(left, low)


NN, NT, TN = ((1,), (0,)), ((1,), (1,)), ((0,), (0,))


def block_tables(count, rate, rows):
    spot = lax.broadcasted_iota(jnp.int32, (rows, 1), 0)
    live = spot < count
    behind = jnp.where(live, jnp.exp(-rate * spot.astype(jnp.float32)), 0.0)
    ahead = jnp.where(live, jnp.exp(-rate * (count - spot).astype(jnp.float32)), 0.0)
    fade = jnp.exp(jnp.full((1, HEAD_DIM), -rate * count.astype(jnp.float32), jnp.float32))
    return live, behind, ahead, fade


def fill_decay(base, rates):
    heads, rows, _ = base.shape
    gap = lax.broadcasted_iota(jnp.int32, (rows, rows), 0) - lax.broadcasted_iota(jnp.int32, (rows, rows), 1)
    far = jnp.maximum(gap, 0).astype(jnp.float32)
    for t in range(heads):
        base[t] = jnp.where(gap >= 0, jnp.exp(-rates[t] * far), 0.0)


def own_rates(decay, heads):
    _, y, x, core = place()
    return [decay[4 * (heads * core + t) + 2 * y + x] for t in range(heads)]


def unmix_kernel(
    counts, decay, low, weight, pre, attn_gate, qkv, entering, scale, inner, product, early, late, hidden,
    grads_out, out_term, term_out, down_out,
    base, state, total, product_here, down_here, hidden_here, grads, term, down_own, s_in, s_out, *buffers
):
    step = pl.program_id(0)
    steps = pl.num_programs(0)
    b = steps - 1 - step
    rows, width = low.shape
    wide = weight.shape[0]
    rates = own_rates(decay, state.shape[0])
    spot = z, y, x, core = place()
    fetch = [
        pltpu.make_async_copy(src, dst, s_in.at[n])
        for n, (src, dst) in enumerate((
            (product, product_here),
            (early, down_here.at[pl.ds(0, early.shape[0])]),
            (late, down_here.at[pl.ds(early.shape[0], late.shape[0])]),
            (hidden, hidden_here),
        ))
    ]
    leave = [
        pltpu.make_async_copy(src, dst, s_out.at[n])
        for n, (src, dst) in enumerate(((grads, grads_out), (down_own, down_out)))
    ]

    def leave_term(t):
        at = pl.ds(pl.multiple_of(t * SIDE, SIDE), SIDE)
        return pltpu.make_async_copy(term.at[at], term_out.at[at], s_out.at[2 + t])


    def right_tile(part, t, cols):
        return matmul(part, down_here[:, cols])

    _, piece, relay, finish, drain = scatter_steps(spot, product_here, right_tile, None, down_own, buffers)

    @pl.when(step == 0)
    def _():
        for copy in fetch[:3]:
            copy.start()
        fill_decay(base, rates)
        state[...] = jnp.zeros_like(state)
        total[...] = jnp.zeros_like(total)
        greet([(z, d) for d in plane_peers(y, x, core)])
        for copy in fetch[:3]:
            copy.wait()

    for n in range(PIECES):
        pl.when(step == n // 2)(functools.partial(piece, n))
    pl.when(step == 1)(fetch[3].start)

    count = counts[b, 0]

    def column(ref):
        here = lax.broadcasted_iota(jnp.int32, (8, rows), 0) == b
        turned = jnp.transpose(jnp.where(here, ref, 0.0))
        return jnp.sum(turned, axis=1, keepdims=True)

    here = pl.ds(pl.multiple_of(b * rows, rows), rows)
    factor, inside = column(scale[...]), column(inner[:, 0])
    attn, gate = attn_gate[:, :wide], attn_gate[:, wide:]
    normal = attn * factor
    grad = matmul_nt(low[...], weight[...])
    grads[here, 3 * wide :] = (grad * normal).astype(jnp.bfloat16)
    grad_attn = (factor * grad * gate - normal * factor * inside * (1.0 / width)).astype(jnp.bfloat16)
    total[...] += matmul_tn((normal * gate).astype(jnp.bfloat16), low[...])
    for t in range(state.shape[0]):
        at = slice(t * HEAD_DIM, (t + 1) * HEAD_DIM)
        q, k, v = (qkv[:, i * wide + t * HEAD_DIM : i * wide + (t + 1) * HEAD_DIM] for i in range(3))
        g = grad_attn[:, at]
        live, behind, ahead, fade = block_tables(count, rates[t], rows)
        mask = jnp.where(live, base[t], 0.0)
        probs = (matmul_nt(q, k) * mask).astype(jnp.bfloat16)
        raw = (matmul_nt(g, v) * mask).astype(jnp.bfloat16)
        leaving = jnp.where(count < rows, 0.0, state[t])
        grad_q = matmul(raw, k) + behind * dot_fine(g, entering[0, t], NT)
        grad_k = matmul_tn(raw, q) + ahead * dot_fine(v, leaving, NT)
        grad_v = matmul_tn(probs, g) + ahead * dot_fine(k, leaving, NN)
        state[t] = dot_fine(q, g.astype(jnp.float32) * behind, TN) + fade * leaving
        grads[here, at] = (grad_q * silu_slope(pre[:, at])).astype(jnp.bfloat16)
        after = slice(wide + t * HEAD_DIM, wide + (t + 1) * HEAD_DIM)
        grads[here, after] = (grad_k * silu_slope(pre[:, after])).astype(jnp.bfloat16)
        grads[here, 2 * wide + t * HEAD_DIM : 2 * wide + (t + 1) * HEAD_DIM] = grad_v.astype(jnp.bfloat16)

    @pl.when(step == 4)
    def _():
        relay()

    @pl.when(step == steps - 1)
    def _():
        leave[0].start()
        out_term[...] = total[...].astype(jnp.bfloat16)
        fetch[3].wait()
        side_tiles(hidden_here, grads, term, leave_term)
        finish()
        leave[1].start()
        drain()
        for copy in leave:
            copy.wait()
        for t in range(term.shape[0] // SIDE):
            leave_term(t).wait()


def unmix_heads(counts, decay, low, weight, pre, attn_gate, qkv, entering, scale, inner, product, early, late, hidden, number):
    rows, width = low.shape[0] // 8, low.shape[1]
    wide = weight.shape[0]
    heads = wide // HEAD_DIM
    f32, bf = jnp.float32, jnp.bfloat16

    def by_block(columns):
        return pl.BlockSpec((rows, columns), lambda s: (7 - s, 0))

    def whole(*shape):
        return pl.BlockSpec(shape, lambda s: (0,) * len(shape))

    return pl.pallas_call(
        unmix_kernel,
        grid=(8,),
        out_shape=[
            jax.ShapeDtypeStruct((8 * rows, 4 * wide), bf),
            jax.ShapeDtypeStruct((wide, width), bf),
            jax.ShapeDtypeStruct((hidden.shape[1], 4 * wide), bf),
            jax.ShapeDtypeStruct((rows, width), f32),
        ],
        in_specs=[
            SMEM,
            SMEM,
            by_block(width),
            whole(wide, width),
            by_block(2 * wide),
            by_block(2 * wide),
            by_block(3 * wide),
            pl.BlockSpec((1, heads, HEAD_DIM, HEAD_DIM), lambda s: (7 - s, 0, 0, 0)),
            whole(8, rows),
            whole(8, 8, rows),
            ANY,
            ANY,
            ANY,
            ANY,
        ],
        out_specs=[ANY, whole(wide, width), ANY, ANY],
        scratch_shapes=[
            pltpu.VMEM((heads, rows, rows), f32),
            pltpu.VMEM((heads, HEAD_DIM, HEAD_DIM), f32),
            pltpu.VMEM((wide, width), f32),
            pltpu.VMEM(product.shape, bf),
            pltpu.VMEM((product.shape[1], width), bf),
            pltpu.VMEM(hidden.shape, bf),
            pltpu.VMEM((8 * rows, 4 * wide), bf),
            pltpu.VMEM((hidden.shape[1], 4 * wide), bf),
            pltpu.VMEM((rows, width), f32),
            pltpu.SemaphoreType.DMA((4,)),
            pltpu.SemaphoreType.DMA((2 + hidden.shape[1] // SIDE,)),
        ]
        + scatter_buffers(rows, width),
        compiler_params=pltpu.CompilerParams(
            collective_id=number,
            has_side_effects=True,
            dimension_semantics=("arbitrary",),
            vmem_limit_bytes=VMEM_BYTES,
        ),
        cost_estimate=pl.CostEstimate(flops=0, bytes_accessed=2**20, transcendentals=0),
        name="unmix_heads",
    )(counts, decay, low, weight, pre, attn_gate, qkv, entering, scale, inner, product, early, late, hidden)


def after(value, *others):
    return lax.optimization_barrier((value, *others))[0]


def fast_plan(
    tokens,
    block_counts,
    decay_rate,
    query_weight,
    key_weight,
    value_weight,
    gate_weight,
    out_weight,
    first_weight,
    second_weight,
    down_weight,
    cotangent,
):
    rows, width = tokens.shape
    nz = lax.axis_size("dp")
    nf = lax.axis_size("fsdp")
    chips = nf // 2
    plane = lax.axis_index("fsdp")
    core = plane % 2
    bf = jnp.bfloat16
    half = HEADS // nf
    own = half * HEAD_DIM
    units = first_weight.shape[1] // nf

    head_spots = tuple(
        (2 * c + k, n, HEAD_DIM * (chips * (half * k + t) + c), 0, n * own + t * HEAD_DIM, HEAD_DIM)
        for c in range(chips) for k in range(2) for n in range(4) for t in range(half)
    )
    run = units // nz
    early = 64
    unit_spots = tuple(
        (f, n, run * (nf * g + f) + skip, 0, n * units + nz * skip + g * wide, wide)
        for f in range(nf) for n in range(2) for g in range(nz) for skip, wide in ((0, early), (early, run - early))
    )
    swap = [(i, i ^ 1) for i in range(nf)]

    def uncross(x):
        keep = lax.dynamic_index_in_dim(x, core, 1, False)
        send = lax.dynamic_index_in_dim(x, 1 - core, 1, False)
        got = lax.ppermute(send, "fsdp", swap)
        return jnp.concatenate([jnp.where(core == 0, keep, got), jnp.where(core == 0, got, keep)], axis=0)

    note = jnp.broadcast_to(block_counts, (8, 128))
    hidden, cot, w_heads, out_rows, wd_early, w_units, counts, pre, attn_gate, qkv, entering, squares = open_attention(
        tokens, cotangent, (query_weight, key_weight, value_weight, gate_weight), (first_weight, second_weight),
        out_weight, down_weight, note, decay_rate, head_spots, unit_spots, 4 * own, 2 * units, early, 0,
    )
    hidden, cot, wd_early = (a.reshape(-1, width) for a in (hidden, cot, wd_early))
    w_heads = w_heads.reshape(-1, 4 * own)
    counts = counts[:, 0]
    middle, mid, scale, w_units, wd_late, both, product, down_term, wo = turn_mid(
        attn_gate, out_rows, squares, tokens, w_units.reshape(-1, 2 * units), down_weight, cot, run - early, 2
    )
    down_term = down_term.reshape(units, width)
    mid, wd_late = mid.reshape(-1, width), wd_late.reshape(-1, width)
    w_units = w_units.reshape(-1, 2 * units)
    inputs = tokens.astype(jnp.float32)
    down_sum = lax.psum_scatter(down_term, "dp", scatter_dimension=0, tiled=True)
    grad_units, units_term = units_back(wd_early, wd_late, cot, both, mid)
    units_sum = lax.psum_scatter(units_term, "dp", scatter_dimension=0, tiled=True)
    grad_middle, low, inner = turn_back(grad_units, w_units, middle, tokens, cotangent, 3)
    grad_heads, out_term, heads_term, down_own = unmix_heads(
        counts, decay_rate, after(low, down_sum), wo, pre, attn_gate, qkv, entering, scale, inner, product, wd_early, wd_late, hidden, 4
    )
    block_out = (middle + down_own).astype(bf)
    heads_sum = lax.psum_scatter(heads_term, "dp", scatter_dimension=0, tiled=True)
    out_term = uncross(out_term.reshape(half, 2, -1, width))
    out_sum = lax.psum_scatter(out_term, "dp", scatter_dimension=0, tiled=False)
    grad_hidden, units_grad = plane_tail(after(grad_heads, out_term), w_heads, units_sum, 5)
    tokens_grad = grad_middle + norm_back(inputs, normed(inputs)[1], grad_hidden)
    down_grad = down_sum.astype(jnp.float32)
    first_grad, second_grad = unpack(units_grad, unit_spots, nf * units, 2)
    heads_sum = after(heads_sum, first_grad, grad_hidden)
    heads_grad = plane_collect(heads_sum, 7)
    grads = unpack(heads_grad, head_spots, width, 4)
    out_grad = after(out_sum, *grads).astype(jnp.float32)
    return (block_out, tokens_grad, *grads, out_grad, first_grad, second_grad, down_grad)


def fits(mesh):
    return mesh.shape["dp"] == 4 and mesh.shape["fsdp"] == 8


def solution(mesh):
    return jax.shard_map(
        fast_plan if fits(mesh) else shards,
        mesh=mesh,
        in_specs=(
            P(("dp", "fsdp"), None),
            P("dp", "fsdp"),
            P(),
            P(("dp", "fsdp"), None),
            P(("dp", "fsdp"), None),
            P(("dp", "fsdp"), None),
            P(("dp", "fsdp"), None),
            P(("dp", "fsdp"), None),
            P(("dp", "fsdp"), None),
            P(("dp", "fsdp"), None),
            P(("dp", "fsdp"), None),
            P(("dp", "fsdp"), None),
        ),
        out_specs=(
            P(("dp", "fsdp"), None),
            P(("dp", "fsdp"), None),
            P(("dp", "fsdp"), None),
            P(("dp", "fsdp"), None),
            P(("dp", "fsdp"), None),
            P(("dp", "fsdp"), None),
            P(("dp", "fsdp"), None),
            P(("dp", "fsdp"), None),
            P(("dp", "fsdp"), None),
            P(("dp", "fsdp"), None),
        ),
        check_vma=False,
    )
```
